32 devices in a mesh: dp: 8 (over z, x), seq: 4 (over y, core).
Axes of the slice: x: 2, y: 2, z: 4, core: 2. Of those that a mesh axis runs over, the one named last changes fastest.
Arguments:
- tokens_in: bfloat16 [2, 8, 1024, 512], P(None, 'dp', 'seq'), may hold values from -6 to 6
- grad_output: bfloat16 [2, 8, 1024, 512], P(None, 'dp', 'seq'), may hold values from -6 to 6
- prefix_len: int32 [2, 8], P(None, 'dp'), may hold values from 0 to 511
- w_qkv: bfloat16 [2, 512, 1536], P(None, ('dp', 'seq')), may hold values from -0.25 to 0.25
- w_out: bfloat16 [2, 512, 512], P(None, ('dp', 'seq')), may hold values from -0.75 to 0.75
- w_up: bfloat16 [2, 512, 2048], P(None, ('dp', 'seq')), may hold values from -0.25 to 0.25
- w_down: bfloat16 [2, 2048, 512], P(None, ('dp', 'seq')), may hold values from -0.125 to 0.125
- norm_gains: bfloat16 [2, 2, 512], P(None, None, ('dp', 'seq')), may hold values from 0.5 to 1.5
- bias_rows: bfloat16 [2, 6, 512], P(None, None, ('dp', 'seq')), may hold values from -1.5 to 1.5
- up_bias: bfloat16 [2, 2048], P(None, ('dp', 'seq')), may hold values from -1.5 to 1.5
Outputs:
- out_act: bfloat16 [2, 8, 1024, 512], P(None, 'dp', 'seq')
- grad_in: float32 [2, 8, 1024, 512], P(None, 'dp', 'seq')
- grad_qkv: float32 [2, 512, 1536], P(None, ('dp', 'seq'))
- grad_wout: float32 [2, 512, 512], P(None, ('dp', 'seq'))
- grad_wup: float32 [2, 512, 2048], P(None, ('dp', 'seq'))
- grad_wdown: float32 [2, 2048, 512], P(None, ('dp', 'seq'))
- grad_gains: float32 [2, 2, 512], P(None, None, ('dp', 'seq'))
- grad_biases: float32 [2, 6, 512], P(None, None, ('dp', 'seq'))
- grad_upbias: float32 [2, 2048], P(None, ('dp', 'seq'))
The draws below stay inside these ranges and needn't reach their ends.
Inputs may be any that keep to these rules, and one draw needn't show every extreme that they name: `prefix_len`: the number of leading positions of a row whose incoming gradient is zero.
All inputs are finite; a program needn't handle non-finite values.
Results may differ from the reference program's by a relative error of at most 0.009.
Values may be sent and summed in bfloat16 or wider, within the bound.
A program may use at most 320 MiB of HBM per device.

```python
from functools import reduce
import jax
import jax.numpy as jnp
from jax import lax

D = 512
HDIM = 64
FF = 2048
BLOCK = 16
LEVELS = 6
LAYERS = 2
MICRO = 2
SEQ_LEN = 1024
ROWS_ALL = 8


def touch_ends(array, key, smallest, high):
    dims = array.shape
    place = [jax.random.randint(jax.random.fold_in(key, axis), (), 0, dims[axis]) for axis in range(len(dims))]
    array = array.at[tuple(place)].set(smallest)
    longest = dims.index(max(dims))
    place[longest] = (place[longest] + 1) % dims[longest]
    return array.at[tuple(place)].set(high)


def level_of(key, extent, shards, low, top_value):
    level, own = 1.0, jax.random.fold_in(key, 6)
    for dim, blocks in shards:
        heights = jnp.exp(jax.random.uniform(jax.random.fold_in(own, dim), (blocks,), jnp.float32, low / len(shards), top_value / len(shards)))
        level = level * jnp.repeat(heights, extent[dim] // blocks).reshape([-1 if axis == dim else 1 for axis in range(len(extent))])
    return level


def gaussian(own_key, extent, scale, most, pieces=(), held_as=jnp.bfloat16):
    values = jax.random.normal(own_key, extent, jnp.float32) * scale
    if len(pieces) > 0:
        values = level_of(own_key, extent, pieces, -0.22, 0.18) * values
    return jnp.clip(values, min=-most, max=most).astype(held_as)


def setup_inputs(seed: int = 0) -> dict:
    key_of = jax.random.split(jax.random.key(seed), 11)
    return {
        "tokens_in": gaussian(key_of[0], (MICRO, ROWS_ALL, SEQ_LEN, D), 1.0, 6.0, ((1, 8), (2, 4))),
        "grad_output": gaussian(key_of[1], (MICRO, ROWS_ALL, SEQ_LEN, D), 1.0, 6.0, ((1, 8), (2, 4))),
        "prefix_len": touch_ends(jax.random.randint(key_of[2], (MICRO, ROWS_ALL), 0, SEQ_LEN // 2), jax.random.fold_in(key_of[2], 1), 0, (SEQ_LEN // 2) - 1).astype(jnp.int32),
        "w_qkv": gaussian(key_of[3], (LAYERS, D, 3 * D), D ** -0.5, 0.25, ((1, 32),)),
        "w_out": gaussian(key_of[4], (LAYERS, D, D), HDIM ** -0.5, 0.75, ((1, 32),)),
        "w_up": gaussian(key_of[5], (LAYERS, D, FF), D ** -0.5, 0.25, ((1, 32),)),
        "w_down": gaussian(key_of[6], (LAYERS, FF, D), FF ** -0.5, 0.125, ((1, 32),)),
        "norm_gains": jnp.clip(1.0 + 0.1 * jax.random.normal(key_of[7], (LAYERS, 2, D), jnp.float32), 0.5, 1.5).astype(jnp.bfloat16),
        "bias_rows": gaussian(key_of[8], (LAYERS, 6, D), 0.3, 1.5, ((2, 32),)),
        "up_bias": gaussian(key_of[9], (LAYERS, FF), 0.3, 1.5, ((1, 32),)),
    }


@jax.custom_vjp
def low(v):
    return lax.optimization_barrier(v.astype(jnp.bfloat16)).astype(jnp.float32)

@jax.custom_vjp
def low_back(v):
    return v

def low_keep(v):
    return (low(v), None)

def low_pass(kept, grad):
    return (grad,)

def back_keep(v):
    return (v, None)

def back_low(kept, grad):
    return (low(grad),)
low.defvjp(low_keep, low_pass)
low_back.defvjp(back_keep, back_low)
highest = lax.Precision.HIGHEST

def layer_norm(values, gain, shift):
    centred = values - lax.optimization_barrier(jnp.mean(values, axis=-1, keepdims=True))
    spread = lax.optimization_barrier(jnp.mean(centred * centred, axis=-1, keepdims=True))
    return centred * lax.rsqrt(spread + 1e-05) * gain + shift

def coarsen(field):
    return 0.5 * (field[0::2] + field[1::2])

def windows(field):
    blocks = field.shape[0] // BLOCK
    padded = jnp.pad(field, ((BLOCK, BLOCK), (0, 0), (0, 0)))
    stacked = padded.reshape(blocks + 2, BLOCK, field.shape[1], field.shape[2])
    return jnp.concatenate([stacked[:-2], stacked[1:-1], stacked[2:]], axis=1)

def key_mask(blocks, offset, total, level_id):
    places = jnp.arange(3 * BLOCK, dtype=jnp.int32) // BLOCK
    owners = jnp.arange(blocks, dtype=jnp.int32)[:, None] + offset + places[None, :] - 1
    inside = (owners >= 0) & (owners < total)
    if level_id > 0:
        inside = inside & (places[None, :] != 1)
    return inside

def weigh(scores, inside, factor):
    masked = jnp.where(inside, scores, -1e+30)
    peak_rows = lax.optimization_barrier(jnp.max(masked, axis=-1))
    weights = jnp.where(inside, jnp.exp(masked - peak_rows[..., None]), 0.0)
    return (weights, peak_rows, factor * lax.optimization_barrier(jnp.sum(weights, axis=-1)))

def combine(numers, maxima, level_sums, axis):
    stretched = [jnp.repeat(piece_max, 2 ** level_id, axis=axis) for level_id, piece_max in enumerate(maxima)]
    summit = reduce(jnp.maximum, stretched)
    numerator = jnp.zeros_like(numers[0])
    denominator = jnp.zeros_like(maxima[0])
    for level_id in range(len(numers)):
        scaling = jnp.exp(stretched[level_id] - summit)
        numerator = numerator + scaling[..., None] * jnp.repeat(numers[level_id], 2 ** level_id, axis=axis)
        denominator = denominator + scaling * jnp.repeat(level_sums[level_id], 2 ** level_id, axis=axis)
    return numerator / denominator[..., None]

def hierarchy(queries, key_rows, value_rows):
    head_count, head_width = (queries.shape[1], queries.shape[2])
    scaling = head_width ** (-0.5)
    numers, maxima, level_sums = ([], [], [])
    for level_id in range(LEVELS):
        if level_id > 0:
            queries = low(coarsen(queries))
            key_rows = low(coarsen(key_rows))
            value_rows = low(coarsen(value_rows))
        factor = 2.0 ** level_id
        blocks = queries.shape[0] // BLOCK
        query_blocks = queries.reshape(blocks, BLOCK, head_count, head_width)
        scores = low_back(jnp.einsum('bihd,bjhd->bhij', query_blocks, windows(key_rows), precision=highest) * scaling)
        inside = key_mask(blocks, 0, blocks, level_id)[:, None, None, :]
        weights, peak_rows, totals = weigh(scores, inside, factor)
        numer_blk = low_back(factor * jnp.einsum('bhij,bjhd->bihd', low(weights), windows(value_rows), precision=highest))
        numers.append(numer_blk.reshape(blocks * BLOCK, head_count, head_width))
        maxima.append(peak_rows.transpose(0, 2, 1).reshape(blocks * BLOCK, head_count))
        level_sums.append(totals.transpose(0, 2, 1).reshape(blocks * BLOCK, head_count))
    return combine(numers, maxima, level_sums, 0)

def block_layer(inputs, params):
    w_qkv, w_out, w_up, w_down, norm_gains, bias_rows, up_bias = params
    model = inputs.shape[-1]
    head_count = model // HDIM
    normed = low(layer_norm(inputs, norm_gains[0], bias_rows[0]))
    mixed = jnp.dot(normed, w_qkv, precision=highest)
    queries = low_back(low(mixed[:, :model] + bias_rows[1]))
    key_rows = low_back(low(mixed[:, model:2 * model]))
    value_rows = low_back(low(mixed[:, 2 * model:] + bias_rows[2]))
    attended = hierarchy(queries.reshape(-1, head_count, HDIM), key_rows.reshape(-1, head_count, HDIM), value_rows.reshape(-1, head_count, HDIM))
    attended = low_back(low(attended.reshape(-1, model)))
    branch = low_back(jnp.dot(attended, w_out, precision=highest) + bias_rows[3])
    middle = inputs + branch
    second = low(layer_norm(middle, norm_gains[1], bias_rows[4]))
    hidden = low_back(jnp.dot(second, w_up, precision=highest) + up_bias)
    active = low(jax.nn.gelu(hidden, approximate=True))
    branch_two = low_back(jnp.dot(active, w_down, precision=highest) + bias_rows[5])
    return middle + branch_two

def reference(tokens_in, grad_output, prefix_len, w_qkv, w_out, w_up, w_down, norm_gains, bias_rows, up_bias):
    params = tuple((weight_arr.astype(jnp.float32) for weight_arr in (w_qkv, w_out, w_up, w_down, norm_gains, bias_rows, up_bias)))
    seq_rows = tokens_in.reshape(-1, SEQ_LEN, D)
    cot_rows = grad_output.reshape(-1, SEQ_LEN, D)
    prefixes = prefix_len.reshape(-1)
    positions = jnp.arange(SEQ_LEN, dtype=jnp.int32)

    def forward(inputs, layer_params):
        state = inputs
        for layer_id in range(LAYERS):
            state = block_layer(state, tuple((weight_arr[layer_id] for weight_arr in layer_params)))
        return state

    def one_row(running, entry):
        row_in, row_cot, row_prefix = entry
        result, pullback = jax.vjp(forward, row_in.astype(jnp.float32), params)
        keep_rows = (positions >= row_prefix).astype(jnp.float32)
        cotangent = row_cot.astype(jnp.float32) * keep_rows[:, None]
        grad_row, grad_params = pullback(cotangent)
        running = jax.tree.map(lambda earlier, update: earlier + update, running, grad_params)
        return (running, (result.astype(jnp.bfloat16), grad_row))
    start = tuple((jnp.zeros_like(weight_arr) for weight_arr in params))
    totals, (results, grads) = lax.scan(one_row, start, (seq_rows, cot_rows, prefixes))
    return (results.reshape(tokens_in.shape), grads.reshape(tokens_in.shape), totals[0], totals[1], totals[2], totals[3], totals[4], totals[5], totals[6])
```

```python
import functools
import math

import jax
import jax.numpy as jnp
from jax import lax
from jax.experimental import pallas as pl
from jax.experimental.pallas import tpu as pltpu
from jax.sharding import PartitionSpec as P

HDIM = 64
BLOCK = 16
LEVELS = 6
LAYERS = 2
TOP = LEVELS - 1
CHUNK = 64
LN2 = math.log(2.0)
F32 = jnp.float32
BF16 = jnp.bfloat16
NEG = -1e30
VMEM_LIMIT = 60 * 2**20
AXES = ("dp", "seq")


def dot_nn(a, b):
    return lax.dot_general(a, b, (((1,), (0,)), ((), ())), preferred_element_type=F32)


def dot_nt(a, b):
    return lax.dot_general(a, b, (((1,), (1,)), ((), ())), preferred_element_type=F32)


def dot_tn(a, b):
    return lax.dot_general(a, b, (((0,), (0,)), ((), ())), preferred_element_type=F32)


class Sizes:
    def __init__(self, rows, run, model, hidden, seq):
        self.rows, self.run, self.model, self.hidden, self.seq = rows, run, model, hidden, seq
        self.tokens = rows * run
        self.pairs = model // 128
        self.chunks = run // CHUNK
        self.count = [run >> level for level in range(LEVELS)]
        self.top_keys = self.count[TOP] * seq
        self.offset, at = [], 0
        for level in range(TOP):
            self.offset.append(at)
            at += self.count[level] + 2 * BLOCK
        self.offset.append(at)
        self.bank = at + self.top_keys
        self.keys = [CHUNK + 2 * BLOCK, CHUNK // 2 + 2 * BLOCK] + [2 * BLOCK] * (TOP - 2) + [self.top_keys]
        self.start = [sum(self.keys[:level]) for level in range(LEVELS)]
        self.width = sum(self.keys)
        self.rim = rows * TOP * 2 * BLOCK


def normalise(values):
    centred = values - jnp.mean(values, axis=-1, keepdims=True)
    spread = jnp.mean(centred * centred, axis=-1, keepdims=True)
    inverse = lax.rsqrt(spread + 1e-05)
    return centred * inverse, inverse


def norm_back(grad, hat, inverse, gain):
    scaled = grad * gain
    first = jnp.mean(scaled, axis=-1, keepdims=True)
    second = jnp.mean(scaled * hat, axis=-1, keepdims=True)
    return inverse * (scaled - first - hat * second)


GELU_C = math.sqrt(2.0 / math.pi)


def gelu(v):
    return 0.5 * v * (1.0 + jnp.tanh(GELU_C * (v + 0.044715 * (v * v * v))))


def gelu_both(v):
    square = v * v
    t = jnp.tanh(GELU_C * (v + 0.044715 * (square * v)))
    half = 0.5 * (1.0 + t)
    slope = half + 0.5 * v * (1.0 - t * t) * (GELU_C * (1.0 + 3.0 * 0.044715 * square))
    return v * half, slope


def row_loop(total, step, body):
    def go(j, carry):
        body(pl.ds(pl.multiple_of(j * step, step), step))
        return carry

    lax.fori_loop(0, total // step, go, 0)


def coarse_matrix(run):
    row = lax.broadcasted_iota(jnp.int32, (run, run), 0)
    col = lax.broadcasted_iota(jnp.int32, (run, run), 1)
    out = jnp.zeros((run, run), F32)
    base = 0
    for level in range(1, LEVELS):
        n = run >> level
        hit = (row >= base) & (row < base + n) & ((col >> level) == row - base)
        out = jnp.where(hit, 2.0**-level, out)
        base += n
    return out.astype(BF16)


def spread_matrix():
    row = lax.broadcasted_iota(jnp.int32, (TOP * CHUNK, CHUNK), 0)
    col = lax.broadcasted_iota(jnp.int32, (TOP * CHUNK, CHUNK), 1)
    out = jnp.zeros((TOP * CHUNK, CHUNK), F32)
    for level in range(1, LEVELS):
        base = (level - 1) * CHUNK
        hit = (row >= base) & (row < base + CHUNK) & (((row - base) >> level) == (col >> level))
        out = jnp.where(hit, 2.0**-level, out)
    return out.astype(BF16)


def fill_mask(sz, mask_ref):
    place = lax.axis_index("seq")
    for i in range(sz.chunks):
        for level in range(LEVELS):
            shape = (sz.keys[level], 128)
            key = lax.broadcasted_iota(jnp.int32, shape, 0)
            token = lax.broadcasted_iota(jnp.int32, shape, 1) % CHUNK
            per_run = sz.count[level] // BLOCK
            if level == TOP:
                query_block = ((place * sz.run + i * CHUNK + token) >> TOP) // BLOCK
                allowed = jnp.abs(query_block - key // BLOCK) == 1
            else:
                own = (i * CHUNK >> level) // BLOCK
                if level >= 2:
                    key_block = own - 1 + 2 * (key // BLOCK)
                    allowed = key >= 0
                else:
                    key_block = own - 1 + key // BLOCK
                    distance = jnp.abs(key_block - own - (token >> level) // BLOCK)
                    allowed = distance <= 1 if level == 0 else distance == 1
                whole = place * per_run + key_block
                allowed = allowed & (whole >= 0) & (whole < per_run * sz.seq)
            mask_ref[i, pl.ds(sz.start[level], sz.keys[level])] = jnp.where(allowed, level * LN2, NEG)


def key_slices(sz, i, level):
    if level == TOP:
        return [(sz.offset[TOP], sz.top_keys)]
    if level < 2:
        return [(sz.offset[level] + (CHUNK >> level) * i, sz.keys[level])]
    own = (i * CHUNK) // (BLOCK << level)
    return [(sz.offset[level] + BLOCK * own, BLOCK), (sz.offset[level] + BLOCK * (own + 2), BLOCK)]


def take(ref, r, pieces, lanes):
    parts = [ref[r, pl.ds(pl.multiple_of(at, BLOCK) if not isinstance(at, int) else at, size), lanes] for at, size in pieces]
    return parts[0] if len(parts) == 1 else jnp.concatenate(parts, axis=0)


def give(ref, r, pieces, lanes, value):
    done = 0
    for at, size in pieces:
        rows = pl.ds(pl.multiple_of(at, BLOCK) if not isinstance(at, int) else at, size)
        ref[r, rows, lanes] += value[done : done + size]
        done += size


def two_heads(block):
    first = lax.broadcasted_iota(jnp.int32, block.shape, 1) < HDIM
    zero = jnp.zeros_like(block)
    return jnp.concatenate([jnp.where(first, block, zero), jnp.where(first, zero, block)], axis=0)


def one_row(block):
    first = lax.broadcasted_iota(jnp.int32, (CHUNK, 128), 1) < HDIM
    return jnp.where(first, block[:CHUNK], block[CHUNK:])


def chunk_queries(sz, q_ref, spread, r, i):
    tokens = pl.ds(pl.multiple_of(i * CHUNK, CHUNK), CHUNK)
    fine = q_ref[r, tokens, :]
    coarse = dot_nn(spread, fine).astype(BF16)
    return [fine] + [coarse[level * CHUNK : (level + 1) * CHUNK] for level in range(TOP)]


def attend(sz, q_ref, key_ref, value_ref, mask_ref, att_ref, lse_ref):
    spread = spread_matrix()

    def chunk(step, carry):
        r, i = step // sz.chunks, step % sz.chunks
        tokens = pl.ds(pl.multiple_of(i * CHUNK, CHUNK), CHUNK)
        queries = chunk_queries(sz, q_ref, spread, r, i)
        for pair in range(sz.pairs):
            lanes = slice(128 * pair, 128 * pair + 128)
            scores, values = [], []
            for level in range(LEVELS):
                pieces = key_slices(sz, i, level)
                keys = take(key_ref, r, pieces, lanes)
                values.append(take(value_ref, r, pieces, lanes))
                scores.append(dot_nt(keys, two_heads(queries[level][:, lanes])))
            scores = jnp.concatenate(scores, axis=0) + mask_ref[i]
            peak = jnp.max(scores, axis=0, keepdims=True)
            weights = jnp.exp(scores - peak)
            total = jnp.sum(weights, axis=0, keepdims=True)
            weights = (weights * (1.0 / total)).astype(BF16)
            mixed = dot_tn(weights, jnp.concatenate(values, axis=0))
            att_ref[r, tokens, lanes] = one_row(mixed).astype(BF16)
            lse_ref[step, pair : pair + 1, :] = peak + jnp.log(total)
        return carry

    lax.fori_loop(0, sz.rows * sz.chunks, chunk, 0)


def attend_back(sz, q_ref, key_ref, value_ref, mask_ref, lse_ref, go_ref, dq_ref, dkey_ref, dvalue_ref):
    spread = spread_matrix()
    dkey_ref[...] = jnp.zeros_like(dkey_ref)
    dvalue_ref[...] = jnp.zeros_like(dvalue_ref)

    def chunk(step, carry):
        r, i = step // sz.chunks, step % sz.chunks
        tokens = pl.ds(pl.multiple_of(i * CHUNK, CHUNK), CHUNK)
        queries = chunk_queries(sz, q_ref, spread, r, i)
        for pair in range(sz.pairs):
            lanes = slice(128 * pair, 128 * pair + 128)
            pieces = [key_slices(sz, i, level) for level in range(LEVELS)]
            keys = [take(key_ref, r, piece, lanes) for piece in pieces]
            values = jnp.concatenate([take(value_ref, r, piece, lanes) for piece in pieces], axis=0)
            doubled = [two_heads(level_queries[:, lanes]) for level_queries in queries]
            scores = jnp.concatenate([dot_nt(k, q) for k, q in zip(keys, doubled)], axis=0) + mask_ref[i]
            weights = jnp.exp(scores - lse_ref[step, pair : pair + 1, :])
            go = two_heads(go_ref[r, tokens, lanes])
            dweights = dot_nt(values, go)
            inner = jnp.sum(weights * dweights, axis=0, keepdims=True)
            dscores = (weights * (dweights - inner)).astype(BF16)
            dvalues = dot_nn(weights.astype(BF16), go)
            fine, coarse = None, []
            for level in range(LEVELS):
                part = slice(sz.start[level], sz.start[level] + sz.keys[level])
                give(dvalue_ref, r, pieces[level], lanes, dvalues[part])
                give(dkey_ref, r, pieces[level], lanes, dot_nn(dscores[part], doubled[level]))
                dquery = one_row(dot_tn(dscores[part], keys[level]))
                if level == 0:
                    fine = dquery
                else:
                    coarse.append(dquery.astype(BF16))
            fine = fine + dot_tn(spread, jnp.concatenate(coarse, axis=0))
            dq_ref[r, tokens, lanes] = (fine * HDIM**-0.5).astype(BF16)
        return carry

    lax.fori_loop(0, sz.rows * sz.chunks, chunk, 0)


def rim_rows(r, level, kind):
    return pl.ds(((r * TOP + level) * 2 + kind) * BLOCK, BLOCK)


def unpack_small(sz, small, vec_ref, up_ref):
    lane = lax.broadcasted_iota(jnp.int32, (BLOCK, 128), 1)
    tiles = [small[BLOCK * i : BLOCK * i + BLOCK, :].astype(F32) for i in range(sz.model // BLOCK)]
    for c in range(sz.model // 128):
        total = tiles[8 * c]
        for j in range(1, 8):
            total = jnp.where(lane // 16 == j, tiles[8 * c + j], total)
        vec_ref[:, 128 * c : 128 * c + 128] = total[:8]
    wide = sz.hidden * BLOCK // sz.model
    for c in range(sz.hidden // 128):
        total = tiles[2 * c]
        total = jnp.where(lane >= wide, tiles[2 * c + 1], total)
        up_ref[:, 128 * c : 128 * c + 128] = total[8:9]


def before_kernel(sz, x_ref, w_ref, q_ref, key_ref, value_ref, rims_ref, top_ref, vec_ref, up_ref):
    model = sz.model
    unpack_small(sz, w_ref[:, 8 * model : 8 * model + 128], vec_ref, up_ref)
    coarse = coarse_matrix(sz.run)
    for r in range(sz.rows):
        hat, _ = normalise(x_ref[pl.ds(r * sz.run, sz.run), :])
        normed = (hat * vec_ref[0:1, :] + vec_ref[2:3, :]).astype(BF16)
        queries = (dot_nn(normed, w_ref[:, :model]) + vec_ref[3:4, :]).astype(BF16)
        q_ref[r] = queries * jnp.asarray(HDIM**-0.5, BF16)
        for kind, bank in ((0, key_ref), (1, value_ref)):
            mixed = dot_nn(normed, w_ref[:, (1 + kind) * model : (2 + kind) * model])
            if kind == 1:
                mixed = mixed + vec_ref[4:5, :]
            mixed = mixed.astype(BF16)
            levels = dot_nn(coarse, mixed).astype(BF16)
            base = 0
            for level in range(LEVELS):
                n = sz.count[level]
                if level == 0:
                    now = mixed
                else:
                    now = levels[base : base + n]
                    base += n
                if level < TOP:
                    bank[r, pl.ds(sz.offset[level] + BLOCK, n), :] = now
                    rims_ref[0, rim_rows(r, level, kind), :] = now[n - BLOCK :]
                    rims_ref[1, rim_rows(r, level, kind), :] = now[:BLOCK]
                    bank[r, pl.ds(sz.offset[level], BLOCK), :] = jnp.zeros((BLOCK, model), BF16)
                    bank[r, pl.ds(sz.offset[level] + BLOCK + n, BLOCK), :] = jnp.zeros((BLOCK, model), BF16)
                else:
                    if kind == 0:
                        top_now = now
                    else:
                        top_ref[r] = jnp.concatenate([top_now, now], axis=0)


def place_rims(sz, low_ref, high_ref, tops_ref, key_ref, value_ref):
    for r in range(sz.rows):
        for kind, bank in ((0, key_ref), (1, value_ref)):
            for level in range(TOP):
                bank[r, pl.ds(sz.offset[level], BLOCK), :] = low_ref[rim_rows(r, level, kind), :]
                bank[r, pl.ds(sz.offset[level] + BLOCK + sz.count[level], BLOCK), :] = high_ref[rim_rows(r, level, kind), :]
            n = sz.count[TOP]
            for s in range(0, sz.seq, 2):
                both = jnp.concatenate(
                    [tops_ref[s, r, kind * n : kind * n + n, :], tops_ref[s + 1, r, kind * n : kind * n + n, :]], axis=0
                )
                bank[r, pl.ds(sz.offset[TOP] + s * n, 2 * n), :] = both


def after_kernel(
    sz, x_ref, q_ref, key_in, value_in, low_ref, high_ref, tops_ref, w_ref, down_ref, vec_ref, up_ref,
    att_ref, lse_ref, middle_ref, out_ref, key_ref, value_ref, mask_ref, second_ref,
):
    model = sz.model
    key_ref[...] = key_in[...]
    value_ref[...] = value_in[...]
    place_rims(sz, low_ref, high_ref, tops_ref, key_ref, value_ref)
    fill_mask(sz, mask_ref)
    attend(sz, q_ref, key_ref, value_ref, mask_ref, att_ref, lse_ref)
    for r in range(sz.rows):
        rows = pl.ds(r * sz.run, sz.run)
        middle = x_ref[rows, :] + dot_nn(att_ref[r], w_ref[:, 3 * model : 4 * model]) + vec_ref[5:6, :]
        middle_ref[rows, :] = middle
        hat, _ = normalise(middle)
        second_ref[rows, :] = (hat * vec_ref[1:2, :] + vec_ref[6:7, :]).astype(BF16)
        out_ref[rows, :] = middle + vec_ref[7:8, :]

    def part(c, carry):
        cols = pl.ds(pl.multiple_of(4 * model + c * model, 128), model)
        units = pl.ds(pl.multiple_of(c * model, 128), model)
        for r in range(sz.rows):
            rows = pl.ds(r * sz.run, sz.run)
            hidden = dot_nn(second_ref[rows, :], w_ref[:, cols]) + up_ref[:, units]
            out_ref[rows, :] += dot_nn(gelu(hidden).astype(BF16), down_ref[units, :])
        return carry

    lax.fori_loop(0, sz.hidden // model, part, 0)


def back_kernel(
    sz, g_ref, middle_ref, att_ref, q_ref, key_ref, value_ref, lse_ref, w_ref, down_ref, vec_ref, up_ref,
    dq_ref, dkey_ref, dvalue_ref, gm_ref, gout_ref, gup_ref, gdown_ref, gvec_ref, gupb_ref, rims_ref, tops_ref,
    mask_ref, second_ref, gd_ref, gs_ref, go_ref,
):
    model = sz.model
    fill_mask(sz, mask_ref)
    gvec_ref[...] = jnp.zeros_like(gvec_ref)
    for r in range(sz.rows):
        rows = pl.ds(r * sz.run, sz.run)
        hat, _ = normalise(middle_ref[rows, :])
        second_ref[rows, :] = (hat * vec_ref[1:2, :] + vec_ref[6:7, :]).astype(BF16)
        grad = g_ref[rows, :].astype(BF16)
        gd_ref[rows, :] = grad
        gvec_ref[7:8, :] += jnp.sum(grad.astype(F32), axis=0, keepdims=True)
        gs_ref[rows, :] = jnp.zeros((sz.run, model), F32)

    def part(c, carry):
        cols = pl.ds(pl.multiple_of(4 * model + c * model, 128), model)
        units = pl.ds(pl.multiple_of(c * model, 128), model)
        hidden = dot_nn(second_ref[...], w_ref[:, cols]) + up_ref[:, units]
        active, slope = gelu_both(hidden)
        gdown_ref[units, :] = dot_tn(active.astype(BF16), gd_ref[...]).astype(BF16)
        grad_hidden = (slope * dot_nt(gd_ref[...], down_ref[units, :])).astype(BF16)
        gupb_ref[:, units] = jnp.sum(grad_hidden.astype(F32), axis=0, keepdims=True)
        gup_ref[:, units] = dot_tn(second_ref[...], grad_hidden).astype(BF16)
        gs_ref[...] += dot_nt(grad_hidden, w_ref[:, cols])
        return carry

    lax.fori_loop(0, sz.hidden // model, part, 0)
    for r in range(sz.rows):
        rows = pl.ds(r * sz.run, sz.run)
        hat, inverse = normalise(middle_ref[rows, :])
        grad = gs_ref[rows, :]
        gvec_ref[1:2, :] += jnp.sum(grad * hat, axis=0, keepdims=True)
        gvec_ref[6:7, :] += jnp.sum(grad, axis=0, keepdims=True)
        gm = g_ref[rows, :] + norm_back(grad, hat, inverse, vec_ref[1:2, :])
        gm_ref[rows, :] = gm
        branch = gm.astype(BF16)
        gd_ref[rows, :] = branch
        gvec_ref[5:6, :] += jnp.sum(branch.astype(F32), axis=0, keepdims=True)
        go_ref[r] = dot_nt(branch, w_ref[:, 3 * model : 4 * model]).astype(BF16)
    gout_ref[...] = sum(
        dot_tn(att_ref[r], gd_ref[pl.ds(r * sz.run, sz.run), :]) for r in range(sz.rows)
    ).astype(BF16)
    attend_back(sz, q_ref, key_ref, value_ref, mask_ref, lse_ref, go_ref, dq_ref, dkey_ref, dvalue_ref)
    n = sz.count[TOP]
    for r in range(sz.rows):
        for kind, bank in ((0, dkey_ref), (1, dvalue_ref)):
            for level in range(TOP):
                rims_ref[0, rim_rows(r, level, kind), :] = bank[r, pl.ds(sz.offset[level], BLOCK), :].astype(BF16)
                rims_ref[1, rim_rows(r, level, kind), :] = bank[
                    r, pl.ds(sz.offset[level] + BLOCK + sz.count[level], BLOCK), :
                ].astype(BF16)
        for s in range(sz.seq):
            at = pl.ds(sz.offset[TOP] + s * n, n)
            tops_ref[s, r] = jnp.concatenate([dkey_ref[r, at, :], dvalue_ref[r, at, :]], axis=0).astype(BF16)


def last_kernel(
    sz, x_ref, gm_ref, dq_ref, dkey_ref, dvalue_ref, low_ref, high_ref, tops_ref, w_ref, vec_ref, gvec_in, gupb_ref,
    gin_ref, gqkv_ref, small_ref, gvec_ref, dk_ref, dv_ref, levels_ref, normed_ref,
):
    model = sz.model
    coarse = coarse_matrix(sz.run)
    gvec_ref[...] = gvec_in[...]
    for r in range(sz.rows):
        for kind, bank, out in ((0, dkey_ref, dk_ref), (1, dvalue_ref, dv_ref)):
            base = 0
            for level in range(LEVELS):
                n = sz.count[level]
                if level == TOP:
                    levels_ref[pl.ds(base, 2 * n), :] = jnp.concatenate(
                        [
                            sum(tops_ref[s, r, kind * n : kind * n + n, :].astype(F32) for s in range(sz.seq)),
                            jnp.zeros((n, model), F32),
                        ],
                        axis=0,
                    ).astype(BF16)
                    continue
                own = bank[r, pl.ds(sz.offset[level] + BLOCK, n), :]
                first = high_ref[rim_rows(r, level, kind), :].astype(F32)
                final = low_ref[rim_rows(r, level, kind), :].astype(F32)
                if n == BLOCK:
                    own = own + first + final
                else:
                    middle = [own[BLOCK : n - BLOCK]] if n > 2 * BLOCK else []
                    own = jnp.concatenate([own[:BLOCK] + first, *middle, own[n - BLOCK :] + final], axis=0)
                if level == 0:
                    fine = own
                else:
                    levels_ref[pl.ds(base, n), :] = own.astype(BF16)
                    base += n
            out[pl.ds(r * sz.run, sz.run), :] = (fine + dot_tn(coarse, levels_ref[...])).astype(BF16)
    for r in range(sz.rows):
        rows = pl.ds(r * sz.run, sz.run)
        gvec_ref[3:4, :] += jnp.sum(dq_ref[r].astype(F32), axis=0, keepdims=True)
        gvec_ref[4:5, :] += jnp.sum(dv_ref[rows, :].astype(F32), axis=0, keepdims=True)
        grad = dot_nt(dq_ref[r], w_ref[:, :model])
        grad = grad + dot_nt(dk_ref[rows, :], w_ref[:, model : 2 * model])
        grad = grad + dot_nt(dv_ref[rows, :], w_ref[:, 2 * model : 3 * model])
        hat, inverse = normalise(x_ref[rows, :])
        normed_ref[r] = (hat * vec_ref[0:1, :] + vec_ref[2:3, :]).astype(BF16)
        gvec_ref[0:1, :] += jnp.sum(grad * hat, axis=0, keepdims=True)
        gvec_ref[2:3, :] += jnp.sum(grad, axis=0, keepdims=True)
        gin_ref[rows, :] = gm_ref[rows, :] + norm_back(grad, hat, inverse, vec_ref[0:1, :])
    run = sz.run
    gqkv_ref[:, :model] = sum(dot_tn(normed_ref[r], dq_ref[r]) for r in range(sz.rows)).astype(BF16)
    gqkv_ref[:, model : 2 * model] = sum(
        dot_tn(normed_ref[r], dk_ref[pl.ds(r * run, run), :]) for r in range(sz.rows)
    ).astype(BF16)
    gqkv_ref[:, 2 * model :] = sum(
        dot_tn(normed_ref[r], dv_ref[pl.ds(r * run, run), :]) for r in range(sz.rows)
    ).astype(BF16)
    for i in range(model // BLOCK):
        top = gvec_ref[:, 128 * (i // 8) : 128 * (i // 8) + 128]
        up = jnp.broadcast_to(gupb_ref[:, 128 * (i // 2) : 128 * (i // 2) + 128], (8, 128))
        small_ref[pl.ds(BLOCK * i, BLOCK), :] = jnp.concatenate([top, up], axis=0).astype(BF16)


def call(kernel, name, outs, scratch, *args):
    whole = pl.BlockSpec(memory_space=pltpu.VMEM)
    return pl.pallas_call(
        kernel,
        out_shape=[jax.ShapeDtypeStruct(shape, dtype) for shape, dtype in outs],
        in_specs=[whole] * len(args),
        out_specs=[whole] * len(outs),
        scratch_shapes=[pltpu.VMEM(shape, dtype) for shape, dtype in scratch],
        compiler_params=pltpu.CompilerParams(vmem_limit_bytes=VMEM_LIMIT),
        name=name,
    )(*args)


def layer_before(sz, x, w):
    n, bank = sz.model, (sz.rows, sz.bank, sz.model)
    return call(
        functools.partial(before_kernel, sz),
        "before",
        [
            ((sz.rows, sz.run, n), BF16), (bank, BF16), (bank, BF16), ((2, sz.rim, n), BF16),
            ((sz.rows, BLOCK, n), BF16), ((8, n), F32), ((1, sz.hidden), F32),
        ],
        [],
        x, w,
    )


def layer_after(sz, x, q, keys, values, low, high, tops, w, down, vec, up):
    n, bank = sz.model, (sz.rows, sz.bank, sz.model)
    return call(
        functools.partial(after_kernel, sz),
        "after",
        [
            ((sz.rows, sz.run, n), BF16), ((sz.rows * sz.chunks, sz.pairs, 128), F32), ((sz.tokens, n), F32),
            ((sz.tokens, n), F32), (bank, BF16), (bank, BF16),
        ],
        [((sz.chunks, sz.width, 128), F32), ((sz.tokens, n), BF16)],
        x, q, keys, values, low, high, tops, w, down, vec, up,
    )


def layer_back(sz, g, middle, att, q, keys, values, lse, w, down, vec, up):
    n, bank = sz.model, (sz.rows, sz.bank, sz.model)
    return call(
        functools.partial(back_kernel, sz),
        "back",
        [
            ((sz.rows, sz.run, n), BF16), (bank, F32), (bank, F32), ((sz.tokens, n), F32), ((n, n), BF16),
            ((n, sz.hidden), BF16), ((sz.hidden, n), BF16), ((8, n), F32), ((1, sz.hidden), F32),
            ((2, sz.rim, n), BF16), ((sz.seq, sz.rows, BLOCK, n), BF16),
        ],
        [
            ((sz.chunks, sz.width, 128), F32), ((sz.tokens, n), BF16), ((sz.tokens, n), BF16), ((sz.tokens, n), F32),
            ((sz.rows, sz.run, n), BF16),
        ],
        g, middle, att, q, keys, values, lse, w, down, vec, up,
    )


def layer_last(sz, x, gm, dq, dkeys, dvalues, low, high, tops, w, vec, gvec, gupb):
    n = sz.model
    return call(
        functools.partial(last_kernel, sz),
        "last",
        [((sz.tokens, n), F32), ((n, 3 * n), BF16), ((n, 128), BF16)],
        [
            ((8, n), F32), ((sz.tokens, n), BF16), ((sz.tokens, n), BF16), ((sz.run, n), BF16),
            ((sz.rows, sz.run, n), BF16),
        ],
        x, gm, dq, dkeys, dvalues, low, high, tops, w, vec, gvec, gupb,
    )


MESH = pl.DeviceIdType.MESH
ORDERS = ("zyx", "zxy", "zxy", "zyx")


class Grid:
    def __init__(self, depth):
        dp, seq = lax.axis_index("dp"), lax.axis_index("seq")
        self.depth = depth
        self.z, self.x, self.y, self.c = dp // 2, dp % 2, seq // 2, seq % 2

    def at(self, z, x, y, c):
        return (z * 2 + x, y * 2 + c)

    def index(self, z, x, y, c):
        return z * 8 + x * 4 + y * 2 + c

    def partner(self, axis):
        z, x, y, c = self.z, self.x, self.y, self.c
        return self.at(z, 1 - x if axis == "x" else x, 1 - y if axis == "y" else y, 1 - c if axis == "c" else c)

    def up(self, by):
        return self.at(self.z + by, self.x, self.y, self.c)


def greet(devices):
    barrier = pltpu.get_barrier_semaphore()
    peers = jnp.int32(0)
    for where, condition in devices:
        signal = functools.partial(pl.semaphore_signal, barrier, inc=1, device_id=where, device_id_type=MESH)
        if condition is None:
            signal()
            peers += 1
        else:
            pl.when(condition)(signal)
            peers += condition.astype(jnp.int32)
    pl.semaphore_wait(barrier, peers)


def both(first, second):
    if first is None:
        return second
    return first if second is None else first & second


def when(condition, act):
    if condition is None:
        act()
    else:
        pl.when(condition)(act)


def gather_kernel(depth, big_ref, down_ref, big_out, down_out, local_sem, send_sem, recv_sem):
    grid = Grid(depth)
    z, x, y, c = grid.z, grid.x, grid.y, grid.c
    greet(
        [(grid.partner(axis), None) for axis in "cxy"] + [(grid.up(1), z + 1 < depth), (grid.up(-1), z > 0)]
    )
    pieces = []
    for layer in range(LAYERS):
        pieces.append((big_ref.at[layer], big_out.at[layer], big_ref.shape[1]))
        pieces.append((down_ref.at[layer], down_out.at[layer], down_ref.shape[1]))
    me = grid.index(z, x, y, c)
    sends, used = [], [0] * len(pieces)

    def copy(p, source, block, slot, to):
        _, out, rows = pieces[p]
        target = out.at[pl.ds(pl.multiple_of(block * rows, BLOCK), rows)]
        return pltpu.make_async_remote_copy(
            src_ref=target if source is None else source,
            dst_ref=target,
            send_sem=send_sem.at[p, slot],
            recv_sem=recv_sem.at[p, block],
            device_id=to,
            device_id_type=MESH,
        )

    def local(p):
        source, out, rows = pieces[p]
        return pltpu.make_async_copy(
            source, out.at[pl.ds(pl.multiple_of(me * rows, BLOCK), rows)], local_sem.at[p]
        )

    def send(p, source, block, to, condition):
        slot = used[p]
        used[p] += 1
        when(condition, lambda: copy(p, source, block, slot, to).start())
        sends.append((p, block, slot, to, condition))

    def receive(p, block, condition):
        when(condition, lambda: copy(p, None, block, 0, grid.partner("c")).wait_recv())

    def pass_on(p, source, block, axes, condition):
        for axis in axes:
            if axis == "z":
                send(p, source, block, grid.up(1), both(condition, z + 1 < depth))
                send(p, source, block, grid.up(-1), both(condition, z > 0))
            else:
                send(p, source, block, grid.partner(axis), condition)

    def start(p):
        local(p).start()
        pass_on(p, pieces[p][0], me, ORDERS[p % len(ORDERS)] + "c", None)

    def arrive(p, dz, sign, dx, dy):
        order = ORDERS[p % len(ORDERS)]
        from_z = z - sign * dz
        valid = (from_z >= 0) & (from_z < depth) if dz else None
        block = grid.index(from_z, 1 - x if dx else x, 1 - y if dy else y, c)
        receive(p, block, valid)
        away = {"z": dz, "x": dx, "y": dy}
        final = max(j for j, axis in enumerate(order) if away[axis])
        if order[final] == "z" and dz < depth - 1:
            onward = z + sign
            send(p, None, block, grid.up(sign), both(valid, (onward >= 0) & (onward < depth)))
        pass_on(p, None, block, order[final + 1 :] + "c", valid)

    for p in range(len(pieces)):
        start(p)
    events = []
    for p in range(len(pieces)):
        for dx in range(2):
            for dy in range(2):
                for dz in range(depth):
                    for sign in (1, -1) if dz else (1,):
                        if dx + dy + dz:
                            events.append((dx + dy + dz, p, dz, sign, dx, dy))
    for _, p, dz, sign, dx, dy in sorted(events, key=lambda event: event[:2]):
        arrive(p, dz, sign, dx, dy)
    for p in range(len(pieces)):
        local(p).wait()
        for zz in range(depth):
            for xx in range(2):
                for yy in range(2):
                    receive(p, grid.index(zz, xx, yy, 1 - c), None)
    for p, block, slot, to, condition in sends:
        when(condition, lambda: copy(p, None, block, slot, to).wait_send())


def scatter_kernel(depth, *refs):
    count = (len(refs) - 2) // 7
    pieces, sums = refs[:count], refs[count : 2 * count]
    buffers = [refs[2 * count + 5 * p : 2 * count + 5 * p + 5] for p in range(count)]
    send_sem, recv_sem = refs[-2], refs[-1]
    grid = Grid(depth)
    z, x, y, c = grid.z, grid.x, grid.y, grid.c
    others = [lax.rem(z + k, depth) for k in range(1, depth)]
    greet([(grid.partner(axis), None) for axis in "cxy"] + [(grid.at(other, x, y, c), None) for other in others])
    sends = []

    def move(p, stage, source, target, to):
        return pltpu.make_async_remote_copy(
            src_ref=source, dst_ref=target, send_sem=send_sem.at[p, stage], recv_sem=recv_sem.at[p, stage],
            device_id=to, device_id_type=MESH,
        )

    def first(p, stage):
        copy = move(p, stage, pieces[p].at[:, :, :, 1 - c], buffers[p][0], grid.partner("c"))
        copy.start()
        sends.append(copy)

    def swap(p, stage):
        piece, (from_core, from_first, from_second, held, _) = pieces[p], buffers[p]
        sends[p + (stage - 1) * count].wait_recv()
        axis = ("xy", "yx")[p % 2][stage - 1]
        lead = ("xy", "yx")[p % 2][0]
        if stage == 1:
            for zz in range(depth):
                for xx in range(2):
                    for yy in range(2):
                        total = piece[zz, xx, yy, c].astype(F32) + from_core[zz, xx, yy].astype(F32)
                        from_core[zz, xx, yy] = total.astype(BF16)
            source = from_core.at[:, 1 - x] if axis == "x" else from_core.at[:, :, 1 - y]
            copy = move(p, stage, source, from_first, grid.partner(axis))
        else:
            for zz in range(depth):
                for k in range(2):
                    kept = from_core[zz, x, k] if lead == "x" else from_core[zz, k, y]
                    from_first[zz, k] = (kept.astype(F32) + from_first[zz, k].astype(F32)).astype(BF16)
            other = 1 - (x if axis == "x" else y)
            copy = move(p, stage, from_first.at[:, other], from_second, grid.partner(axis))
        copy.start()
        sends.append(copy)

    def along(p):
        _, from_first, from_second, held, from_z = buffers[p]
        sends[p + 2 * count].wait_recv()
        mine = (y, x)[p % 2]
        for zz in range(depth):
            held[zz] = (from_first[zz, mine].astype(F32) + from_second[zz].astype(F32)).astype(BF16)
        for k, other in enumerate(others):
            copy = move(p, 3 + k, held.at[other], from_z.at[k], grid.at(other, x, y, c))
            copy.start()
            sends.append(copy)

    def finish(p):
        held, from_z = buffers[p][3], buffers[p][4]
        total = held[z].astype(F32)
        for k in range(depth - 1):
            sends[3 * count + p * (depth - 1) + k].wait_recv()
            total = total + from_z[k].astype(F32)
        sums[p][...] = total

    for p in range(count):
        first(p, 0)
    for p in range(count):
        swap(p, 1)
    for p in range(count):
        swap(p, 2)
    for p in range(count):
        along(p)
    for p in range(count):
        finish(p)
    for copy in sends:
        copy.wait_send()


def rim_kernel(seq, to_next_ref, to_last_ref, tops_ref, low_ref, high_ref, all_ref, send_sem, recv_sem):
    me, dp = lax.axis_index("seq"), lax.axis_index("dp")
    others = [lax.rem(me + k, seq) for k in range(1, seq)]
    greet([((dp, other), None) for other in others])
    ahead = pltpu.make_async_remote_copy(
        src_ref=to_next_ref, dst_ref=low_ref, send_sem=send_sem.at[0], recv_sem=recv_sem.at[0],
        device_id=(dp, me + 1), device_id_type=MESH,
    )
    behind = pltpu.make_async_remote_copy(
        src_ref=to_last_ref, dst_ref=high_ref, send_sem=send_sem.at[1], recv_sem=recv_sem.at[1],
        device_id=(dp, me - 1), device_id_type=MESH,
    )
    when(me + 1 < seq, ahead.start)
    when(me > 0, behind.start)
    tops = []
    for k, other in enumerate(others):
        source = tops_ref.at[0] if tops_ref.shape[0] == 1 else tops_ref.at[other]
        tops.append(
            pltpu.make_async_remote_copy(
                src_ref=source, dst_ref=all_ref.at[me], send_sem=send_sem.at[2 + k], recv_sem=recv_sem.at[2 + k],
                device_id=(dp, other), device_id_type=MESH,
            )
        )
        tops[-1].start()
    all_ref[me] = tops_ref[0] if tops_ref.shape[0] == 1 else tops_ref[me]

    @pl.when(me == 0)
    def _():
        low_ref[...] = jnp.zeros_like(low_ref)

    @pl.when(me == seq - 1)
    def _():
        high_ref[...] = jnp.zeros_like(high_ref)

    when(me > 0, ahead.wait_recv)
    when(me + 1 < seq, behind.wait_recv)
    for copy in tops:
        copy.wait_recv()
    when(me + 1 < seq, ahead.wait_send)
    when(me > 0, behind.wait_send)
    for copy in tops:
        copy.wait_send()


def exchange(sz, collective, to_next, to_last, tops):
    whole = pl.BlockSpec(memory_space=pltpu.VMEM)
    rim = jax.ShapeDtypeStruct(to_next.shape, BF16)
    return pl.pallas_call(
        functools.partial(rim_kernel, sz.seq),
        out_shape=[rim, rim, jax.ShapeDtypeStruct((sz.seq,) + tops.shape[1:], BF16)],
        in_specs=[whole] * 3,
        out_specs=[whole] * 3,
        scratch_shapes=[pltpu.SemaphoreType.DMA((sz.seq + 1,)), pltpu.SemaphoreType.DMA((sz.seq + 1,))],
        compiler_params=pltpu.CompilerParams(
            collective_id=collective, has_side_effects=True, vmem_limit_bytes=VMEM_LIMIT
        ),
        name=("rims", "rims_back")[collective - 1],
    )(to_next, to_last, tops)


def direct(rows):
    return lax.axis_size("seq") == 4 and lax.axis_size("dp") % 2 == 0 and rows % BLOCK == 0


def pack_small(gains, biases, up_bias):
    layers, _, features = gains.shape
    tiles = features // BLOCK
    vec = jnp.concatenate([gains, biases], axis=1).reshape(layers, 8, tiles, BLOCK).transpose(0, 2, 1, 3)
    vec = jnp.tile(vec, (1, 1, 1, 128 // BLOCK))
    up = up_bias.reshape(layers, tiles, 1, up_bias.shape[1] // tiles)
    up = jnp.broadcast_to(jnp.tile(up, (1, 1, 1, 128 // up.shape[3])), (layers, tiles, 8, 128))
    return jnp.concatenate([vec, up], axis=2).reshape(layers, features, 128)


def gather_weights(w_qkv, w_out, w_up, w_down, gains, biases, up_bias):
    whole = lambda array, axis: lax.all_gather(array, AXES, axis=axis, tiled=True)
    if not direct(w_qkv.shape[1]):
        big = whole(jnp.concatenate([w_qkv, w_out, w_up], axis=2), 1)
        small = pack_small(whole(gains, 2), whole(biases, 2), whole(up_bias, 1))
        return jnp.concatenate([big, small], axis=2), whole(w_down, 1)
    big = jnp.concatenate([w_qkv, w_out, w_up, pack_small(gains, biases, up_bias)], axis=2)
    depth = lax.axis_size("dp") // 2
    blocks = 8 * depth
    anywhere = pl.BlockSpec(memory_space=pl.ANY)
    outs = [
        jax.ShapeDtypeStruct((LAYERS, blocks * array.shape[1], array.shape[2]), BF16) for array in (big, w_down)
    ]
    return pl.pallas_call(
        functools.partial(gather_kernel, depth),
        out_shape=outs,
        in_specs=[anywhere] * 2,
        out_specs=[anywhere] * 2,
        scratch_shapes=[
            pltpu.SemaphoreType.DMA((2 * LAYERS,)),
            pltpu.SemaphoreType.DMA((2 * LAYERS, 16 * depth)),
            pltpu.SemaphoreType.DMA((2 * LAYERS, blocks)),
        ],
        compiler_params=pltpu.CompilerParams(collective_id=0, has_side_effects=True),
        name="gather",
    )(big, w_down)


def unpack_grads(sz, qkv, out, up, small, down):
    wide = sz.hidden * BLOCK // sz.model
    per = 128 // wide
    place = lax.axis_index("dp") * lax.axis_size("seq") + lax.axis_index("seq")
    vec = lax.dynamic_slice(small, (0, BLOCK * (place % 8)), (8, BLOCK))
    return qkv, out, up, down, vec[:2], vec[2:], lax.dynamic_slice(small, (8, wide * (place % per)), (1, wide))[0]


def scatter_grads(sz, layers):
    if direct(sz.model // (lax.axis_size("dp") * lax.axis_size("seq"))):
        depth = lax.axis_size("dp") // 2
        whole = pl.BlockSpec(memory_space=pltpu.VMEM)
        pieces = [
            array.reshape((depth, 2, 2, 2, array.shape[0] // (8 * depth), array.shape[1]))
            for parts in layers
            for array in parts
        ]
        outs, scratch = [], []
        for piece in pieces:
            block = piece.shape[4:]
            outs.append(jax.ShapeDtypeStruct(block, F32))
            for lead in ((depth, 2, 2), (depth, 2), (depth,), (depth,), (depth - 1,)):
                scratch.append(pltpu.VMEM(lead + block, BF16))
        stages = 2 + depth
        sums = pl.pallas_call(
            functools.partial(scatter_kernel, depth),
            out_shape=outs,
            in_specs=[whole] * len(pieces),
            out_specs=[whole] * len(pieces),
            scratch_shapes=scratch + [pltpu.SemaphoreType.DMA((len(pieces), stages))] * 2,
            compiler_params=pltpu.CompilerParams(
                collective_id=3, has_side_effects=True, vmem_limit_bytes=VMEM_LIMIT
            ),
            name="scatter",
        )(*pieces)
        per = len(sums) // LAYERS
        return [unpack_grads(sz, *sums[per * layer : per * layer + per]) for layer in range(LAYERS)]
    return [scatter_by_sums(sz, parts) for parts in layers]


def scatter_by_sums(sz, parts):
    gqkv, gout, gup, small, gdown = parts
    spread = lambda array, axis: lax.psum_scatter(
        array.astype(F32), AXES, scatter_dimension=axis, tiled=True
    )
    tiles = small.reshape(sz.model // BLOCK, BLOCK, 128)
    vec = jnp.concatenate(
        [tiles[i, :8, BLOCK * (i % 8) : BLOCK * (i % 8) + BLOCK] for i in range(sz.model // BLOCK)], axis=1
    )
    wide = sz.hidden * BLOCK // sz.model
    per = 128 // wide
    up = jnp.concatenate(
        [tiles[i, 8, wide * (i % per) : wide * (i % per) + wide] for i in range(sz.model // BLOCK)], axis=0
    )
    vec = spread(vec, 1)
    return spread(gqkv, 0), spread(gout, 0), spread(gup, 0), spread(gdown, 0), vec[:2], vec[2:], spread(up, 0)


def on_device(
    tokens_in, grad_output, prefix_len, w_qkv, w_out, w_up, w_down, norm_gains, bias_rows, up_bias
):
    micro, rows, run, model = tokens_in.shape
    hidden = w_up.shape[2]
    seq = lax.axis_size("seq")
    sz = Sizes(micro * rows, run, model, hidden, seq)
    big, down = gather_weights(w_qkv, w_out, w_up, w_down, norm_gains, bias_rows, up_bias)
    state = tokens_in.astype(F32).reshape(sz.tokens, model)
    kept = []
    for layer in range(LAYERS):
        q, keys, values, rims, top, vec, up = layer_before(sz, state, big[layer])
        low, high, tops = exchange(sz, 1, rims[0], rims[1], top[None])
        att, lse, middle, out, keys, values = layer_after(
            sz, state, q, keys, values, low, high, tops, big[layer], down[layer], vec, up
        )
        kept.append((state, q, keys, values, att, lse, middle, vec, up))
        state = out
    out_act = state.astype(BF16).reshape(tokens_in.shape)
    positions = lax.axis_index("seq") * run + jnp.arange(run, dtype=jnp.int32)
    keep = positions >= prefix_len[..., None]
    grad = jnp.where(keep[..., None], grad_output.astype(F32), 0.0).reshape(sz.tokens, model)
    grads = [None] * LAYERS
    for layer in reversed(range(LAYERS)):
        x, q, keys, values, att, lse, middle, vec, up = kept[layer]
        dq, dkeys, dvalues, gm, gout, gup, gdown, gvec, gupb, rims, tops = layer_back(
            sz, grad, middle, att, q, keys, values, lse, big[layer], down[layer], vec, up
        )
        high, low, tops = exchange(sz, 2, rims[1], rims[0], tops)
        grad, gqkv, small = layer_last(sz, x, gm, dq, dkeys, dvalues, low, high, tops, big[layer], vec, gvec, gupb)
        grads[layer] = (gqkv, gout, gup, small, gdown)
    grads = scatter_grads(sz, grads)
    stacked = [jnp.stack([grads[layer][k] for layer in range(LAYERS)], axis=0) for k in range(7)]
    return (out_act, grad.reshape(tokens_in.shape), *stacked)


def solution(mesh):
    tokens, shard = P(None, "dp", "seq", None), P(None, AXES, None)
    small, bias = P(None, None, AXES), P(None, AXES)
    return jax.shard_map(
        on_device,
        mesh=mesh,
        in_specs=(tokens, tokens, P(None, "dp"), shard, shard, shard, shard, small, small, bias),
        out_specs=(tokens, tokens, shard, shard, shard, shard, small, small, bias),
        check_vma=False,
    )
```

```python
import functools
import math

import jax
import jax.numpy as jnp
from jax import lax
from jax.experimental import pallas as pl
from jax.experimental.pallas import tpu as pltpu
from jax.sharding import PartitionSpec as P

HDIM = 64
BLOCK = 16
LEVELS = 6
LAYERS = 2
TOP = LEVELS - 1
CHUNK = 64
LN2 = math.log(2.0)
F32 = jnp.float32
BF16 = jnp.bfloat16
NEG = -1e30
VMEM_LIMIT = 60 * 2**20
AXES = ("dp", "seq")


def dot_nn(a, b):
    return lax.dot_general(a, b, (((1,), (0,)), ((), ())), preferred_element_type=F32)


def dot_nt(a, b):
    return lax.dot_general(a, b, (((1,), (1,)), ((), ())), preferred_element_type=F32)


def dot_tn(a, b):
    return lax.dot_general(a, b, (((0,), (0,)), ((), ())), preferred_element_type=F32)


class Sizes:
    def __init__(self, rows, run, model, hidden, seq):
        self.rows, self.run, self.model, self.hidden, self.seq = rows, run, model, hidden, seq
        self.tokens = rows * run
        self.pairs = model // 128
        self.chunks = run // CHUNK
        self.count = [run >> level for level in range(LEVELS)]
        self.top_keys = self.count[TOP] * seq
        self.offset, at = [], 0
        for level in range(TOP):
            self.offset.append(at)
            at += self.count[level] + 2 * BLOCK
        self.offset.append(at)
        self.bank = at + self.top_keys
        self.keys = [CHUNK + 2 * BLOCK, CHUNK // 2 + 2 * BLOCK] + [2 * BLOCK] * (TOP - 2) + [self.top_keys]
        self.start = [sum(self.keys[:level]) for level in range(LEVELS)]
        self.width = sum(self.keys)
        self.rim = rows * TOP * 2 * BLOCK


def normalise(values):
    centred = values - jnp.mean(values, axis=-1, keepdims=True)
    spread = jnp.mean(centred * centred, axis=-1, keepdims=True)
    inverse = lax.rsqrt(spread + 1e-05)
    return centred * inverse, inverse


def norm_back(grad, hat, inverse, gain):
    scaled = grad * gain
    first = jnp.mean(scaled, axis=-1, keepdims=True)
    second = jnp.mean(scaled * hat, axis=-1, keepdims=True)
    return inverse * (scaled - first - hat * second)


GELU_C = math.sqrt(2.0 / math.pi)


def gelu(v):
    return 0.5 * v * (1.0 + jnp.tanh(GELU_C * (v + 0.044715 * (v * v * v))))


def gelu_both(v):
    square = v * v
    t = jnp.tanh(GELU_C * (v + 0.044715 * (square * v)))
    half = 0.5 * (1.0 + t)
    slope = half + 0.5 * v * (1.0 - t * t) * (GELU_C * (1.0 + 3.0 * 0.044715 * square))
    return v * half, slope


def row_loop(total, step, body):
    def go(j, carry):
        body(pl.ds(pl.multiple_of(j * step, step), step))
        return carry

    lax.fori_loop(0, total // step, go, 0)


def coarse_matrix(run):
    row = lax.broadcasted_iota(jnp.int32, (run, run), 0)
    col = lax.broadcasted_iota(jnp.int32, (run, run), 1)
    out = jnp.zeros((run, run), F32)
    base = 0
    for level in range(1, LEVELS):
        n = run >> level
        hit = (row >= base) & (row < base + n) & ((col >> level) == row - base)
        out = jnp.where(hit, 2.0**-level, out)
        base += n
    return out.astype(BF16)


def spread_matrix():
    row = lax.broadcasted_iota(jnp.int32, (TOP * CHUNK, CHUNK), 0)
    col = lax.broadcasted_iota(jnp.int32, (TOP * CHUNK, CHUNK), 1)
    out = jnp.zeros((TOP * CHUNK, CHUNK), F32)
    for level in range(1, LEVELS):
        base = (level - 1) * CHUNK
        hit = (row >= base) & (row < base + CHUNK) & (((row - base) >> level) == (col >> level))
        out = jnp.where(hit, 2.0**-level, out)
    return out.astype(BF16)


def fill_mask(sz, mask_ref):
    place = lax.axis_index("seq")
    for i in range(sz.chunks):
        for level in range(LEVELS):
            shape = (sz.keys[level], 128)
            key = lax.broadcasted_iota(jnp.int32, shape, 0)
            token = lax.broadcasted_iota(jnp.int32, shape, 1) % CHUNK
            per_run = sz.count[level] // BLOCK
            if level == TOP:
                query_block = ((place * sz.run + i * CHUNK + token) >> TOP) // BLOCK
                allowed = jnp.abs(query_block - key // BLOCK) == 1
            else:
                own = (i * CHUNK >> level) // BLOCK
                if level >= 2:
                    key_block = own - 1 + 2 * (key // BLOCK)
                    allowed = key >= 0
                else:
                    key_block = own - 1 + key // BLOCK
                    distance = jnp.abs(key_block - own - (token >> level) // BLOCK)
                    allowed = distance <= 1 if level == 0 else distance == 1
                whole = place * per_run + key_block
                allowed = allowed & (whole >= 0) & (whole < per_run * sz.seq)
            mask_ref[i, pl.ds(sz.start[level], sz.keys[level])] = jnp.where(allowed, level * LN2, NEG)


def key_slices(sz, i, level):
    if level == TOP:
        return [(sz.offset[TOP], sz.top_keys)]
    if level < 2:
        return [(sz.offset[level] + (CHUNK >> level) * i, sz.keys[level])]
    own = (i * CHUNK) // (BLOCK << level)
    return [(sz.offset[level] + BLOCK * own, BLOCK), (sz.offset[level] + BLOCK * (own + 2), BLOCK)]


def take(ref, pieces, lanes):
    parts = [ref[rows_at(at, size), lanes] for at, size in pieces]
    return parts[0] if len(parts) == 1 else jnp.concatenate(parts, axis=0)


def rows_at(at, size):
    return pl.ds(at if isinstance(at, int) else pl.multiple_of(at, BLOCK), size)


def give(ref, pieces, lanes, value):
    done = 0
    for at, size in pieces:
        ref[rows_at(at, size), lanes] += value[done : done + size]
        done += size


def two_heads(block):
    first = lax.broadcasted_iota(jnp.int32, block.shape, 1) < HDIM
    zero = jnp.zeros_like(block)
    return jnp.concatenate([jnp.where(first, block, zero), jnp.where(first, zero, block)], axis=0)


def one_row(block):
    first = lax.broadcasted_iota(jnp.int32, (CHUNK, 128), 1) < HDIM
    return jnp.where(first, block[:CHUNK], block[CHUNK:])


def chunk_queries(q_ref, spread, tokens):
    fine = q_ref[tokens, :]
    coarse = dot_nn(spread, fine).astype(BF16)
    return [fine] + [coarse[level * CHUNK : (level + 1) * CHUNK] for level in range(TOP)]


def chunks_from(first, count, body):
    if count == 1:
        body(first)
        return

    def go(i, carry):
        body(i)
        return carry

    lax.fori_loop(first, first + count, go, 0)


def attend(sz, spread, q_ref, key_ref, value_ref, mask_ref, att_ref, lse_ref, first, count):
    def chunk(i):
        tokens = rows_at(i * CHUNK, CHUNK)
        queries = chunk_queries(q_ref, spread, tokens)
        for pair in range(sz.pairs):
            lanes = slice(128 * pair, 128 * pair + 128)
            scores, values = [], []
            for level in range(LEVELS):
                pieces = key_slices(sz, i, level)
                values.append(take(value_ref, pieces, lanes))
                scores.append(dot_nt(take(key_ref, pieces, lanes), two_heads(queries[level][:, lanes])))
            scores = jnp.concatenate(scores, axis=0) + mask_ref[i]
            peak = jnp.max(scores, axis=0, keepdims=True)
            weights = jnp.exp(scores - peak)
            total = jnp.sum(weights, axis=0, keepdims=True)
            weights = (weights * (1.0 / total)).astype(BF16)
            mixed = dot_tn(weights, jnp.concatenate(values, axis=0))
            att_ref[tokens, lanes] = one_row(mixed).astype(BF16)
            lse_ref[i, pair : pair + 1, :] = peak + jnp.log(total)

    chunks_from(first, count, chunk)


def attend_back(
    sz, spread, q_ref, key_ref, value_ref, mask_ref, lse_ref, go_ref, dq_ref, dkey_ref, dvalue_ref, first, count
):
    def chunk(i):
        tokens = rows_at(i * CHUNK, CHUNK)
        queries = chunk_queries(q_ref, spread, tokens)
        for pair in range(sz.pairs):
            lanes = slice(128 * pair, 128 * pair + 128)
            pieces = [key_slices(sz, i, level) for level in range(LEVELS)]
            keys = [take(key_ref, piece, lanes) for piece in pieces]
            values = jnp.concatenate([take(value_ref, piece, lanes) for piece in pieces], axis=0)
            doubled = [two_heads(level_queries[:, lanes]) for level_queries in queries]
            scores = jnp.concatenate([dot_nt(k, q) for k, q in zip(keys, doubled)], axis=0) + mask_ref[i]
            weights = jnp.exp(scores - lse_ref[i, pair : pair + 1, :])
            go = two_heads(go_ref[tokens, lanes])
            dweights = dot_nt(values, go)
            inner = jnp.sum(weights * dweights, axis=0, keepdims=True)
            dscores = (weights * (dweights - inner)).astype(BF16)
            dvalues = dot_nn(weights.astype(BF16), go)
            fine, coarse = None, []
            for level in range(LEVELS):
                part = slice(sz.start[level], sz.start[level] + sz.keys[level])
                give(dvalue_ref, pieces[level], lanes, dvalues[part])
                give(dkey_ref, pieces[level], lanes, dot_nn(dscores[part], doubled[level]))
                dquery = one_row(dot_tn(dscores[part], keys[level]))
                if level == 0:
                    fine = dquery
                else:
                    coarse.append(dquery.astype(BF16))
            fine = fine + dot_tn(spread, jnp.concatenate(coarse, axis=0))
            dq_ref[tokens, lanes] = (fine * HDIM**-0.5).astype(BF16)

    chunks_from(first, count, chunk)


def rim_rows(level, kind):
    return pl.ds((level * 2 + kind) * BLOCK, BLOCK)


def unpack_small(sz, small, vec_ref, up_ref):
    lane = lax.broadcasted_iota(jnp.int32, (BLOCK, 128), 1)
    tiles = [small[BLOCK * i : BLOCK * i + BLOCK, :].astype(F32) for i in range(sz.model // BLOCK)]
    for c in range(sz.model // 128):
        total = tiles[8 * c]
        for j in range(1, 8):
            total = jnp.where(lane // 16 == j, tiles[8 * c + j], total)
        vec_ref[:, 128 * c : 128 * c + 128] = total[:8]
    wide = sz.hidden * BLOCK // sz.model
    for c in range(sz.hidden // 128):
        total = tiles[2 * c]
        total = jnp.where(lane >= wide, tiles[2 * c + 1], total)
        up_ref[:, 128 * c : 128 * c + 128] = total[8:9]


def place_rims(sz, low_ref, high_ref, tops_ref, key_ref, value_ref):
    for kind, bank in ((0, key_ref), (1, value_ref)):
        for level in range(TOP):
            bank[pl.ds(sz.offset[level], BLOCK), :] = low_ref[rim_rows(level, kind), :]
            bank[pl.ds(sz.offset[level] + BLOCK + sz.count[level], BLOCK), :] = high_ref[rim_rows(level, kind), :]
        n = sz.count[TOP]
        for s in range(0, sz.seq, 2):
            pair = [tops_ref[s + k, kind * n : kind * n + n, :] for k in range(2)]
            bank[pl.ds(sz.offset[TOP] + s * n, 2 * n), :] = jnp.concatenate(pair, axis=0)


MESH = pl.DeviceIdType.MESH


class Grid:
    def __init__(self, depth):
        dp, seq = lax.axis_index("dp"), lax.axis_index("seq")
        self.depth = depth
        self.z, self.x, self.y, self.c = dp // 2, dp % 2, seq // 2, seq % 2

    def at(self, z, x, y, c):
        return (z * 2 + x, y * 2 + c)

    def index(self, z, x, y, c):
        return z * 8 + x * 4 + y * 2 + c

    def partner(self, axis):
        z, x, y, c = self.z, self.x, self.y, self.c
        return self.at(z, 1 - x if axis == "x" else x, 1 - y if axis == "y" else y, 1 - c if axis == "c" else c)

    def up(self, by):
        return self.at(self.z + by, self.x, self.y, self.c)


def greet(devices):
    barrier = pltpu.get_barrier_semaphore()
    peers = jnp.int32(0)
    for where, condition in devices:
        signal = functools.partial(pl.semaphore_signal, barrier, inc=1, device_id=where, device_id_type=MESH)
        if condition is None:
            signal()
            peers += 1
        else:
            pl.when(condition)(signal)
            peers += condition.astype(jnp.int32)
    pl.semaphore_wait(barrier, peers)


def both(first, second):
    if first is None:
        return second
    return first if second is None else first & second


def when(condition, act):
    if condition is None:
        act()
    else:
        pl.when(condition)(act)


class Gather:
    def __init__(self, grid, pieces, local_sem, send_sem, recv_sem):
        self.grid, self.pieces = grid, pieces
        self.local_sem, self.send_sem, self.recv_sem = local_sem, send_sem, recv_sem
        self.used, self.sends = [0] * len(pieces), []
        z, x, y, c = grid.z, grid.x, grid.y, grid.c
        self.me = grid.index(z, x, y, c)
        self.one = grid.at(z, jnp.where(c == 0, x, 1 - x), jnp.where(c == 0, 1 - y, y), c)
        self.two = grid.at(z, jnp.where(c == 0, 1 - x, x), jnp.where(c == 0, y, 1 - y), c)

    def block(self, z, one, two):
        grid, c = self.grid, self.grid.c
        dx, dy = (two, one), (one, two)
        x = jnp.where(c == 0, grid.x ^ dx[0], grid.x ^ dx[1])
        y = jnp.where(c == 0, grid.y ^ dy[0], grid.y ^ dy[1])
        return grid.index(z, x, y, c)

    def copy(self, p, source, block, slot, to):
        _, out = self.pieces[p]
        rows = self.pieces[p][0].shape[0]
        target = out.at[pl.ds(pl.multiple_of(block * rows, BLOCK), rows)]
        return pltpu.make_async_remote_copy(
            src_ref=target if source is None else source,
            dst_ref=target,
            send_sem=self.send_sem.at[p, slot],
            recv_sem=self.recv_sem.at[p, block],
            device_id=to,
            device_id_type=MESH,
        )

    def local(self, p):
        share, out = self.pieces[p]
        rows = share.shape[0]
        return pltpu.make_async_copy(
            share, out.at[pl.ds(pl.multiple_of(self.me * rows, BLOCK), rows)], self.local_sem.at[p]
        )

    def send(self, p, source, block, to, condition):
        slot = self.used[p]
        self.used[p] += 1
        when(condition, lambda: self.copy(p, source, block, slot, to).start())
        self.sends.append((p, block, slot, to, condition))

    def receive(self, p, block, condition):
        when(condition, lambda: self.copy(p, None, block, 0, self.grid.partner("c")).wait_recv())

    def start(self, p):
        grid, share = self.grid, self.pieces[p][0]
        self.local(p).start()
        self.send(p, share, self.me, grid.up(1), grid.z + 1 < grid.depth)
        self.send(p, share, self.me, grid.up(-1), grid.z > 0)
        for to in (self.one, self.two, grid.partner("c")):
            self.send(p, share, self.me, to, None)

    def arrive(self, p, dz, sign, one, two):
        grid = self.grid
        source = grid.z - sign * dz
        valid = (source >= 0) & (source < grid.depth) if dz else None
        block = self.block(source, one, two)
        self.receive(p, block, valid)
        if one + two == 0 and dz < grid.depth - 1:
            onward = grid.z + sign
            self.send(p, None, block, grid.up(sign), both(valid, (onward >= 0) & (onward < grid.depth)))
        if one + two == 0:
            self.send(p, None, block, self.one, valid)
        if two == 0:
            self.send(p, None, block, self.two, valid)
        self.send(p, None, block, grid.partner("c"), valid)

    def events(self, p):
        found = []
        for two in range(2):
            for one in range(2):
                for dz in range(self.grid.depth):
                    for sign in (1, -1) if dz else (1,):
                        if one + two + dz:
                            found.append((one + two + dz, functools.partial(self.arrive, p, dz, sign, one, two)))
        return found

    def finish(self, p):
        self.local(p).wait()
        grid = self.grid
        for zz in range(grid.depth):
            for xx in range(2):
                for yy in range(2):
                    self.receive(p, grid.index(zz, xx, yy, 1 - grid.c), None)

    def drain(self):
        for p, block, slot, to, condition in self.sends:
            when(condition, lambda: self.copy(p, None, block, slot, to).wait_send())


class Scatter:
    STAGES = 3

    def __init__(self, grid, pieces, buffers, sums, send_sem, recv_sem):
        self.grid, self.pieces, self.buffers, self.sums = grid, pieces, buffers, sums
        self.send_sem, self.recv_sem = send_sem, recv_sem
        self.copies = [[] for _ in pieces]
        z, x, y, c = grid.z, grid.x, grid.y, grid.c
        self.others = [lax.rem(z + k, grid.depth) for k in range(1, grid.depth)]
        self.one = grid.at(z, jnp.where(c == 0, 1 - x, x), jnp.where(c == 0, y, 1 - y), c)
        self.two = grid.at(z, jnp.where(c == 0, x, 1 - x), jnp.where(c == 0, 1 - y, y), c)

    def move(self, p, source, target, to):
        stage = len(self.copies[p])
        copy = pltpu.make_async_remote_copy(
            src_ref=source, dst_ref=target, send_sem=self.send_sem.at[p, stage], recv_sem=self.recv_sem.at[p, stage],
            device_id=to, device_id_type=MESH,
        )
        copy.start()
        self.copies[p].append(copy)

    def begin(self, p):
        self.move(p, self.pieces[p].at[:, :, :, 1 - self.grid.c], self.buffers[p][0], self.grid.partner("c"))

    def first(self, p):
        grid, c = self.grid, self.grid.c
        piece, (from_core, ordered, from_one, _, _) = self.pieces[p], self.buffers[p][:5]
        self.copies[p][0].wait_recv()
        for kind in range(2):
            away = 1 - kind
            for zz in range(grid.depth):
                for second in range(2):
                    xx = jnp.where(c == 0, grid.x ^ away, second)
                    yy = jnp.where(c == 0, second, grid.y ^ away)
                    total = piece[zz, xx, yy, c].astype(F32) + from_core[zz, xx, yy].astype(F32)
                    ordered[kind, zz, second] = total.astype(BF16)
            if kind == 0:
                self.move(p, ordered.at[0], from_one, self.one)

    def second(self, p):
        grid, c = self.grid, self.grid.c
        _, ordered, from_one, held, from_two = self.buffers[p][:5]
        self.copies[p][1].wait_recv()
        mine = jnp.where(c == 0, grid.y, grid.x)
        for kind in range(2):
            place = mine ^ (1 - kind)
            for zz in range(grid.depth):
                total = ordered[1, zz, place].astype(F32) + from_one[zz, place].astype(F32)
                held[kind, zz] = total.astype(BF16)
            if kind == 0:
                self.move(p, held.at[0], from_two, self.two)

    def along(self, p):
        grid = self.grid
        held, from_two, ready, from_z = self.buffers[p][3:7]
        self.copies[p][2].wait_recv()
        for zz in range(grid.depth):
            ready[zz] = (held[1, zz].astype(F32) + from_two[zz].astype(F32)).astype(BF16)
        for k, other in enumerate(self.others):
            self.move(p, ready.at[other], from_z.at[k], grid.at(other, grid.x, grid.y, grid.c))

    def finish(self, p):
        ready, from_z = self.buffers[p][5:7]
        total = ready[self.grid.z].astype(F32)
        for k in range(self.grid.depth - 1):
            self.copies[p][3 + k].wait_recv()
            total = total + from_z[k].astype(F32)
        self.sums[p][...] = total

    def stages(self, p):
        return [functools.partial(act, p) for act in (self.begin, self.first, self.second, self.along, self.finish)]

    def drain(self):
        for copies in self.copies:
            for copy in copies:
                copy.wait_send()


SCATTER_BUFFERS = 7


def scatter_buffers(depth, block):
    leads = ((depth, 2, 2), (2, depth, 2), (depth, 2), (2, depth), (depth,), (depth,), (depth - 1,))
    return [pltpu.VMEM(lead + tuple(block), BF16) for lead in leads]


class Rims:
    def __init__(self, sz, ahead, behind, tops, low, high, all_tops, send_sem, recv_sem):
        self.sz, self.low, self.high, self.all_tops, self.tops = sz, low, high, all_tops, tops
        self.me, self.dp = lax.axis_index("seq"), lax.axis_index("dp")
        me, dp, seq = self.me, self.dp, sz.seq
        make = lambda source, target, k, to: pltpu.make_async_remote_copy(
            src_ref=source, dst_ref=target, send_sem=send_sem.at[k], recv_sem=recv_sem.at[k],
            device_id=(dp, to), device_id_type=MESH,
        )
        self.ahead = lambda: make(ahead, low, 0, me + 1)
        self.behind = lambda: make(behind, high, 1, me - 1)
        self.rest = []
        for k in range(1, seq):
            other = lax.rem(me + k, seq)
            source = tops.at[0] if tops.shape[0] == 1 else tops.at[other]
            self.rest.append(make(source, all_tops.at[me], 1 + k, other))

    def start(self):
        when(self.me + 1 < self.sz.seq, lambda: self.ahead().start())
        when(self.me > 0, lambda: self.behind().start())
        for copy in self.rest:
            copy.start()
        self.all_tops[self.me] = self.tops[0] if self.tops.shape[0] == 1 else self.tops[self.me]

        def no_low():
            self.low[...] = jnp.zeros_like(self.low)

        def no_high():
            self.high[...] = jnp.zeros_like(self.high)

        when(self.me == 0, no_low)
        when(self.me == self.sz.seq - 1, no_high)

    def arrive(self):
        when(self.me > 0, lambda: self.ahead().wait_recv())
        when(self.me + 1 < self.sz.seq, lambda: self.behind().wait_recv())
        for copy in self.rest:
            copy.wait_recv()

    def drain(self):
        when(self.me + 1 < self.sz.seq, lambda: self.ahead().wait_send())
        when(self.me > 0, lambda: self.behind().wait_send())
        for copy in self.rest:
            copy.wait_send()


class Plan:
    def __init__(self):
        self.acts = []

    def add(self, *acts):
        self.acts.extend(acts)

    def step(self, count=1):
        for _ in range(min(count, len(self.acts))):
            self.acts.pop(0)()

    def until(self, mark):
        while mark in self.acts:
            self.acts.pop(0)()


QKV = 0


def forward_kernel(sz, depth, *refs):
    refs = list(refs)
    take_refs = lambda n: [refs.pop(0) for _ in range(n)]
    (tokens_ref,) = take_refs(1)
    shares = take_refs(3)
    out_act_ref, x_ref, q_ref, key_ref, value_ref, att_ref, lse_ref, middle_ref, vec_ref, up_ref = take_refs(10)
    wholes_out = take_refs(3) if depth else []
    wholes = take_refs(3) if depth else shares
    mask_ref, second_ref, state_ref, rims_out, tops_out, low_ref, high_ref, tops_ref, rim_send, rim_recv = take_refs(10)
    model, run = sz.model, sz.run
    plan = Plan()
    me, dp = lax.axis_index("seq"), lax.axis_index("dp")
    if depth:
        local_sem, send_sem, recv_sem, out_sem = take_refs(4)
        grid = Grid(depth)
        peers = [((dp, lax.rem(me + k, sz.seq)), None) for k in range(1, sz.seq)]
        peers += [(grid.partner("x"), None), (grid.up(1), grid.z + 1 < depth), (grid.up(-1), grid.z > 0)]
        greet(peers)
        pieces = [(share.at[layer], whole.at[layer]) for layer in range(LAYERS) for share, whole in zip(shares, wholes)]
        gather = Gather(grid, pieces, local_sem, send_sem, recv_sem)
        acts = []
        saves = []
        for p in range(len(pieces)):
            acts.append((p * SKEW, p, functools.partial(gather.start, p)))
            for hops, act in gather.events(p):
                acts.append((p * SKEW + hops, p, act))

            def done(p=p):
                gather.finish(p)
                saves.append(
                    pltpu.make_async_copy(wholes[p % 3].at[p // 3], wholes_out[p % 3].at[p // 3], out_sem.at[p])
                )
                saves[-1].start()

            acts.append((p * SKEW + depth + 2, p, done))
        acts.sort(key=lambda act: act[:2])
        marks = {}
        for key in sorted({act[0] for act in acts}):
            group = [act for act in acts if act[0] == key]

            def together(group=group):
                for act in group:
                    act[2]()

            plan.add(together)
            marks[key] = together
        need = lambda layer, k: plan.until(marks[(3 * layer + k) * SKEW + depth + 2])
    else:
        greet([((dp, lax.rem(me + k, sz.seq)), None) for k in range(1, sz.seq)])
        need = lambda layer, k: None

    fill_mask(sz, mask_ref)
    coarse = coarse_matrix(run)
    spread = spread_matrix()
    rows_of = lambda r: pl.ds(r * run, run)
    for r in range(sz.rows):
        state_ref[rows_of(r), :] = tokens_ref[r].astype(F32)
    all_rims = []
    for layer in range(LAYERS):
        need(layer, 0)
        qkv, outup, down = wholes[0].at[layer], wholes[1].at[layer], wholes[2].at[layer]
        vec, up = vec_ref.at[layer], up_ref.at[layer]
        unpack_small(sz, qkv[:, 3 * model :], vec, up)
        rims = []
        for r in range(sz.rows):
            hat, _ = normalise(state_ref[rows_of(r), :])
            normed = (hat * vec[0:1, :] + vec[2:3, :]).astype(BF16)
            tops = []
            for kind, bank in ((0, key_ref.at[layer, r]), (1, value_ref.at[layer, r])):
                mixed = dot_nn(normed, qkv[:, (1 + kind) * model : (2 + kind) * model])
                if kind == 1:
                    mixed = mixed + vec[4:5, :]
                mixed = mixed.astype(BF16)
                levels = dot_nn(coarse, mixed).astype(BF16)
                base = 0
                for level in range(LEVELS):
                    n = sz.count[level]
                    if level == 0:
                        now = mixed
                    else:
                        now = levels[base : base + n]
                        base += n
                    if level < TOP:
                        bank[pl.ds(sz.offset[level] + BLOCK, n), :] = now
                        rims_out[layer, r, 0, rim_rows(level, kind), :] = now[n - BLOCK :]
                        rims_out[layer, r, 1, rim_rows(level, kind), :] = now[:BLOCK]
                    else:
                        tops.append(now)
            tops_out[layer, r, 0] = jnp.concatenate(tops, axis=0)
            rims.append(
                Rims(
                    sz, rims_out.at[layer, r, 0], rims_out.at[layer, r, 1], tops_out.at[layer, r], low_ref.at[layer, r],
                    high_ref.at[layer, r], tops_ref.at[layer, r], rim_send.at[layer, r], rim_recv.at[layer, r],
                )
            )
            rims[-1].start()
            queries = (dot_nn(normed, qkv[:, :model]) + vec[3:4, :]).astype(BF16)
            q_ref[layer, r] = queries * jnp.asarray(HDIM**-0.5, BF16)
            plan.step()
        all_rims += rims
        for r in range(sz.rows):
            rims[r].arrive()
            place_rims(sz, low_ref.at[layer, r], high_ref.at[layer, r], tops_ref.at[layer, r], key_ref.at[layer, r], value_ref.at[layer, r])
            for part in range(2):
                half = sz.chunks // 2
                attend(
                    sz, spread, q_ref.at[layer, r], key_ref.at[layer, r], value_ref.at[layer, r], mask_ref,
                    att_ref.at[layer, r], lse_ref.at[layer, r], part * half, half,
                )
                plan.step()
        need(layer, 1)
        for r in range(sz.rows):
            rows = rows_of(r)
            middle = state_ref[rows, :] + dot_nn(att_ref[layer, r], outup[:, :model]) + vec[5:6, :]
            middle_ref[layer, rows, :] = middle
            hat, _ = normalise(middle)
            second_ref[rows, :] = (hat * vec[1:2, :] + vec[6:7, :]).astype(BF16)
            state_ref[rows, :] = middle + vec[7:8, :]
        plan.step()
        need(layer, 2)
        for c in range(sz.hidden // model):
            units = slice(c * model, (c + 1) * model)
            for r in range(sz.rows):
                rows = rows_of(r)
                hidden = dot_nn(second_ref[rows, :], outup[:, (c + 1) * model : (c + 2) * model]) + up[:, units]
                state_ref[rows, :] += dot_nn(gelu(hidden).astype(BF16), down[units, :])
            plan.step()
        if layer == 0:
            x_ref[...] = state_ref[...]
        else:
            for r in range(sz.rows):
                out_act_ref[r] = state_ref[rows_of(r), :].astype(BF16)
    for rims in all_rims:
        rims.drain()
    if depth:
        gather.drain()
        for copy in saves:
            copy.wait()


SKEW = 2


def forward(sz, depth, tokens, shares):
    n, rows, run = sz.model, sz.rows, sz.run
    whole, anywhere = pl.BlockSpec(memory_space=pltpu.VMEM), pl.BlockSpec(memory_space=pl.ANY)
    kept = [
        ((rows, run, n), BF16), ((sz.tokens, n), F32), ((LAYERS, rows, run, n), BF16),
        ((LAYERS, rows, sz.bank, n), BF16), ((LAYERS, rows, sz.bank, n), BF16), ((LAYERS, rows, run, n), BF16),
        ((LAYERS, rows, sz.chunks, sz.pairs, 128), F32), ((LAYERS, sz.tokens, n), F32), ((LAYERS, 8, n), F32),
        ((LAYERS, 1, sz.hidden), F32),
    ]
    out_shape = [jax.ShapeDtypeStruct(shape, dtype) for shape, dtype in kept]
    out_specs = [whole] * len(kept)
    scratch = []
    if depth:
        full = [(LAYERS, 8 * depth * share.shape[1], share.shape[2]) for share in shares]
        out_shape += [jax.ShapeDtypeStruct(shape, BF16) for shape in full]
        out_specs += [anywhere] * 3
        scratch += [pltpu.VMEM(shape, BF16) for shape in full]
    rim = sz.rim // rows
    scratch += [
        pltpu.VMEM((sz.chunks, sz.width, 128), F32), pltpu.VMEM((sz.tokens, n), BF16), pltpu.VMEM((sz.tokens, n), F32),
        pltpu.VMEM((LAYERS, rows, 2, rim, n), BF16), pltpu.VMEM((LAYERS, rows, 1, BLOCK, n), BF16),
        pltpu.VMEM((LAYERS, rows, rim, n), BF16), pltpu.VMEM((LAYERS, rows, rim, n), BF16),
        pltpu.VMEM((LAYERS, rows, sz.seq, BLOCK, n), BF16),
        pltpu.SemaphoreType.DMA((LAYERS, rows, sz.seq + 1)), pltpu.SemaphoreType.DMA((LAYERS, rows, sz.seq + 1)),
    ]
    if depth:
        pieces = 3 * LAYERS
        scratch += [
            pltpu.SemaphoreType.DMA((pieces,)), pltpu.SemaphoreType.DMA((pieces, 16 * depth)),
            pltpu.SemaphoreType.DMA((pieces, 8 * depth)), pltpu.SemaphoreType.DMA((pieces,)),
        ]
    outs = pl.pallas_call(
        functools.partial(forward_kernel, sz, depth),
        out_shape=out_shape,
        in_specs=[whole] * 4,
        out_specs=out_specs,
        scratch_shapes=scratch,
        compiler_params=pltpu.CompilerParams(
            collective_id=0, has_side_effects=True, vmem_limit_bytes=VMEM_LIMIT
        ),
        name="forward",
    )(tokens, *shares)
    return outs[:10], (outs[10:] if depth else shares)


def store_blocks(ref, at, columns, value):
    per = ref.shape[4]
    for k in range(value.shape[0] // per):
        i = at + k
        ref[i // 8, (i // 4) % 2, (i // 2) % 2, i % 2, :, columns] = value[k * per : (k + 1) * per]


def backward_kernel(sz, depth, carried, last, *refs):
    refs = list(refs)
    take_refs = lambda n: [refs.pop(0) for _ in range(n)]
    g_ref, x_ref, middle_ref, att_ref, q_ref, key_ref, value_ref, lse_ref, vec, up = take_refs(10)
    qkv, outup, down = take_refs(3)
    carried_refs = take_refs(carried)
    gin_ref = take_refs(1)[0]
    grads = take_refs(GRADS)
    gup_a, gup_b, gdown, gout, gq, gk, gv, small_ref = grads
    if depth:
        queue = carried_refs + grads[:4] + (grads[4:] if last else [])
        sums = take_refs(len(queue))
    (
        mask_ref, second_ref, gd_ref, gs_ref, go_ref, gm_ref, dq_ref, dkey_ref, dvalue_ref, gvec_ref, gupb_ref, dk_ref,
        dv_ref, levels_ref, normed_ref, rims_out, tops_out, low_ref, high_ref, tops_ref, rim_send, rim_recv,
    ) = take_refs(22)
    model, run = sz.model, sz.run
    plan = Plan()
    me, dp = lax.axis_index("seq"), lax.axis_index("dp")
    peers = [((dp, lax.rem(me + k, sz.seq)), None) for k in range(1, sz.seq)]
    if depth:
        buffers = [take_refs(SCATTER_BUFFERS) for _ in queue]
        send_sem, recv_sem = take_refs(2)
        grid = Grid(depth)
        scatter = Scatter(grid, queue, buffers, sums, send_sem, recv_sem)
        peers += [(grid.partner("x"), None)] + [(grid.at(other, grid.x, grid.y, grid.c), None) for other in scatter.others]
    greet(peers)
    stage = {}

    def launch(*pieces):
        if not depth:
            return
        stages = [scatter.stages(p) for p in pieces]
        for acts in stages:
            acts[0]()
        for k in range(1, 5):
            plan.add(*[acts[k] for acts in stages])

    if carried:
        launch(*range(carried))
    fill_mask(sz, mask_ref)
    spread, coarse = spread_matrix(), coarse_matrix(run)
    rows_of = lambda r: pl.ds(r * run, run)
    gvec_ref[...] = jnp.zeros_like(gvec_ref)
    for r in range(sz.rows):
        rows = rows_of(r)
        hat, _ = normalise(middle_ref[rows, :])
        second_ref[rows, :] = (hat * vec[1:2, :] + vec[6:7, :]).astype(BF16)
        grad = g_ref[rows, :].astype(BF16)
        gd_ref[rows, :] = grad
        gvec_ref[7:8, :] += jnp.sum(grad.astype(F32), axis=0, keepdims=True)
    plan.step()
    parts = sz.hidden // model
    for c in range(parts):
        cols, units = slice((c + 1) * model, (c + 2) * model), slice(c * model, (c + 1) * model)
        hidden = dot_nn(second_ref[...], outup[:, cols]) + up[:, units]
        active, slope = gelu_both(hidden)
        per = gdown.shape[4]
        store_blocks(gdown, c * model // per, slice(None), dot_tn(active.astype(BF16), gd_ref[...]).astype(BF16))
        grad_hidden = (slope * dot_nt(gd_ref[...], down[units, :])).astype(BF16)
        gupb_ref[:, units] = jnp.sum(grad_hidden.astype(F32), axis=0, keepdims=True)
        target, half = (gup_a, gup_b)[c * 2 // parts], c % (parts // 2)
        store_blocks(
            target, 0, slice(half * model, (half + 1) * model), dot_tn(second_ref[...], grad_hidden).astype(BF16)
        )
        back = dot_nt(grad_hidden, outup[:, cols])
        if c == 0:
            gs_ref[...] = back
        else:
            gs_ref[...] += back
        plan.step()
        if c == parts // 2 - 1:
            launch(carried)
    launch(carried + 1, carried + 2)
    for r in range(sz.rows):
        rows = rows_of(r)
        hat, inverse = normalise(middle_ref[rows, :])
        grad = gs_ref[rows, :]
        gvec_ref[1:2, :] += jnp.sum(grad * hat, axis=0, keepdims=True)
        gvec_ref[6:7, :] += jnp.sum(grad, axis=0, keepdims=True)
        gm = g_ref[rows, :] + norm_back(grad, hat, inverse, vec[1:2, :])
        gm_ref[rows, :] = gm
        branch = gm.astype(BF16)
        gd_ref[rows, :] = branch
        gvec_ref[5:6, :] += jnp.sum(branch.astype(F32), axis=0, keepdims=True)
        go_ref[r] = dot_nt(branch, outup[:, :model]).astype(BF16)
    plan.step()
    store_blocks(
        gout, 0, slice(None), sum(dot_tn(att_ref[r], gd_ref[rows_of(r), :]) for r in range(sz.rows)).astype(BF16)
    )
    launch(carried + 3)
    rims = []
    n = sz.count[TOP]
    for r in range(sz.rows):
        dkey, dvalue = dkey_ref.at[r], dvalue_ref.at[r]
        dkey[...] = jnp.zeros(dkey.shape, F32)
        dvalue[...] = jnp.zeros(dvalue.shape, F32)
        for i in range(sz.chunks):
            attend_back(
                sz, spread, q_ref.at[r], key_ref.at[r], value_ref.at[r], mask_ref, lse_ref.at[r], go_ref.at[r],
                dq_ref.at[r], dkey, dvalue, i, 1,
            )
            plan.step(2)
        for kind, bank in ((0, dkey), (1, dvalue)):
            for level in range(TOP):
                rims_out[r, 0, rim_rows(level, kind), :] = bank[pl.ds(sz.offset[level], BLOCK), :].astype(BF16)
                rims_out[r, 1, rim_rows(level, kind), :] = bank[
                    pl.ds(sz.offset[level] + BLOCK + sz.count[level], BLOCK), :
                ].astype(BF16)
        for s in range(sz.seq):
            at = pl.ds(sz.offset[TOP] + s * n, n)
            tops_out[r, s] = jnp.concatenate([dkey[at, :], dvalue[at, :]], axis=0).astype(BF16)
        rims.append(
            Rims(
                sz, rims_out.at[r, 1], rims_out.at[r, 0], tops_out.at[r], low_ref.at[r], high_ref.at[r], tops_ref.at[r],
                rim_send.at[r], rim_recv.at[r],
            )
        )
        rims[-1].start()
    for r in range(sz.rows):
        hat, _ = normalise(x_ref[rows_of(r), :].astype(F32))
        normed_ref[r] = (hat * vec[0:1, :] + vec[2:3, :]).astype(BF16)
        gvec_ref[3:4, :] += jnp.sum(dq_ref[r].astype(F32), axis=0, keepdims=True)
    store_blocks(gq, 0, slice(None), sum(dot_tn(normed_ref[r], dq_ref[r]) for r in range(sz.rows)).astype(BF16))
    if last:
        launch(carried + 4)
    for r in range(sz.rows):
        rims[r].arrive()
        for kind, bank, out in ((0, dkey_ref.at[r], dk_ref), (1, dvalue_ref.at[r], dv_ref)):
            base = 0
            for level in range(LEVELS):
                n = sz.count[level]
                if level == TOP:
                    top = sum(tops_ref[r, s, kind * n : kind * n + n, :].astype(F32) for s in range(sz.seq))
                    levels_ref[pl.ds(base, 2 * n), :] = jnp.concatenate([top, jnp.zeros((n, model), F32)], axis=0).astype(BF16)
                    continue
                own = bank[pl.ds(sz.offset[level] + BLOCK, n), :]
                first = low_ref[r, rim_rows(level, kind), :].astype(F32)
                final = high_ref[r, rim_rows(level, kind), :].astype(F32)
                if n == BLOCK:
                    own = own + first + final
                else:
                    between = [own[BLOCK : n - BLOCK]] if n > 2 * BLOCK else []
                    own = jnp.concatenate([own[:BLOCK] + first, *between, own[n - BLOCK :] + final], axis=0)
                if level == 0:
                    fine = own
                else:
                    levels_ref[pl.ds(base, n), :] = own.astype(BF16)
                    base += n
            out[rows_of(r), :] = (fine + dot_tn(coarse, levels_ref[...])).astype(BF16)
        gvec_ref[4:5, :] += jnp.sum(dv_ref[rows_of(r), :].astype(F32), axis=0, keepdims=True)
        plan.step(2)
    for out, source in ((gk, dk_ref), (gv, dv_ref)):
        store_blocks(
            out, 0, slice(None), sum(dot_tn(normed_ref[r], source[rows_of(r), :]) for r in range(sz.rows)).astype(BF16)
        )
    if last:
        launch(carried + 5, carried + 6)
    for r in range(sz.rows):
        rows = rows_of(r)
        grad = dot_nt(dq_ref[r], qkv[:, :model])
        grad = grad + dot_nt(dk_ref[rows, :], qkv[:, model : 2 * model])
        grad = grad + dot_nt(dv_ref[rows, :], qkv[:, 2 * model : 3 * model])
        hat, inverse = normalise(x_ref[rows, :].astype(F32))
        gvec_ref[0:1, :] += jnp.sum(grad * hat, axis=0, keepdims=True)
        gvec_ref[2:3, :] += jnp.sum(grad, axis=0, keepdims=True)
        gin_ref[rows, :] = gm_ref[rows, :] + norm_back(grad, hat, inverse, vec[0:1, :])
        plan.step()
    for i in range(model // BLOCK):
        top = gvec_ref[:, 128 * (i // 8) : 128 * (i // 8) + 128]
        side = jnp.broadcast_to(gupb_ref[:, 128 * (i // 2) : 128 * (i // 2) + 128], (8, 128))
        store_blocks(small_ref, i, slice(None), jnp.concatenate([top, side], axis=0).astype(BF16))
    if last:
        launch(carried + 7)
    plan.step(len(plan.acts))
    for rim in rims:
        rim.drain()
    if depth:
        scatter.drain()


GRADS = 8


def backward(sz, depth, collective, last, g, x, kept, weights, carried):
    n, rows, run = sz.model, sz.rows, sz.run
    whole = pl.BlockSpec(memory_space=pltpu.VMEM)
    per = sz.hidden * BLOCK // n
    tiles = n // BLOCK // 8
    lead = (tiles, 2, 2, 2)
    half = sz.hidden // 2
    blocks = [(BLOCK, half), (BLOCK, half), (per, n), (BLOCK, n), (BLOCK, n), (BLOCK, n), (BLOCK, n), (BLOCK, 128)]
    outs = [jax.ShapeDtypeStruct((sz.tokens, n), F32)]
    outs += [jax.ShapeDtypeStruct(lead + block, BF16) for block in blocks]
    rim = sz.rim // rows
    scratch = [
        pltpu.VMEM((sz.chunks, sz.width, 128), F32), pltpu.VMEM((sz.tokens, n), BF16), pltpu.VMEM((sz.tokens, n), BF16),
        pltpu.VMEM((sz.tokens, n), F32), pltpu.VMEM((rows, run, n), BF16), pltpu.VMEM((sz.tokens, n), F32),
        pltpu.VMEM((rows, run, n), BF16), pltpu.VMEM((rows, sz.bank, n), F32), pltpu.VMEM((rows, sz.bank, n), F32),
        pltpu.VMEM((8, n), F32), pltpu.VMEM((1, sz.hidden), F32), pltpu.VMEM((sz.tokens, n), BF16),
        pltpu.VMEM((sz.tokens, n), BF16), pltpu.VMEM((run, n), BF16), pltpu.VMEM((rows, run, n), BF16),
        pltpu.VMEM((rows, 2, rim, n), BF16), pltpu.VMEM((rows, sz.seq, BLOCK, n), BF16),
        pltpu.VMEM((rows, rim, n), BF16), pltpu.VMEM((rows, rim, n), BF16), pltpu.VMEM((rows, sz.seq, BLOCK, n), BF16),
        pltpu.SemaphoreType.DMA((rows, sz.seq + 1)), pltpu.SemaphoreType.DMA((rows, sz.seq + 1)),
    ]
    count = 0
    if depth:
        queue = [piece.shape[4:] for piece in carried] + blocks[:4] + (blocks[4:] if last else [])
        count = len(queue)
        outs += [jax.ShapeDtypeStruct(block, F32) for block in queue]
        for block in queue:
            scratch += scatter_buffers(depth, block)
        scratch += [pltpu.SemaphoreType.DMA((count, 2 + depth))] * 2
    result = pl.pallas_call(
        functools.partial(backward_kernel, sz, depth, len(carried), last),
        out_shape=outs,
        in_specs=[whole] * (13 + len(carried)),
        out_specs=[whole] * len(outs),
        scratch_shapes=scratch,
        compiler_params=pltpu.CompilerParams(
            collective_id=collective, has_side_effects=True, vmem_limit_bytes=VMEM_LIMIT
        ),
        name="backward_last" if last else "backward",
    )(g, x, *kept, *weights, *carried)
    return result[0], list(result[1 : 1 + GRADS]), list(result[1 + GRADS :])


def direct(rows):
    return lax.axis_size("seq") == 4 and lax.axis_size("dp") % 2 == 0 and rows % BLOCK == 0


def pack_small(gains, biases, up_bias):
    layers, _, features = gains.shape
    tiles = features // BLOCK
    vec = jnp.concatenate([gains, biases], axis=1).reshape(layers, 8, tiles, BLOCK).transpose(0, 2, 1, 3)
    vec = jnp.tile(vec, (1, 1, 1, 128 // BLOCK))
    up = up_bias.reshape(layers, tiles, 1, up_bias.shape[1] // tiles)
    up = jnp.broadcast_to(jnp.tile(up, (1, 1, 1, 128 // up.shape[3])), (layers, tiles, 8, 128))
    return jnp.concatenate([vec, up], axis=2).reshape(layers, features, 128)


def place_weights(w_qkv, w_out, w_up, w_down, gains, biases, up_bias):
    whole = (lambda array, axis: array) if direct(w_qkv.shape[1]) else (
        lambda array, axis: lax.all_gather(array, AXES, axis=axis, tiled=True)
    )
    small = pack_small(whole(gains, 2), whole(biases, 2), whole(up_bias, 1))
    return (
        jnp.concatenate([whole(w_qkv, 1), small], axis=2),
        whole(jnp.concatenate([w_out, w_up], axis=2), 1),
        whole(w_down, 1),
    )


def unpack_grads(sz, qkv, out, up, small, down):
    wide = sz.hidden * BLOCK // sz.model
    per = 128 // wide
    place = lax.axis_index("dp") * lax.axis_size("seq") + lax.axis_index("seq")
    vec = lax.dynamic_slice(small, (0, BLOCK * (place % 8)), (8, BLOCK))
    return qkv, out, up, down, vec[:2], vec[2:], lax.dynamic_slice(small, (8, wide * (place % per)), (1, wide))[0]


def scatter_by_sums(sz, parts):
    gqkv, gout, gup, small, gdown = parts
    spread = lambda array, axis: lax.psum_scatter(
        array.astype(F32), AXES, scatter_dimension=axis, tiled=True
    )
    tiles = small.reshape(sz.model // BLOCK, BLOCK, 128)
    vec = jnp.concatenate(
        [tiles[i, :8, BLOCK * (i % 8) : BLOCK * (i % 8) + BLOCK] for i in range(sz.model // BLOCK)], axis=1
    )
    wide = sz.hidden * BLOCK // sz.model
    per = 128 // wide
    up = jnp.concatenate(
        [tiles[i, 8, wide * (i % per) : wide * (i % per) + wide] for i in range(sz.model // BLOCK)], axis=0
    )
    vec = spread(vec, 1)
    return spread(gqkv, 0), spread(gout, 0), spread(gup, 0), spread(gdown, 0), vec[:2], vec[2:], spread(up, 0)


def on_device(
    tokens_in, grad_output, prefix_len, w_qkv, w_out, w_up, w_down, norm_gains, bias_rows, up_bias
):
    micro, rows, run, model = tokens_in.shape
    sz = Sizes(micro * rows, run, model, w_up.shape[2], lax.axis_size("seq"))
    depth = lax.axis_size("dp") // 2 if direct(w_qkv.shape[1]) else 0
    shares = place_weights(w_qkv, w_out, w_up, w_down, norm_gains, bias_rows, up_bias)
    tokens = tokens_in.reshape(sz.rows, run, model)
    kept, weights = forward(sz, depth, tokens, shares)
    out_act, x_one, q, keys, values, att, lse, middle, vec, up = kept
    positions = lax.axis_index("seq") * run + jnp.arange(run, dtype=jnp.int32)
    keep = positions >= prefix_len[..., None]
    grad = jnp.where(keep[..., None], grad_output.astype(F32), 0.0).reshape(sz.tokens, model)
    inputs = (tokens_in.reshape(sz.tokens, model), x_one)
    grads, sums, carried = [None] * LAYERS, [None] * LAYERS, []
    for layer in reversed(range(LAYERS)):
        saved = [array[layer] for array in (middle, att, q, keys, values, lse, vec, up)]
        last = layer == 0
        grad, grads[layer], sums[layer] = backward(
            sz, depth, 1 + layer, last, grad, inputs[layer], saved, [array[layer] for array in weights], carried
        )
        carried = grads[layer][4:] if depth else []
    if depth:
        late = sums[0][:4]
        sums = [sums[0][4:], sums[1] + late]
        parts = []
        for up_a, up_b, down, out, dq, dk, dv, small in sums:
            qkv = jnp.concatenate([dq, dk, dv], axis=1)
            parts.append(unpack_grads(sz, qkv, out, jnp.concatenate([up_a, up_b], axis=1), small, down))
    else:
        parts = []
        for layer in range(LAYERS):
            flat = [piece.reshape(-1, piece.shape[-1]) for piece in grads[layer]]
            up_a, up_b, down, out, dq, dk, dv, small = flat
            parts.append(
                scatter_by_sums(
                    sz,
                    (
                        jnp.concatenate([dq, dk, dv], axis=1), out, jnp.concatenate([up_a, up_b], axis=1), small, down,
                    ),
                )
            )
    stacked = [jnp.stack([parts[layer][k] for layer in range(LAYERS)], axis=0) for k in range(7)]
    return (out_act.reshape(tokens_in.shape), grad.reshape(tokens_in.shape), *stacked)


def solution(mesh):
    tokens, shard = P(None, "dp", "seq", None), P(None, AXES, None)
    small, bias = P(None, None, AXES), P(None, AXES)
    return jax.shard_map(
        on_device,
        mesh=mesh,
        in_specs=(tokens, tokens, P(None, "dp"), shard, shard, shard, shard, small, small, bias),
        out_specs=(tokens, tokens, shard, shard, shard, shard, small, small, bias),
        check_vma=False,
    )
```

```python
import functools
import math

import jax
import jax.numpy as jnp
from jax import lax
from jax.experimental import pallas as pl
from jax.experimental.pallas import tpu as pltpu
from jax.sharding import PartitionSpec as P

HDIM = 64
BLOCK = 16
LEVELS = 6
LAYERS = 2
TOP = LEVELS - 1
CHUNK = 64
LN2 = math.log(2.0)
F32 = jnp.float32
BF16 = jnp.bfloat16
NEG = -1e30
VMEM_LIMIT = 60 * 2**20
AXES = ("dp", "seq")


def dot_nn(a, b):
    return lax.dot_general(a, b, (((1,), (0,)), ((), ())), preferred_element_type=F32)


def dot_nt(a, b):
    return lax.dot_general(a, b, (((1,), (1,)), ((), ())), preferred_element_type=F32)


def dot_tn(a, b):
    return lax.dot_general(a, b, (((0,), (0,)), ((), ())), preferred_element_type=F32)


class Sizes:
    def __init__(self, rows, run, model, hidden, seq):
        self.rows, self.run, self.model, self.hidden, self.seq = rows, run, model, hidden, seq
        self.tokens = rows * run
        self.pairs = model // 128
        self.chunks = run // CHUNK
        self.count = [run >> level for level in range(LEVELS)]
        self.top_keys = self.count[TOP] * seq
        self.offset, at = [], 0
        for level in range(TOP):
            self.offset.append(at)
            at += self.count[level] + 2 * BLOCK
        self.offset.append(at)
        self.bank = at + self.top_keys
        self.keys = [CHUNK + 2 * BLOCK, CHUNK // 2 + 2 * BLOCK] + [2 * BLOCK] * (TOP - 2) + [self.top_keys]
        self.start = [sum(self.keys[:level]) for level in range(LEVELS)]
        self.width = sum(self.keys)
        self.rim = rows * TOP * 2 * BLOCK


def normalise(values):
    centred = values - jnp.mean(values, axis=-1, keepdims=True)
    spread = jnp.mean(centred * centred, axis=-1, keepdims=True)
    inverse = lax.rsqrt(spread + 1e-05)
    return centred * inverse, inverse


def norm_back(grad, hat, inverse, gain):
    scaled = grad * gain
    first = jnp.mean(scaled, axis=-1, keepdims=True)
    second = jnp.mean(scaled * hat, axis=-1, keepdims=True)
    return inverse * (scaled - first - hat * second)


GELU_C = math.sqrt(2.0 / math.pi)


def gelu(v):
    return 0.5 * v * (1.0 + jnp.tanh(GELU_C * (v + 0.044715 * (v * v * v))))


def gelu_both(v):
    square = v * v
    t = jnp.tanh(GELU_C * (v + 0.044715 * (square * v)))
    half = 0.5 * (1.0 + t)
    slope = half + 0.5 * v * (1.0 - t * t) * (GELU_C * (1.0 + 3.0 * 0.044715 * square))
    return v * half, slope


def row_loop(total, step, body):
    def go(j, carry):
        body(pl.ds(pl.multiple_of(j * step, step), step))
        return carry

    lax.fori_loop(0, total // step, go, 0)


def coarse_matrix(run):
    row = lax.broadcasted_iota(jnp.int32, (run, run), 0)
    col = lax.broadcasted_iota(jnp.int32, (run, run), 1)
    out = jnp.zeros((run, run), F32)
    base = 0
    for level in range(1, LEVELS):
        n = run >> level
        hit = (row >= base) & (row < base + n) & ((col >> level) == row - base)
        out = jnp.where(hit, 2.0**-level, out)
        base += n
    return out.astype(BF16)


def spread_matrix():
    row = lax.broadcasted_iota(jnp.int32, (TOP * CHUNK, CHUNK), 0)
    col = lax.broadcasted_iota(jnp.int32, (TOP * CHUNK, CHUNK), 1)
    out = jnp.zeros((TOP * CHUNK, CHUNK), F32)
    for level in range(1, LEVELS):
        base = (level - 1) * CHUNK
        hit = (row >= base) & (row < base + CHUNK) & (((row - base) >> level) == (col >> level))
        out = jnp.where(hit, 2.0**-level, out)
    return out.astype(BF16)


def fill_mask(sz, mask_ref):
    place = lax.axis_index("seq")
    for i in range(sz.chunks):
        for level in range(LEVELS):
            shape = (sz.keys[level], 128)
            key = lax.broadcasted_iota(jnp.int32, shape, 0)
            token = lax.broadcasted_iota(jnp.int32, shape, 1) % CHUNK
            per_run = sz.count[level] // BLOCK
            if level == TOP:
                query_block = ((place * sz.run + i * CHUNK + token) >> TOP) // BLOCK
                allowed = jnp.abs(query_block - key // BLOCK) == 1
            else:
                own = (i * CHUNK >> level) // BLOCK
                if level >= 2:
                    key_block = own - 1 + 2 * (key // BLOCK)
                    allowed = key >= 0
                else:
                    key_block = own - 1 + key // BLOCK
                    distance = jnp.abs(key_block - own - (token >> level) // BLOCK)
                    allowed = distance <= 1 if level == 0 else distance == 1
                whole = place * per_run + key_block
                allowed = allowed & (whole >= 0) & (whole < per_run * sz.seq)
            mask_ref[i, pl.ds(sz.start[level], sz.keys[level])] = jnp.where(allowed, level * LN2, NEG)


def key_slices(sz, i, level):
    if level == TOP:
        return [(sz.offset[TOP], sz.top_keys)]
    if level < 2:
        return [(sz.offset[level] + (CHUNK >> level) * i, sz.keys[level])]
    own = (i * CHUNK) // (BLOCK << level)
    return [(sz.offset[level] + BLOCK * own, BLOCK), (sz.offset[level] + BLOCK * (own + 2), BLOCK)]


def take(ref, pieces, lanes):
    parts = [ref[rows_at(at, size), lanes] for at, size in pieces]
    return parts[0] if len(parts) == 1 else jnp.concatenate(parts, axis=0)


def rows_at(at, size):
    return pl.ds(at if isinstance(at, int) else pl.multiple_of(at, BLOCK), size)


def give(ref, pieces, lanes, value):
    done = 0
    for at, size in pieces:
        ref[rows_at(at, size), lanes] += value[done : done + size]
        done += size


def two_heads(block):
    first = lax.broadcasted_iota(jnp.int32, block.shape, 1) < HDIM
    zero = jnp.zeros_like(block)
    return jnp.concatenate([jnp.where(first, block, zero), jnp.where(first, zero, block)], axis=0)


def one_row(block):
    first = lax.broadcasted_iota(jnp.int32, (CHUNK, 128), 1) < HDIM
    return jnp.where(first, block[:CHUNK], block[CHUNK:])


def chunk_queries(q_ref, spread, tokens):
    fine = q_ref[tokens, :]
    coarse = dot_nn(spread, fine).astype(BF16)
    return [fine] + [coarse[level * CHUNK : (level + 1) * CHUNK] for level in range(TOP)]


def chunks_from(first, count, body):
    if count == 1:
        body(first)
        return

    def go(i, carry):
        body(i)
        return carry

    lax.fori_loop(first, first + count, go, 0)


def attend(sz, spread, q_ref, key_ref, value_ref, mask_ref, att_ref, lse_ref, first, count):
    def chunk(i):
        tokens = rows_at(i * CHUNK, CHUNK)
        queries = chunk_queries(q_ref, spread, tokens)
        for pair in range(sz.pairs):
            lanes = slice(128 * pair, 128 * pair + 128)
            scores, values = [], []
            for level in range(LEVELS):
                pieces = key_slices(sz, i, level)
                values.append(take(value_ref, pieces, lanes))
                scores.append(dot_nt(take(key_ref, pieces, lanes), two_heads(queries[level][:, lanes])))
            scores = jnp.concatenate(scores, axis=0) + mask_ref[i]
            peak = jnp.max(scores, axis=0, keepdims=True)
            weights = jnp.exp(scores - peak)
            total = jnp.sum(weights, axis=0, keepdims=True)
            weights = (weights * (1.0 / total)).astype(BF16)
            mixed = dot_tn(weights, jnp.concatenate(values, axis=0))
            att_ref[tokens, lanes] = one_row(mixed).astype(BF16)
            lse_ref[i, pair : pair + 1, :] = peak + jnp.log(total)

    chunks_from(first, count, chunk)


def attend_back(
    sz, spread, q_ref, key_ref, value_ref, mask_ref, lse_ref, go_ref, dq_ref, dkey_ref, dvalue_ref, first, count
):
    def chunk(i):
        tokens = rows_at(i * CHUNK, CHUNK)
        queries = chunk_queries(q_ref, spread, tokens)
        for pair in range(sz.pairs):
            lanes = slice(128 * pair, 128 * pair + 128)
            pieces = [key_slices(sz, i, level) for level in range(LEVELS)]
            keys = [take(key_ref, piece, lanes) for piece in pieces]
            values = jnp.concatenate([take(value_ref, piece, lanes) for piece in pieces], axis=0)
            doubled = [two_heads(level_queries[:, lanes]) for level_queries in queries]
            scores = jnp.concatenate([dot_nt(k, q) for k, q in zip(keys, doubled)], axis=0) + mask_ref[i]
            weights = jnp.exp(scores - lse_ref[i, pair : pair + 1, :])
            go = two_heads(go_ref[tokens, lanes])
            dweights = dot_nt(values, go)
            inner = jnp.sum(weights * dweights, axis=0, keepdims=True)
            dscores = (weights * (dweights - inner)).astype(BF16)
            dvalues = dot_nn(weights.astype(BF16), go)
            fine, coarse = None, []
            for level in range(LEVELS):
                part = slice(sz.start[level], sz.start[level] + sz.keys[level])
                give(dvalue_ref, pieces[level], lanes, dvalues[part])
                give(dkey_ref, pieces[level], lanes, dot_nn(dscores[part], doubled[level]))
                dquery = one_row(dot_tn(dscores[part], keys[level]))
                if level == 0:
                    fine = dquery
                else:
                    coarse.append(dquery.astype(BF16))
            fine = fine + dot_tn(spread, jnp.concatenate(coarse, axis=0))
            dq_ref[tokens, lanes] = (fine * HDIM**-0.5).astype(BF16)

    chunks_from(first, count, chunk)


def rim_rows(level, kind):
    return pl.ds((level * 2 + kind) * BLOCK, BLOCK)


def unpack_small(sz, small, vec_ref, up_ref):
    lane = lax.broadcasted_iota(jnp.int32, (BLOCK, 128), 1)
    tiles = [small[BLOCK * i : BLOCK * i + BLOCK, :].astype(F32) for i in range(sz.model // BLOCK)]
    for c in range(sz.model // 128):
        total = tiles[8 * c]
        for j in range(1, 8):
            total = jnp.where(lane // 16 == j, tiles[8 * c + j], total)
        vec_ref[:, 128 * c : 128 * c + 128] = total[:8]
    wide = sz.hidden * BLOCK // sz.model
    for c in range(sz.hidden // 128):
        total = tiles[2 * c]
        total = jnp.where(lane >= wide, tiles[2 * c + 1], total)
        up_ref[:, 128 * c : 128 * c + 128] = total[8:9]


def place_rims(sz, low_ref, high_ref, tops_ref, key_ref, value_ref):
    for kind, bank in ((0, key_ref), (1, value_ref)):
        for level in range(TOP):
            bank[pl.ds(sz.offset[level], BLOCK), :] = low_ref[rim_rows(level, kind), :]
            bank[pl.ds(sz.offset[level] + BLOCK + sz.count[level], BLOCK), :] = high_ref[rim_rows(level, kind), :]
        n = sz.count[TOP]
        for s in range(0, sz.seq, 2):
            pair = [tops_ref[s + k, kind * n : kind * n + n, :] for k in range(2)]
            bank[pl.ds(sz.offset[TOP] + s * n, 2 * n), :] = jnp.concatenate(pair, axis=0)


MESH = pl.DeviceIdType.MESH


class Grid:
    def __init__(self, depth):
        dp, seq = lax.axis_index("dp"), lax.axis_index("seq")
        self.depth = depth
        self.z, self.x, self.y, self.c = dp // 2, dp % 2, seq // 2, seq % 2

    def at(self, z, x, y, c):
        return (z * 2 + x, y * 2 + c)

    def index(self, z, x, y, c):
        return z * 8 + x * 4 + y * 2 + c

    def partner(self, axis):
        z, x, y, c = self.z, self.x, self.y, self.c
        return self.at(z, 1 - x if axis == "x" else x, 1 - y if axis == "y" else y, 1 - c if axis == "c" else c)

    def up(self, by):
        return self.at(self.z + by, self.x, self.y, self.c)


def greet(devices):
    barrier = pltpu.get_barrier_semaphore()
    peers = jnp.int32(0)
    for where, condition in devices:
        signal = functools.partial(pl.semaphore_signal, barrier, inc=1, device_id=where, device_id_type=MESH)
        if condition is None:
            signal()
            peers += 1
        else:
            pl.when(condition)(signal)
            peers += condition.astype(jnp.int32)
    pl.semaphore_wait(barrier, peers)


def both(first, second):
    if first is None:
        return second
    return first if second is None else first & second


def when(condition, act):
    if condition is None:
        act()
    else:
        pl.when(condition)(act)


class Plan:
    RATE = {"core": 450e3, "plane": 85e3, "z": 85e3}
    HOP = 1.5

    def __init__(self):
        self.now, self.count, self.waiting = 0.0, 0, []
        self.free = dict.fromkeys(self.RATE, 0.0)

    def send(self, link, size):
        self.free[link] = max(self.now, self.free[link]) + size / self.RATE[link]
        return self.free[link] + self.HOP

    def later(self, ready, act):
        self.count += 1
        self.waiting.append((ready, self.count, act))

    def pop(self):
        first = min(self.waiting, key=lambda entry: entry[:2])
        self.waiting.remove(first)
        self.now = max(self.now, first[0])
        first[2]()

    def advance(self, time):
        self.now += time
        while self.waiting and min(entry[0] for entry in self.waiting) <= self.now:
            self.pop()

    def until(self, done):
        while not done():
            self.pop()

    def flush(self):
        while self.waiting:
            self.pop()


class Gather:
    def __init__(self, grid, plan, pieces, local_sem, send_sem, recv_sem):
        self.grid, self.plan, self.pieces = grid, plan, pieces
        self.local_sem, self.send_sem, self.recv_sem = local_sem, send_sem, recv_sem
        z, x, y, c = grid.z, grid.x, grid.y, grid.c
        self.others = [lax.rem(z + k, grid.depth) for k in range(1, grid.depth)]
        one, two = (jnp.where(c == 0, x, 1 - x), jnp.where(c == 0, 1 - y, y)), (
            jnp.where(c == 0, 1 - x, x), jnp.where(c == 0, y, 1 - y),
        )
        self.one, self.two = grid.at(z, *one, c), grid.at(z, *two, c)
        self.lines = [(x, y), one, two, (1 - x, 1 - y)]
        self.ids, self.count = [], 0
        for piece in pieces:
            self.ids.append(list(range(self.count, self.count + len(piece))))
            self.count += len(piece)
        self.sends = []
        self.done = [False] * len(pieces)

    def size(self, p):
        return sum(2 * share.shape[0] * share.shape[1] for share, _ in self.pieces[p])

    def copy(self, array, source, target, slot, landing, to):
        return pltpu.make_async_remote_copy(
            src_ref=source, dst_ref=target, send_sem=self.send_sem.at[array, slot],
            recv_sem=self.recv_sem.at[array, landing], device_id=to, device_id_type=MESH,
        )

    def begin(self, p):
        grid = self.grid
        for array, (share, whole) in zip(self.ids[p], self.pieces[p]):
            mine = whole.at[grid.z, grid.x, grid.y, grid.c]
            pltpu.make_async_copy(share, mine, self.local_sem.at[array]).start()
            for k, other in enumerate(self.others):
                copy = self.copy(array, share, mine, k, k, grid.at(other, grid.x, grid.y, grid.c))
                copy.start()
                self.sends.append(copy)
        ready = self.plan.send("z", 2 * grid.depth * self.size(p))
        self.plan.later(ready, functools.partial(self.along, p))

    def line(self, whole, k):
        xx, yy = self.lines[k]
        return whole.at[:, xx, yy, self.grid.c]

    def pass_line(self, p, k, slots, landing):
        xx, yy = self.lines[k]
        for array, (_, whole) in zip(self.ids[p], self.pieces[p]):
            line = self.line(whole, k)
            for name, slot in slots.items():
                if name == "core":
                    copy = self.copy(array, line, line, slot, 2 + self.grid.depth + xx * 2 + yy, self.grid.partner("c"))
                else:
                    copy = self.copy(array, line, line, slot, landing[name], {"one": self.one, "two": self.two}[name])
                copy.start()
                self.sends.append(copy)

    def receive(self, p, landing, k):
        for array, (_, whole) in zip(self.ids[p], self.pieces[p]):
            line = self.line(whole, k)
            self.copy(array, line, line, 0, landing, self.one).wait_recv()

    def along(self, p):
        grid, size, plan = self.grid, self.size(p), self.plan
        base = grid.depth - 1
        for array, (share, whole) in zip(self.ids[p], self.pieces[p]):
            mine = whole.at[grid.z, grid.x, grid.y, grid.c]
            pltpu.make_async_copy(share, mine, self.local_sem.at[array]).wait()
            for k in range(grid.depth - 1):
                self.copy(array, share, mine, k, k, self.one).wait_recv()
        self.pass_line(p, 0, {"one": base, "two": base + 1, "core": base + 2}, {"one": base, "two": base + 1})
        line = grid.depth * size
        plan.later(plan.send("plane", line), functools.partial(self.after_one, p))
        plan.later(plan.send("plane", line), functools.partial(self.after_two, p))
        plan.send("core", line)

    def after_one(self, p):
        grid, plan = self.grid, self.plan
        base = grid.depth - 1
        self.receive(p, base, 1)
        self.pass_line(p, 1, {"two": base + 3, "core": base + 4}, {"two": base + 2})
        line = grid.depth * self.size(p)
        plan.later(plan.send("plane", line), functools.partial(self.after_both, p))
        plan.send("core", line)

    def after_two(self, p):
        base = self.grid.depth - 1
        self.receive(p, base + 1, 2)
        self.pass_line(p, 2, {"core": base + 5}, {})
        self.plan.send("core", self.grid.depth * self.size(p))

    def after_both(self, p):
        base = self.grid.depth - 1
        self.receive(p, base + 2, 3)
        self.pass_line(p, 3, {"core": base + 6}, {})
        ready = self.plan.send("core", self.grid.depth * self.size(p))
        self.plan.later(ready, functools.partial(self.finish, p))

    def finish(self, p):
        grid = self.grid
        for array, (_, whole) in zip(self.ids[p], self.pieces[p]):
            for k, (xx, yy) in enumerate(self.lines):
                line = whole.at[:, xx, yy, 1 - grid.c]
                self.copy(array, line, line, 0, 2 + grid.depth + xx * 2 + yy, self.one).wait_recv()
        self.done[p] = True

    def need(self, p):
        self.plan.until(lambda: self.done[p])

    def drain(self):
        for copy in self.sends:
            copy.wait_send()


class Scatter:
    def __init__(self, grid, plan, pieces, buffers, sums, send_sem, recv_sem):
        self.grid, self.plan, self.pieces, self.buffers, self.sums = grid, plan, pieces, buffers, sums
        self.done = [False] * len(pieces)
        self.send_sem, self.recv_sem = send_sem, recv_sem
        self.copies = [[] for _ in pieces]
        z, x, y, c = grid.z, grid.x, grid.y, grid.c
        self.others = [lax.rem(z + k, grid.depth) for k in range(1, grid.depth)]
        self.one = grid.at(z, jnp.where(c == 0, 1 - x, x), jnp.where(c == 0, y, 1 - y), c)
        self.two = grid.at(z, jnp.where(c == 0, x, 1 - x), jnp.where(c == 0, 1 - y, y), c)

    def move(self, p, source, target, to):
        stage = len(self.copies[p])
        copy = pltpu.make_async_remote_copy(
            src_ref=source, dst_ref=target, send_sem=self.send_sem.at[p, stage], recv_sem=self.recv_sem.at[p, stage],
            device_id=to, device_id_type=MESH,
        )
        copy.start()
        self.copies[p].append(copy)

    def step(self, link, blocks, p, act):
        piece = self.pieces[p]
        ready = self.plan.send(link, 2 * blocks * piece.shape[4] * piece.shape[5])
        self.plan.later(ready, functools.partial(act, p))

    def begin(self, p):
        self.move(p, self.pieces[p].at[:, :, :, 1 - self.grid.c], self.buffers[p][0], self.grid.partner("c"))
        self.step("core", 4 * self.grid.depth, p, self.first)

    def first(self, p):
        grid, c = self.grid, self.grid.c
        piece, (from_core, ordered, from_one, _, _) = self.pieces[p], self.buffers[p][:5]
        self.copies[p][0].wait_recv()
        for kind in range(2):
            away = 1 - kind
            for zz in range(grid.depth):
                for second in range(2):
                    xx = jnp.where(c == 0, grid.x ^ away, second)
                    yy = jnp.where(c == 0, second, grid.y ^ away)
                    total = piece[zz, xx, yy, c].astype(F32) + from_core[zz, xx, yy].astype(F32)
                    ordered[kind, zz, second] = total.astype(BF16)
            if kind == 0:
                self.move(p, ordered.at[0], from_one, self.one)
                self.step("plane", 2 * grid.depth, p, self.second)

    def second(self, p):
        grid, c = self.grid, self.grid.c
        _, ordered, from_one, held, from_two = self.buffers[p][:5]
        self.copies[p][1].wait_recv()
        mine = jnp.where(c == 0, grid.y, grid.x)
        for kind in range(2):
            place = mine ^ (1 - kind)
            for zz in range(grid.depth):
                total = ordered[1, zz, place].astype(F32) + from_one[zz, place].astype(F32)
                held[kind, zz] = total.astype(BF16)
            if kind == 0:
                self.move(p, held.at[0], from_two, self.two)
                self.step("plane", grid.depth, p, self.along)

    def along(self, p):
        grid = self.grid
        held, from_two, ready, from_z = self.buffers[p][3:7]
        self.copies[p][2].wait_recv()
        for zz in range(grid.depth):
            ready[zz] = (held[1, zz].astype(F32) + from_two[zz].astype(F32)).astype(BF16)
        for k, other in enumerate(self.others):
            self.move(p, ready.at[other], from_z.at[k], grid.at(other, grid.x, grid.y, grid.c))
        self.step("z", 2 * grid.depth, p, self.finish)

    def finish(self, p):
        ready, from_z = self.buffers[p][5:7]
        total = ready[self.grid.z].astype(F32)
        for k in range(self.grid.depth - 1):
            self.copies[p][3 + k].wait_recv()
            total = total + from_z[k].astype(F32)
        self.sums[p][...] = total
        self.done[p] = True

    def drain(self):
        for copies in self.copies:
            for copy in copies:
                copy.wait_send()


SCATTER_BUFFERS = 7


def scatter_buffers(depth, block):
    leads = ((depth, 2, 2), (2, depth, 2), (depth, 2), (2, depth), (depth,), (depth,), (depth - 1,))
    return [pltpu.VMEM(lead + tuple(block), BF16) for lead in leads]


class Rims:
    def __init__(self, sz, ahead, behind, tops, low, high, all_tops, send_sem, recv_sem):
        self.sz, self.low, self.high, self.all_tops, self.tops = sz, low, high, all_tops, tops
        self.me, self.dp = lax.axis_index("seq"), lax.axis_index("dp")
        me, dp, seq = self.me, self.dp, sz.seq
        make = lambda source, target, k, to: pltpu.make_async_remote_copy(
            src_ref=source, dst_ref=target, send_sem=send_sem.at[k], recv_sem=recv_sem.at[k],
            device_id=(dp, to), device_id_type=MESH,
        )
        self.ahead = lambda: make(ahead, low, 0, me + 1)
        self.behind = lambda: make(behind, high, 1, me - 1)
        self.rest = []
        for k in range(1, seq):
            other = lax.rem(me + k, seq)
            source = tops.at[0] if tops.shape[0] == 1 else tops.at[other]
            self.rest.append(make(source, all_tops.at[me], 1 + k, other))

    def start(self):
        when(self.me + 1 < self.sz.seq, lambda: self.ahead().start())
        when(self.me > 0, lambda: self.behind().start())
        for copy in self.rest:
            copy.start()
        self.all_tops[self.me] = self.tops[0] if self.tops.shape[0] == 1 else self.tops[self.me]

        def no_low():
            self.low[...] = jnp.zeros_like(self.low)

        def no_high():
            self.high[...] = jnp.zeros_like(self.high)

        when(self.me == 0, no_low)
        when(self.me == self.sz.seq - 1, no_high)

    def arrive(self):
        when(self.me > 0, lambda: self.ahead().wait_recv())
        when(self.me + 1 < self.sz.seq, lambda: self.behind().wait_recv())
        for copy in self.rest:
            copy.wait_recv()

    def drain(self):
        when(self.me + 1 < self.sz.seq, lambda: self.ahead().wait_send())
        when(self.me > 0, lambda: self.behind().wait_send())
        for copy in self.rest:
            copy.wait_send()


class Copies:
    def __init__(self, sem):
        self.sem, self.open, self.count = sem, {}, 0

    def start(self, name, source, target):
        copy = pltpu.make_async_copy(source, target, self.sem.at[self.count])
        self.count += 1
        copy.start()
        self.open[name] = copy

    def wait(self, *names):
        for name in names:
            if name in self.open:
                self.open.pop(name).wait()

    def drain(self):
        self.wait(*list(self.open))


def whole_rows(ref, columns):
    value = ref[:, :, :, :, :, columns]
    return value.reshape(-1, value.shape[-1])


def some_rows(ref, at, rows):
    per = ref.shape[4]
    blocks = [ref[i // 8, (i // 4) % 2, (i // 2) % 2, i % 2] for i in range(at // per, (at + rows) // per)]
    return jnp.concatenate(blocks, axis=0)


def make_share(sz, gains, biases, up, wide_ref, share_ref):
    wide = up.shape[-1]
    wide_ref[...] = jnp.zeros_like(wide_ref)
    wide_ref[0:2, 0:BLOCK] = gains.astype(F32)
    wide_ref[2:8, 0:BLOCK] = biases.astype(F32)
    wide_ref[8:16, 0:wide] = jnp.broadcast_to(up.astype(F32), (8, wide))
    row = lax.broadcasted_iota(jnp.int32, (128, 128), 0)
    lane = lax.broadcasted_iota(jnp.int32, (128, 128), 1)
    top = jnp.where((row < BLOCK) & (lane % BLOCK == row), 1.0, 0.0).astype(BF16)
    low = jnp.where((row < wide) & (lane % wide == row), 1.0, 0.0).astype(BF16)
    values = wide_ref[...].astype(BF16)
    share_ref[...] = jnp.concatenate([dot_nn(values, top)[:8], dot_nn(values, low)[8:]], axis=0).astype(BF16)


SAVED = 6
TIMES = {"before": 2.2, "attend": 1.6, "project": 1.0, "forward": 1.4, "start": 2.0, "back": 2.8, "branch": 2.0, "attend_back": 2.6,
         "levels": 1.0, "finish": 1.2}


def forward_kernel(sz, depth, *refs):
    refs = list(refs)
    take_refs = lambda n: [refs.pop(0) for _ in range(n)]
    tokens_ref = take_refs(1)[0]
    if depth:
        shares, (gains_ref, biases_ref, upb_ref) = take_refs(4), take_refs(3)
    else:
        wholes = take_refs(5)
    out_act_ref, x_out = take_refs(2)
    saved_out = take_refs(SAVED)
    if depth:
        wholes_out, wholes = take_refs(5), take_refs(5)
    q_ref, key_ref, value_ref, att_ref, lse_ref, middle_ref = take_refs(SAVED)
    x_ref, vec, up, mask_ref, second_ref, state_ref = take_refs(6)
    rims_out, tops_out, low_ref, high_ref, tops_ref, rim_send, rim_recv, copy_sem = take_refs(8)
    model, run = sz.model, sz.run
    wq, wo, wu, wd, ws = wholes
    plan, copies = Plan(), Copies(copy_sem)
    me, dp = lax.axis_index("seq"), lax.axis_index("dp")
    peers = [((dp, lax.rem(me + k, sz.seq)), None) for k in range(1, sz.seq)]
    if depth:
        wide_ref, share_ref, local_sem, send_sem, recv_sem = take_refs(5)
        grid = Grid(depth)
        half = sz.hidden // 2
        pieces = []
        for layer in range(LAYERS):
            part = lambda k, columns: (shares[k].at[layer, :, columns], wholes[k].at[layer, :, :, :, :, :, columns])
            pieces.append([part(0, slice(None)), (share_ref.at[layer], ws.at[layer])])
            pieces.append([part(1, slice(None)), part(2, slice(0, half))])
            pieces.append([part(2, slice(half, None))])
            pieces.append([part(3, slice(None))])
        gather = Gather(grid, plan, pieces, local_sem, send_sem, recv_sem)
        peers += [(grid.partner("x"), None)] + [(grid.at(other, grid.x, grid.y, grid.c), None) for other in gather.others]
        greet(peers)
        for layer in range(LAYERS):
            make_share(
                sz, gains_ref[layer], biases_ref[layer], upb_ref[layer : layer + 1, :], wide_ref, share_ref.at[layer]
            )
        gather.begin(0)
        for p in range(1, 4):
            plan.later(3.0 + 3.0 * p, functools.partial(gather.begin, p))
        for p in range(4, 8):
            plan.later(14.0 + 3.0 * (p - 4), functools.partial(gather.begin, p))

        def need(layer, k):
            gather.need(4 * layer + k)

        def keep(layer):
            for k in range(5):
                copies.start(("weights", layer, k), wholes[k].at[layer], wholes_out[k].at[layer])
    else:
        greet(peers)
        need = lambda layer, k: None
        keep = lambda layer: None

    def save(k, layer):
        source = (q_ref, key_ref, value_ref, att_ref, lse_ref, middle_ref)[k]
        copies.start(("saved", k, layer), source.at[layer], saved_out[k].at[layer])

    fill_mask(sz, mask_ref)
    coarse = coarse_matrix(run)
    spread = spread_matrix()
    rows_of = lambda r: pl.ds(r * run, run)
    for r in range(sz.rows):
        state_ref[rows_of(r), :] = tokens_ref[r].astype(F32)
    all_rims = []
    for layer in range(LAYERS):
        need(layer, 0)
        unpack_small(sz, whole_rows(ws.at[layer], slice(None)), vec, up)
        rims = []
        for r in range(sz.rows):
            hat, _ = normalise(state_ref[rows_of(r), :])
            normed = (hat * vec[0:1, :] + vec[2:3, :]).astype(BF16)
            tops = []
            for kind, bank in ((0, key_ref.at[layer, r]), (1, value_ref.at[layer, r])):
                mixed = dot_nn(normed, whole_rows(wq.at[layer], slice((1 + kind) * model, (2 + kind) * model)))
                if kind == 1:
                    mixed = mixed + vec[4:5, :]
                mixed = mixed.astype(BF16)
                levels = dot_nn(coarse, mixed).astype(BF16)
                base = 0
                for level in range(LEVELS):
                    n = sz.count[level]
                    if level == 0:
                        now = mixed
                    else:
                        now = levels[base : base + n]
                        base += n
                    if level < TOP:
                        bank[pl.ds(sz.offset[level] + BLOCK, n), :] = now
                        rims_out[layer, r, 0, rim_rows(level, kind), :] = now[n - BLOCK :]
                        rims_out[layer, r, 1, rim_rows(level, kind), :] = now[:BLOCK]
                    else:
                        tops.append(now)
            tops_out[layer, r, 0] = jnp.concatenate(tops, axis=0)
            rims.append(
                Rims(
                    sz, rims_out.at[layer, r, 0], rims_out.at[layer, r, 1], tops_out.at[layer, r], low_ref.at[layer, r],
                    high_ref.at[layer, r], tops_ref.at[layer, r], rim_send.at[layer, r], rim_recv.at[layer, r],
                )
            )
            rims[-1].start()
            queries = (dot_nn(normed, whole_rows(wq.at[layer], slice(0, model))) + vec[3:4, :]).astype(BF16)
            q_ref[layer, r] = queries * jnp.asarray(HDIM**-0.5, BF16)
            plan.advance(TIMES["before"])
        save(0, layer)
        all_rims += rims
        for r in range(sz.rows):
            rims[r].arrive()
            place_rims(
                sz, low_ref.at[layer, r], high_ref.at[layer, r], tops_ref.at[layer, r], key_ref.at[layer, r],
                value_ref.at[layer, r],
            )
            for i in range(sz.chunks):
                attend(
                    sz, spread, q_ref.at[layer, r], key_ref.at[layer, r], value_ref.at[layer, r], mask_ref,
                    att_ref.at[layer, r], lse_ref.at[layer, r], i, 1,
                )
                plan.advance(TIMES["attend"])
        for k in (1, 2, 3, 4):
            save(k, layer)
        need(layer, 1)
        for r in range(sz.rows):
            rows = rows_of(r)
            middle = state_ref[rows, :] + dot_nn(att_ref[layer, r], whole_rows(wo.at[layer], slice(None))) + vec[5:6, :]
            middle_ref[layer, rows, :] = middle
            hat, _ = normalise(middle)
            second_ref[rows, :] = (hat * vec[1:2, :] + vec[6:7, :]).astype(BF16)
            state_ref[rows, :] = middle + vec[7:8, :]
            plan.advance(TIMES["project"])
        save(5, layer)
        need(layer, 3)
        parts = sz.hidden // model
        for c in range(parts):
            if c == parts // 2:
                need(layer, 2)
            units = slice(c * model, (c + 1) * model)
            for r in range(sz.rows):
                rows = rows_of(r)
                hidden = dot_nn(second_ref[rows, :], whole_rows(wu.at[layer], units)) + up[:, units]
                state_ref[rows, :] += dot_nn(gelu(hidden).astype(BF16), some_rows(wd.at[layer], c * model, model))
            plan.advance(TIMES["forward"])
        keep(layer)
        if layer == 0:
            x_ref[...] = state_ref[...]
            copies.start("x", x_ref, x_out)
        else:
            for r in range(sz.rows):
                out_act_ref[r] = state_ref[rows_of(r), :].astype(BF16)
    plan.flush()
    for rims in all_rims:
        rims.drain()
    if depth:
        gather.drain()
    copies.drain()


WHOLE = pl.BlockSpec(memory_space=pltpu.VMEM)
ANYWHERE = pl.BlockSpec(memory_space=pl.ANY)


def forward(sz, depth, tokens, weights):
    n, rows, run = sz.model, sz.rows, sz.run
    saved = [
        ((LAYERS, rows, run, n), BF16), ((LAYERS, rows, sz.bank, n), BF16), ((LAYERS, rows, sz.bank, n), BF16),
        ((LAYERS, rows, run, n), BF16), ((LAYERS, rows, sz.chunks, sz.pairs, 128), F32), ((LAYERS, sz.tokens, n), F32),
    ]
    outs = [((rows, run, n), BF16), ((sz.tokens, n), F32)] + saved
    out_specs = [WHOLE] + [ANYWHERE] * (1 + SAVED)
    scratch = []
    if depth:
        full = [((LAYERS, depth, 2, 2, 2) + share.shape[1:], BF16) for share in weights[:4]]
        full.append(((LAYERS, depth, 2, 2, 2, BLOCK, 128), BF16))
        outs += full
        out_specs += [ANYWHERE] * 5
        scratch += full
    rim = sz.rim // rows
    scratch += saved + [
        ((sz.tokens, n), F32), ((8, n), F32), ((1, sz.hidden), F32), ((sz.chunks, sz.width, 128), F32),
        ((sz.tokens, n), BF16), ((sz.tokens, n), F32), ((LAYERS, rows, 2, rim, n), BF16),
        ((LAYERS, rows, 1, BLOCK, n), BF16), ((LAYERS, rows, rim, n), BF16), ((LAYERS, rows, rim, n), BF16),
        ((LAYERS, rows, sz.seq, BLOCK, n), BF16),
    ]
    scratch = [pltpu.VMEM(shape, dtype) for shape, dtype in scratch]
    scratch += [pltpu.SemaphoreType.DMA((LAYERS, rows, sz.seq + 1))] * 2
    scratch += [pltpu.SemaphoreType.DMA((LAYERS * (SAVED + 5) + 1,))]
    if depth:
        arrays = 6 * LAYERS
        scratch += [pltpu.VMEM((BLOCK, 128), F32), pltpu.VMEM((LAYERS, BLOCK, 128), BF16)]
        scratch += [pltpu.SemaphoreType.DMA((arrays,))] + [pltpu.SemaphoreType.DMA((arrays, depth + 6))] * 2
    results = pl.pallas_call(
        functools.partial(forward_kernel, sz, depth),
        out_shape=[jax.ShapeDtypeStruct(shape, dtype) for shape, dtype in outs],
        in_specs=[WHOLE] * (1 + len(weights)),
        out_specs=out_specs,
        scratch_shapes=scratch,
        compiler_params=pltpu.CompilerParams(
            collective_id=0, has_side_effects=True, vmem_limit_bytes=VMEM_LIMIT
        ),
        name="forward",
    )(tokens, *weights)
    return results[0], results[1], results[2 : 2 + SAVED], (results[2 + SAVED :] if depth else weights)


def store_blocks(ref, at, columns, value):
    per = ref.shape[4]
    for k in range(value.shape[0] // per):
        i = at + k
        ref[i // 8, (i // 4) % 2, (i // 2) % 2, i % 2, :, columns] = value[k * per : (k + 1) * per]


def unpack_share(sz, small, gains_ref, biases_ref, up_ref):
    place = lax.axis_index("dp") * lax.axis_size("seq") + lax.axis_index("seq")
    wide = up_ref.shape[-1]
    vec, up = small[0:8, 0:BLOCK], small[8:9, 0:wide]
    for j in range(1, 128 // BLOCK):
        vec = jnp.where(place % (128 // BLOCK) == j, small[0:8, j * BLOCK : (j + 1) * BLOCK], vec)
    for j in range(1, 128 // wide):
        up = jnp.where(place % (128 // wide) == j, small[8:9, j * wide : (j + 1) * wide], up)
    gains_ref[...] = vec[0:2]
    biases_ref[...] = vec[2:8]
    up_ref[...] = up


GRADS = 8
EARLY = 4


def backward_kernel(sz, depth, layer, *refs):
    refs = list(refs)
    take_refs = lambda n: [refs.pop(0) for _ in range(n)]
    top_layer, bottom = layer == LAYERS - 1, layer == 0
    if top_layer:
        prefix_ref, cot_ref, x_ref = take_refs(3)
    else:
        g_ref, x_ref = take_refs(2)
    saved_in, wholes_in = take_refs(SAVED), take_refs(5)
    carried, late, gin_ref = [], [], None
    if depth and bottom:
        carried, above = take_refs(GRADS - EARLY), take_refs(3)
    gin_ref = take_refs(1)[0]
    sums = []
    if depth and bottom:
        out_refs = take_refs(7)
    elif depth:
        out_refs = take_refs(3)
    if depth and bottom:
        grads = None
    else:
        late_out = take_refs(GRADS - EARLY) if depth else take_refs(GRADS)
    (q_ref, key_ref, value_ref, att_ref, lse_ref, middle_ref), wholes = take_refs(SAVED), take_refs(5)
    if depth:
        grads = take_refs(EARLY) + (take_refs(GRADS - EARLY) if bottom else late_out)
    else:
        grads = late_out
    if top_layer:
        g_ref = take_refs(1)[0]
    (
        vec, up, mask_ref, second_ref, gd_ref, gs_ref, go_ref, gm_ref, dq_ref, dkey_ref, dvalue_ref, gvec_ref, gupb_ref,
        dk_ref, dv_ref, levels_ref, normed_ref, rims_out, tops_out, low_ref, high_ref, tops_ref, rim_send, rim_recv,
        copy_sem,
    ) = take_refs(25)
    gup_a, gup_b, gdown, gout, gq, gk, gv, small_ref = grads
    wq, wo, wu, wd, ws = wholes
    model, run = sz.model, sz.run
    half = sz.hidden // 2
    plan, copies = Plan(), Copies(copy_sem)
    for name, source, target in (
        ("middle", saved_in[5], middle_ref), ("ws", wholes_in[4], ws), ("wu", wholes_in[2], wu), ("wd", wholes_in[3], wd),
        ("wo", wholes_in[1], wo), ("att", saved_in[3], att_ref), ("q", saved_in[0], q_ref), ("key", saved_in[1], key_ref),
        ("value", saved_in[2], value_ref), ("lse", saved_in[4], lse_ref), ("wq", wholes_in[0], wq),
    ):
        copies.start(name, source.at[layer], target)
    me, dp = lax.axis_index("seq"), lax.axis_index("dp")
    peers = [((dp, lax.rem(me + k, sz.seq)), None) for k in range(1, sz.seq)]
    if depth:
        queue = list(carried) + grads[:EARLY] + (grads[EARLY:] if bottom else [])
        take_buffers = [take_refs(SCATTER_BUFFERS) for _ in queue]
        send_sem, recv_sem = take_refs(2)
        if bottom:
            gqkv, gwout, gwup, gwdown = out_refs[:4]
            small_sums = take_refs(1)[0]
            qkv_views = lambda at: [gqkv.at[at, :, k * model : (k + 1) * model] for k in range(3)] + [small_sums.at[at]]
            sums = qkv_views(1)
            sums += [gwup.at[0, :, 0:half], gwup.at[0, :, half:], gwdown.at[0], gwout.at[0]] + qkv_views(0)
        else:
            gwout, gwup, gwdown = out_refs
            sums = [gwup.at[:, 0:half], gwup.at[:, half:], gwdown, gwout]
        grid = Grid(depth)
        scatter = Scatter(grid, plan, queue, take_buffers, sums, send_sem, recv_sem)
        peers += [(grid.partner("x"), None)] + [(grid.at(other, grid.x, grid.y, grid.c), None) for other in scatter.others]
    greet(peers)
    first_own = len(carried)

    def launch(*pieces):
        if depth:
            for p in pieces:
                scatter.begin(p)

    launch(*range(first_own))
    fill_mask(sz, mask_ref)
    spread, coarse = spread_matrix(), coarse_matrix(run)
    rows_of = lambda r: pl.ds(r * run, run)
    gvec_ref[...] = jnp.zeros_like(gvec_ref)
    if depth and bottom:
        gwout[1] = above[0][...]
        gwup[1] = above[1][...]
        gwdown[1] = above[2][...]
    if top_layer:
        per_micro = prefix_ref.shape[1]
        place = me * run + lax.broadcasted_iota(jnp.int32, (run, model), 0)
        for r in range(sz.rows):
            kept = place >= prefix_ref[r // per_micro, r % per_micro]
            g_ref[rows_of(r), :] = jnp.where(kept, cot_ref[r].astype(F32), 0.0)
    copies.wait("middle", "ws")
    unpack_small(sz, whole_rows(ws, slice(None)), vec, up)
    for r in range(sz.rows):
        rows = rows_of(r)
        hat, _ = normalise(middle_ref[rows, :])
        second_ref[rows, :] = (hat * vec[1:2, :] + vec[6:7, :]).astype(BF16)
        grad = g_ref[rows, :].astype(BF16)
        gd_ref[rows, :] = grad
        gvec_ref[7:8, :] += jnp.sum(grad.astype(F32), axis=0, keepdims=True)
    copies.wait("wu", "wd")
    plan.advance(TIMES["start"])
    parts = sz.hidden // model
    for c in range(parts):
        units = slice(c * model, (c + 1) * model)
        w_up = whole_rows(wu, units)
        hidden = dot_nn(second_ref[...], w_up) + up[:, units]
        active, slope = gelu_both(hidden)
        per = gdown.shape[4]
        store_blocks(gdown, c * model // per, slice(None), dot_tn(active.astype(BF16), gd_ref[...]).astype(BF16))
        grad_hidden = (slope * dot_nt(gd_ref[...], some_rows(wd, c * model, model))).astype(BF16)
        gupb_ref[:, units] = jnp.sum(grad_hidden.astype(F32), axis=0, keepdims=True)
        target, at = (gup_a, gup_b)[c * 2 // parts], c % (parts // 2)
        store_blocks(target, 0, slice(at * model, (at + 1) * model), dot_tn(second_ref[...], grad_hidden).astype(BF16))
        back = dot_nt(grad_hidden, w_up)
        if c == 0:
            gs_ref[...] = back
        else:
            gs_ref[...] += back
        if c == parts // 2 - 1:
            launch(first_own)
        plan.advance(TIMES["back"])
    launch(first_own + 2, first_own + 1)
    copies.wait("wo")
    for r in range(sz.rows):
        rows = rows_of(r)
        hat, inverse = normalise(middle_ref[rows, :])
        grad = gs_ref[rows, :]
        gvec_ref[1:2, :] += jnp.sum(grad * hat, axis=0, keepdims=True)
        gvec_ref[6:7, :] += jnp.sum(grad, axis=0, keepdims=True)
        gm = g_ref[rows, :] + norm_back(grad, hat, inverse, vec[1:2, :])
        gm_ref[rows, :] = gm
        branch = gm.astype(BF16)
        gd_ref[rows, :] = branch
        gvec_ref[5:6, :] += jnp.sum(branch.astype(F32), axis=0, keepdims=True)
        go_ref[r] = dot_nt(branch, whole_rows(wo, slice(None))).astype(BF16)
    plan.advance(TIMES["branch"])
    copies.wait("att", "q", "key", "value", "lse")
    store_blocks(
        gout, 0, slice(None), sum(dot_tn(att_ref[r], gd_ref[rows_of(r), :]) for r in range(sz.rows)).astype(BF16)
    )
    launch(first_own + 3)
    rims = []
    n = sz.count[TOP]
    for r in range(sz.rows):
        dkey, dvalue = dkey_ref.at[r], dvalue_ref.at[r]
        dkey[...] = jnp.zeros(dkey.shape, F32)
        dvalue[...] = jnp.zeros(dvalue.shape, F32)
        for i in range(sz.chunks):
            attend_back(
                sz, spread, q_ref.at[r], key_ref.at[r], value_ref.at[r], mask_ref, lse_ref.at[r], go_ref.at[r],
                dq_ref.at[r], dkey, dvalue, i, 1,
            )
            plan.advance(TIMES["attend_back"])
        for kind, bank in ((0, dkey), (1, dvalue)):
            for level in range(TOP):
                rims_out[r, 0, rim_rows(level, kind), :] = bank[pl.ds(sz.offset[level], BLOCK), :].astype(BF16)
                rims_out[r, 1, rim_rows(level, kind), :] = bank[
                    pl.ds(sz.offset[level] + BLOCK + sz.count[level], BLOCK), :
                ].astype(BF16)
        for s in range(sz.seq):
            at = pl.ds(sz.offset[TOP] + s * n, n)
            tops_out[r, s] = jnp.concatenate([dkey[at, :], dvalue[at, :]], axis=0).astype(BF16)
        rims.append(
            Rims(
                sz, rims_out.at[r, 1], rims_out.at[r, 0], tops_out.at[r], low_ref.at[r], high_ref.at[r], tops_ref.at[r],
                rim_send.at[r], rim_recv.at[r],
            )
        )
        rims[-1].start()
    for r in range(sz.rows):
        hat, _ = normalise(x_ref[rows_of(r), :].astype(F32))
        normed_ref[r] = (hat * vec[0:1, :] + vec[2:3, :]).astype(BF16)
        gvec_ref[3:4, :] += jnp.sum(dq_ref[r].astype(F32), axis=0, keepdims=True)
    store_blocks(gq, 0, slice(None), sum(dot_tn(normed_ref[r], dq_ref[r]) for r in range(sz.rows)).astype(BF16))
    if bottom:
        launch(first_own + 4)
    plan.advance(TIMES["levels"])
    for r in range(sz.rows):
        rims[r].arrive()
        for kind, bank, out in ((0, dkey_ref.at[r], dk_ref), (1, dvalue_ref.at[r], dv_ref)):
            base = 0
            for level in range(LEVELS):
                n = sz.count[level]
                if level == TOP:
                    top = sum(tops_ref[r, s, kind * n : kind * n + n, :].astype(F32) for s in range(sz.seq))
                    levels_ref[pl.ds(base, 2 * n), :] = jnp.concatenate(
                        [top, jnp.zeros((n, model), F32)], axis=0
                    ).astype(BF16)
                    continue
                own = bank[pl.ds(sz.offset[level] + BLOCK, n), :]
                first = low_ref[r, rim_rows(level, kind), :].astype(F32)
                final = high_ref[r, rim_rows(level, kind), :].astype(F32)
                if n == BLOCK:
                    own = own + first + final
                else:
                    between = [own[BLOCK : n - BLOCK]] if n > 2 * BLOCK else []
                    own = jnp.concatenate([own[:BLOCK] + first, *between, own[n - BLOCK :] + final], axis=0)
                if level == 0:
                    fine = own
                else:
                    levels_ref[pl.ds(base, n), :] = own.astype(BF16)
                    base += n
            out[rows_of(r), :] = (fine + dot_tn(coarse, levels_ref[...])).astype(BF16)
        gvec_ref[4:5, :] += jnp.sum(dv_ref[rows_of(r), :].astype(F32), axis=0, keepdims=True)
        plan.advance(TIMES["levels"])
    for k, (out, source) in enumerate(((gk, dk_ref), (gv, dv_ref))):
        store_blocks(
            out, 0, slice(None), sum(dot_tn(normed_ref[r], source[rows_of(r), :]) for r in range(sz.rows)).astype(BF16)
        )
        if bottom:
            launch(first_own + 5 + k)
    copies.wait("wq")
    for r in range(sz.rows):
        rows = rows_of(r)
        grad = dot_nt(dq_ref[r], whole_rows(wq, slice(0, model)))
        grad = grad + dot_nt(dk_ref[rows, :], whole_rows(wq, slice(model, 2 * model)))
        grad = grad + dot_nt(dv_ref[rows, :], whole_rows(wq, slice(2 * model, 3 * model)))
        hat, inverse = normalise(x_ref[rows, :].astype(F32))
        gvec_ref[0:1, :] += jnp.sum(grad * hat, axis=0, keepdims=True)
        gvec_ref[2:3, :] += jnp.sum(grad, axis=0, keepdims=True)
        gin_ref[rows, :] = gm_ref[rows, :] + norm_back(grad, hat, inverse, vec[0:1, :])
        plan.advance(TIMES["finish"])
    for i in range(model // BLOCK):
        top = gvec_ref[:, 128 * (i // 8) : 128 * (i // 8) + 128]
        side = jnp.broadcast_to(gupb_ref[:, 128 * (i // 2) : 128 * (i // 2) + 128], (8, 128))
        store_blocks(small_ref, i, slice(None), jnp.concatenate([top, side], axis=0).astype(BF16))
    if bottom:
        launch(first_own + 7)
    plan.flush()
    if depth and bottom:
        for at in range(LAYERS):
            unpack_share(sz, small_sums[at], out_refs[4].at[at], out_refs[5].at[at], out_refs[6].at[at])
    for rim in rims:
        rim.drain()
    if depth:
        scatter.drain()


def backward(sz, depth, layer, g, x, saved, wholes, carried, above):
    n, rows, run = sz.model, sz.rows, sz.run
    top_layer, bottom = layer == LAYERS - 1, layer == 0
    per = sz.hidden * BLOCK // n
    lead = (n // BLOCK // 8, 2, 2, 2)
    half = sz.hidden // 2
    blocks = [(BLOCK, half), (BLOCK, half), (per, n), (BLOCK, n), (BLOCK, n), (BLOCK, n), (BLOCK, n), (BLOCK, 128)]
    pieces = [(lead + block, BF16) for block in blocks]
    outs = [((sz.tokens, n), F32)]
    if depth and bottom:
        outs += [((LAYERS,) + shape, F32) for shape in (
            (BLOCK, 3 * n), (BLOCK, n), (BLOCK, sz.hidden), (per, n), (2, BLOCK), (6, BLOCK), (1, per)
        )]
    elif depth:
        outs += [((BLOCK, n), F32), ((BLOCK, sz.hidden), F32), ((per, n), F32)] + pieces[EARLY:]
    else:
        outs += pieces
    rim = sz.rim // rows
    scratch = [(array.shape[1:], array.dtype) for array in list(saved) + list(wholes)]
    if depth:
        scratch += pieces[:EARLY] + (pieces[EARLY:] if bottom else [])
    if top_layer:
        scratch += [((sz.tokens, n), F32)]
    scratch += [
        ((8, n), F32), ((1, sz.hidden), F32), ((sz.chunks, sz.width, 128), F32), ((sz.tokens, n), BF16),
        ((sz.tokens, n), BF16), ((sz.tokens, n), F32), ((rows, run, n), BF16), ((sz.tokens, n), F32),
        ((rows, run, n), BF16), ((rows, sz.bank, n), F32), ((rows, sz.bank, n), F32), ((8, n), F32),
        ((1, sz.hidden), F32), ((sz.tokens, n), BF16), ((sz.tokens, n), BF16), ((run, n), BF16), ((rows, run, n), BF16),
        ((rows, 2, rim, n), BF16), ((rows, sz.seq, BLOCK, n), BF16), ((rows, rim, n), BF16), ((rows, rim, n), BF16),
        ((rows, sz.seq, BLOCK, n), BF16),
    ]
    scratch = [pltpu.VMEM(shape, dtype) for shape, dtype in scratch]
    scratch += [pltpu.SemaphoreType.DMA((rows, sz.seq + 1))] * 2 + [pltpu.SemaphoreType.DMA((SAVED + 5,))]
    if depth:
        queue = [piece.shape[4:] for piece in carried] + blocks[:EARLY] + (blocks[EARLY:] if bottom else [])
        for block in queue:
            scratch += scatter_buffers(depth, block)
        scratch += [pltpu.SemaphoreType.DMA((len(queue), 2 + depth))] * 2
        if bottom:
            scratch += [pltpu.VMEM((LAYERS, BLOCK, 128), F32)]
    first = [pl.BlockSpec(memory_space=pltpu.SMEM), WHOLE] if top_layer else [WHOLE]
    result = pl.pallas_call(
        functools.partial(backward_kernel, sz, depth, layer),
        out_shape=[jax.ShapeDtypeStruct(shape, dtype) for shape, dtype in outs],
        in_specs=first + [WHOLE] + [ANYWHERE] * (SAVED + 5) + [WHOLE] * (len(carried) + len(above)),
        out_specs=[WHOLE] * len(outs),
        scratch_shapes=scratch,
        compiler_params=pltpu.CompilerParams(
            collective_id=1 + layer, has_side_effects=True, vmem_limit_bytes=VMEM_LIMIT
        ),
        name="backward_%d" % layer,
    )(*g, x, *saved, *wholes, *carried, *above)
    return result[0], list(result[1:])


def direct(rows):
    return lax.axis_size("seq") == 4 and lax.axis_size("dp") % 2 == 0 and rows % BLOCK == 0


def pack_small(gains, biases, up_bias):
    layers, _, features = gains.shape
    tiles = features // BLOCK
    vec = jnp.concatenate([gains, biases], axis=1).reshape(layers, 8, tiles, BLOCK).transpose(0, 2, 1, 3)
    vec = jnp.tile(vec, (1, 1, 1, 128 // BLOCK))
    up = up_bias.reshape(layers, tiles, 1, up_bias.shape[1] // tiles)
    up = jnp.broadcast_to(jnp.tile(up, (1, 1, 1, 128 // up.shape[3])), (layers, tiles, 8, 128))
    return jnp.concatenate([vec, up], axis=2).reshape(layers, features, 128)


def whole_weights(w_qkv, w_out, w_up, w_down, gains, biases, up_bias):
    whole = lambda array, axis: lax.all_gather(array, AXES, axis=axis, tiled=True)
    small = pack_small(whole(gains, 2), whole(biases, 2), whole(up_bias, 1))
    tiles = small.shape[1] // BLOCK
    arrays = (whole(w_qkv, 1), whole(w_out, 1), whole(w_up, 1), whole(w_down, 1), small)
    return [
        array.reshape(LAYERS, tiles // 8, 2, 2, 2, array.shape[1] // tiles, array.shape[2]) for array in arrays
    ]


def scatter_by_sums(sz, parts):
    gqkv, gout, gup, small, gdown = parts
    spread = lambda array, axis: lax.psum_scatter(
        array.astype(F32), AXES, scatter_dimension=axis, tiled=True
    )
    tiles = small.reshape(sz.model // BLOCK, BLOCK, 128)
    vec = jnp.concatenate(
        [tiles[i, :8, BLOCK * (i % 8) : BLOCK * (i % 8) + BLOCK] for i in range(sz.model // BLOCK)], axis=1
    )
    wide = sz.hidden * BLOCK // sz.model
    per = 128 // wide
    up = jnp.concatenate(
        [tiles[i, 8, wide * (i % per) : wide * (i % per) + wide] for i in range(sz.model // BLOCK)], axis=0
    )
    vec = spread(vec, 1)
    return spread(gqkv, 0), spread(gout, 0), spread(gup, 0), spread(gdown, 0), vec[:2], vec[2:], spread(up, 0)


def on_device(
    tokens_in, grad_output, prefix_len, w_qkv, w_out, w_up, w_down, norm_gains, bias_rows, up_bias
):
    micro, rows, run, model = tokens_in.shape
    sz = Sizes(micro * rows, run, model, w_up.shape[2], lax.axis_size("seq"))
    depth = lax.axis_size("dp") // 2 if direct(w_qkv.shape[1]) else 0
    weights = (w_qkv, w_out, w_up, w_down, norm_gains, bias_rows, up_bias)
    if not depth:
        weights = whole_weights(*weights)
    by_row = (sz.rows, run, model)
    out_act, x_one, saved, wholes = forward(sz, depth, tokens_in.reshape(by_row), weights)
    first = [prefix_len, grad_output.reshape(by_row)]
    grad, parts = backward(sz, depth, 1, first, x_one, saved, wholes, [], [])
    x_zero = tokens_in.reshape(sz.tokens, model)
    if depth:
        grad, totals = backward(sz, depth, 0, [grad], x_zero, saved, wholes, parts[3:], parts[:3])
        gqkv, gout, gup, gdown, gains, biases, ups = totals
        results = (gqkv, gout, gup, gdown, gains, biases, ups.reshape(up_bias.shape))
    else:
        grad, own = backward(sz, depth, 0, [grad], x_zero, saved, wholes, [], [])
        layers = []
        for pieces in (own, parts):
            up_a, up_b, down, out, dq, dk, dv, small = [piece.reshape(-1, piece.shape[-1]) for piece in pieces]
            qkv, up = jnp.concatenate([dq, dk, dv], axis=1), jnp.concatenate([up_a, up_b], axis=1)
            layers.append(scatter_by_sums(sz, (qkv, out, up, small, down)))
        results = [jnp.stack([layer[k] for layer in layers], axis=0) for k in range(7)]
    return (out_act.reshape(tokens_in.shape), grad.reshape(tokens_in.shape), *results)


def solution(mesh):
    tokens, shard = P(None, "dp", "seq", None), P(None, AXES, None)
    small, bias = P(None, None, AXES), P(None, AXES)
    return jax.shard_map(
        on_device,
        mesh=mesh,
        in_specs=(tokens, tokens, P(None, "dp"), shard, shard, shard, shard, small, small, bias),
        out_specs=(tokens, tokens, shard, shard, shard, shard, small, small, bias),
        check_vma=False,
    )
```

```python
import functools
import math

import jax
import jax.numpy as jnp
from jax import lax
from jax.experimental import pallas as pl
from jax.experimental.pallas import tpu as pltpu
from jax.sharding import PartitionSpec as P

HDIM = 64
BLOCK = 16
LEVELS = 6
LAYERS = 2
TOP = LEVELS - 1
CHUNK = 64
LN2 = math.log(2.0)
F32 = jnp.float32
BF16 = jnp.bfloat16
NEG = -1e30
VMEM_LIMIT = 62 * 2**20
AXES = ("dp", "seq")


def dot_nn(a, b):
    return lax.dot_general(a, b, (((1,), (0,)), ((), ())), preferred_element_type=F32)


def dot_nt(a, b):
    return lax.dot_general(a, b, (((1,), (1,)), ((), ())), preferred_element_type=F32)


def dot_tn(a, b):
    return lax.dot_general(a, b, (((0,), (0,)), ((), ())), preferred_element_type=F32)


class Sizes:
    def __init__(self, rows, run, model, hidden, seq):
        self.rows, self.run, self.model, self.hidden, self.seq = rows, run, model, hidden, seq
        self.tokens = rows * run
        self.pairs = model // 128
        self.chunks = run // CHUNK
        self.count = [run >> level for level in range(LEVELS)]
        self.top_keys = self.count[TOP] * seq
        self.offset, at = [], 0
        for level in range(TOP):
            self.offset.append(at)
            at += self.count[level] + 2 * BLOCK
        self.offset.append(at)
        self.bank = at + self.top_keys
        self.keys = [CHUNK + 2 * BLOCK, CHUNK // 2 + 2 * BLOCK] + [2 * BLOCK] * (TOP - 2) + [self.top_keys]
        self.start = [sum(self.keys[:level]) for level in range(LEVELS)]
        self.width = sum(self.keys)
        self.rim = rows * TOP * 2 * BLOCK


def normalise(values):
    centred = values - jnp.mean(values, axis=-1, keepdims=True)
    spread = jnp.mean(centred * centred, axis=-1, keepdims=True)
    inverse = lax.rsqrt(spread + 1e-05)
    return centred * inverse, inverse


def norm_back(grad, hat, inverse, gain):
    scaled = grad * gain
    first = jnp.mean(scaled, axis=-1, keepdims=True)
    second = jnp.mean(scaled * hat, axis=-1, keepdims=True)
    return inverse * (scaled - first - hat * second)


GELU_C = math.sqrt(2.0 / math.pi)


def gelu(v):
    return 0.5 * v * (1.0 + jnp.tanh(GELU_C * (v + 0.044715 * (v * v * v))))


def gelu_both(v):
    square = v * v
    t = jnp.tanh(GELU_C * (v + 0.044715 * (square * v)))
    half = 0.5 * (1.0 + t)
    slope = half + 0.5 * v * (1.0 - t * t) * (GELU_C * (1.0 + 3.0 * 0.044715 * square))
    return v * half, slope


def row_loop(total, step, body):
    def go(j, carry):
        body(pl.ds(pl.multiple_of(j * step, step), step))
        return carry

    lax.fori_loop(0, total // step, go, 0)


def coarse_matrix(run):
    row = lax.broadcasted_iota(jnp.int32, (run, run), 0)
    col = lax.broadcasted_iota(jnp.int32, (run, run), 1)
    out = jnp.zeros((run, run), F32)
    base = 0
    for level in range(1, LEVELS):
        n = run >> level
        hit = (row >= base) & (row < base + n) & ((col >> level) == row - base)
        out = jnp.where(hit, 2.0**-level, out)
        base += n
    return out.astype(BF16)


COARSE = [0] + [CHUNK - (CHUNK >> (level - 1)) for level in range(1, LEVELS + 1)]


def chunk_matrix():
    row = lax.broadcasted_iota(jnp.int32, (CHUNK, CHUNK), 0)
    col = lax.broadcasted_iota(jnp.int32, (CHUNK, CHUNK), 1)
    out = jnp.zeros((CHUNK, CHUNK), F32)
    for level in range(1, LEVELS):
        at, end = COARSE[level], COARSE[level + 1]
        out = jnp.where((row >= at) & (row < end) & ((col >> level) == row - at), 2.0**-level, out)
    return out.astype(BF16)


def sum_matrix():
    token = lax.broadcasted_iota(jnp.int32, (128, 128), 0)
    col = lax.broadcasted_iota(jnp.int32, (128, 128), 1)
    place, within = col % CHUNK, token % CHUNK
    out = jnp.zeros((128, 128), F32)
    for level in range(1, LEVELS):
        at, end = COARSE[level], COARSE[level + 1]
        out = jnp.where((place >= at) & (place < end) & ((within >> level) == place - at), 1.0, out)
    return jnp.where(token // CHUNK == col // CHUNK, out, 0.0).astype(BF16)


def fill_index(sz, index_ref):
    lane = lax.broadcasted_iota(jnp.int32, (8, 128), 1)
    for level in range(1, LEVELS):
        value = (lane // CHUNK) * CHUNK + COARSE[level] + ((lane % CHUNK) >> level)
        for k in range(sz.keys[level] // 8):
            index_ref[pl.ds(sz.start[level] - sz.start[1] + 8 * k, 8), :] = value


def fill_own(sz, own_ref):
    place = lax.broadcasted_iota(jnp.int32, (8, 128), 1) % CHUNK
    for level in range(1, LEVELS):
        value = jnp.where((place >= COARSE[level]) & (place < COARSE[level + 1]), 1.0, 0.0)
        for k in range(sz.keys[level] // 8):
            own_ref[pl.ds(sz.start[level] - sz.start[1] + 8 * k, 8), :] = value


def fill_mask(sz, mask_ref):
    place = lax.axis_index("seq")
    for i in range(sz.chunks):
        for level in range(LEVELS):
            shape = (sz.keys[level], 128)
            key = lax.broadcasted_iota(jnp.int32, shape, 0)
            token = lax.broadcasted_iota(jnp.int32, shape, 1) % CHUNK
            per_run = sz.count[level] // BLOCK
            if level == TOP:
                query_block = ((place * sz.run + i * CHUNK + token) >> TOP) // BLOCK
                allowed = jnp.abs(query_block - key // BLOCK) == 1
            else:
                own = (i * CHUNK >> level) // BLOCK
                if level >= 2:
                    key_block = own - 1 + 2 * (key // BLOCK)
                    allowed = key >= 0
                else:
                    key_block = own - 1 + key // BLOCK
                    distance = jnp.abs(key_block - own - (token >> level) // BLOCK)
                    allowed = distance <= 1 if level == 0 else distance == 1
                whole = place * per_run + key_block
                allowed = allowed & (whole >= 0) & (whole < per_run * sz.seq)
            mask_ref[i, pl.ds(sz.start[level], sz.keys[level])] = jnp.where(allowed, level * LN2, NEG)


def key_slices(sz, i, level):
    if level == TOP:
        return [(sz.offset[TOP], sz.top_keys)]
    if level < 2:
        return [(sz.offset[level] + (CHUNK >> level) * i, sz.keys[level])]
    own = (i * CHUNK) // (BLOCK << level)
    return [(sz.offset[level] + BLOCK * own, BLOCK), (sz.offset[level] + BLOCK * (own + 2), BLOCK)]


def take(ref, pieces, lanes):
    parts = [ref[rows_at(at, size), lanes] for at, size in pieces]
    return parts[0] if len(parts) == 1 else jnp.concatenate(parts, axis=0)


def rows_at(at, size):
    return pl.ds(at if isinstance(at, int) else pl.multiple_of(at, BLOCK), size)


def give(ref, pieces, lanes, value):
    done = 0
    for at, size in pieces:
        ref[rows_at(at, size), lanes] += value[done : done + size]
        done += size


def two_heads(block):
    first = lax.broadcasted_iota(jnp.int32, block.shape, 1) < HDIM
    zero = jnp.zeros_like(block)
    return jnp.concatenate([jnp.where(first, block, zero), jnp.where(first, zero, block)], axis=0)


def one_row(block):
    first = lax.broadcasted_iota(jnp.int32, (CHUNK, 128), 1) < HDIM
    return jnp.where(first, block[:CHUNK], block[CHUNK:])


class Units:
    def __init__(self, sz, q_ref, key_ref, value_ref):
        self.sz, self.q_ref, self.key_ref, self.value_ref = sz, q_ref, key_ref, value_ref
        self.all = [(i, pair) for i in range(sz.chunks) for pair in range(sz.pairs)]
        self.pieces = []
        for i in range(sz.chunks):
            levels = [key_slices(sz, i, level) for level in range(LEVELS)]
            self.pieces.append((levels[0], sum(levels[1:], [])))
        matrix = chunk_matrix()
        self.fine = [q_ref[self.tokens(i), :] for i in range(sz.chunks)]
        self.coarse = [dot_nn(matrix, fine).astype(BF16) for fine in self.fine]

    def tokens(self, i):
        return pl.ds(i * CHUNK, CHUNK)

    def lanes(self, pair):
        return slice(128 * pair, 128 * pair + 128)

    def queries(self, i, pair):
        lanes = self.lanes(pair)
        return two_heads(self.fine[i][:, lanes]), two_heads(self.coarse[i][:, lanes])

    def keys(self, i, pair):
        return [take(self.key_ref, pieces, self.lanes(pair)) for pieces in self.pieces[i]]

    def values(self, i, pair):
        return take(self.value_ref, self.pieces[i][0] + self.pieces[i][1], self.lanes(pair))

    def scores(self, u, i, pair, mask_ref, index_ref, out_ref):
        base = self.sz.start[1]
        (fine_keys, coarse_keys), (fine, coarse) = self.keys(i, pair), self.queries(i, pair)
        out_ref[u, :base] = dot_nt(fine_keys, fine) + mask_ref[i, :base]
        upper = jnp.take_along_axis(dot_nt(coarse_keys, coarse), index_ref[...], axis=1)
        out_ref[u, base:] = upper + mask_ref[i, base:]


def attend(sz, q_ref, key_ref, value_ref, mask_ref, index_ref, att_ref, lse_ref, score_ref, weight_ref, pause):
    units = Units(sz, q_ref, key_ref, value_ref)
    for u, (i, pair) in enumerate(units.all):
        units.scores(u, i, pair, mask_ref, index_ref, score_ref)
    pause()
    for u, (i, pair) in enumerate(units.all):
        scores = score_ref[u]
        peak = jnp.max(scores, axis=0, keepdims=True)
        weights = jnp.exp(scores - peak)
        total = jnp.sum(weights, axis=0, keepdims=True)
        lse_ref[i, pair : pair + 1, :] = peak + jnp.log(total)
        weight_ref[u] = (weights * (1.0 / total)).astype(BF16)
    pause()
    for u, (i, pair) in enumerate(units.all):
        mixed = dot_tn(weight_ref[u], units.values(i, pair))
        att_ref[units.tokens(i), units.lanes(pair)] = one_row(mixed).astype(BF16)
    pause()


def attend_back(
    sz, q_ref, key_ref, value_ref, mask_ref, index_ref, own_ref, lse_ref, go_ref, dq_ref, dkey_ref, dvalue_ref,
    score_ref, back_ref, weight_ref, dscore_ref, coarse_ref, pause
):
    units = Units(sz, q_ref, key_ref, value_ref)
    sums, matrix, base = sum_matrix(), chunk_matrix(), sz.start[1]
    for u, (i, pair) in enumerate(units.all):
        units.scores(u, i, pair, mask_ref, index_ref, score_ref)
    pause()
    for u, (i, pair) in enumerate(units.all):
        go = two_heads(go_ref[units.tokens(i), units.lanes(pair)])
        back_ref[u] = dot_nt(units.values(i, pair), go)
    for u, (i, pair) in enumerate(units.all):
        weights = jnp.exp(score_ref[u] - lse_ref[i, pair : pair + 1, :])
        weight_ref[u] = weights.astype(BF16)
        back = back_ref[u]
        inner = jnp.sum(weights * back, axis=0, keepdims=True)
        dscore_ref[u] = (weights * (back - inner)).astype(BF16)
    pause()
    for u, (i, pair) in enumerate(units.all):
        go = two_heads(go_ref[units.tokens(i), units.lanes(pair)])
        give(dvalue_ref, units.pieces[i][0] + units.pieces[i][1], units.lanes(pair), dot_nn(weight_ref[u], go))
    for u, (i, pair) in enumerate(units.all):
        coarse_ref[u] = (dot_nn(dscore_ref[u, base:], sums) * own_ref[...]).astype(BF16)
    pause()
    for u, (i, pair) in enumerate(units.all):
        (first, upper), (fine, coarse) = units.pieces[i], units.queries(i, pair)
        give(dkey_ref, first, units.lanes(pair), dot_nn(dscore_ref[u, :base], fine))
        give(dkey_ref, upper, units.lanes(pair), dot_nn(coarse_ref[u], coarse))
    pause()
    for u, (i, pair) in enumerate(units.all):
        fine_keys, coarse_keys = units.keys(i, pair)
        fine = one_row(dot_tn(dscore_ref[u, :base], fine_keys))
        coarse = one_row(dot_tn(coarse_ref[u], coarse_keys)).astype(BF16)
        dq_ref[units.tokens(i), units.lanes(pair)] = ((fine + dot_tn(matrix, coarse)) * HDIM**-0.5).astype(BF16)
    pause()


def rim_rows(level, kind):
    return pl.ds((level * 2 + kind) * BLOCK, BLOCK)


def unpack_small(sz, small, vec_ref, up_ref):
    lane = lax.broadcasted_iota(jnp.int32, (BLOCK, 128), 1)
    tiles = [small[BLOCK * i : BLOCK * i + BLOCK, :].astype(F32) for i in range(sz.model // BLOCK)]
    for c in range(sz.model // 128):
        total = tiles[8 * c]
        for j in range(1, 8):
            total = jnp.where(lane // 16 == j, tiles[8 * c + j], total)
        vec_ref[:, 128 * c : 128 * c + 128] = total[:8]
    wide = sz.hidden * BLOCK // sz.model
    for c in range(sz.hidden // 128):
        total = tiles[2 * c]
        total = jnp.where(lane >= wide, tiles[2 * c + 1], total)
        up_ref[:, 128 * c : 128 * c + 128] = total[8:9]


def place_rims(sz, low_ref, high_ref, tops_ref, key_ref, value_ref):
    for kind, bank in ((0, key_ref), (1, value_ref)):
        for level in range(TOP):
            bank[pl.ds(sz.offset[level], BLOCK), :] = low_ref[rim_rows(level, kind), :]
            bank[pl.ds(sz.offset[level] + BLOCK + sz.count[level], BLOCK), :] = high_ref[rim_rows(level, kind), :]
        n = sz.count[TOP]
        for s in range(0, sz.seq, 2):
            pair = [tops_ref[s + k, kind * n : kind * n + n, :] for k in range(2)]
            bank[pl.ds(sz.offset[TOP] + s * n, 2 * n), :] = jnp.concatenate(pair, axis=0)


MESH = pl.DeviceIdType.MESH


class Grid:
    def __init__(self, depth):
        dp, seq = lax.axis_index("dp"), lax.axis_index("seq")
        self.depth = depth
        self.z, self.x, self.y, self.c = dp // 2, dp % 2, seq // 2, seq % 2

    def at(self, z, x, y, c):
        return (z * 2 + x, y * 2 + c)

    def index(self, z, x, y, c):
        return z * 8 + x * 4 + y * 2 + c

    def partner(self, axis):
        z, x, y, c = self.z, self.x, self.y, self.c
        return self.at(z, 1 - x if axis == "x" else x, 1 - y if axis == "y" else y, 1 - c if axis == "c" else c)

    def up(self, by):
        return self.at(self.z + by, self.x, self.y, self.c)


def greet(devices):
    barrier = pltpu.get_barrier_semaphore()
    peers = jnp.int32(0)
    for where, condition in devices:
        signal = functools.partial(pl.semaphore_signal, barrier, inc=1, device_id=where, device_id_type=MESH)
        if condition is None:
            signal()
            peers += 1
        else:
            pl.when(condition)(signal)
            peers += condition.astype(jnp.int32)
    pl.semaphore_wait(barrier, peers)


def both(first, second):
    if first is None:
        return second
    return first if second is None else first & second


def when(condition, act):
    if condition is None:
        act()
    else:
        pl.when(condition)(act)


class Plan:
    RATE = {"core": 450e3, "plane": 85e3, "z": 85e3}
    HOP = 1.5

    def __init__(self):
        self.now, self.count, self.waiting = 0.0, 0, []
        self.free = dict.fromkeys(self.RATE, 0.0)

    def send(self, link, size):
        self.free[link] = max(self.now, self.free[link]) + size / self.RATE[link]
        return self.free[link] + self.HOP

    def later(self, ready, act):
        self.count += 1
        self.waiting.append((ready, self.count, act))

    def pop(self):
        first = min(self.waiting, key=lambda entry: entry[:2])
        self.waiting.remove(first)
        self.now = max(self.now, first[0])
        first[2]()

    def advance(self, time):
        self.now += time
        while self.waiting and min(entry[0] for entry in self.waiting) <= self.now:
            self.pop()

    def until(self, done):
        while not done():
            self.pop()

    def flush(self):
        while self.waiting:
            self.pop()


class Gather:
    def __init__(self, grid, plan, pieces, local_sem, send_sem, recv_sem):
        self.grid, self.plan, self.pieces = grid, plan, pieces
        self.local_sem, self.send_sem, self.recv_sem = local_sem, send_sem, recv_sem
        z, x, y, c = grid.z, grid.x, grid.y, grid.c
        self.others = [lax.rem(z + k, grid.depth) for k in range(1, grid.depth)]
        self.one, self.two, self.lines = [], [], []
        for p in range(len(pieces)):
            y_first = (c ^ (FLIP * (p % 2))) == 0
            pick = lambda first, second: jnp.where(y_first, first, second)
            one, two = (pick(x, 1 - x), pick(1 - y, y)), (pick(1 - x, x), pick(y, 1 - y))
            self.one.append(grid.at(z, *one, c))
            self.two.append(grid.at(z, *two, c))
            self.lines.append([(x, y), one, two, (1 - x, 1 - y)])
        self.ids, self.count = [], 0
        for piece in pieces:
            self.ids.append(list(range(self.count, self.count + len(piece))))
            self.count += len(piece)
        self.sends = []
        self.done = [False] * len(pieces)
        self.passed, self.parked = [False] * len(pieces), []

    def size(self, p):
        return sum(2 * share.shape[0] * share.shape[1] for share, _ in self.pieces[p])

    def copy(self, array, source, target, slot, landing, to):
        return pltpu.make_async_remote_copy(
            src_ref=source, dst_ref=target, send_sem=self.send_sem.at[array, slot],
            recv_sem=self.recv_sem.at[array, landing], device_id=to, device_id_type=MESH,
        )

    def begin(self, p):
        grid = self.grid
        for array, (share, whole) in zip(self.ids[p], self.pieces[p]):
            mine = whole.at[grid.z, grid.x, grid.y, grid.c]
            pltpu.make_async_copy(share, mine, self.local_sem.at[array]).start()
            for k, other in enumerate(self.others):
                copy = self.copy(array, share, mine, k, k, grid.at(other, grid.x, grid.y, grid.c))
                copy.start()
                self.sends.append(copy)
        ready = self.plan.send("z", 2 * grid.depth * self.size(p))
        self.plan.later(ready, functools.partial(self.enter, p))

    def enter(self, p):
        if p >= GATE and not self.passed[p - GATE]:
            self.parked.append(p)
        else:
            self.along(p)

    def line(self, p, whole, k):
        xx, yy = self.lines[p][k]
        return whole.at[:, xx, yy, self.grid.c]

    def pass_line(self, p, k, slots, landing):
        xx, yy = self.lines[p][k]
        for array, (_, whole) in zip(self.ids[p], self.pieces[p]):
            line = self.line(p, whole, k)
            for name, slot in slots.items():
                if name == "core":
                    copy = self.copy(array, line, line, slot, 2 + self.grid.depth + xx * 2 + yy, self.grid.partner("c"))
                else:
                    copy = self.copy(array, line, line, slot, landing[name], {"one": self.one[p], "two": self.two[p]}[name])
                copy.start()
                self.sends.append(copy)

    def receive(self, p, landing, k):
        for array, (_, whole) in zip(self.ids[p], self.pieces[p]):
            line = self.line(p, whole, k)
            self.copy(array, line, line, 0, landing, self.one[p]).wait_recv()

    def along(self, p):
        grid, size, plan = self.grid, self.size(p), self.plan
        base = grid.depth - 1
        for array, (share, whole) in zip(self.ids[p], self.pieces[p]):
            mine = whole.at[grid.z, grid.x, grid.y, grid.c]
            pltpu.make_async_copy(share, mine, self.local_sem.at[array]).wait()
            for k in range(grid.depth - 1):
                self.copy(array, share, mine, k, k, self.one[p]).wait_recv()
        self.pass_line(p, 0, {"one": base, "two": base + 1, "core": base + 2}, {"one": base, "two": base + 1})
        line = grid.depth * size
        plan.later(plan.send("plane", line), functools.partial(self.after_one, p))
        plan.later(plan.send("plane", line), functools.partial(self.after_two, p))
        plan.send("core", line)

    def after_one(self, p):
        grid, plan = self.grid, self.plan
        base = grid.depth - 1
        self.receive(p, base, 1)
        self.pass_line(p, 1, {"two": base + 3, "core": base + 4}, {"two": base + 2})
        line = grid.depth * self.size(p)
        plan.later(plan.send("plane", line), functools.partial(self.after_both, p))
        plan.send("core", line)
        self.passed[p] = True
        if p + GATE in self.parked:
            self.parked.remove(p + GATE)
            self.along(p + GATE)

    def after_two(self, p):
        base = self.grid.depth - 1
        self.receive(p, base + 1, 2)
        self.pass_line(p, 2, {"core": base + 5}, {})
        self.plan.send("core", self.grid.depth * self.size(p))

    def after_both(self, p):
        base = self.grid.depth - 1
        self.receive(p, base + 2, 3)
        self.pass_line(p, 3, {"core": base + 6}, {})
        ready = self.plan.send("core", self.grid.depth * self.size(p))
        self.plan.later(ready, functools.partial(self.finish, p))

    def finish(self, p):
        grid = self.grid
        for array, (_, whole) in zip(self.ids[p], self.pieces[p]):
            for xx, yy in self.lines[p]:
                line = whole.at[:, xx, yy, 1 - grid.c]
                self.copy(array, line, line, 0, 2 + grid.depth + xx * 2 + yy, self.one[p]).wait_recv()
        self.done[p] = True

    def need(self, p):
        self.plan.until(lambda: self.done[p])

    def drain(self):
        for copy in self.sends:
            copy.wait_send()


class Scatter:
    def __init__(self, grid, plan, pieces, buffers, sums, send_sem, recv_sem, free_sem, again, more):
        self.grid, self.plan, self.pieces, self.buffers, self.sums = grid, plan, pieces, buffers, sums
        self.free_sem, self.again, self.more = free_sem, again, more
        self.next = {}
        self.done = [False] * len(pieces)
        self.send_sem, self.recv_sem = send_sem, recv_sem
        self.copies = [[] for _ in pieces]
        z, x, y, c = grid.z, grid.x, grid.y, grid.c
        self.others = [lax.rem(z + k, grid.depth) for k in range(1, grid.depth)]
        self.x_first = [(c ^ (FLIP * (p % 2))) == 0 for p in range(len(pieces))]
        pick = lambda p, first, second: jnp.where(self.x_first[p], first, second)
        self.one = [grid.at(z, pick(p, 1 - x, x), pick(p, y, 1 - y), c) for p in range(len(pieces))]
        self.two = [grid.at(z, pick(p, x, 1 - x), pick(p, 1 - y, y), c) for p in range(len(pieces))]
        self.mine = [(pick(p, x, y), pick(p, y, x)) for p in range(len(pieces))]

    def move(self, p, source, target, to):
        stage = len(self.copies[p])
        copy = pltpu.make_async_remote_copy(
            src_ref=source, dst_ref=target, send_sem=self.send_sem.at[p, stage], recv_sem=self.recv_sem.at[p, stage],
            device_id=to, device_id_type=MESH,
        )
        copy.start()
        self.copies[p].append(copy)

    def step(self, link, blocks, p, act):
        piece = self.pieces[p]
        ready = self.plan.send(link, 2 * blocks * piece.shape[4] * piece.shape[5])
        self.plan.later(ready, functools.partial(act, p))

    def senders(self):
        grid = self.grid
        along = [grid.at(other, grid.x, grid.y, grid.c) for other in self.others]
        return [grid.partner("c"), grid.partner("x"), grid.partner("y")] + along

    def begin(self, p):
        if self.again:
            pl.semaphore_wait(self.free_sem.at[p], len(self.senders()))
        self.move(p, self.pieces[p].at[:, :, :, 1 - self.grid.c], self.buffers[p][0], self.grid.partner("c"))
        self.step("core", 4 * self.grid.depth, p, self.first)

    def place(self, p, one, two):
        return jnp.where(self.x_first[p], one, two), jnp.where(self.x_first[p], two, one)

    def first(self, p):
        grid = self.grid
        piece, (from_core, to_one, from_one) = self.pieces[p], self.buffers[p][:3]
        self.copies[p][0].wait_recv()
        for zz in range(grid.depth):
            for two in range(2):
                xx, yy = self.place(p, 1 - self.mine[p][0], two)
                total = piece[zz, xx, yy, grid.c].astype(F32) + from_core[zz, xx, yy].astype(F32)
                to_one[zz, two] = total.astype(BF16)
        self.move(p, to_one, from_one, self.one[p])
        self.step("plane", 2 * grid.depth, p, self.second)

    def second(self, p):
        grid = self.grid
        piece, (from_core, _, from_one, to_two, from_two) = self.pieces[p], self.buffers[p][:5]
        self.copies[p][1].wait_recv()
        other = 1 - self.mine[p][1]
        xx, yy = self.place(p, self.mine[p][0], other)
        for zz in range(grid.depth):
            total = piece[zz, xx, yy, grid.c].astype(F32) + from_core[zz, xx, yy].astype(F32)
            to_two[zz] = (total + from_one[zz, other].astype(F32)).astype(BF16)
        self.move(p, to_two, from_two, self.two[p])
        self.step("plane", grid.depth, p, self.along)

    def along(self, p):
        grid = self.grid
        piece, (from_core, _, from_one, _, from_two, ready, from_z) = self.pieces[p], self.buffers[p]
        self.copies[p][2].wait_recv()
        for zz in range(grid.depth):
            total = piece[zz, grid.x, grid.y, grid.c].astype(F32) + from_core[zz, grid.x, grid.y].astype(F32)
            total = total + from_one[zz, self.mine[p][1]].astype(F32) + from_two[zz].astype(F32)
            ready[zz] = total.astype(BF16)
        for k, other in enumerate(self.others):
            self.move(p, ready.at[other], from_z.at[k], grid.at(other, grid.x, grid.y, grid.c))
        self.step("z", 2 * grid.depth, p, self.finish)

    def finish(self, p):
        ready, from_z = self.buffers[p][5:7]
        total = ready[self.grid.z].astype(F32)
        for k in range(self.grid.depth - 1):
            self.copies[p][3 + k].wait_recv()
            total = total + from_z[k].astype(F32)
        self.sums[p][...] = total
        if self.more:
            for copy in self.copies[p]:
                copy.wait_send()
            for device in self.senders():
                pl.semaphore_signal(self.free_sem.at[p], inc=1, device_id=device, device_id_type=MESH)
        self.done[p] = True
        if p in self.next:
            self.next.pop(p)()

    def need(self, p):
        self.plan.until(lambda: self.done[p])

    def drain(self):
        for copies in self.copies:
            for copy in copies if not self.more else []:
                copy.wait_send()


FLIP = 1
GATE = 2
SCATTER_BUFFERS = 7


def scatter_buffers(depth, block):
    leads = ((depth, 2, 2), (depth, 2), (depth, 2), (depth,), (depth,), (depth,), (depth - 1,))
    return [pltpu.VMEM(lead + tuple(block), BF16) for lead in leads]


class Rims:
    def __init__(self, sz, ahead, behind, tops, low, high, all_tops, send_sem, recv_sem):
        self.sz, self.low, self.high, self.all_tops, self.tops = sz, low, high, all_tops, tops
        self.me, self.dp = lax.axis_index("seq"), lax.axis_index("dp")
        me, dp, seq = self.me, self.dp, sz.seq
        make = lambda source, target, k, to: pltpu.make_async_remote_copy(
            src_ref=source, dst_ref=target, send_sem=send_sem.at[k], recv_sem=recv_sem.at[k],
            device_id=(dp, to), device_id_type=MESH,
        )
        self.ahead = lambda: make(ahead, low, 0, me + 1)
        self.behind = lambda: make(behind, high, 1, me - 1)
        self.rest = []
        for k in range(1, seq):
            other = lax.rem(me + k, seq)
            source = tops.at[0] if tops.shape[0] == 1 else tops.at[other]
            self.rest.append(make(source, all_tops.at[me], 1 + k, other))

    def start(self):
        when(self.me + 1 < self.sz.seq, lambda: self.ahead().start())
        when(self.me > 0, lambda: self.behind().start())
        for copy in self.rest:
            copy.start()
        self.all_tops[self.me] = self.tops[0] if self.tops.shape[0] == 1 else self.tops[self.me]

        def no_low():
            self.low[...] = jnp.zeros_like(self.low)

        def no_high():
            self.high[...] = jnp.zeros_like(self.high)

        when(self.me == 0, no_low)
        when(self.me == self.sz.seq - 1, no_high)

    def arrive(self):
        when(self.me > 0, lambda: self.ahead().wait_recv())
        when(self.me + 1 < self.sz.seq, lambda: self.behind().wait_recv())
        for copy in self.rest:
            copy.wait_recv()

    def drain(self):
        when(self.me + 1 < self.sz.seq, lambda: self.ahead().wait_send())
        when(self.me > 0, lambda: self.behind().wait_send())
        for copy in self.rest:
            copy.wait_send()


class Copies:
    def __init__(self, sem):
        self.sem, self.open, self.count = sem, {}, 0

    def start(self, name, source, target):
        copy = pltpu.make_async_copy(source, target, self.sem.at[self.count])
        self.count += 1
        copy.start()
        self.open[name] = copy

    def wait(self, *names):
        for name in names:
            if name in self.open:
                self.open.pop(name).wait()

    def drain(self):
        self.wait(*list(self.open))


def whole_rows(ref, columns):
    value = ref[:, :, :, :, :, columns]
    return value.reshape(-1, value.shape[-1])


def some_rows(ref, at, rows):
    per = ref.shape[4]
    blocks = [ref[i // 8, (i // 4) % 2, (i // 2) % 2, i % 2] for i in range(at // per, (at + rows) // per)]
    return jnp.concatenate(blocks, axis=0)


def make_share(sz, gains, biases, up, wide_ref, share_ref):
    wide = up.shape[-1]
    wide_ref[...] = jnp.zeros_like(wide_ref)
    wide_ref[0:2, 0:BLOCK] = gains.astype(F32)
    wide_ref[2:8, 0:BLOCK] = biases.astype(F32)
    wide_ref[8:16, 0:wide] = jnp.broadcast_to(up.astype(F32), (8, wide))
    row = lax.broadcasted_iota(jnp.int32, (128, 128), 0)
    lane = lax.broadcasted_iota(jnp.int32, (128, 128), 1)
    top = jnp.where((row < BLOCK) & (lane % BLOCK == row), 1.0, 0.0).astype(BF16)
    low = jnp.where((row < wide) & (lane % wide == row), 1.0, 0.0).astype(BF16)
    values = wide_ref[...].astype(BF16)
    share_ref[...] = jnp.concatenate([dot_nn(values, top)[:8], dot_nn(values, low)[8:]], axis=0).astype(BF16)


SAVED = 6
TIMES = {"before": 2.2, "attend": 0.8, "project": 1.0, "forward": 1.4, "start": 1.5, "back": 1.9, "branch": 2.0, "attend_back": 0.6,
         "levels": 1.0, "finish": 1.2}


def forward_kernel(sz, depth, *refs):
    refs = list(refs)
    take_refs = lambda n: [refs.pop(0) for _ in range(n)]
    tokens_ref = take_refs(1)[0]
    if depth:
        shares, (gains_ref, biases_ref, upb_ref) = take_refs(4), take_refs(3)
    else:
        wholes = take_refs(5)
    out_act_ref, x_out = take_refs(2)
    saved_out = take_refs(SAVED)
    if depth:
        wholes_out, wholes = take_refs(5), take_refs(5)
    q_ref, key_ref, value_ref, att_ref, lse_ref, middle_ref = take_refs(SAVED)
    x_ref, vec, up, mask_ref, second_ref, state_ref = take_refs(6)
    index_ref, score_ref, weight_ref = take_refs(3)
    rims_out, tops_out, low_ref, high_ref, tops_ref, rim_send, rim_recv, copy_sem = take_refs(8)
    model, run = sz.model, sz.run
    wq, wo, wu, wd, ws = wholes
    plan, copies = Plan(), Copies(copy_sem)
    me, dp = lax.axis_index("seq"), lax.axis_index("dp")
    peers = [((dp, lax.rem(me + k, sz.seq)), None) for k in range(1, sz.seq)]
    if depth:
        wide_ref, share_ref, local_sem, send_sem, recv_sem = take_refs(5)
        grid = Grid(depth)
        half = sz.hidden // 2
        pieces = []
        for layer in range(LAYERS):
            part = lambda k, columns: (shares[k].at[layer, :, columns], wholes[k].at[layer, :, :, :, :, :, columns])
            pieces.append([part(0, slice(None)), (share_ref.at[layer], ws.at[layer])])
            pieces.append([part(1, slice(None)), part(2, slice(0, half))])
            pieces.append([part(2, slice(half, None))])
            pieces.append([part(3, slice(None))])
        gather = Gather(grid, plan, pieces, local_sem, send_sem, recv_sem)
        peers += [(grid.partner("x"), None)] + [(grid.at(other, grid.x, grid.y, grid.c), None) for other in gather.others]
        greet(peers)
        for layer in range(LAYERS):
            make_share(
                sz, gains_ref[layer], biases_ref[layer], upb_ref[layer : layer + 1, :], wide_ref, share_ref.at[layer]
            )
        gather.begin(0)
        for p in range(1, 4):
            plan.later(3.0 + 3.0 * p, functools.partial(gather.begin, p))
        for p in range(4, 8):
            plan.later(14.0 + 3.0 * (p - 4), functools.partial(gather.begin, p))

        def need(layer, k):
            gather.need(4 * layer + k)

        def keep(layer):
            for k in range(5):
                copies.start(("weights", layer, k), wholes[k].at[layer], wholes_out[k].at[layer])
    else:
        greet(peers)
        need = lambda layer, k: None
        keep = lambda layer: None

    def save(k, layer):
        source = (q_ref, key_ref, value_ref, att_ref, lse_ref, middle_ref)[k]
        copies.start(("saved", k, layer), source.at[layer], saved_out[k].at[layer])

    fill_mask(sz, mask_ref)
    fill_index(sz, index_ref)
    coarse = coarse_matrix(run)
    rows_of = lambda r: pl.ds(r * run, run)
    for r in range(sz.rows):
        state_ref[rows_of(r), :] = tokens_ref[r].astype(F32)
    all_rims = []
    for layer in range(LAYERS):
        need(layer, 0)
        unpack_small(sz, whole_rows(ws.at[layer], slice(None)), vec, up)
        rims = []
        for r in range(sz.rows):
            hat, _ = normalise(state_ref[rows_of(r), :])
            normed = (hat * vec[0:1, :] + vec[2:3, :]).astype(BF16)
            tops = []
            for kind, bank in ((0, key_ref.at[layer, r]), (1, value_ref.at[layer, r])):
                mixed = dot_nn(normed, whole_rows(wq.at[layer], slice((1 + kind) * model, (2 + kind) * model)))
                if kind == 1:
                    mixed = mixed + vec[4:5, :]
                mixed = mixed.astype(BF16)
                levels = dot_nn(coarse, mixed).astype(BF16)
                base = 0
                for level in range(LEVELS):
                    n = sz.count[level]
                    if level == 0:
                        now = mixed
                    else:
                        now = levels[base : base + n]
                        base += n
                    if level < TOP:
                        bank[pl.ds(sz.offset[level] + BLOCK, n), :] = now
                        rims_out[layer, r, 0, rim_rows(level, kind), :] = now[n - BLOCK :]
                        rims_out[layer, r, 1, rim_rows(level, kind), :] = now[:BLOCK]
                    else:
                        tops.append(now)
            tops_out[layer, r, 0] = jnp.concatenate(tops, axis=0)
            rims.append(
                Rims(
                    sz, rims_out.at[layer, r, 0], rims_out.at[layer, r, 1], tops_out.at[layer, r], low_ref.at[layer, r],
                    high_ref.at[layer, r], tops_ref.at[layer, r], rim_send.at[layer, r], rim_recv.at[layer, r],
                )
            )
            rims[-1].start()
            queries = (dot_nn(normed, whole_rows(wq.at[layer], slice(0, model))) + vec[3:4, :]).astype(BF16)
            q_ref[layer, r] = queries * jnp.asarray(HDIM**-0.5, BF16)
            plan.advance(TIMES["before"])
        save(0, layer)
        all_rims += rims
        for r in range(sz.rows):
            rims[r].arrive()
            place_rims(
                sz, low_ref.at[layer, r], high_ref.at[layer, r], tops_ref.at[layer, r], key_ref.at[layer, r],
                value_ref.at[layer, r],
            )
            attend(
                sz, q_ref.at[layer, r], key_ref.at[layer, r], value_ref.at[layer, r], mask_ref, index_ref,
                att_ref.at[layer, r], lse_ref.at[layer, r], score_ref, weight_ref,
                functools.partial(plan.advance, TIMES["attend"]),
            )
        for k in (1, 2, 3, 4):
            save(k, layer)
        need(layer, 1)
        for r in range(sz.rows):
            rows = rows_of(r)
            middle = state_ref[rows, :] + dot_nn(att_ref[layer, r], whole_rows(wo.at[layer], slice(None))) + vec[5:6, :]
            middle_ref[layer, rows, :] = middle
            hat, _ = normalise(middle)
            second_ref[rows, :] = (hat * vec[1:2, :] + vec[6:7, :]).astype(BF16)
            state_ref[rows, :] = middle + vec[7:8, :]
            plan.advance(TIMES["project"])
        save(5, layer)
        need(layer, 3)
        parts = sz.hidden // model
        for c in range(parts):
            if c == parts // 2:
                need(layer, 2)
            units = slice(c * model, (c + 1) * model)
            for r in range(sz.rows):
                rows = rows_of(r)
                hidden = dot_nn(second_ref[rows, :], whole_rows(wu.at[layer], units)) + up[:, units]
                state_ref[rows, :] += dot_nn(gelu(hidden).astype(BF16), some_rows(wd.at[layer], c * model, model))
            plan.advance(TIMES["forward"])
        keep(layer)
        if layer == 0:
            x_ref[...] = state_ref[...]
            copies.start("x", x_ref, x_out)
        else:
            for r in range(sz.rows):
                out_act_ref[r] = state_ref[rows_of(r), :].astype(BF16)
    plan.flush()
    for rims in all_rims:
        rims.drain()
    if depth:
        gather.drain()
    copies.drain()


WHOLE = pl.BlockSpec(memory_space=pltpu.VMEM)
ANYWHERE = pl.BlockSpec(memory_space=pl.ANY)


def attend_scratch(sz):
    units = sz.chunks * sz.pairs
    coarse = sz.width - sz.start[1]
    wide = ((units, sz.width, 128), F32)
    return [
        ((coarse, 128), jnp.int32), wide, (wide[0], BF16), ((coarse, 128), F32), wide, (wide[0], BF16),
        ((units, coarse, 128), BF16),
    ]


def forward(sz, depth, tokens, weights):
    n, rows, run = sz.model, sz.rows, sz.run
    saved = [
        ((LAYERS, rows, run, n), BF16), ((LAYERS, rows, sz.bank, n), BF16), ((LAYERS, rows, sz.bank, n), BF16),
        ((LAYERS, rows, run, n), BF16), ((LAYERS, rows, sz.chunks, sz.pairs, 128), F32), ((LAYERS, sz.tokens, n), F32),
    ]
    outs = [((rows, run, n), BF16), ((sz.tokens, n), F32)] + saved
    out_specs = [WHOLE] + [ANYWHERE] * (1 + SAVED)
    scratch = []
    if depth:
        full = [((LAYERS, depth, 2, 2, 2) + share.shape[1:], BF16) for share in weights[:4]]
        full.append(((LAYERS, depth, 2, 2, 2, BLOCK, 128), BF16))
        outs += full
        out_specs += [ANYWHERE] * 5
        scratch += full
    rim = sz.rim // rows
    scratch += saved + [
        ((sz.tokens, n), F32), ((8, n), F32), ((1, sz.hidden), F32), ((sz.chunks, sz.width, 128), F32),
        ((sz.tokens, n), BF16), ((sz.tokens, n), F32)] + attend_scratch(sz)[:3] + [((LAYERS, rows, 2, rim, n), BF16),
        ((LAYERS, rows, 1, BLOCK, n), BF16), ((LAYERS, rows, rim, n), BF16), ((LAYERS, rows, rim, n), BF16),
        ((LAYERS, rows, sz.seq, BLOCK, n), BF16),
    ]
    scratch = [pltpu.VMEM(shape, dtype) for shape, dtype in scratch]
    scratch += [pltpu.SemaphoreType.DMA((LAYERS, rows, sz.seq + 1))] * 2
    scratch += [pltpu.SemaphoreType.DMA((LAYERS * (SAVED + 5) + 1,))]
    if depth:
        arrays = 6 * LAYERS
        scratch += [pltpu.VMEM((BLOCK, 128), F32), pltpu.VMEM((LAYERS, BLOCK, 128), BF16)]
        scratch += [pltpu.SemaphoreType.DMA((arrays,))] + [pltpu.SemaphoreType.DMA((arrays, depth + 6))] * 2
    results = pl.pallas_call(
        functools.partial(forward_kernel, sz, depth),
        out_shape=[jax.ShapeDtypeStruct(shape, dtype) for shape, dtype in outs],
        in_specs=[WHOLE] * (1 + len(weights)),
        out_specs=out_specs,
        scratch_shapes=scratch,
        compiler_params=pltpu.CompilerParams(
            collective_id=0, has_side_effects=True, vmem_limit_bytes=VMEM_LIMIT
        ),
        name="forward",
    )(tokens, *weights)
    return results[0], results[1], results[2 : 2 + SAVED], (results[2 + SAVED :] if depth else weights)


def store_blocks(ref, at, columns, value):
    per = ref.shape[4]
    for k in range(value.shape[0] // per):
        i = at + k
        ref[i // 8, (i // 4) % 2, (i // 2) % 2, i % 2, :, columns] = value[k * per : (k + 1) * per]


def unpack_share(sz, small, gains_ref, biases_ref, up_ref):
    place = lax.axis_index("dp") * lax.axis_size("seq") + lax.axis_index("seq")
    wide = up_ref.shape[-1]
    vec, up = small[0:8, 0:BLOCK], small[8:9, 0:wide]
    for j in range(1, 128 // BLOCK):
        vec = jnp.where(place % (128 // BLOCK) == j, small[0:8, j * BLOCK : (j + 1) * BLOCK], vec)
    for j in range(1, 128 // wide):
        up = jnp.where(place % (128 // wide) == j, small[8:9, j * wide : (j + 1) * wide], up)
    gains_ref[...] = vec[0:2]
    biases_ref[...] = vec[2:8]
    up_ref[...] = up


GRADS = 8
EARLY = 4


def backward_kernel(sz, depth, *refs):
    refs = list(refs)
    take_refs = lambda n: [refs.pop(0) for _ in range(n)]
    prefix_ref, cot_ref, tokens_ref, x_in = take_refs(4)
    saved_in, wholes_in = take_refs(SAVED), take_refs(5)
    gin_ref = take_refs(1)[0]
    out_refs = take_refs(7) if depth else [take_refs(GRADS) for _ in range(LAYERS)]
    (q_ref, key_ref, value_ref, att_ref, lse_ref, middle_ref), (wq, wo, wu, wd, ws) = take_refs(SAVED), take_refs(5)
    (
        x_ref, g_ref, vec, up, mask_ref, second_ref, gd_ref, gs_ref, go_ref, gm_ref, dq_ref, dkey_ref, dvalue_ref,
        gvec_ref, gupb_ref, dk_ref, dv_ref, levels_ref, normed_ref, rims_out, tops_out, low_ref, high_ref, tops_ref,
    ) = take_refs(24)
    index_ref, score_ref, weight_ref, own_ref, back_ref, dscore_ref, coarse_ref = take_refs(7)
    rim_send, rim_recv, copy_sem = take_refs(3)
    model, run = sz.model, sz.run
    half = sz.hidden // 2
    plan, copies = Plan(), Copies(copy_sem)
    inside = {"q": q_ref, "key": key_ref, "value": value_ref, "att": att_ref, "lse": lse_ref, "middle": middle_ref,
              "wq": wq, "wo": wo, "wu": wu, "wd": wd, "ws": ws}
    outside = dict(zip(inside, list(saved_in) + list(wholes_in)))

    def load(layer, *names):
        if layer >= 0:
            for name in names:
                copies.start(name, outside[name].at[layer], inside[name])

    load(LAYERS - 1, "middle", "ws", "wu", "wd", "wo", "att", "q", "key", "value", "lse", "wq")
    copies.start("x", x_in, x_ref)
    me, dp = lax.axis_index("seq"), lax.axis_index("dp")
    peers = [((dp, lax.rem(me + k, sz.seq)), None) for k in range(1, sz.seq)]
    scatters = {}
    if depth:
        grads = take_refs(GRADS)
        early = take_refs(EARLY)
        own_grads = lambda layer: (early if layer == 0 else grads[:EARLY]) + grads[EARLY:]
        buffers = [take_refs(SCATTER_BUFFERS) for _ in grads]
        send_sem, recv_sem, free_sem, small_sums = take_refs(4)
        gqkv, gwout, gwup, gwdown = out_refs[:4]
        grid = Grid(depth)
        for layer in reversed(range(LAYERS)):
            sums = [gwup.at[layer, :, 0:half], gwup.at[layer, :, half:], gwdown.at[layer], gwout.at[layer]]
            sums += [gqkv.at[layer, :, k * model : (k + 1) * model] for k in range(3)] + [small_sums.at[layer]]
            scatters[layer] = Scatter(
                grid, plan, own_grads(layer), buffers, sums, send_sem.at[layer], recv_sem.at[layer], free_sem,
                layer < LAYERS - 1, layer > 0,
            )
        peers += [(grid.partner("x"), None)]
        peers += [(grid.at(other, grid.x, grid.y, grid.c), None) for other in scatters[0].others]
    greet(peers)
    fill_mask(sz, mask_ref)
    fill_index(sz, index_ref)
    fill_own(sz, own_ref)
    coarse = coarse_matrix(run)
    rows_of = lambda r: pl.ds(r * run, run)
    per_micro = prefix_ref.shape[1]
    place = me * run + lax.broadcasted_iota(jnp.int32, (run, model), 0)
    for r in range(sz.rows):
        kept = place >= prefix_ref[r // per_micro, r % per_micro]
        g_ref[rows_of(r), :] = jnp.where(kept, cot_ref[r].astype(F32), 0.0)
    all_rims = []
    for layer in reversed(range(LAYERS)):
        gup_a, gup_b, gdown, gout, gq, gk, gv, small_ref = own_grads(layer) if depth else out_refs[layer]

        def launch(*pieces, layer=layer):
            for p in pieces if depth else ():
                begin = functools.partial(scatters[layer].begin, p)
                above = scatters.get(layer + 1)
                if above is None or above.done[p]:
                    begin()
                else:
                    above.next[p] = begin

        def room(*pieces, layer=layer):
            if depth and layer < LAYERS - 1:
                for p in pieces:
                    scatters[layer + 1].need(p)

        gvec_ref[...] = jnp.zeros_like(gvec_ref)
        copies.wait("middle", "ws")
        unpack_small(sz, whole_rows(ws, slice(None)), vec, up)
        load(layer - 1, "ws")
        for r in range(sz.rows):
            rows = rows_of(r)
            hat, _ = normalise(middle_ref[rows, :])
            second_ref[rows, :] = (hat * vec[1:2, :] + vec[6:7, :]).astype(BF16)
            grad = g_ref[rows, :].astype(BF16)
            gd_ref[rows, :] = grad
            gvec_ref[7:8, :] += jnp.sum(grad.astype(F32), axis=0, keepdims=True)
        copies.wait("wu", "wd")
        plan.advance(TIMES["start"])
        parts = sz.hidden // model
        for c in range(parts):
            units = slice(c * model, (c + 1) * model)
            w_up = whole_rows(wu, units)
            hidden = dot_nn(second_ref[...], w_up) + up[:, units]
            active, slope = gelu_both(hidden)
            per = gdown.shape[4]
            store_blocks(gdown, c * model // per, slice(None), dot_tn(active.astype(BF16), gd_ref[...]).astype(BF16))
            grad_hidden = (slope * dot_nt(gd_ref[...], some_rows(wd, c * model, model))).astype(BF16)
            gupb_ref[:, units] = jnp.sum(grad_hidden.astype(F32), axis=0, keepdims=True)
            target, at = (gup_a, gup_b)[c * 2 // parts], c % (parts // 2)
            store_blocks(
                target, 0, slice(at * model, (at + 1) * model), dot_tn(second_ref[...], grad_hidden).astype(BF16)
            )
            back = dot_nt(grad_hidden, w_up)
            if c == 0:
                gs_ref[...] = back
            else:
                gs_ref[...] += back
            if c == parts // 2 - 1:
                launch(0)
            plan.advance(TIMES["back"])
        launch(2, 1)
        load(layer - 1, "wu", "wd")
        copies.wait("wo")
        for r in range(sz.rows):
            rows = rows_of(r)
            hat, inverse = normalise(middle_ref[rows, :])
            grad = gs_ref[rows, :]
            gvec_ref[1:2, :] += jnp.sum(grad * hat, axis=0, keepdims=True)
            gvec_ref[6:7, :] += jnp.sum(grad, axis=0, keepdims=True)
            gm = g_ref[rows, :] + norm_back(grad, hat, inverse, vec[1:2, :])
            gm_ref[rows, :] = gm
            branch = gm.astype(BF16)
            gd_ref[rows, :] = branch
            gvec_ref[5:6, :] += jnp.sum(branch.astype(F32), axis=0, keepdims=True)
            go_ref[r] = dot_nt(branch, whole_rows(wo, slice(None))).astype(BF16)
        plan.advance(TIMES["branch"])
        load(layer - 1, "middle", "wo")
        copies.wait("att", "q", "key", "value", "lse")
        store_blocks(
            gout, 0, slice(None), sum(dot_tn(att_ref[r], gd_ref[rows_of(r), :]) for r in range(sz.rows)).astype(BF16)
        )
        launch(3)
        rims = []
        n = sz.count[TOP]
        for r in range(sz.rows):
            dkey, dvalue = dkey_ref.at[r], dvalue_ref.at[r]
            dkey[...] = jnp.zeros(dkey.shape, F32)
            dvalue[...] = jnp.zeros(dvalue.shape, F32)
            attend_back(
                sz, q_ref.at[r], key_ref.at[r], value_ref.at[r], mask_ref, index_ref, own_ref, lse_ref.at[r],
                go_ref.at[r], dq_ref.at[r], dkey, dvalue, score_ref, back_ref, weight_ref, dscore_ref, coarse_ref,
                functools.partial(plan.advance, TIMES["attend_back"]),
            )
            for kind, bank in ((0, dkey), (1, dvalue)):
                for level in range(TOP):
                    rims_out[layer, r, 0, rim_rows(level, kind), :] = bank[pl.ds(sz.offset[level], BLOCK), :].astype(BF16)
                    rims_out[layer, r, 1, rim_rows(level, kind), :] = bank[
                        pl.ds(sz.offset[level] + BLOCK + sz.count[level], BLOCK), :
                    ].astype(BF16)
            for s in range(sz.seq):
                at = pl.ds(sz.offset[TOP] + s * n, n)
                tops_out[layer, r, s] = jnp.concatenate([dkey[at, :], dvalue[at, :]], axis=0).astype(BF16)
            rims.append(
                Rims(
                    sz, rims_out.at[layer, r, 1], rims_out.at[layer, r, 0], tops_out.at[layer, r], low_ref.at[layer, r],
                    high_ref.at[layer, r], tops_ref.at[layer, r], rim_send.at[layer, r], rim_recv.at[layer, r],
                )
            )
            rims[-1].start()
        all_rims += rims
        load(layer - 1, "att", "q", "key", "value", "lse")
        if layer == LAYERS - 1:
            copies.wait("x")
        layer_input = (lambda r: tokens_ref[r].astype(F32)) if layer == 0 else (lambda r: x_ref[rows_of(r), :])
        for r in range(sz.rows):
            hat, _ = normalise(layer_input(r))
            normed_ref[r] = (hat * vec[0:1, :] + vec[2:3, :]).astype(BF16)
            gvec_ref[3:4, :] += jnp.sum(dq_ref[r].astype(F32), axis=0, keepdims=True)
        room(4)
        store_blocks(gq, 0, slice(None), sum(dot_tn(normed_ref[r], dq_ref[r]) for r in range(sz.rows)).astype(BF16))
        launch(4)
        plan.advance(TIMES["levels"])
        for r in range(sz.rows):
            rims[r].arrive()
            for kind, bank, out in ((0, dkey_ref.at[r], dk_ref), (1, dvalue_ref.at[r], dv_ref)):
                base = 0
                for level in range(LEVELS):
                    n = sz.count[level]
                    if level == TOP:
                        top = sum(tops_ref[layer, r, s, kind * n : kind * n + n, :].astype(F32) for s in range(sz.seq))
                        levels_ref[pl.ds(base, 2 * n), :] = jnp.concatenate(
                            [top, jnp.zeros((n, model), F32)], axis=0
                        ).astype(BF16)
                        continue
                    own = bank[pl.ds(sz.offset[level] + BLOCK, n), :]
                    first = low_ref[layer, r, rim_rows(level, kind), :].astype(F32)
                    final = high_ref[layer, r, rim_rows(level, kind), :].astype(F32)
                    if n == BLOCK:
                        own = own + first + final
                    else:
                        between = [own[BLOCK : n - BLOCK]] if n > 2 * BLOCK else []
                        own = jnp.concatenate([own[:BLOCK] + first, *between, own[n - BLOCK :] + final], axis=0)
                    if level == 0:
                        fine = own
                    else:
                        levels_ref[pl.ds(base, n), :] = own.astype(BF16)
                        base += n
                out[rows_of(r), :] = (fine + dot_tn(coarse, levels_ref[...])).astype(BF16)
            gvec_ref[4:5, :] += jnp.sum(dv_ref[rows_of(r), :].astype(F32), axis=0, keepdims=True)
            plan.advance(TIMES["levels"])
        for k, (out, source) in enumerate(((gk, dk_ref), (gv, dv_ref))):
            room(5 + k)
            store_blocks(
                out, 0, slice(None),
                sum(dot_tn(normed_ref[r], source[rows_of(r), :]) for r in range(sz.rows)).astype(BF16),
            )
            launch(5 + k)
        copies.wait("wq")
        for r in range(sz.rows):
            rows = rows_of(r)
            grad = dot_nt(dq_ref[r], whole_rows(wq, slice(0, model)))
            grad = grad + dot_nt(dk_ref[rows, :], whole_rows(wq, slice(model, 2 * model)))
            grad = grad + dot_nt(dv_ref[rows, :], whole_rows(wq, slice(2 * model, 3 * model)))
            hat, inverse = normalise(layer_input(r))
            gvec_ref[0:1, :] += jnp.sum(grad * hat, axis=0, keepdims=True)
            gvec_ref[2:3, :] += jnp.sum(grad, axis=0, keepdims=True)
            g_ref[rows, :] = gm_ref[rows, :] + norm_back(grad, hat, inverse, vec[0:1, :])
            plan.advance(TIMES["finish"])
        load(layer - 1, "wq")
        if layer == 0:
            copies.start("gin", g_ref, gin_ref)
        room(7)
        for i in range(model // BLOCK):
            top = gvec_ref[:, 128 * (i // 8) : 128 * (i // 8) + 128]
            side = jnp.broadcast_to(gupb_ref[:, 128 * (i // 2) : 128 * (i // 2) + 128], (8, 128))
            store_blocks(small_ref, i, slice(None), jnp.concatenate([top, side], axis=0).astype(BF16))
        launch(7)
    plan.flush()
    if depth:
        for layer in range(LAYERS):
            unpack_share(sz, small_sums[layer], out_refs[4].at[layer], out_refs[5].at[layer], out_refs[6].at[layer])
    for rim in all_rims:
        rim.drain()
    for scatter in scatters.values():
        scatter.drain()
    copies.drain()


def backward(sz, depth, prefix_len, cotangent, tokens, x, saved, wholes):
    n, rows, run = sz.model, sz.rows, sz.run
    per = sz.hidden * BLOCK // n
    lead = (n // BLOCK // 8, 2, 2, 2)
    half = sz.hidden // 2
    blocks = [(BLOCK, half), (BLOCK, half), (per, n), (BLOCK, n), (BLOCK, n), (BLOCK, n), (BLOCK, n), (BLOCK, 128)]
    pieces = [(lead + block, BF16) for block in blocks]
    outs = [((sz.tokens, n), F32)]
    if depth:
        outs += [((LAYERS,) + shape, F32) for shape in (
            (BLOCK, 3 * n), (BLOCK, n), (BLOCK, sz.hidden), (per, n), (2, BLOCK), (6, BLOCK), (1, per)
        )]
    else:
        outs += pieces * LAYERS
    rim = sz.rim // rows
    scratch = [(array.shape[1:], array.dtype) for array in list(saved) + list(wholes)]
    scratch += [
        ((sz.tokens, n), F32), ((sz.tokens, n), F32), ((8, n), F32), ((1, sz.hidden), F32),
        ((sz.chunks, sz.width, 128), F32), ((sz.tokens, n), BF16),
        ((sz.tokens, n), BF16), ((sz.tokens, n), F32), ((rows, run, n), BF16), ((sz.tokens, n), F32),
        ((rows, run, n), BF16), ((rows, sz.bank, n), F32), ((rows, sz.bank, n), F32), ((8, n), F32),
        ((1, sz.hidden), F32), ((sz.tokens, n), BF16), ((sz.tokens, n), BF16), ((run, n), BF16), ((rows, run, n), BF16),
        ((LAYERS, rows, 2, rim, n), BF16), ((LAYERS, rows, sz.seq, BLOCK, n), BF16), ((LAYERS, rows, rim, n), BF16),
        ((LAYERS, rows, rim, n), BF16), ((LAYERS, rows, sz.seq, BLOCK, n), BF16),
    ]
    scratch += attend_scratch(sz)
    scratch = [pltpu.VMEM(shape, dtype) for shape, dtype in scratch]
    scratch += [pltpu.SemaphoreType.DMA((LAYERS, rows, sz.seq + 1))] * 2
    scratch += [pltpu.SemaphoreType.DMA((LAYERS * (SAVED + 5) + 2,))]
    if depth:
        scratch += [pltpu.VMEM(shape, dtype) for shape, dtype in pieces + pieces[:EARLY]]
        for block in blocks:
            scratch += scatter_buffers(depth, block)
        scratch += [pltpu.SemaphoreType.DMA((LAYERS, GRADS, 2 + depth))] * 2
        scratch += [pltpu.SemaphoreType.REGULAR((GRADS,)), pltpu.VMEM((LAYERS, BLOCK, 128), F32)]
    result = pl.pallas_call(
        functools.partial(backward_kernel, sz, depth),
        out_shape=[jax.ShapeDtypeStruct(shape, dtype) for shape, dtype in outs],
        in_specs=[pl.BlockSpec(memory_space=pltpu.SMEM), WHOLE, WHOLE] + [ANYWHERE] * (1 + SAVED + 5),
        out_specs=[ANYWHERE] + [WHOLE] * (len(outs) - 1),
        scratch_shapes=scratch,
        compiler_params=pltpu.CompilerParams(
            collective_id=1, has_side_effects=True, vmem_limit_bytes=VMEM_LIMIT
        ),
        name="backward",
    )(prefix_len, cotangent, tokens, x, *saved, *wholes)
    return result[0], list(result[1:])


def direct(rows):
    return lax.axis_size("seq") == 4 and lax.axis_size("dp") % 2 == 0 and rows % BLOCK == 0


def pack_small(gains, biases, up_bias):
    layers, _, features = gains.shape
    tiles = features // BLOCK
    vec = jnp.concatenate([gains, biases], axis=1).reshape(layers, 8, tiles, BLOCK).transpose(0, 2, 1, 3)
    vec = jnp.tile(vec, (1, 1, 1, 128 // BLOCK))
    up = up_bias.reshape(layers, tiles, 1, up_bias.shape[1] // tiles)
    up = jnp.broadcast_to(jnp.tile(up, (1, 1, 1, 128 // up.shape[3])), (layers, tiles, 8, 128))
    return jnp.concatenate([vec, up], axis=2).reshape(layers, features, 128)


def whole_weights(w_qkv, w_out, w_up, w_down, gains, biases, up_bias):
    whole = lambda array, axis: lax.all_gather(array, AXES, axis=axis, tiled=True)
    small = pack_small(whole(gains, 2), whole(biases, 2), whole(up_bias, 1))
    tiles = small.shape[1] // BLOCK
    arrays = (whole(w_qkv, 1), whole(w_out, 1), whole(w_up, 1), whole(w_down, 1), small)
    return [
        array.reshape(LAYERS, tiles // 8, 2, 2, 2, array.shape[1] // tiles, array.shape[2]) for array in arrays
    ]


def scatter_by_sums(sz, parts):
    gqkv, gout, gup, small, gdown = parts
    spread = lambda array, axis: lax.psum_scatter(
        array.astype(F32), AXES, scatter_dimension=axis, tiled=True
    )
    tiles = small.reshape(sz.model // BLOCK, BLOCK, 128)
    vec = jnp.concatenate(
        [tiles[i, :8, BLOCK * (i % 8) : BLOCK * (i % 8) + BLOCK] for i in range(sz.model // BLOCK)], axis=1
    )
    wide = sz.hidden * BLOCK // sz.model
    per = 128 // wide
    up = jnp.concatenate(
        [tiles[i, 8, wide * (i % per) : wide * (i % per) + wide] for i in range(sz.model // BLOCK)], axis=0
    )
    vec = spread(vec, 1)
    return spread(gqkv, 0), spread(gout, 0), spread(gup, 0), spread(gdown, 0), vec[:2], vec[2:], spread(up, 0)


def on_device(
    tokens_in, grad_output, prefix_len, w_qkv, w_out, w_up, w_down, norm_gains, bias_rows, up_bias
):
    micro, rows, run, model = tokens_in.shape
    sz = Sizes(micro * rows, run, model, w_up.shape[2], lax.axis_size("seq"))
    depth = lax.axis_size("dp") // 2 if direct(w_qkv.shape[1]) else 0
    weights = (w_qkv, w_out, w_up, w_down, norm_gains, bias_rows, up_bias)
    if not depth:
        weights = whole_weights(*weights)
    by_row = (sz.rows, run, model)
    out_act, x_one, saved, wholes = forward(sz, depth, tokens_in.reshape(by_row), weights)
    grad, parts = backward(
        sz, depth, prefix_len, grad_output.reshape(by_row), tokens_in.reshape(by_row), x_one, saved, wholes
    )
    if depth:
        gqkv, gout, gup, gdown, gains, biases, ups = parts
        results = (gqkv, gout, gup, gdown, gains, biases, ups.reshape(up_bias.shape))
    else:
        layers = []
        for layer in range(LAYERS):
            pieces = [piece.reshape(-1, piece.shape[-1]) for piece in parts[GRADS * layer : GRADS * (layer + 1)]]
            up_a, up_b, down, out, dq, dk, dv, small = pieces
            qkv, up = jnp.concatenate([dq, dk, dv], axis=1), jnp.concatenate([up_a, up_b], axis=1)
            layers.append(scatter_by_sums(sz, (qkv, out, up, small, down)))
        results = [jnp.stack([layer[k] for layer in layers], axis=0) for k in range(7)]
    return (out_act.reshape(tokens_in.shape), grad.reshape(tokens_in.shape), *results)


def solution(mesh):
    tokens, shard = P(None, "dp", "seq", None), P(None, AXES, None)
    small, bias = P(None, None, AXES), P(None, AXES)
    return jax.shard_map(
        on_device,
        mesh=mesh,
        in_specs=(tokens, tokens, P(None, "dp"), shard, shard, shard, shard, small, small, bias),
        out_specs=(tokens, tokens, shard, shard, shard, shard, small, small, bias),
        check_vma=False,
    )
```

```python
import functools
import math

import jax
import jax.numpy as jnp
from jax import lax
from jax.experimental import pallas as pl
from jax.experimental.pallas import tpu as pltpu
from jax.sharding import PartitionSpec as P

HDIM = 64
BLOCK = 16
LEVELS = 6
LAYERS = 2
TOP = LEVELS - 1
CHUNK = 64
LN2 = math.log(2.0)
F32 = jnp.float32
BF16 = jnp.bfloat16
NEG = -1e30
VMEM_LIMIT = 62 * 2**20
AXES = ("dp", "seq")


def dot_nn(a, b):
    return lax.dot_general(a, b, (((1,), (0,)), ((), ())), preferred_element_type=F32)


def dot_nt(a, b):
    return lax.dot_general(a, b, (((1,), (1,)), ((), ())), preferred_element_type=F32)


def dot_tn(a, b):
    return lax.dot_general(a, b, (((0,), (0,)), ((), ())), preferred_element_type=F32)


class Sizes:
    def __init__(self, rows, run, model, hidden, seq):
        self.rows, self.run, self.model, self.hidden, self.seq = rows, run, model, hidden, seq
        self.tokens = rows * run
        self.pairs = model // 128
        self.chunks = run // CHUNK
        self.count = [run >> level for level in range(LEVELS)]
        self.top_keys = self.count[TOP] * seq
        self.offset, at = [], 0
        for level in range(TOP):
            self.offset.append(at)
            at += self.count[level] + 2 * BLOCK
        self.offset.append(at)
        self.bank = at + self.top_keys
        self.keys = [CHUNK + 2 * BLOCK, CHUNK // 2 + 2 * BLOCK] + [2 * BLOCK] * (TOP - 2) + [self.top_keys]
        self.start = [sum(self.keys[:level]) for level in range(LEVELS)]
        self.width = sum(self.keys)
        self.rim = rows * TOP * 2 * BLOCK


def normalise(values):
    centred = values - jnp.mean(values, axis=-1, keepdims=True)
    spread = jnp.mean(centred * centred, axis=-1, keepdims=True)
    inverse = lax.rsqrt(spread + 1e-05)
    return centred * inverse, inverse


def norm_back(grad, hat, inverse, gain):
    scaled = grad * gain
    first = jnp.mean(scaled, axis=-1, keepdims=True)
    second = jnp.mean(scaled * hat, axis=-1, keepdims=True)
    return inverse * (scaled - first - hat * second)


GELU_C = math.sqrt(2.0 / math.pi)


def gelu(v):
    return 0.5 * v * (1.0 + jnp.tanh(GELU_C * (v + 0.044715 * (v * v * v))))


def gelu_both(v):
    square = v * v
    t = jnp.tanh(GELU_C * (v + 0.044715 * (square * v)))
    half = 0.5 * (1.0 + t)
    slope = half + 0.5 * v * (1.0 - t * t) * (GELU_C * (1.0 + 3.0 * 0.044715 * square))
    return v * half, slope


def row_loop(total, step, body):
    def go(j, carry):
        body(pl.ds(pl.multiple_of(j * step, step), step))
        return carry

    lax.fori_loop(0, total // step, go, 0)


def coarse_matrix(run):
    row = lax.broadcasted_iota(jnp.int32, (run, run), 0)
    col = lax.broadcasted_iota(jnp.int32, (run, run), 1)
    out = jnp.zeros((run, run), F32)
    base = 0
    for level in range(1, LEVELS):
        n = run >> level
        hit = (row >= base) & (row < base + n) & ((col >> level) == row - base)
        out = jnp.where(hit, 2.0**-level, out)
        base += n
    return out.astype(BF16)


COARSE = [0] + [CHUNK - (CHUNK >> (level - 1)) for level in range(1, LEVELS + 1)]


def chunk_matrix():
    row = lax.broadcasted_iota(jnp.int32, (CHUNK, CHUNK), 0)
    col = lax.broadcasted_iota(jnp.int32, (CHUNK, CHUNK), 1)
    out = jnp.zeros((CHUNK, CHUNK), F32)
    for level in range(1, LEVELS):
        at, end = COARSE[level], COARSE[level + 1]
        out = jnp.where((row >= at) & (row < end) & ((col >> level) == row - at), 2.0**-level, out)
    return out.astype(BF16)


def sum_matrix():
    token = lax.broadcasted_iota(jnp.int32, (128, 128), 0)
    col = lax.broadcasted_iota(jnp.int32, (128, 128), 1)
    place, within = col % CHUNK, token % CHUNK
    out = jnp.zeros((128, 128), F32)
    for level in range(1, LEVELS):
        at, end = COARSE[level], COARSE[level + 1]
        out = jnp.where((place >= at) & (place < end) & ((within >> level) == place - at), 1.0, out)
    return jnp.where(token // CHUNK == col // CHUNK, out, 0.0).astype(BF16)


def fill_index(sz, index_ref):
    lane = lax.broadcasted_iota(jnp.int32, (8, 128), 1)
    for level in range(1, LEVELS):
        value = (lane // CHUNK) * CHUNK + COARSE[level] + ((lane % CHUNK) >> level)
        for k in range(sz.keys[level] // 8):
            index_ref[pl.ds(sz.start[level] - sz.start[1] + 8 * k, 8), :] = value


def fill_own(sz, own_ref):
    place = lax.broadcasted_iota(jnp.int32, (8, 128), 1) % CHUNK
    for level in range(1, LEVELS):
        value = jnp.where((place >= COARSE[level]) & (place < COARSE[level + 1]), 1.0, 0.0)
        for k in range(sz.keys[level] // 8):
            own_ref[pl.ds(sz.start[level] - sz.start[1] + 8 * k, 8), :] = value


def fill_mask(sz, mask_ref):
    place = lax.axis_index("seq")
    for i in range(sz.chunks):
        for level in range(LEVELS):
            shape = (sz.keys[level], 128)
            key = lax.broadcasted_iota(jnp.int32, shape, 0)
            token = lax.broadcasted_iota(jnp.int32, shape, 1) % CHUNK
            per_run = sz.count[level] // BLOCK
            if level == TOP:
                query_block = ((place * sz.run + i * CHUNK + token) >> TOP) // BLOCK
                allowed = jnp.abs(query_block - key // BLOCK) == 1
            else:
                own = (i * CHUNK >> level) // BLOCK
                if level >= 2:
                    key_block = own - 1 + 2 * (key // BLOCK)
                    allowed = key >= 0
                else:
                    key_block = own - 1 + key // BLOCK
                    distance = jnp.abs(key_block - own - (token >> level) // BLOCK)
                    allowed = distance <= 1 if level == 0 else distance == 1
                whole = place * per_run + key_block
                allowed = allowed & (whole >= 0) & (whole < per_run * sz.seq)
            mask_ref[i, pl.ds(sz.start[level], sz.keys[level])] = jnp.where(allowed, level * LN2, NEG)


def key_slices(sz, i, level):
    if level == TOP:
        return [(sz.offset[TOP], sz.top_keys)]
    if level < 2:
        return [(sz.offset[level] + (CHUNK >> level) * i, sz.keys[level])]
    own = (i * CHUNK) // (BLOCK << level)
    return [(sz.offset[level] + BLOCK * own, BLOCK), (sz.offset[level] + BLOCK * (own + 2), BLOCK)]


def take(ref, pieces, lanes):
    parts = [ref[rows_at(at, size), lanes] for at, size in pieces]
    return parts[0] if len(parts) == 1 else jnp.concatenate(parts, axis=0)


def rows_at(at, size):
    return pl.ds(at if isinstance(at, int) else pl.multiple_of(at, BLOCK), size)


def give(ref, pieces, lanes, value):
    done = 0
    for at, size in pieces:
        ref[rows_at(at, size), lanes] += value[done : done + size]
        done += size


def two_heads(block):
    first = lax.broadcasted_iota(jnp.int32, block.shape, 1) < HDIM
    zero = jnp.zeros_like(block)
    return jnp.concatenate([jnp.where(first, block, zero), jnp.where(first, zero, block)], axis=0)


def one_row(block):
    first = lax.broadcasted_iota(jnp.int32, (CHUNK, 128), 1) < HDIM
    return jnp.where(first, block[:CHUNK], block[CHUNK:])


class Units:
    def __init__(self, sz, q_ref, key_ref, value_ref):
        self.sz, self.q_ref, self.key_ref, self.value_ref = sz, q_ref, key_ref, value_ref
        self.all = [(i, pair) for i in range(sz.chunks) for pair in range(sz.pairs)]
        self.pieces = []
        for i in range(sz.chunks):
            levels = [key_slices(sz, i, level) for level in range(LEVELS)]
            self.pieces.append((levels[0], sum(levels[1:], [])))
        matrix = chunk_matrix()
        self.fine = [q_ref[self.tokens(i), :] for i in range(sz.chunks)]
        self.coarse = [dot_nn(matrix, fine).astype(BF16) for fine in self.fine]

    def tokens(self, i):
        return pl.ds(i * CHUNK, CHUNK)

    def lanes(self, pair):
        return slice(128 * pair, 128 * pair + 128)

    def queries(self, i, pair):
        lanes = self.lanes(pair)
        return two_heads(self.fine[i][:, lanes]), two_heads(self.coarse[i][:, lanes])

    def keys(self, i, pair):
        return [take(self.key_ref, pieces, self.lanes(pair)) for pieces in self.pieces[i]]

    def values(self, i, pair):
        return take(self.value_ref, self.pieces[i][0] + self.pieces[i][1], self.lanes(pair))

    def scores(self, u, i, pair, mask_ref, index_ref, out_ref):
        base = self.sz.start[1]
        (fine_keys, coarse_keys), (fine, coarse) = self.keys(i, pair), self.queries(i, pair)
        out_ref[u, :base] = dot_nt(fine_keys, fine) + mask_ref[i, :base]
        upper = jnp.take_along_axis(dot_nt(coarse_keys, coarse), index_ref[...], axis=1)
        out_ref[u, base:] = upper + mask_ref[i, base:]


def attend(sz, q_ref, key_ref, value_ref, mask_ref, index_ref, att_ref, lse_ref, score_ref, weight_ref, pause):
    units = Units(sz, q_ref, key_ref, value_ref)
    for u, (i, pair) in enumerate(units.all):
        units.scores(u, i, pair, mask_ref, index_ref, score_ref)
    pause()
    for u, (i, pair) in enumerate(units.all):
        scores = score_ref[u]
        peak = jnp.max(scores, axis=0, keepdims=True)
        weights = jnp.exp(scores - peak)
        total = jnp.sum(weights, axis=0, keepdims=True)
        lse_ref[i, pair : pair + 1, :] = peak + jnp.log(total)
        weight_ref[u] = (weights * (1.0 / total)).astype(BF16)
    pause()
    for u, (i, pair) in enumerate(units.all):
        mixed = dot_tn(weight_ref[u], units.values(i, pair))
        att_ref[units.tokens(i), units.lanes(pair)] = one_row(mixed).astype(BF16)
    pause()


def attend_back(
    sz, q_ref, key_ref, value_ref, mask_ref, index_ref, own_ref, lse_ref, go_ref, dq_ref, dkey_ref, dvalue_ref,
    score_ref, back_ref, weight_ref, dscore_ref, coarse_ref, pause
):
    units = Units(sz, q_ref, key_ref, value_ref)
    sums, matrix, base = sum_matrix(), chunk_matrix(), sz.start[1]
    for u, (i, pair) in enumerate(units.all):
        units.scores(u, i, pair, mask_ref, index_ref, score_ref)
    pause()
    for u, (i, pair) in enumerate(units.all):
        go = two_heads(go_ref[units.tokens(i), units.lanes(pair)])
        back_ref[u] = dot_nt(units.values(i, pair), go)
    for u, (i, pair) in enumerate(units.all):
        weights = jnp.exp(score_ref[u] - lse_ref[i, pair : pair + 1, :])
        weight_ref[u] = weights.astype(BF16)
        back = back_ref[u]
        inner = jnp.sum(weights * back, axis=0, keepdims=True)
        dscore_ref[u] = (weights * (back - inner)).astype(BF16)
    pause()
    for u, (i, pair) in enumerate(units.all):
        go = two_heads(go_ref[units.tokens(i), units.lanes(pair)])
        give(dvalue_ref, units.pieces[i][0] + units.pieces[i][1], units.lanes(pair), dot_nn(weight_ref[u], go))
    for u, (i, pair) in enumerate(units.all):
        coarse_ref[u] = (dot_nn(dscore_ref[u, base:], sums) * own_ref[...]).astype(BF16)
    pause()
    for u, (i, pair) in enumerate(units.all):
        (first, upper), (fine, coarse) = units.pieces[i], units.queries(i, pair)
        give(dkey_ref, first, units.lanes(pair), dot_nn(dscore_ref[u, :base], fine))
        give(dkey_ref, upper, units.lanes(pair), dot_nn(coarse_ref[u], coarse))
    pause()
    for u, (i, pair) in enumerate(units.all):
        fine_keys, coarse_keys = units.keys(i, pair)
        fine = one_row(dot_tn(dscore_ref[u, :base], fine_keys))
        coarse = one_row(dot_tn(coarse_ref[u], coarse_keys)).astype(BF16)
        dq_ref[units.tokens(i), units.lanes(pair)] = ((fine + dot_tn(matrix, coarse)) * HDIM**-0.5).astype(BF16)
    pause()


def rim_rows(level, kind):
    return pl.ds((level * 2 + kind) * BLOCK, BLOCK)


def unpack_small(sz, small, vec_ref, up_ref):
    lane = lax.broadcasted_iota(jnp.int32, (BLOCK, 128), 1)
    tiles = [small[BLOCK * i : BLOCK * i + BLOCK, :].astype(F32) for i in range(sz.model // BLOCK)]
    for c in range(sz.model // 128):
        total = tiles[8 * c]
        for j in range(1, 8):
            total = jnp.where(lane // 16 == j, tiles[8 * c + j], total)
        vec_ref[:, 128 * c : 128 * c + 128] = total[:8]
    wide = sz.hidden * BLOCK // sz.model
    for c in range(sz.hidden // 128):
        total = tiles[2 * c]
        total = jnp.where(lane >= wide, tiles[2 * c + 1], total)
        up_ref[:, 128 * c : 128 * c + 128] = total[8:9]


def place_rims(sz, low_ref, high_ref, tops_ref, key_ref, value_ref):
    for kind, bank in ((0, key_ref), (1, value_ref)):
        for level in range(TOP):
            bank[pl.ds(sz.offset[level], BLOCK), :] = low_ref[rim_rows(level, kind), :]
            bank[pl.ds(sz.offset[level] + BLOCK + sz.count[level], BLOCK), :] = high_ref[rim_rows(level, kind), :]
        n = sz.count[TOP]
        for s in range(0, sz.seq, 2):
            pair = [tops_ref[s + k, kind * n : kind * n + n, :] for k in range(2)]
            bank[pl.ds(sz.offset[TOP] + s * n, 2 * n), :] = jnp.concatenate(pair, axis=0)


MESH = pl.DeviceIdType.MESH


class Grid:
    def __init__(self, depth):
        dp, seq = lax.axis_index("dp"), lax.axis_index("seq")
        self.depth = depth
        self.z, self.x, self.y, self.c = dp // 2, dp % 2, seq // 2, seq % 2

    def at(self, z, x, y, c):
        return (z * 2 + x, y * 2 + c)

    def index(self, z, x, y, c):
        return z * 8 + x * 4 + y * 2 + c

    def partner(self, axis):
        z, x, y, c = self.z, self.x, self.y, self.c
        return self.at(z, 1 - x if axis == "x" else x, 1 - y if axis == "y" else y, 1 - c if axis == "c" else c)

    def up(self, by):
        return self.at(self.z + by, self.x, self.y, self.c)


def greet(devices):
    barrier = pltpu.get_barrier_semaphore()
    peers = jnp.int32(0)
    for where, condition in devices:
        signal = functools.partial(pl.semaphore_signal, barrier, inc=1, device_id=where, device_id_type=MESH)
        if condition is None:
            signal()
            peers += 1
        else:
            pl.when(condition)(signal)
            peers += condition.astype(jnp.int32)
    pl.semaphore_wait(barrier, peers)


def both(first, second):
    if first is None:
        return second
    return first if second is None else first & second


def when(condition, act):
    if condition is None:
        act()
    else:
        pl.when(condition)(act)


class Plan:
    HOP = 1.5

    def __init__(self, core, links):
        self.rate = {"core": core, "plane": links, "z": links}
        self.now, self.count, self.waiting = 0.0, 0, []
        self.free = dict.fromkeys(self.rate, 0.0)

    def send(self, link, size):
        self.free[link] = max(self.now, self.free[link]) + size / self.rate[link]
        return self.free[link] + self.HOP

    def later(self, ready, act):
        self.count += 1
        self.waiting.append((ready, self.count, act))

    def pop(self):
        first = min(self.waiting, key=lambda entry: entry[:2])
        self.waiting.remove(first)
        self.now = max(self.now, first[0])
        first[2]()

    def advance(self, time):
        self.now += time
        while self.waiting and min(entry[0] for entry in self.waiting) <= self.now:
            self.pop()

    def until(self, done):
        while not done():
            self.pop()

    def flush(self):
        while self.waiting:
            self.pop()


class Gather:
    def __init__(self, grid, plan, pieces, local_sem, send_sem, recv_sem):
        self.grid, self.plan, self.pieces = grid, plan, pieces
        self.local_sem, self.send_sem, self.recv_sem = local_sem, send_sem, recv_sem
        z, x, y, c = grid.z, grid.x, grid.y, grid.c
        self.others = [lax.rem(z + k, grid.depth) for k in range(1, grid.depth)]
        self.one, self.two, self.lines = [], [], []
        for p in range(len(pieces)):
            y_first = (c ^ (FLIP * (p % 2))) == 0
            pick = lambda first, second: jnp.where(y_first, first, second)
            one, two = (pick(x, 1 - x), pick(1 - y, y)), (pick(1 - x, x), pick(y, 1 - y))
            self.one.append(grid.at(z, *one, c))
            self.two.append(grid.at(z, *two, c))
            self.lines.append([(x, y), one, two, (1 - x, 1 - y)])
        self.ids, self.count = [], 0
        for piece in pieces:
            self.ids.append(list(range(self.count, self.count + len(piece))))
            self.count += len(piece)
        self.sends = []
        self.done = [False] * len(pieces)
        self.passed, self.parked = [False] * len(pieces), []

    def size(self, p):
        return sum(2 * share.shape[0] * share.shape[1] for share, _ in self.pieces[p])

    def copy(self, array, source, target, slot, landing, to):
        return pltpu.make_async_remote_copy(
            src_ref=source, dst_ref=target, send_sem=self.send_sem.at[array, slot],
            recv_sem=self.recv_sem.at[array, landing], device_id=to, device_id_type=MESH,
        )

    def begin(self, p):
        grid = self.grid
        for array, (share, whole) in zip(self.ids[p], self.pieces[p]):
            mine = whole.at[grid.z, grid.x, grid.y, grid.c]
            pltpu.make_async_copy(share, mine, self.local_sem.at[array]).start()
            for k, other in enumerate(self.others):
                copy = self.copy(array, share, mine, k, k, grid.at(other, grid.x, grid.y, grid.c))
                copy.start()
                self.sends.append(copy)
        ready = self.plan.send("z", 2 * grid.depth * self.size(p))
        self.plan.later(ready, functools.partial(self.enter, p))

    def enter(self, p):
        if p >= GATE and not self.passed[p - GATE]:
            self.parked.append(p)
        else:
            self.along(p)

    def line(self, p, whole, k):
        xx, yy = self.lines[p][k]
        return whole.at[:, xx, yy, self.grid.c]

    def pass_line(self, p, k, slots, landing):
        xx, yy = self.lines[p][k]
        for array, (_, whole) in zip(self.ids[p], self.pieces[p]):
            line = self.line(p, whole, k)
            for name, slot in slots.items():
                if name == "core":
                    copy = self.copy(array, line, line, slot, 2 + self.grid.depth + xx * 2 + yy, self.grid.partner("c"))
                else:
                    copy = self.copy(array, line, line, slot, landing[name], {"one": self.one[p], "two": self.two[p]}[name])
                copy.start()
                self.sends.append(copy)

    def receive(self, p, landing, k):
        for array, (_, whole) in zip(self.ids[p], self.pieces[p]):
            line = self.line(p, whole, k)
            self.copy(array, line, line, 0, landing, self.one[p]).wait_recv()

    def along(self, p):
        grid, size, plan = self.grid, self.size(p), self.plan
        base = grid.depth - 1
        for array, (share, whole) in zip(self.ids[p], self.pieces[p]):
            mine = whole.at[grid.z, grid.x, grid.y, grid.c]
            pltpu.make_async_copy(share, mine, self.local_sem.at[array]).wait()
            for k in range(grid.depth - 1):
                self.copy(array, share, mine, k, k, self.one[p]).wait_recv()
        self.pass_line(p, 0, {"one": base, "two": base + 1, "core": base + 2}, {"one": base, "two": base + 1})
        line = grid.depth * size
        plan.later(plan.send("plane", line), functools.partial(self.after_one, p))
        plan.later(plan.send("plane", line), functools.partial(self.after_two, p))
        plan.send("core", line)

    def after_one(self, p):
        grid, plan = self.grid, self.plan
        base = grid.depth - 1
        self.receive(p, base, 1)
        self.pass_line(p, 1, {"two": base + 3, "core": base + 4}, {"two": base + 2})
        line = grid.depth * self.size(p)
        plan.later(plan.send("plane", line), functools.partial(self.after_both, p))
        plan.send("core", line)
        self.passed[p] = True
        if p + GATE in self.parked:
            self.parked.remove(p + GATE)
            self.along(p + GATE)

    def after_two(self, p):
        base = self.grid.depth - 1
        self.receive(p, base + 1, 2)
        self.pass_line(p, 2, {"core": base + 5}, {})
        self.plan.send("core", self.grid.depth * self.size(p))

    def after_both(self, p):
        base = self.grid.depth - 1
        self.receive(p, base + 2, 3)
        self.pass_line(p, 3, {"core": base + 6}, {})
        ready = self.plan.send("core", self.grid.depth * self.size(p))
        self.plan.later(ready, functools.partial(self.finish, p))

    def finish(self, p):
        grid = self.grid
        for array, (_, whole) in zip(self.ids[p], self.pieces[p]):
            for xx, yy in self.lines[p]:
                line = whole.at[:, xx, yy, 1 - grid.c]
                self.copy(array, line, line, 0, 2 + grid.depth + xx * 2 + yy, self.one[p]).wait_recv()
        self.done[p] = True

    def need(self, p):
        self.plan.until(lambda: self.done[p])

    def drain(self):
        for copy in self.sends:
            copy.wait_send()


class Scatter:
    def __init__(self, grid, plan, pieces, buffers, sums, send_sem, recv_sem, free_sem, again, more):
        self.grid, self.plan, self.pieces, self.buffers, self.sums = grid, plan, pieces, buffers, sums
        self.free_sem, self.again, self.more = free_sem, again, more
        self.next = {}
        self.done = [False] * len(pieces)
        self.send_sem, self.recv_sem = send_sem, recv_sem
        self.copies = [[] for _ in pieces]
        z, x, y, c = grid.z, grid.x, grid.y, grid.c
        self.others = [lax.rem(z + k, grid.depth) for k in range(1, grid.depth)]
        self.x_first = [(c ^ (FLIP * (p % 2))) == 0 for p in range(len(pieces))]
        pick = lambda p, first, second: jnp.where(self.x_first[p], first, second)
        self.one = [grid.at(z, pick(p, 1 - x, x), pick(p, y, 1 - y), c) for p in range(len(pieces))]
        self.two = [grid.at(z, pick(p, x, 1 - x), pick(p, 1 - y, y), c) for p in range(len(pieces))]
        self.mine = [(pick(p, x, y), pick(p, y, x)) for p in range(len(pieces))]

    def move(self, p, source, target, to):
        stage = len(self.copies[p])
        copy = pltpu.make_async_remote_copy(
            src_ref=source, dst_ref=target, send_sem=self.send_sem.at[p, stage], recv_sem=self.recv_sem.at[p, stage],
            device_id=to, device_id_type=MESH,
        )
        copy.start()
        self.copies[p].append(copy)

    def step(self, link, blocks, p, act):
        piece = self.pieces[p]
        ready = self.plan.send(link, 2 * blocks * piece.shape[4] * piece.shape[5])
        self.plan.later(ready, functools.partial(act, p))

    def senders(self):
        grid = self.grid
        along = [grid.at(other, grid.x, grid.y, grid.c) for other in self.others]
        return [grid.partner("c"), grid.partner("x"), grid.partner("y")] + along

    def begin(self, p):
        if self.again:
            pl.semaphore_wait(self.free_sem.at[p], len(self.senders()))
        self.move(p, self.pieces[p].at[:, :, :, 1 - self.grid.c], self.buffers[p][0], self.grid.partner("c"))
        self.step("core", 4 * self.grid.depth, p, self.first)

    def place(self, p, one, two):
        return jnp.where(self.x_first[p], one, two), jnp.where(self.x_first[p], two, one)

    def first(self, p):
        grid = self.grid
        piece, (from_core, to_one, from_one) = self.pieces[p], self.buffers[p][:3]
        self.copies[p][0].wait_recv()
        for zz in range(grid.depth):
            for two in range(2):
                xx, yy = self.place(p, 1 - self.mine[p][0], two)
                total = piece[zz, xx, yy, grid.c].astype(F32) + from_core[zz, xx, yy].astype(F32)
                to_one[zz, two] = total.astype(BF16)
        self.move(p, to_one, from_one, self.one[p])
        self.step("plane", 2 * grid.depth, p, self.second)

    def second(self, p):
        grid = self.grid
        piece, (from_core, _, from_one, to_two, from_two) = self.pieces[p], self.buffers[p][:5]
        self.copies[p][1].wait_recv()
        other = 1 - self.mine[p][1]
        xx, yy = self.place(p, self.mine[p][0], other)
        for zz in range(grid.depth):
            total = piece[zz, xx, yy, grid.c].astype(F32) + from_core[zz, xx, yy].astype(F32)
            to_two[zz] = (total + from_one[zz, other].astype(F32)).astype(BF16)
        self.move(p, to_two, from_two, self.two[p])
        self.step("plane", grid.depth, p, self.along)

    def along(self, p):
        grid = self.grid
        piece, (from_core, _, from_one, _, from_two, ready, from_z) = self.pieces[p], self.buffers[p]
        self.copies[p][2].wait_recv()
        for zz in range(grid.depth):
            total = piece[zz, grid.x, grid.y, grid.c].astype(F32) + from_core[zz, grid.x, grid.y].astype(F32)
            total = total + from_one[zz, self.mine[p][1]].astype(F32) + from_two[zz].astype(F32)
            ready[zz] = total.astype(BF16)
        for k, other in enumerate(self.others):
            self.move(p, ready.at[other], from_z.at[k], grid.at(other, grid.x, grid.y, grid.c))
        self.step("z", 2 * grid.depth, p, self.finish)

    def finish(self, p):
        ready, from_z = self.buffers[p][5:7]
        total = ready[self.grid.z].astype(F32)
        for k in range(self.grid.depth - 1):
            self.copies[p][3 + k].wait_recv()
            total = total + from_z[k].astype(F32)
        self.sums[p][...] = total
        if self.more:
            for copy in self.copies[p]:
                copy.wait_send()
            for device in self.senders():
                pl.semaphore_signal(self.free_sem.at[p], inc=1, device_id=device, device_id_type=MESH)
        self.done[p] = True
        if p in self.next:
            self.next.pop(p)()

    def need(self, p):
        self.plan.until(lambda: self.done[p])

    def drain(self):
        for copies in self.copies:
            for copy in copies if not self.more else []:
                copy.wait_send()


FLIP = 1
GATE = 2
SCATTER_BUFFERS = 7


def scatter_buffers(depth, block):
    leads = ((depth, 2, 2), (depth, 2), (depth, 2), (depth,), (depth,), (depth,), (depth - 1,))
    return [pltpu.VMEM(lead + tuple(block), BF16) for lead in leads]


class Rims:
    def __init__(self, sz, ahead, behind, tops, low, high, all_tops, send_sem, recv_sem):
        self.sz, self.low, self.high, self.all_tops, self.tops = sz, low, high, all_tops, tops
        self.me, self.dp = lax.axis_index("seq"), lax.axis_index("dp")
        me, dp, seq = self.me, self.dp, sz.seq
        make = lambda source, target, k, to: pltpu.make_async_remote_copy(
            src_ref=source, dst_ref=target, send_sem=send_sem.at[k], recv_sem=recv_sem.at[k],
            device_id=(dp, to), device_id_type=MESH,
        )
        self.ahead = lambda: make(ahead, low, 0, me + 1)
        self.behind = lambda: make(behind, high, 1, me - 1)
        self.rest = []
        for k in range(1, seq):
            other = lax.rem(me + k, seq)
            source = tops.at[0] if tops.shape[0] == 1 else tops.at[other]
            self.rest.append(make(source, all_tops.at[me], 1 + k, other))

    def start(self):
        when(self.me + 1 < self.sz.seq, lambda: self.ahead().start())
        when(self.me > 0, lambda: self.behind().start())
        for copy in self.rest:
            copy.start()
        self.all_tops[self.me] = self.tops[0] if self.tops.shape[0] == 1 else self.tops[self.me]

        def no_low():
            self.low[...] = jnp.zeros_like(self.low)

        def no_high():
            self.high[...] = jnp.zeros_like(self.high)

        when(self.me == 0, no_low)
        when(self.me == self.sz.seq - 1, no_high)

    def arrive(self):
        when(self.me > 0, lambda: self.ahead().wait_recv())
        when(self.me + 1 < self.sz.seq, lambda: self.behind().wait_recv())
        for copy in self.rest:
            copy.wait_recv()

    def drain(self):
        when(self.me + 1 < self.sz.seq, lambda: self.ahead().wait_send())
        when(self.me > 0, lambda: self.behind().wait_send())
        for copy in self.rest:
            copy.wait_send()


class Copies:
    def __init__(self, sem):
        self.sem, self.open, self.count = sem, {}, 0

    def start(self, name, source, target):
        copy = pltpu.make_async_copy(source, target, self.sem.at[self.count])
        self.count += 1
        copy.start()
        self.open[name] = copy

    def wait(self, *names):
        for name in names:
            if name in self.open:
                self.open.pop(name).wait()

    def drain(self):
        self.wait(*list(self.open))


def whole_rows(ref, columns):
    value = ref[:, :, :, :, :, columns]
    return value.reshape(-1, value.shape[-1])


def some_rows(ref, at, rows):
    per = ref.shape[4]
    blocks = [ref[i // 8, (i // 4) % 2, (i // 2) % 2, i % 2] for i in range(at // per, (at + rows) // per)]
    return jnp.concatenate(blocks, axis=0)


def make_share(sz, gains, biases_ref, layer, up, wide_ref, share_ref):
    wide = up.shape[-1]
    wide_ref[...] = jnp.zeros_like(wide_ref)
    wide_ref[0:2, 0:BLOCK] = gains.astype(F32)
    for k in range(6):
        wide_ref[2 + k : 3 + k, 0:BLOCK] = biases_ref[k, layer : layer + 1, :].astype(F32)
    wide_ref[8:16, 0:wide] = jnp.broadcast_to(up.astype(F32), (8, wide))
    row = lax.broadcasted_iota(jnp.int32, (128, 128), 0)
    lane = lax.broadcasted_iota(jnp.int32, (128, 128), 1)
    top = jnp.where((row < BLOCK) & (lane % BLOCK == row), 1.0, 0.0).astype(BF16)
    low = jnp.where((row < wide) & (lane % wide == row), 1.0, 0.0).astype(BF16)
    values = wide_ref[...].astype(BF16)
    share_ref[...] = jnp.concatenate([dot_nn(values, top)[:8], dot_nn(values, low)[8:]], axis=0).astype(BF16)


SAVED = 6
TIMES = {"before": 2.2, "attend": 0.8, "project": 1.0, "forward": 1.4, "start": 1.5, "back": 1.9, "branch": 2.0, "attend_back": 0.6,
         "levels": 1.0, "finish": 1.2}


def forward_kernel(sz, depth, *refs):
    refs = list(refs)
    take_refs = lambda n: [refs.pop(0) for _ in range(n)]
    tokens_ref = take_refs(1)[0]
    if depth:
        shares, (gains_ref, biases_ref, upb_ref) = take_refs(4), take_refs(3)
    else:
        wholes = take_refs(5)
    out_act_ref, x_out = take_refs(2)
    saved_out = take_refs(SAVED)
    if depth:
        wholes_out, wholes = take_refs(5), take_refs(5)
    q_ref, key_ref, value_ref, att_ref, lse_ref, middle_ref = take_refs(SAVED)
    x_ref, vec, up, mask_ref, second_ref, state_ref = take_refs(6)
    index_ref, score_ref, weight_ref = take_refs(3)
    rims_out, tops_out, low_ref, high_ref, tops_ref, rim_send, rim_recv, copy_sem = take_refs(8)
    model, run = sz.model, sz.run
    wq, wo, wu, wd, ws = wholes
    plan, copies = Plan(450e3, 110e3), Copies(copy_sem)
    me, dp = lax.axis_index("seq"), lax.axis_index("dp")
    peers = [((dp, lax.rem(me + k, sz.seq)), None) for k in range(1, sz.seq)]
    if depth:
        wide_ref, share_ref, local_sem, send_sem, recv_sem = take_refs(5)
        grid = Grid(depth)
        half = sz.hidden // 2
        pieces = []
        for layer in range(LAYERS):
            part = lambda k, columns: (shares[k].at[layer, :, columns], wholes[k].at[layer, :, :, :, :, :, columns])
            pieces.append([part(0, slice(None)), (share_ref.at[layer], ws.at[layer])])
            pieces.append([part(1, slice(None)), part(2, slice(0, half))])
            pieces.append([part(2, slice(half, None))])
            pieces.append([part(3, slice(None))])
        gather = Gather(grid, plan, pieces, local_sem, send_sem, recv_sem)
        peers += [(grid.partner("x"), None)] + [(grid.at(other, grid.x, grid.y, grid.c), None) for other in gather.others]
        greet(peers)
        for layer in range(LAYERS):
            make_share(
                sz, gains_ref[layer], biases_ref, layer, upb_ref[layer : layer + 1, :], wide_ref, share_ref.at[layer]
            )
        gather.begin(0)
        for p in range(1, 4):
            plan.later(3.0 + 3.0 * p, functools.partial(gather.begin, p))
        for p in range(4, 8):
            plan.later(14.0 + 3.0 * (p - 4), functools.partial(gather.begin, p))

        def need(layer, k):
            gather.need(4 * layer + k)

        def keep(layer):
            for k in range(5):
                copies.start(("weights", layer, k), wholes[k].at[layer], wholes_out[k].at[layer])
    else:
        greet(peers)
        need = lambda layer, k: None
        keep = lambda layer: None

    def save(k, layer):
        source = (q_ref, key_ref, value_ref, att_ref, lse_ref, middle_ref)[k]
        copies.start(("saved", k, layer), source.at[layer], saved_out[k].at[layer])

    fill_mask(sz, mask_ref)
    fill_index(sz, index_ref)
    coarse = coarse_matrix(run)
    rows_of = lambda r: pl.ds(r * run, run)
    for r in range(sz.rows):
        state_ref[rows_of(r), :] = tokens_ref[r].astype(F32)
    all_rims = []
    for layer in range(LAYERS):
        need(layer, 0)
        unpack_small(sz, whole_rows(ws.at[layer], slice(None)), vec, up)
        rims = []
        for r in range(sz.rows):
            hat, _ = normalise(state_ref[rows_of(r), :])
            normed = (hat * vec[0:1, :] + vec[2:3, :]).astype(BF16)
            tops = []
            for kind, bank in ((0, key_ref.at[layer, r]), (1, value_ref.at[layer, r])):
                mixed = dot_nn(normed, whole_rows(wq.at[layer], slice((1 + kind) * model, (2 + kind) * model)))
                if kind == 1:
                    mixed = mixed + vec[4:5, :]
                mixed = mixed.astype(BF16)
                levels = dot_nn(coarse, mixed).astype(BF16)
                base = 0
                for level in range(LEVELS):
                    n = sz.count[level]
                    if level == 0:
                        now = mixed
                    else:
                        now = levels[base : base + n]
                        base += n
                    if level < TOP:
                        bank[pl.ds(sz.offset[level] + BLOCK, n), :] = now
                        rims_out[layer, r, 0, rim_rows(level, kind), :] = now[n - BLOCK :]
                        rims_out[layer, r, 1, rim_rows(level, kind), :] = now[:BLOCK]
                    else:
                        tops.append(now)
            tops_out[layer, r, 0] = jnp.concatenate(tops, axis=0)
            rims.append(
                Rims(
                    sz, rims_out.at[layer, r, 0], rims_out.at[layer, r, 1], tops_out.at[layer, r], low_ref.at[layer, r],
                    high_ref.at[layer, r], tops_ref.at[layer, r], rim_send.at[layer, r], rim_recv.at[layer, r],
                )
            )
            rims[-1].start()
            queries = (dot_nn(normed, whole_rows(wq.at[layer], slice(0, model))) + vec[3:4, :]).astype(BF16)
            q_ref[layer, r] = queries * jnp.asarray(HDIM**-0.5, BF16)
            plan.advance(TIMES["before"])
        save(0, layer)
        all_rims += rims
        for r in range(sz.rows):
            rims[r].arrive()
            place_rims(
                sz, low_ref.at[layer, r], high_ref.at[layer, r], tops_ref.at[layer, r], key_ref.at[layer, r],
                value_ref.at[layer, r],
            )
            attend(
                sz, q_ref.at[layer, r], key_ref.at[layer, r], value_ref.at[layer, r], mask_ref, index_ref,
                att_ref.at[layer, r], lse_ref.at[layer, r], score_ref, weight_ref,
                functools.partial(plan.advance, TIMES["attend"]),
            )
        for k in (1, 2, 3, 4):
            save(k, layer)
        need(layer, 1)
        for r in range(sz.rows):
            rows = rows_of(r)
            middle = state_ref[rows, :] + dot_nn(att_ref[layer, r], whole_rows(wo.at[layer], slice(None))) + vec[5:6, :]
            middle_ref[layer, rows, :] = middle
            hat, _ = normalise(middle)
            second_ref[rows, :] = (hat * vec[1:2, :] + vec[6:7, :]).astype(BF16)
            state_ref[rows, :] = middle + vec[7:8, :]
            plan.advance(TIMES["project"])
        save(5, layer)
        need(layer, 3)
        parts = sz.hidden // model
        for c in range(parts):
            if c == parts // 2:
                need(layer, 2)
            units = slice(c * model, (c + 1) * model)
            for r in range(sz.rows):
                rows = rows_of(r)
                hidden = dot_nn(second_ref[rows, :], whole_rows(wu.at[layer], units)) + up[:, units]
                state_ref[rows, :] += dot_nn(gelu(hidden).astype(BF16), some_rows(wd.at[layer], c * model, model))
            plan.advance(TIMES["forward"])
        keep(layer)
        if layer == 0:
            x_ref[...] = state_ref[...]
            copies.start("x", x_ref, x_out)
        else:
            for r in range(sz.rows):
                out_act_ref[r] = state_ref[rows_of(r), :].astype(BF16)
    plan.flush()
    for rims in all_rims:
        rims.drain()
    if depth:
        gather.drain()
    copies.drain()


WHOLE = pl.BlockSpec(memory_space=pltpu.VMEM)
ANYWHERE = pl.BlockSpec(memory_space=pl.ANY)


def attend_scratch(sz):
    units = sz.chunks * sz.pairs
    coarse = sz.width - sz.start[1]
    wide = ((units, sz.width, 128), F32)
    return [
        ((coarse, 128), jnp.int32), wide, (wide[0], BF16), ((coarse, 128), F32), wide, (wide[0], BF16),
        ((units, coarse, 128), BF16),
    ]


def forward(sz, depth, tokens, weights):
    n, rows, run = sz.model, sz.rows, sz.run
    saved = [
        ((LAYERS, rows, run, n), BF16), ((LAYERS, rows, sz.bank, n), BF16), ((LAYERS, rows, sz.bank, n), BF16),
        ((LAYERS, rows, run, n), BF16), ((LAYERS, rows, sz.chunks, sz.pairs, 128), F32), ((LAYERS, sz.tokens, n), F32),
    ]
    outs = [((rows, run, n), BF16), ((sz.tokens, n), F32)] + saved
    out_specs = [WHOLE] + [ANYWHERE] * (1 + SAVED)
    scratch = []
    if depth:
        full = [((LAYERS, depth, 2, 2, 2) + share.shape[1:], BF16) for share in weights[:4]]
        full.append(((LAYERS, depth, 2, 2, 2, BLOCK, 128), BF16))
        outs += full
        out_specs += [ANYWHERE] * 5
        scratch += full
    rim = sz.rim // rows
    scratch += saved + [
        ((sz.tokens, n), F32), ((8, n), F32), ((1, sz.hidden), F32), ((sz.chunks, sz.width, 128), F32),
        ((sz.tokens, n), BF16), ((sz.tokens, n), F32)] + attend_scratch(sz)[:3] + [((LAYERS, rows, 2, rim, n), BF16),
        ((LAYERS, rows, 1, BLOCK, n), BF16), ((LAYERS, rows, rim, n), BF16), ((LAYERS, rows, rim, n), BF16),
        ((LAYERS, rows, sz.seq, BLOCK, n), BF16),
    ]
    scratch = [pltpu.VMEM(shape, dtype) for shape, dtype in scratch]
    scratch += [pltpu.SemaphoreType.DMA((LAYERS, rows, sz.seq + 1))] * 2
    scratch += [pltpu.SemaphoreType.DMA((LAYERS * (SAVED + 5) + 1,))]
    if depth:
        arrays = 6 * LAYERS
        scratch += [pltpu.VMEM((BLOCK, 128), F32), pltpu.VMEM((LAYERS, BLOCK, 128), BF16)]
        scratch += [pltpu.SemaphoreType.DMA((arrays,))] + [pltpu.SemaphoreType.DMA((arrays, depth + 6))] * 2
    results = pl.pallas_call(
        functools.partial(forward_kernel, sz, depth),
        out_shape=[jax.ShapeDtypeStruct(shape, dtype) for shape, dtype in outs],
        in_specs=[WHOLE] * (1 + len(weights)),
        out_specs=out_specs,
        scratch_shapes=scratch,
        compiler_params=pltpu.CompilerParams(
            collective_id=0, has_side_effects=True, vmem_limit_bytes=VMEM_LIMIT
        ),
        name="forward",
    )(tokens, *weights)
    return results[0], results[1], results[2 : 2 + SAVED], (results[2 + SAVED :] if depth else weights)


def store_blocks(ref, at, columns, value):
    per = ref.shape[4]
    for k in range(value.shape[0] // per):
        i = at + k
        ref[i // 8, (i // 4) % 2, (i // 2) % 2, i % 2, :, columns] = value[k * per : (k + 1) * per]


def unpack_share(sz, small, layer, gains_ref, biases_ref, up_ref):
    place = lax.axis_index("dp") * lax.axis_size("seq") + lax.axis_index("seq")
    wide = up_ref.shape[-1]
    vec, up = small[0:8, 0:BLOCK], small[8:9, 0:wide]
    for j in range(1, 128 // BLOCK):
        vec = jnp.where(place % (128 // BLOCK) == j, small[0:8, j * BLOCK : (j + 1) * BLOCK], vec)
    for j in range(1, 128 // wide):
        up = jnp.where(place % (128 // wide) == j, small[8:9, j * wide : (j + 1) * wide], up)
    gains_ref[layer] = vec[0:2]
    for k in range(6):
        biases_ref[k, layer : layer + 1, :] = vec[2 + k : 3 + k]
    up_ref[layer : layer + 1, :] = up


GRADS = 8
EARLY = 4


def backward_kernel(sz, depth, *refs):
    refs = list(refs)
    take_refs = lambda n: [refs.pop(0) for _ in range(n)]
    prefix_ref, cot_ref, tokens_ref, x_in = take_refs(4)
    saved_in, wholes_in = take_refs(SAVED), take_refs(5)
    gin_ref = take_refs(1)[0]
    out_refs = take_refs(7) if depth else [take_refs(GRADS) for _ in range(LAYERS)]
    (q_ref, key_ref, value_ref, att_ref, lse_ref, middle_ref), (wq, wo, wu, wd, ws) = take_refs(SAVED), take_refs(5)
    (
        x_ref, g_ref, vec, up, mask_ref, second_ref, gd_ref, gs_ref, go_ref, gm_ref, dq_ref, dkey_ref, dvalue_ref,
        gvec_ref, gupb_ref, dk_ref, dv_ref, levels_ref, normed_ref, rims_out, tops_out, low_ref, high_ref, tops_ref,
    ) = take_refs(24)
    index_ref, score_ref, weight_ref, own_ref, back_ref, dscore_ref, coarse_ref = take_refs(7)
    rim_send, rim_recv, copy_sem = take_refs(3)
    model, run = sz.model, sz.run
    half = sz.hidden // 2
    plan, copies = Plan(600e3, 150e3), Copies(copy_sem)
    inside = {"q": q_ref, "key": key_ref, "value": value_ref, "att": att_ref, "lse": lse_ref, "middle": middle_ref,
              "wq": wq, "wo": wo, "wu": wu, "wd": wd, "ws": ws}
    outside = dict(zip(inside, list(saved_in) + list(wholes_in)))

    def load(layer, *names):
        if layer >= 0:
            for name in names:
                copies.start(name, outside[name].at[layer], inside[name])

    load(LAYERS - 1, "middle", "ws", "wu", "wd", "wo", "att", "q", "key", "value", "lse", "wq")
    copies.start("x", x_in, x_ref)
    me, dp = lax.axis_index("seq"), lax.axis_index("dp")
    peers = [((dp, lax.rem(me + k, sz.seq)), None) for k in range(1, sz.seq)]
    scatters = {}
    if depth:
        grads = take_refs(GRADS)
        early = take_refs(EARLY)
        own_grads = lambda layer: (early if layer == 0 else grads[:EARLY]) + grads[EARLY:]
        buffers = [take_refs(SCATTER_BUFFERS) for _ in grads]
        send_sem, recv_sem, free_sem, small_sums = take_refs(4)
        gqkv, gwout, gwup, gwdown = out_refs[:4]
        grid = Grid(depth)
        for layer in reversed(range(LAYERS)):
            sums = [gwup.at[layer, :, 0:half], gwup.at[layer, :, half:], gwdown.at[layer], gwout.at[layer]]
            sums += [gqkv.at[layer, :, k * model : (k + 1) * model] for k in range(3)] + [small_sums.at[layer]]
            scatters[layer] = Scatter(
                grid, plan, own_grads(layer), buffers, sums, send_sem.at[layer], recv_sem.at[layer], free_sem,
                layer < LAYERS - 1, layer > 0,
            )
        peers += [(grid.partner("x"), None)]
        peers += [(grid.at(other, grid.x, grid.y, grid.c), None) for other in scatters[0].others]
    greet(peers)
    fill_mask(sz, mask_ref)
    fill_index(sz, index_ref)
    fill_own(sz, own_ref)
    coarse = coarse_matrix(run)
    rows_of = lambda r: pl.ds(r * run, run)
    per_micro = prefix_ref.shape[0]
    place = me * run + lax.broadcasted_iota(jnp.int32, (run, model), 0)
    for r in range(sz.rows):
        kept = place >= prefix_ref[r % per_micro, r // per_micro]
        g_ref[rows_of(r), :] = jnp.where(kept, cot_ref[r].astype(F32), 0.0)
    all_rims = []
    for layer in reversed(range(LAYERS)):
        gup_a, gup_b, gdown, gout, gq, gk, gv, small_ref = own_grads(layer) if depth else out_refs[layer]

        def launch(*pieces, layer=layer):
            for p in pieces if depth else ():
                begin = functools.partial(scatters[layer].begin, p)
                above = scatters.get(layer + 1)
                if above is None or above.done[p]:
                    begin()
                else:
                    above.next[p] = begin

        def room(*pieces, layer=layer):
            if depth and layer < LAYERS - 1:
                for p in pieces:
                    scatters[layer + 1].need(p)

        gvec_ref[...] = jnp.zeros_like(gvec_ref)
        copies.wait("middle", "ws")
        unpack_small(sz, whole_rows(ws, slice(None)), vec, up)
        load(layer - 1, "ws")
        for r in range(sz.rows):
            rows = rows_of(r)
            hat, _ = normalise(middle_ref[rows, :])
            second_ref[rows, :] = (hat * vec[1:2, :] + vec[6:7, :]).astype(BF16)
            grad = g_ref[rows, :].astype(BF16)
            gd_ref[rows, :] = grad
            gvec_ref[7:8, :] += jnp.sum(grad.astype(F32), axis=0, keepdims=True)
        copies.wait("wu", "wd")
        plan.advance(TIMES["start"])
        parts = sz.hidden // model
        for c in range(parts):
            units = slice(c * model, (c + 1) * model)
            w_up = whole_rows(wu, units)
            hidden = dot_nn(second_ref[...], w_up) + up[:, units]
            active, slope = gelu_both(hidden)
            per = gdown.shape[4]
            store_blocks(gdown, c * model // per, slice(None), dot_tn(active.astype(BF16), gd_ref[...]).astype(BF16))
            grad_hidden = (slope * dot_nt(gd_ref[...], some_rows(wd, c * model, model))).astype(BF16)
            gupb_ref[:, units] = jnp.sum(grad_hidden.astype(F32), axis=0, keepdims=True)
            target, at = (gup_a, gup_b)[c * 2 // parts], c % (parts // 2)
            store_blocks(
                target, 0, slice(at * model, (at + 1) * model), dot_tn(second_ref[...], grad_hidden).astype(BF16)
            )
            back = dot_nt(grad_hidden, w_up)
            if c == 0:
                gs_ref[...] = back
            else:
                gs_ref[...] += back
            if c == parts // 2 - 1:
                launch(0)
            plan.advance(TIMES["back"])
        launch(2, 1)
        load(layer - 1, "wu", "wd")
        copies.wait("wo")
        for r in range(sz.rows):
            rows = rows_of(r)
            hat, inverse = normalise(middle_ref[rows, :])
            grad = gs_ref[rows, :]
            gvec_ref[1:2, :] += jnp.sum(grad * hat, axis=0, keepdims=True)
            gvec_ref[6:7, :] += jnp.sum(grad, axis=0, keepdims=True)
            gm = g_ref[rows, :] + norm_back(grad, hat, inverse, vec[1:2, :])
            gm_ref[rows, :] = gm
            branch = gm.astype(BF16)
            gd_ref[rows, :] = branch
            gvec_ref[5:6, :] += jnp.sum(branch.astype(F32), axis=0, keepdims=True)
            go_ref[r] = dot_nt(branch, whole_rows(wo, slice(None))).astype(BF16)
        plan.advance(TIMES["branch"])
        load(layer - 1, "middle", "wo")
        copies.wait("att", "q", "key", "value", "lse")
        store_blocks(
            gout, 0, slice(None), sum(dot_tn(att_ref[r], gd_ref[rows_of(r), :]) for r in range(sz.rows)).astype(BF16)
        )
        launch(3)
        rims = []
        n = sz.count[TOP]
        for r in range(sz.rows):
            dkey, dvalue = dkey_ref.at[r], dvalue_ref.at[r]
            dkey[...] = jnp.zeros(dkey.shape, F32)
            dvalue[...] = jnp.zeros(dvalue.shape, F32)
            attend_back(
                sz, q_ref.at[r], key_ref.at[r], value_ref.at[r], mask_ref, index_ref, own_ref, lse_ref.at[r],
                go_ref.at[r], dq_ref.at[r], dkey, dvalue, score_ref, back_ref, weight_ref, dscore_ref, coarse_ref,
                functools.partial(plan.advance, TIMES["attend_back"]),
            )
            for kind, bank in ((0, dkey), (1, dvalue)):
                for level in range(TOP):
                    rims_out[layer, r, 0, rim_rows(level, kind), :] = bank[pl.ds(sz.offset[level], BLOCK), :].astype(BF16)
                    rims_out[layer, r, 1, rim_rows(level, kind), :] = bank[
                        pl.ds(sz.offset[level] + BLOCK + sz.count[level], BLOCK), :
                    ].astype(BF16)
            for s in range(sz.seq):
                at = pl.ds(sz.offset[TOP] + s * n, n)
                tops_out[layer, r, s] = jnp.concatenate([dkey[at, :], dvalue[at, :]], axis=0).astype(BF16)
            rims.append(
                Rims(
                    sz, rims_out.at[layer, r, 1], rims_out.at[layer, r, 0], tops_out.at[layer, r], low_ref.at[layer, r],
                    high_ref.at[layer, r], tops_ref.at[layer, r], rim_send.at[layer, r], rim_recv.at[layer, r],
                )
            )
            rims[-1].start()
        all_rims += rims
        load(layer - 1, "att", "q", "key", "value", "lse")
        if layer == LAYERS - 1:
            copies.wait("x")
        layer_input = (lambda r: tokens_ref[r].astype(F32)) if layer == 0 else (lambda r: x_ref[rows_of(r), :])
        for r in range(sz.rows):
            hat, _ = normalise(layer_input(r))
            normed_ref[r] = (hat * vec[0:1, :] + vec[2:3, :]).astype(BF16)
            gvec_ref[3:4, :] += jnp.sum(dq_ref[r].astype(F32), axis=0, keepdims=True)
        room(4)
        store_blocks(gq, 0, slice(None), sum(dot_tn(normed_ref[r], dq_ref[r]) for r in range(sz.rows)).astype(BF16))
        launch(4)
        plan.advance(TIMES["levels"])
        for r in range(sz.rows):
            rims[r].arrive()
            for kind, bank, out in ((0, dkey_ref.at[r], dk_ref), (1, dvalue_ref.at[r], dv_ref)):
                base = 0
                for level in range(LEVELS):
                    n = sz.count[level]
                    if level == TOP:
                        top = sum(tops_ref[layer, r, s, kind * n : kind * n + n, :].astype(F32) for s in range(sz.seq))
                        levels_ref[pl.ds(base, 2 * n), :] = jnp.concatenate(
                            [top, jnp.zeros((n, model), F32)], axis=0
                        ).astype(BF16)
                        continue
                    own = bank[pl.ds(sz.offset[level] + BLOCK, n), :]
                    first = low_ref[layer, r, rim_rows(level, kind), :].astype(F32)
                    final = high_ref[layer, r, rim_rows(level, kind), :].astype(F32)
                    if n == BLOCK:
                        own = own + first + final
                    else:
                        between = [own[BLOCK : n - BLOCK]] if n > 2 * BLOCK else []
                        own = jnp.concatenate([own[:BLOCK] + first, *between, own[n - BLOCK :] + final], axis=0)
                    if level == 0:
                        fine = own
                    else:
                        levels_ref[pl.ds(base, n), :] = own.astype(BF16)
                        base += n
                out[rows_of(r), :] = (fine + dot_tn(coarse, levels_ref[...])).astype(BF16)
            gvec_ref[4:5, :] += jnp.sum(dv_ref[rows_of(r), :].astype(F32), axis=0, keepdims=True)
            plan.advance(TIMES["levels"])
        for k, (out, source) in enumerate(((gk, dk_ref), (gv, dv_ref))):
            room(5 + k)
            store_blocks(
                out, 0, slice(None),
                sum(dot_tn(normed_ref[r], source[rows_of(r), :]) for r in range(sz.rows)).astype(BF16),
            )
            launch(5 + k)
        copies.wait("wq")
        for r in range(sz.rows):
            rows = rows_of(r)
            grad = dot_nt(dq_ref[r], whole_rows(wq, slice(0, model)))
            grad = grad + dot_nt(dk_ref[rows, :], whole_rows(wq, slice(model, 2 * model)))
            grad = grad + dot_nt(dv_ref[rows, :], whole_rows(wq, slice(2 * model, 3 * model)))
            hat, inverse = normalise(layer_input(r))
            gvec_ref[0:1, :] += jnp.sum(grad * hat, axis=0, keepdims=True)
            gvec_ref[2:3, :] += jnp.sum(grad, axis=0, keepdims=True)
            g_ref[rows, :] = gm_ref[rows, :] + norm_back(grad, hat, inverse, vec[0:1, :])
            plan.advance(TIMES["finish"])
        load(layer - 1, "wq")
        if layer == 0:
            copies.start("gin", g_ref, gin_ref)
        room(7)
        for i in range(model // BLOCK):
            top = gvec_ref[:, 128 * (i // 8) : 128 * (i // 8) + 128]
            side = jnp.broadcast_to(gupb_ref[:, 128 * (i // 2) : 128 * (i // 2) + 128], (8, 128))
            store_blocks(small_ref, i, slice(None), jnp.concatenate([top, side], axis=0).astype(BF16))
        launch(7)
    plan.flush()
    if depth:
        for layer in range(LAYERS):
            unpack_share(sz, small_sums[layer], layer, *out_refs[4:7])
    for rim in all_rims:
        rim.drain()
    for scatter in scatters.values():
        scatter.drain()
    copies.drain()


def backward(sz, depth, prefix_len, cotangent, tokens, x, saved, wholes):
    n, rows, run = sz.model, sz.rows, sz.run
    per = sz.hidden * BLOCK // n
    lead = (n // BLOCK // 8, 2, 2, 2)
    half = sz.hidden // 2
    blocks = [(BLOCK, half), (BLOCK, half), (per, n), (BLOCK, n), (BLOCK, n), (BLOCK, n), (BLOCK, n), (BLOCK, 128)]
    pieces = [(lead + block, BF16) for block in blocks]
    outs = [((sz.tokens, n), F32)]
    if depth:
        outs += [((LAYERS,) + shape, F32) for shape in (
            (BLOCK, 3 * n), (BLOCK, n), (BLOCK, sz.hidden), (per, n), (2, BLOCK)
        )]
        outs += [((6, LAYERS, BLOCK), F32), ((LAYERS, per), F32)]
    else:
        outs += pieces * LAYERS
    rim = sz.rim // rows
    scratch = [(array.shape[1:], array.dtype) for array in list(saved) + list(wholes)]
    scratch += [
        ((sz.tokens, n), F32), ((sz.tokens, n), F32), ((8, n), F32), ((1, sz.hidden), F32),
        ((sz.chunks, sz.width, 128), F32), ((sz.tokens, n), BF16),
        ((sz.tokens, n), BF16), ((sz.tokens, n), F32), ((rows, run, n), BF16), ((sz.tokens, n), F32),
        ((rows, run, n), BF16), ((rows, sz.bank, n), F32), ((rows, sz.bank, n), F32), ((8, n), F32),
        ((1, sz.hidden), F32), ((sz.tokens, n), BF16), ((sz.tokens, n), BF16), ((run, n), BF16), ((rows, run, n), BF16),
        ((LAYERS, rows, 2, rim, n), BF16), ((LAYERS, rows, sz.seq, BLOCK, n), BF16), ((LAYERS, rows, rim, n), BF16),
        ((LAYERS, rows, rim, n), BF16), ((LAYERS, rows, sz.seq, BLOCK, n), BF16),
    ]
    scratch += attend_scratch(sz)
    scratch = [pltpu.VMEM(shape, dtype) for shape, dtype in scratch]
    scratch += [pltpu.SemaphoreType.DMA((LAYERS, rows, sz.seq + 1))] * 2
    scratch += [pltpu.SemaphoreType.DMA((LAYERS * (SAVED + 5) + 2,))]
    if depth:
        scratch += [pltpu.VMEM(shape, dtype) for shape, dtype in pieces + pieces[:EARLY]]
        for block in blocks:
            scratch += scatter_buffers(depth, block)
        scratch += [pltpu.SemaphoreType.DMA((LAYERS, GRADS, 2 + depth))] * 2
        scratch += [pltpu.SemaphoreType.REGULAR((GRADS,)), pltpu.VMEM((LAYERS, BLOCK, 128), F32)]
    result = pl.pallas_call(
        functools.partial(backward_kernel, sz, depth),
        out_shape=[jax.ShapeDtypeStruct(shape, dtype) for shape, dtype in outs],
        in_specs=[pl.BlockSpec(memory_space=pltpu.SMEM), WHOLE, WHOLE] + [ANYWHERE] * (1 + SAVED + 5),
        out_specs=[ANYWHERE] + [WHOLE] * (len(outs) - 1),
        scratch_shapes=scratch,
        compiler_params=pltpu.CompilerParams(
            collective_id=1, has_side_effects=True, vmem_limit_bytes=VMEM_LIMIT
        ),
        name="backward",
    )(prefix_len, cotangent, tokens, x, *saved, *wholes)
    return result[0], list(result[1:])


def direct(rows):
    return lax.axis_size("seq") == 4 and lax.axis_size("dp") % 2 == 0 and rows % BLOCK == 0


def pack_small(gains, biases, up_bias):
    layers, _, features = gains.shape
    tiles = features // BLOCK
    vec = jnp.concatenate([gains, biases], axis=1).reshape(layers, 8, tiles, BLOCK).transpose(0, 2, 1, 3)
    vec = jnp.tile(vec, (1, 1, 1, 128 // BLOCK))
    up = up_bias.reshape(layers, tiles, 1, up_bias.shape[1] // tiles)
    up = jnp.broadcast_to(jnp.tile(up, (1, 1, 1, 128 // up.shape[3])), (layers, tiles, 8, 128))
    return jnp.concatenate([vec, up], axis=2).reshape(layers, features, 128)


def whole_weights(w_qkv, w_out, w_up, w_down, gains, biases, up_bias):
    whole = lambda array, axis: lax.all_gather(array, AXES, axis=axis, tiled=True)
    small = pack_small(whole(gains, 2), whole(biases, 2), whole(up_bias, 1))
    tiles = small.shape[1] // BLOCK
    arrays = (whole(w_qkv, 1), whole(w_out, 1), whole(w_up, 1), whole(w_down, 1), small)
    return [
        array.reshape(LAYERS, tiles // 8, 2, 2, 2, array.shape[1] // tiles, array.shape[2]) for array in arrays
    ]


def collect_kernel(count, *refs):
    for source, target in zip(refs[:count], refs[count:]):
        target[...] = source[...]


def collect(*arrays):
    count = len(arrays)
    return pl.pallas_call(
        functools.partial(collect_kernel, count),
        out_shape=[jax.ShapeDtypeStruct(array.shape, array.dtype) for array in arrays],
        in_specs=[WHOLE] * count,
        out_specs=[WHOLE] * count,
        compiler_params=pltpu.CompilerParams(vmem_limit_bytes=VMEM_LIMIT),
        name="collect",
    )(*arrays)


def scatter_by_sums(sz, parts):
    gqkv, gout, gup, small, gdown = parts
    spread = lambda array, axis: lax.psum_scatter(
        array.astype(F32), AXES, scatter_dimension=axis, tiled=True
    )
    tiles = small.reshape(sz.model // BLOCK, BLOCK, 128)
    vec = jnp.concatenate(
        [tiles[i, :8, BLOCK * (i % 8) : BLOCK * (i % 8) + BLOCK] for i in range(sz.model // BLOCK)], axis=1
    )
    wide = sz.hidden * BLOCK // sz.model
    per = 128 // wide
    up = jnp.concatenate(
        [tiles[i, 8, wide * (i % per) : wide * (i % per) + wide] for i in range(sz.model // BLOCK)], axis=0
    )
    vec = spread(vec, 1)
    return spread(gqkv, 0), spread(gout, 0), spread(gup, 0), spread(gdown, 0), vec[:2], vec[2:], spread(up, 0)


def on_device(
    tokens_in, grad_output, prefix_len, w_qkv, w_out, w_up, w_down, norm_gains, bias_rows, up_bias
):
    micro, rows, run, model = tokens_in.shape
    sz = Sizes(micro * rows, run, model, w_up.shape[2], lax.axis_size("seq"))
    depth = lax.axis_size("dp") // 2 if direct(w_qkv.shape[1]) else 0
    if depth:
        weights = (w_qkv, w_out, w_up, w_down, norm_gains, bias_rows.transpose(1, 0, 2), up_bias)
    else:
        weights = whole_weights(w_qkv, w_out, w_up, w_down, norm_gains, bias_rows, up_bias)
    by_row = (sz.rows, run, model)
    out_act, x_one, saved, wholes = forward(sz, depth, tokens_in.reshape(by_row), weights)
    grad, parts = backward(
        sz, depth, prefix_len.T, grad_output.reshape(by_row), tokens_in.reshape(by_row), x_one, saved, wholes
    )
    if depth:
        out_act, grad, *parts = collect(out_act, grad, *parts)
        results = parts[:5] + [parts[5].transpose(1, 0, 2), parts[6]]
    else:
        layers = []
        for layer in range(LAYERS):
            pieces = [piece.reshape(-1, piece.shape[-1]) for piece in parts[GRADS * layer : GRADS * (layer + 1)]]
            up_a, up_b, down, out, dq, dk, dv, small = pieces
            qkv, up = jnp.concatenate([dq, dk, dv], axis=1), jnp.concatenate([up_a, up_b], axis=1)
            layers.append(scatter_by_sums(sz, (qkv, out, up, small, down)))
        results = [jnp.stack([layer[k] for layer in layers], axis=0) for k in range(7)]
    return (out_act.reshape(tokens_in.shape), grad.reshape(tokens_in.shape), *results)


def solution(mesh):
    tokens, shard = P(None, "dp", "seq", None), P(None, AXES, None)
    small, bias = P(None, None, AXES), P(None, AXES)
    return jax.shard_map(
        on_device,
        mesh=mesh,
        in_specs=(tokens, tokens, P(None, "dp"), shard, shard, shard, shard, small, small, bias),
        out_specs=(tokens, tokens, shard, shard, shard, shard, small, small, bias),
        check_vma=False,
    )
```

```python
import functools
import math

import jax
import jax.numpy as jnp
from jax import lax
from jax.experimental import pallas as pl
from jax.experimental.pallas import tpu as pltpu
from jax.sharding import PartitionSpec as P

HDIM = 64
BLOCK = 16
LEVELS = 6
LAYERS = 2
TOP = LEVELS - 1
CHUNK = 64
LN2 = math.log(2.0)
F32 = jnp.float32
BF16 = jnp.bfloat16
NEG = -1e30
VMEM_LIMIT = 62 * 2**20
AXES = ("dp", "seq")


def dot_nn(a, b):
    return lax.dot_general(a, b, (((1,), (0,)), ((), ())), preferred_element_type=F32)


def dot_nt(a, b):
    return lax.dot_general(a, b, (((1,), (1,)), ((), ())), preferred_element_type=F32)


def dot_tn(a, b):
    return lax.dot_general(a, b, (((0,), (0,)), ((), ())), preferred_element_type=F32)


class Sizes:
    def __init__(self, rows, run, model, hidden, seq):
        self.rows, self.run, self.model, self.hidden, self.seq = rows, run, model, hidden, seq
        self.tokens = rows * run
        self.pairs = model // 128
        self.chunks = run // CHUNK
        self.count = [run >> level for level in range(LEVELS)]
        self.top_keys = self.count[TOP] * seq
        self.offset, at = [], 0
        for level in range(TOP):
            self.offset.append(at)
            at += self.count[level] + 2 * BLOCK
        self.offset.append(at)
        self.bank = at + self.top_keys
        self.keys = [CHUNK + 2 * BLOCK, CHUNK // 2 + 2 * BLOCK] + [2 * BLOCK] * (TOP - 2) + [self.top_keys]
        self.start = [sum(self.keys[:level]) for level in range(LEVELS)]
        self.width = sum(self.keys)
        self.rim = rows * TOP * 2 * BLOCK


def normalise(values):
    centred = values - jnp.mean(values, axis=-1, keepdims=True)
    spread = jnp.mean(centred * centred, axis=-1, keepdims=True)
    inverse = lax.rsqrt(spread + 1e-05)
    return centred * inverse, inverse


def norm_back(grad, hat, inverse, gain):
    scaled = grad * gain
    first = jnp.mean(scaled, axis=-1, keepdims=True)
    second = jnp.mean(scaled * hat, axis=-1, keepdims=True)
    return inverse * (scaled - first - hat * second)


GELU_C = math.sqrt(2.0 / math.pi)


def gelu(v):
    return 0.5 * v * (1.0 + jnp.tanh(GELU_C * (v + 0.044715 * (v * v * v))))


def gelu_both(v):
    square = v * v
    t = jnp.tanh(GELU_C * (v + 0.044715 * (square * v)))
    half = 0.5 * (1.0 + t)
    slope = half + 0.5 * v * (1.0 - t * t) * (GELU_C * (1.0 + 3.0 * 0.044715 * square))
    return v * half, slope


def row_loop(total, step, body):
    def go(j, carry):
        body(pl.ds(pl.multiple_of(j * step, step), step))
        return carry

    lax.fori_loop(0, total // step, go, 0)


def coarse_matrix(run):
    row = lax.broadcasted_iota(jnp.int32, (run, run), 0)
    col = lax.broadcasted_iota(jnp.int32, (run, run), 1)
    out = jnp.zeros((run, run), F32)
    base = 0
    for level in range(1, LEVELS):
        n = run >> level
        hit = (row >= base) & (row < base + n) & ((col >> level) == row - base)
        out = jnp.where(hit, 2.0**-level, out)
        base += n
    return out.astype(BF16)


COARSE = [0] + [CHUNK - (CHUNK >> (level - 1)) for level in range(1, LEVELS + 1)]


def chunk_matrix():
    row = lax.broadcasted_iota(jnp.int32, (CHUNK, CHUNK), 0)
    col = lax.broadcasted_iota(jnp.int32, (CHUNK, CHUNK), 1)
    out = jnp.zeros((CHUNK, CHUNK), F32)
    for level in range(1, LEVELS):
        at, end = COARSE[level], COARSE[level + 1]
        out = jnp.where((row >= at) & (row < end) & ((col >> level) == row - at), 2.0**-level, out)
    return out.astype(BF16)


def sum_matrix():
    token = lax.broadcasted_iota(jnp.int32, (128, 128), 0)
    col = lax.broadcasted_iota(jnp.int32, (128, 128), 1)
    place, within = col % CHUNK, token % CHUNK
    out = jnp.zeros((128, 128), F32)
    for level in range(1, LEVELS):
        at, end = COARSE[level], COARSE[level + 1]
        out = jnp.where((place >= at) & (place < end) & ((within >> level) == place - at), 1.0, out)
    return jnp.where(token // CHUNK == col // CHUNK, out, 0.0).astype(BF16)


def fill_index(sz, index_ref):
    lane = lax.broadcasted_iota(jnp.int32, (8, 128), 1)
    for level in range(1, LEVELS):
        value = (lane // CHUNK) * CHUNK + COARSE[level] + ((lane % CHUNK) >> level)
        for k in range(sz.keys[level] // 8):
            index_ref[pl.ds(sz.start[level] - sz.start[1] + 8 * k, 8), :] = value


def fill_own(sz, own_ref):
    place = lax.broadcasted_iota(jnp.int32, (8, 128), 1) % CHUNK
    for level in range(1, LEVELS):
        value = jnp.where((place >= COARSE[level]) & (place < COARSE[level + 1]), 1.0, 0.0)
        for k in range(sz.keys[level] // 8):
            own_ref[pl.ds(sz.start[level] - sz.start[1] + 8 * k, 8), :] = value


def fill_mask(sz, mask_ref):
    place = lax.axis_index("seq")
    for i in range(sz.chunks):
        for level in range(LEVELS):
            shape = (sz.keys[level], 128)
            key = lax.broadcasted_iota(jnp.int32, shape, 0)
            token = lax.broadcasted_iota(jnp.int32, shape, 1) % CHUNK
            per_run = sz.count[level] // BLOCK
            if level == TOP:
                query_block = ((place * sz.run + i * CHUNK + token) >> TOP) // BLOCK
                allowed = jnp.abs(query_block - key // BLOCK) == 1
            else:
                own = (i * CHUNK >> level) // BLOCK
                if level >= 2:
                    key_block = own - 1 + 2 * (key // BLOCK)
                    allowed = key >= 0
                else:
                    key_block = own - 1 + key // BLOCK
                    distance = jnp.abs(key_block - own - (token >> level) // BLOCK)
                    allowed = distance <= 1 if level == 0 else distance == 1
                whole = place * per_run + key_block
                allowed = allowed & (whole >= 0) & (whole < per_run * sz.seq)
            mask_ref[i, pl.ds(sz.start[level], sz.keys[level])] = jnp.where(allowed, level * LN2, NEG)


def key_slices(sz, i, level):
    if level == TOP:
        return [(sz.offset[TOP], sz.top_keys)]
    if level < 2:
        return [(sz.offset[level] + (CHUNK >> level) * i, sz.keys[level])]
    own = (i * CHUNK) // (BLOCK << level)
    return [(sz.offset[level] + BLOCK * own, BLOCK), (sz.offset[level] + BLOCK * (own + 2), BLOCK)]


def take(ref, pieces, lanes):
    parts = [ref[rows_at(at, size), lanes] for at, size in pieces]
    return parts[0] if len(parts) == 1 else jnp.concatenate(parts, axis=0)


def rows_at(at, size):
    return pl.ds(at if isinstance(at, int) else pl.multiple_of(at, BLOCK), size)


def give(ref, pieces, lanes, value):
    done = 0
    for at, size in pieces:
        ref[rows_at(at, size), lanes] += value[done : done + size]
        done += size


def two_heads(block):
    first = lax.broadcasted_iota(jnp.int32, block.shape, 1) < HDIM
    zero = jnp.zeros_like(block)
    return jnp.concatenate([jnp.where(first, block, zero), jnp.where(first, zero, block)], axis=0)


def one_row(block):
    first = lax.broadcasted_iota(jnp.int32, (CHUNK, 128), 1) < HDIM
    return jnp.where(first, block[:CHUNK], block[CHUNK:])


class Units:
    def __init__(self, sz, q_ref, key_ref, value_ref):
        self.sz, self.q_ref, self.key_ref, self.value_ref = sz, q_ref, key_ref, value_ref
        self.all = [(i, pair) for i in range(sz.chunks) for pair in range(sz.pairs)]
        self.pieces = []
        for i in range(sz.chunks):
            levels = [key_slices(sz, i, level) for level in range(LEVELS)]
            self.pieces.append((levels[0], sum(levels[1:], [])))
        matrix = chunk_matrix()
        self.fine = [q_ref[self.tokens(i), :] for i in range(sz.chunks)]
        self.coarse = [dot_nn(matrix, fine).astype(BF16) for fine in self.fine]

    def tokens(self, i):
        return pl.ds(i * CHUNK, CHUNK)

    def lanes(self, pair):
        return slice(128 * pair, 128 * pair + 128)

    def queries(self, i, pair):
        lanes = self.lanes(pair)
        return two_heads(self.fine[i][:, lanes]), two_heads(self.coarse[i][:, lanes])

    def keys(self, i, pair):
        return [take(self.key_ref, pieces, self.lanes(pair)) for pieces in self.pieces[i]]

    def values(self, i, pair):
        return take(self.value_ref, self.pieces[i][0] + self.pieces[i][1], self.lanes(pair))

    def scores(self, u, i, pair, mask_ref, index_ref, out_ref):
        base = self.sz.start[1]
        (fine_keys, coarse_keys), (fine, coarse) = self.keys(i, pair), self.queries(i, pair)
        out_ref[u, :base] = dot_nt(fine_keys, fine) + mask_ref[i, :base]
        upper = jnp.take_along_axis(dot_nt(coarse_keys, coarse), index_ref[...], axis=1)
        out_ref[u, base:] = upper + mask_ref[i, base:]


def attend(sz, q_ref, key_ref, value_ref, mask_ref, index_ref, att_ref, lse_ref, score_ref, weight_ref, pause):
    units = Units(sz, q_ref, key_ref, value_ref)
    for u, (i, pair) in enumerate(units.all):
        units.scores(u, i, pair, mask_ref, index_ref, score_ref)
    pause()
    for u, (i, pair) in enumerate(units.all):
        scores = score_ref[u]
        peak = jnp.max(scores, axis=0, keepdims=True)
        weights = jnp.exp(scores - peak)
        total = jnp.sum(weights, axis=0, keepdims=True)
        lse_ref[i, pair : pair + 1, :] = peak + jnp.log(total)
        weight_ref[u] = (weights * (1.0 / total)).astype(BF16)
    pause()
    for u, (i, pair) in enumerate(units.all):
        mixed = dot_tn(weight_ref[u], units.values(i, pair))
        att_ref[units.tokens(i), units.lanes(pair)] = one_row(mixed).astype(BF16)
    pause()


def attend_back(
    sz, q_ref, key_ref, value_ref, mask_ref, index_ref, own_ref, lse_ref, go_ref, dq_ref, dkey_ref, dvalue_ref,
    score_ref, back_ref, weight_ref, dscore_ref, coarse_ref, pause
):
    units = Units(sz, q_ref, key_ref, value_ref)
    sums, matrix, base = sum_matrix(), chunk_matrix(), sz.start[1]
    for u, (i, pair) in enumerate(units.all):
        units.scores(u, i, pair, mask_ref, index_ref, score_ref)
    pause()
    for u, (i, pair) in enumerate(units.all):
        go = two_heads(go_ref[units.tokens(i), units.lanes(pair)])
        back_ref[u] = dot_nt(units.values(i, pair), go)
    for u, (i, pair) in enumerate(units.all):
        weights = jnp.exp(score_ref[u] - lse_ref[i, pair : pair + 1, :])
        weight_ref[u] = weights.astype(BF16)
        back = back_ref[u]
        inner = jnp.sum(weights * back, axis=0, keepdims=True)
        dscore_ref[u] = (weights * (back - inner)).astype(BF16)
    pause()
    for u, (i, pair) in enumerate(units.all):
        go = two_heads(go_ref[units.tokens(i), units.lanes(pair)])
        give(dvalue_ref, units.pieces[i][0] + units.pieces[i][1], units.lanes(pair), dot_nn(weight_ref[u], go))
    for u, (i, pair) in enumerate(units.all):
        coarse_ref[u] = (dot_nn(dscore_ref[u, base:], sums) * own_ref[...]).astype(BF16)
    pause()
    for u, (i, pair) in enumerate(units.all):
        (first, upper), (fine, coarse) = units.pieces[i], units.queries(i, pair)
        give(dkey_ref, first, units.lanes(pair), dot_nn(dscore_ref[u, :base], fine))
        give(dkey_ref, upper, units.lanes(pair), dot_nn(coarse_ref[u], coarse))
    pause()
    for u, (i, pair) in enumerate(units.all):
        fine_keys, coarse_keys = units.keys(i, pair)
        fine = one_row(dot_tn(dscore_ref[u, :base], fine_keys))
        coarse = one_row(dot_tn(coarse_ref[u], coarse_keys)).astype(BF16)
        dq_ref[units.tokens(i), units.lanes(pair)] = ((fine + dot_tn(matrix, coarse)) * HDIM**-0.5).astype(BF16)
    pause()


def rim_rows(level, kind):
    return pl.ds((level * 2 + kind) * BLOCK, BLOCK)


def unpack_small(sz, small, vec_ref, up_ref):
    lane = lax.broadcasted_iota(jnp.int32, (BLOCK, 128), 1)
    tiles = [small[BLOCK * i : BLOCK * i + BLOCK, :].astype(F32) for i in range(sz.model // BLOCK)]
    for c in range(sz.model // 128):
        total = tiles[8 * c]
        for j in range(1, 8):
            total = jnp.where(lane // 16 == j, tiles[8 * c + j], total)
        vec_ref[:, 128 * c : 128 * c + 128] = total[:8]
    wide = sz.hidden * BLOCK // sz.model
    for c in range(sz.hidden // 128):
        total = tiles[2 * c]
        total = jnp.where(lane >= wide, tiles[2 * c + 1], total)
        up_ref[:, 128 * c : 128 * c + 128] = total[8:9]


def place_rims(sz, low_ref, high_ref, tops_ref, key_ref, value_ref):
    for kind, bank in ((0, key_ref), (1, value_ref)):
        for level in range(TOP):
            bank[pl.ds(sz.offset[level], BLOCK), :] = low_ref[rim_rows(level, kind), :]
            bank[pl.ds(sz.offset[level] + BLOCK + sz.count[level], BLOCK), :] = high_ref[rim_rows(level, kind), :]
        n = sz.count[TOP]
        for s in range(0, sz.seq, 2):
            pair = [tops_ref[s + k, kind * n : kind * n + n, :] for k in range(2)]
            bank[pl.ds(sz.offset[TOP] + s * n, 2 * n), :] = jnp.concatenate(pair, axis=0)


MESH = pl.DeviceIdType.MESH


class Grid:
    def __init__(self, depth):
        dp, seq = lax.axis_index("dp"), lax.axis_index("seq")
        self.depth = depth
        self.z, self.x, self.y, self.c = dp // 2, dp % 2, seq // 2, seq % 2

    def at(self, z, x, y, c):
        return (z * 2 + x, y * 2 + c)

    def index(self, z, x, y, c):
        return z * 8 + x * 4 + y * 2 + c

    def partner(self, axis):
        z, x, y, c = self.z, self.x, self.y, self.c
        return self.at(z, 1 - x if axis == "x" else x, 1 - y if axis == "y" else y, 1 - c if axis == "c" else c)

    def up(self, by):
        return self.at(self.z + by, self.x, self.y, self.c)


def greet(devices):
    barrier = pltpu.get_barrier_semaphore()
    peers = jnp.int32(0)
    for where, condition in devices:
        signal = functools.partial(pl.semaphore_signal, barrier, inc=1, device_id=where, device_id_type=MESH)
        if condition is None:
            signal()
            peers += 1
        else:
            pl.when(condition)(signal)
            peers += condition.astype(jnp.int32)
    pl.semaphore_wait(barrier, peers)


def both(first, second):
    if first is None:
        return second
    return first if second is None else first & second


def when(condition, act):
    if condition is None:
        act()
    else:
        pl.when(condition)(act)


class Plan:
    HOP = 1.5

    def __init__(self, core, links):
        self.rate = {"core": core, "plane": links, "z": links}
        self.now, self.count, self.waiting = 0.0, 0, []
        self.free = dict.fromkeys(self.rate, 0.0)

    def send(self, link, size):
        self.free[link] = max(self.now, self.free[link]) + size / self.rate[link]
        return self.free[link] + self.HOP

    def later(self, ready, act):
        self.count += 1
        self.waiting.append((ready, self.count, act))

    def pop(self):
        first = min(self.waiting, key=lambda entry: entry[:2])
        self.waiting.remove(first)
        self.now = max(self.now, first[0])
        first[2]()

    def advance(self, time):
        self.now += time
        while self.waiting and min(entry[0] for entry in self.waiting) <= self.now:
            self.pop()

    def until(self, done):
        while not done():
            self.pop()

    def flush(self):
        while self.waiting:
            self.pop()


class Gather:
    def __init__(self, grid, plan, pieces, local_sem, send_sem, recv_sem):
        self.grid, self.plan, self.pieces = grid, plan, pieces
        self.local_sem, self.send_sem, self.recv_sem = local_sem, send_sem, recv_sem
        z, x, y, c = grid.z, grid.x, grid.y, grid.c
        self.others = [lax.rem(z + k, grid.depth) for k in range(1, grid.depth)]
        self.one, self.two, self.lines = [], [], []
        for p in range(len(pieces)):
            y_first = (c ^ (FLIP * (p % 2))) == 0
            pick = lambda first, second: jnp.where(y_first, first, second)
            one, two = (pick(x, 1 - x), pick(1 - y, y)), (pick(1 - x, x), pick(y, 1 - y))
            self.one.append(grid.at(z, *one, c))
            self.two.append(grid.at(z, *two, c))
            self.lines.append([(x, y), one, two, (1 - x, 1 - y)])
        self.ids, self.count = [], 0
        for piece in pieces:
            self.ids.append(list(range(self.count, self.count + len(piece))))
            self.count += len(piece)
        self.sends = []
        self.done = [False] * len(pieces)
        self.passed, self.parked = [False] * len(pieces), []

    def size(self, p):
        return sum(2 * share.shape[0] * share.shape[1] for share, _ in self.pieces[p])

    def copy(self, array, source, target, slot, landing, to):
        return pltpu.make_async_remote_copy(
            src_ref=source, dst_ref=target, send_sem=self.send_sem.at[array, slot],
            recv_sem=self.recv_sem.at[array, landing], device_id=to, device_id_type=MESH,
        )

    def begin(self, p):
        grid = self.grid
        for array, (share, whole) in zip(self.ids[p], self.pieces[p]):
            mine = whole.at[grid.z, grid.x, grid.y, grid.c]
            pltpu.make_async_copy(share, mine, self.local_sem.at[array]).start()
            for k, other in enumerate(self.others):
                copy = self.copy(array, share, mine, k, k, grid.at(other, grid.x, grid.y, grid.c))
                copy.start()
                self.sends.append(copy)
        ready = self.plan.send("z", 2 * grid.depth * self.size(p))
        self.plan.later(ready, functools.partial(self.enter, p))

    def enter(self, p):
        if p >= GATE and not self.passed[p - GATE]:
            self.parked.append(p)
        else:
            self.along(p)

    def line(self, p, whole, k):
        xx, yy = self.lines[p][k]
        return whole.at[:, xx, yy, self.grid.c]

    def pass_line(self, p, k, slots, landing):
        xx, yy = self.lines[p][k]
        for array, (_, whole) in zip(self.ids[p], self.pieces[p]):
            line = self.line(p, whole, k)
            for name, slot in slots.items():
                if name == "core":
                    copy = self.copy(array, line, line, slot, 2 + self.grid.depth + xx * 2 + yy, self.grid.partner("c"))
                else:
                    copy = self.copy(array, line, line, slot, landing[name], {"one": self.one[p], "two": self.two[p]}[name])
                copy.start()
                self.sends.append(copy)

    def receive(self, p, landing, k):
        for array, (_, whole) in zip(self.ids[p], self.pieces[p]):
            line = self.line(p, whole, k)
            self.copy(array, line, line, 0, landing, self.one[p]).wait_recv()

    def along(self, p):
        grid, size, plan = self.grid, self.size(p), self.plan
        base = grid.depth - 1
        for array, (share, whole) in zip(self.ids[p], self.pieces[p]):
            mine = whole.at[grid.z, grid.x, grid.y, grid.c]
            pltpu.make_async_copy(share, mine, self.local_sem.at[array]).wait()
            for k in range(grid.depth - 1):
                self.copy(array, share, mine, k, k, self.one[p]).wait_recv()
        self.pass_line(p, 0, {"one": base, "two": base + 1, "core": base + 2}, {"one": base, "two": base + 1})
        line = grid.depth * size
        plan.later(plan.send("plane", line), functools.partial(self.after_one, p))
        plan.later(plan.send("plane", line), functools.partial(self.after_two, p))
        plan.send("core", line)

    def after_one(self, p):
        grid, plan = self.grid, self.plan
        base = grid.depth - 1
        self.receive(p, base, 1)
        self.pass_line(p, 1, {"two": base + 3, "core": base + 4}, {"two": base + 2})
        line = grid.depth * self.size(p)
        plan.later(plan.send("plane", line), functools.partial(self.after_both, p))
        plan.send("core", line)
        self.passed[p] = True
        if p + GATE in self.parked:
            self.parked.remove(p + GATE)
            self.along(p + GATE)

    def after_two(self, p):
        base = self.grid.depth - 1
        self.receive(p, base + 1, 2)
        self.pass_line(p, 2, {"core": base + 5}, {})
        self.plan.send("core", self.grid.depth * self.size(p))

    def after_both(self, p):
        base = self.grid.depth - 1
        self.receive(p, base + 2, 3)
        self.pass_line(p, 3, {"core": base + 6}, {})
        ready = self.plan.send("core", self.grid.depth * self.size(p))
        self.plan.later(ready, functools.partial(self.finish, p))

    def finish(self, p):
        grid = self.grid
        for array, (_, whole) in zip(self.ids[p], self.pieces[p]):
            for xx, yy in self.lines[p]:
                line = whole.at[:, xx, yy, 1 - grid.c]
                self.copy(array, line, line, 0, 2 + grid.depth + xx * 2 + yy, self.one[p]).wait_recv()
        self.done[p] = True

    def begin_flat(self, p, z_time):
        grid = self.grid
        self.passed[p] = True
        for array, (share, whole) in zip(self.ids[p], self.pieces[p]):
            mine = whole.at[grid.z, grid.x, grid.y, grid.c]
            pltpu.make_async_copy(share, mine, self.local_sem.at[array]).start()
            for slot, to in enumerate((self.one[p], self.two[p])):
                self.push(array, share, mine, slot, slot, to)
        ready = self.plan.send("plane", 2 * self.size(p))
        self.plan.later(ready, functools.partial(self.flat_plane, p, z_time))

    def push(self, array, source, target, slot, landing, to):
        copy = self.copy(array, source, target, slot, landing, to)
        copy.start()
        self.sends.append(copy)

    def flat_block(self, p, whole, k):
        xx, yy = self.lines[p][k]
        return whole.at[self.grid.z, xx, yy, self.grid.c]

    def flat_receive(self, p, landing, pick):
        for array, (_, whole) in zip(self.ids[p], self.pieces[p]):
            ref = pick(whole)
            self.copy(array, ref, ref, 0, landing, self.one[p]).wait_recv()

    def flat_plane(self, p, z_time):
        self.flat_receive(p, 0, lambda whole: self.flat_block(p, whole, 1))
        for array, (_, whole) in zip(self.ids[p], self.pieces[p]):
            block = self.flat_block(p, whole, 1)
            self.push(array, block, block, 2, 2, self.two[p])
        ready = self.plan.send("plane", self.size(p))
        self.plan.later(max(ready, z_time), functools.partial(self.flat_along, p))

    def flat_along(self, p):
        grid = self.grid
        self.flat_receive(p, 1, lambda whole: self.flat_block(p, whole, 2))
        self.flat_receive(p, 2, lambda whole: self.flat_block(p, whole, 3))
        for array, (share, whole) in zip(self.ids[p], self.pieces[p]):
            mine = whole.at[grid.z, grid.x, grid.y, grid.c]
            pltpu.make_async_copy(share, mine, self.local_sem.at[array]).wait()
            plane = whole.at[grid.z, :, :, grid.c]
            for k, other in enumerate(self.others):
                self.push(array, plane, plane, 3 + k, 3 + k, grid.at(other, grid.x, grid.y, grid.c))
        ready = self.plan.send("z", 8 * grid.depth * self.size(p))
        self.plan.later(ready, functools.partial(self.flat_core, p))

    def flat_core(self, p):
        grid = self.grid
        for k in range(grid.depth - 1):
            self.flat_receive(p, 3 + k, lambda whole: whole.at[grid.z, :, :, grid.c])
        for array, (_, whole) in zip(self.ids[p], self.pieces[p]):
            mine = whole.at[:, :, :, grid.c]
            self.push(array, mine, mine, 2 + grid.depth, 2 + grid.depth, grid.partner("c"))
        ready = self.plan.send("core", 4 * grid.depth * self.size(p))
        self.plan.later(ready, functools.partial(self.flat_finish, p))

    def flat_finish(self, p):
        self.flat_receive(p, 2 + self.grid.depth, lambda whole: whole.at[:, :, :, 1 - self.grid.c])
        self.done[p] = True

    def need(self, p):
        self.plan.until(lambda: self.done[p])

    def drain(self):
        for copy in self.sends:
            copy.wait_send()


class Scatter:
    def __init__(self, grid, plan, pieces, buffers, sums, send_sem, recv_sem, free_sem, again, more):
        self.grid, self.plan, self.pieces, self.buffers, self.sums = grid, plan, pieces, buffers, sums
        self.free_sem, self.again, self.more = free_sem, again, more
        self.next = {}
        self.done = [False] * len(pieces)
        self.send_sem, self.recv_sem = send_sem, recv_sem
        self.copies = [[] for _ in pieces]
        z, x, y, c = grid.z, grid.x, grid.y, grid.c
        self.others = [lax.rem(z + k, grid.depth) for k in range(1, grid.depth)]
        self.x_first = [(c ^ (FLIP * (p % 2))) == 0 for p in range(len(pieces))]
        pick = lambda p, first, second: jnp.where(self.x_first[p], first, second)
        self.one = [grid.at(z, pick(p, 1 - x, x), pick(p, y, 1 - y), c) for p in range(len(pieces))]
        self.two = [grid.at(z, pick(p, x, 1 - x), pick(p, 1 - y, y), c) for p in range(len(pieces))]
        self.mine = [(pick(p, x, y), pick(p, y, x)) for p in range(len(pieces))]

    def move(self, p, source, target, to):
        stage = len(self.copies[p])
        copy = pltpu.make_async_remote_copy(
            src_ref=source, dst_ref=target, send_sem=self.send_sem.at[p, stage], recv_sem=self.recv_sem.at[p, stage],
            device_id=to, device_id_type=MESH,
        )
        copy.start()
        self.copies[p].append(copy)

    def step(self, link, blocks, p, act):
        piece = self.pieces[p]
        ready = self.plan.send(link, 2 * blocks * piece.shape[4] * piece.shape[5])
        self.plan.later(ready, functools.partial(act, p))

    def senders(self):
        grid = self.grid
        along = [grid.at(other, grid.x, grid.y, grid.c) for other in self.others]
        return [grid.partner("c"), grid.partner("x"), grid.partner("y")] + along

    def begin(self, p):
        if self.again:
            pl.semaphore_wait(self.free_sem.at[p], len(self.senders()))
        self.move(p, self.pieces[p].at[:, :, :, 1 - self.grid.c], self.buffers[p][0], self.grid.partner("c"))
        self.step("core", 4 * self.grid.depth, p, self.flat_along if p in FLAT_SUMS else self.first)

    def place(self, p, one, two):
        return jnp.where(self.x_first[p], one, two), jnp.where(self.x_first[p], two, one)

    def first(self, p):
        grid = self.grid
        piece, (from_core, to_one, from_one) = self.pieces[p], self.buffers[p][:3]
        self.copies[p][0].wait_recv()
        for zz in range(grid.depth):
            for two in range(2):
                xx, yy = self.place(p, 1 - self.mine[p][0], two)
                total = piece[zz, xx, yy, grid.c].astype(F32) + from_core[zz, xx, yy].astype(F32)
                to_one[zz, two] = total.astype(BF16)
        self.move(p, to_one, from_one, self.one[p])
        self.step("plane", 2 * grid.depth, p, self.second)

    def second(self, p):
        grid = self.grid
        piece, (from_core, _, from_one, to_two, from_two) = self.pieces[p], self.buffers[p][:5]
        self.copies[p][1].wait_recv()
        other = 1 - self.mine[p][1]
        xx, yy = self.place(p, self.mine[p][0], other)
        for zz in range(grid.depth):
            total = piece[zz, xx, yy, grid.c].astype(F32) + from_core[zz, xx, yy].astype(F32)
            to_two[zz] = (total + from_one[zz, other].astype(F32)).astype(BF16)
        self.move(p, to_two, from_two, self.two[p])
        self.step("plane", grid.depth, p, self.along)

    def along(self, p):
        grid = self.grid
        piece, (from_core, _, from_one, _, from_two, ready, from_z) = self.pieces[p], self.buffers[p]
        self.copies[p][2].wait_recv()
        for zz in range(grid.depth):
            total = piece[zz, grid.x, grid.y, grid.c].astype(F32) + from_core[zz, grid.x, grid.y].astype(F32)
            total = total + from_one[zz, self.mine[p][1]].astype(F32) + from_two[zz].astype(F32)
            ready[zz] = total.astype(BF16)
        for k, other in enumerate(self.others):
            self.move(p, ready.at[other], from_z.at[k], grid.at(other, grid.x, grid.y, grid.c))
        self.step("z", 2 * grid.depth, p, self.finish)

    def flat_total(self, p, xx, yy):
        grid = self.grid
        from_core, _, from_z = self.buffers[p][:3]
        total = self.pieces[p][grid.z, xx, yy, grid.c].astype(F32) + from_core[grid.z, xx, yy].astype(F32)
        for k in range(grid.depth - 1):
            total = total + from_z[k, xx, yy].astype(F32)
        return total

    def flat_along(self, p):
        grid = self.grid
        piece, (from_core, to_z, from_z) = self.pieces[p], self.buffers[p][:3]
        self.copies[p][0].wait_recv()
        for k, other in enumerate(self.others):
            for xx in range(2):
                for yy in range(2):
                    total = piece[other, xx, yy, grid.c].astype(F32) + from_core[other, xx, yy].astype(F32)
                    to_z[k, xx, yy] = total.astype(BF16)
            self.move(p, to_z.at[k], from_z.at[k], grid.at(other, grid.x, grid.y, grid.c))
        self.step("z", 8 * grid.depth, p, self.flat_first)

    def flat_first(self, p):
        to_one, from_one = self.buffers[p][3:5]
        for k in range(self.grid.depth - 1):
            self.copies[p][1 + k].wait_recv()
        for two in range(2):
            to_one[two] = self.flat_total(p, *self.place(p, 1 - self.mine[p][0], two)).astype(BF16)
        self.move(p, to_one, from_one, self.one[p])
        self.step("plane", 2, p, self.flat_second)

    def flat_second(self, p):
        from_one, to_two, from_two = self.buffers[p][4:7]
        self.copies[p][self.grid.depth].wait_recv()
        other = 1 - self.mine[p][1]
        total = self.flat_total(p, *self.place(p, self.mine[p][0], other)) + from_one[other].astype(F32)
        to_two[...] = total.astype(BF16)
        self.move(p, to_two, from_two, self.two[p])
        self.step("plane", 1, p, self.finish)

    def finish(self, p):
        if p in FLAT_SUMS:
            from_one, _, from_two = self.buffers[p][4:7]
            self.copies[p][self.grid.depth + 1].wait_recv()
            total = self.flat_total(p, self.grid.x, self.grid.y) + from_one[self.mine[p][1]].astype(F32)
            self.close(p, total + from_two[...].astype(F32))
            return
        ready, from_z = self.buffers[p][5:7]
        total = ready[self.grid.z].astype(F32)
        for k in range(self.grid.depth - 1):
            self.copies[p][3 + k].wait_recv()
            total = total + from_z[k].astype(F32)
        self.close(p, total)

    def close(self, p, total):
        self.sums[p][...] = total
        if self.more:
            for copy in self.copies[p]:
                copy.wait_send()
            for device in self.senders():
                pl.semaphore_signal(self.free_sem.at[p], inc=1, device_id=device, device_id_type=MESH)
        self.done[p] = True
        if p in self.next:
            self.next.pop(p)()

    def need(self, p):
        self.plan.until(lambda: self.done[p])

    def drain(self):
        for copies in self.copies:
            for copy in copies if not self.more else []:
                copy.wait_send()


FLIP = 1
GATE = 2
FLAT = 5
FLAT_SUMS = (3, 4)
SCATTER_BUFFERS = 7


def scatter_buffers(depth, block, flat):
    leads = ((depth, 2, 2), (depth, 2), (depth, 2), (depth,), (depth,), (depth,), (depth - 1,))
    if flat:
        leads = ((depth, 2, 2), (depth - 1, 2, 2), (depth - 1, 2, 2), (2,), (2,), (), ())
    return [pltpu.VMEM(lead + tuple(block), BF16) for lead in leads]


class Rims:
    def __init__(self, sz, ahead, behind, tops, low, high, all_tops, send_sem, recv_sem):
        self.sz, self.low, self.high, self.all_tops, self.tops = sz, low, high, all_tops, tops
        self.me, self.dp = lax.axis_index("seq"), lax.axis_index("dp")
        me, dp, seq = self.me, self.dp, sz.seq
        make = lambda source, target, k, to: pltpu.make_async_remote_copy(
            src_ref=source, dst_ref=target, send_sem=send_sem.at[k], recv_sem=recv_sem.at[k],
            device_id=(dp, to), device_id_type=MESH,
        )
        self.ahead = lambda: make(ahead, low, 0, me + 1)
        self.behind = lambda: make(behind, high, 1, me - 1)
        self.rest = []
        for k in range(1, seq):
            other = lax.rem(me + k, seq)
            source = tops.at[0] if tops.shape[0] == 1 else tops.at[other]
            self.rest.append(make(source, all_tops.at[me], 1 + k, other))

    def start(self):
        when(self.me + 1 < self.sz.seq, lambda: self.ahead().start())
        when(self.me > 0, lambda: self.behind().start())
        for copy in self.rest:
            copy.start()
        self.all_tops[self.me] = self.tops[0] if self.tops.shape[0] == 1 else self.tops[self.me]

        def no_low():
            self.low[...] = jnp.zeros_like(self.low)

        def no_high():
            self.high[...] = jnp.zeros_like(self.high)

        when(self.me == 0, no_low)
        when(self.me == self.sz.seq - 1, no_high)

    def arrive(self):
        when(self.me > 0, lambda: self.ahead().wait_recv())
        when(self.me + 1 < self.sz.seq, lambda: self.behind().wait_recv())
        for copy in self.rest:
            copy.wait_recv()

    def drain(self):
        when(self.me + 1 < self.sz.seq, lambda: self.ahead().wait_send())
        when(self.me > 0, lambda: self.behind().wait_send())
        for copy in self.rest:
            copy.wait_send()


class Copies:
    def __init__(self, sem):
        self.sem, self.open, self.count = sem, {}, 0

    def start(self, name, source, target):
        copy = pltpu.make_async_copy(source, target, self.sem.at[self.count])
        self.count += 1
        copy.start()
        self.open[name] = copy

    def wait(self, *names):
        for name in names:
            if name in self.open:
                self.open.pop(name).wait()

    def drain(self):
        self.wait(*list(self.open))


def whole_rows(ref, columns):
    value = ref[:, :, :, :, :, columns]
    return value.reshape(-1, value.shape[-1])


def some_rows(ref, at, rows):
    per = ref.shape[4]
    blocks = [ref[i // 8, (i // 4) % 2, (i // 2) % 2, i % 2] for i in range(at // per, (at + rows) // per)]
    return jnp.concatenate(blocks, axis=0)


def make_share(sz, gains, biases_ref, layer, up, wide_ref, share_ref):
    wide = up.shape[-1]
    wide_ref[...] = jnp.zeros_like(wide_ref)
    wide_ref[0:2, 0:BLOCK] = gains.astype(F32)
    for k in range(6):
        wide_ref[2 + k : 3 + k, 0:BLOCK] = biases_ref[k, layer : layer + 1, :].astype(F32)
    wide_ref[8:16, 0:wide] = jnp.broadcast_to(up.astype(F32), (8, wide))
    row = lax.broadcasted_iota(jnp.int32, (128, 128), 0)
    lane = lax.broadcasted_iota(jnp.int32, (128, 128), 1)
    top = jnp.where((row < BLOCK) & (lane % BLOCK == row), 1.0, 0.0).astype(BF16)
    low = jnp.where((row < wide) & (lane % wide == row), 1.0, 0.0).astype(BF16)
    values = wide_ref[...].astype(BF16)
    share_ref[...] = jnp.concatenate([dot_nn(values, top)[:8], dot_nn(values, low)[8:]], axis=0).astype(BF16)


SAVED = 6
TIMES = {"before": 2.2, "attend": 0.8, "project": 1.0, "forward": 1.4, "start": 1.5, "back": 1.9, "branch": 2.0, "attend_back": 0.6,
         "levels": 1.0, "finish": 1.2}


def forward_kernel(sz, depth, *refs):
    refs = list(refs)
    take_refs = lambda n: [refs.pop(0) for _ in range(n)]
    tokens_ref = take_refs(1)[0]
    if depth:
        shares, (gains_ref, biases_ref, upb_ref) = take_refs(4), take_refs(3)
    else:
        wholes = take_refs(5)
    out_act_ref, x_out = take_refs(2)
    saved_out = take_refs(SAVED)
    if depth:
        wholes_out, wholes = take_refs(5), take_refs(5)
    q_ref, key_ref, value_ref, att_ref, lse_ref, middle_ref = take_refs(SAVED)
    x_ref, vec, up, mask_ref, second_ref, state_ref = take_refs(6)
    index_ref, score_ref, weight_ref = take_refs(3)
    rims_out, tops_out, low_ref, high_ref, tops_ref, rim_send, rim_recv, copy_sem = take_refs(8)
    model, run = sz.model, sz.run
    wq, wo, wu, wd, ws = wholes
    plan, copies = Plan(450e3, 110e3), Copies(copy_sem)
    me, dp = lax.axis_index("seq"), lax.axis_index("dp")
    peers = [((dp, lax.rem(me + k, sz.seq)), None) for k in range(1, sz.seq)]
    if depth:
        wide_ref, share_ref, local_sem, send_sem, recv_sem = take_refs(5)
        grid = Grid(depth)
        half = sz.hidden // 2
        pieces = []
        for layer in range(LAYERS):
            part = lambda k, columns: (shares[k].at[layer, :, columns], wholes[k].at[layer, :, :, :, :, :, columns])
            pieces.append([part(0, slice(None)), (share_ref.at[layer], ws.at[layer])])
            pieces.append([part(1, slice(None)), part(2, slice(0, half))])
            pieces.append([part(2, slice(half, None))])
            pieces.append([part(3, slice(None))])
        gather = Gather(grid, plan, pieces, local_sem, send_sem, recv_sem)
        peers += [(grid.partner("x"), None)] + [(grid.at(other, grid.x, grid.y, grid.c), None) for other in gather.others]
        greet(peers)
        for layer in range(LAYERS):
            make_share(
                sz, gains_ref[layer], biases_ref, layer, upb_ref[layer : layer + 1, :], wide_ref, share_ref.at[layer]
            )
        gather.begin(0)
        for p in range(1, 4):
            plan.later(3.0 + 3.0 * p, functools.partial(gather.begin, p))
        for p in range(4, 8):
            if p == FLAT:
                plan.later(1.0, functools.partial(gather.begin_flat, p, 24.0))
            else:
                plan.later(14.0 + 3.0 * (p - 4), functools.partial(gather.begin, p))

        def need(layer, k):
            gather.need(4 * layer + k)

        def keep(layer):
            for k in range(5):
                copies.start(("weights", layer, k), wholes[k].at[layer], wholes_out[k].at[layer])
    else:
        greet(peers)
        need = lambda layer, k: None
        keep = lambda layer: None

    def save(k, layer):
        source = (q_ref, key_ref, value_ref, att_ref, lse_ref, middle_ref)[k]
        copies.start(("saved", k, layer), source.at[layer], saved_out[k].at[layer])

    fill_mask(sz, mask_ref)
    fill_index(sz, index_ref)
    coarse = coarse_matrix(run)
    rows_of = lambda r: pl.ds(r * run, run)
    for r in range(sz.rows):
        state_ref[rows_of(r), :] = tokens_ref[r].astype(F32)
    all_rims = []
    for layer in range(LAYERS):
        need(layer, 0)
        unpack_small(sz, whole_rows(ws.at[layer], slice(None)), vec, up)
        rims = []
        for r in range(sz.rows):
            hat, _ = normalise(state_ref[rows_of(r), :])
            normed = (hat * vec[0:1, :] + vec[2:3, :]).astype(BF16)
            tops = []
            for kind, bank in ((0, key_ref.at[layer, r]), (1, value_ref.at[layer, r])):
                mixed = dot_nn(normed, whole_rows(wq.at[layer], slice((1 + kind) * model, (2 + kind) * model)))
                if kind == 1:
                    mixed = mixed + vec[4:5, :]
                mixed = mixed.astype(BF16)
                levels = dot_nn(coarse, mixed).astype(BF16)
                base = 0
                for level in range(LEVELS):
                    n = sz.count[level]
                    if level == 0:
                        now = mixed
                    else:
                        now = levels[base : base + n]
                        base += n
                    if level < TOP:
                        bank[pl.ds(sz.offset[level] + BLOCK, n), :] = now
                        rims_out[layer, r, 0, rim_rows(level, kind), :] = now[n - BLOCK :]
                        rims_out[layer, r, 1, rim_rows(level, kind), :] = now[:BLOCK]
                    else:
                        tops.append(now)
            tops_out[layer, r, 0] = jnp.concatenate(tops, axis=0)
            rims.append(
                Rims(
                    sz, rims_out.at[layer, r, 0], rims_out.at[layer, r, 1], tops_out.at[layer, r], low_ref.at[layer, r],
                    high_ref.at[layer, r], tops_ref.at[layer, r], rim_send.at[layer, r], rim_recv.at[layer, r],
                )
            )
            rims[-1].start()
            queries = (dot_nn(normed, whole_rows(wq.at[layer], slice(0, model))) + vec[3:4, :]).astype(BF16)
            q_ref[layer, r] = queries * jnp.asarray(HDIM**-0.5, BF16)
            plan.advance(TIMES["before"])
        save(0, layer)
        all_rims += rims
        for r in range(sz.rows):
            rims[r].arrive()
            place_rims(
                sz, low_ref.at[layer, r], high_ref.at[layer, r], tops_ref.at[layer, r], key_ref.at[layer, r],
                value_ref.at[layer, r],
            )
            attend(
                sz, q_ref.at[layer, r], key_ref.at[layer, r], value_ref.at[layer, r], mask_ref, index_ref,
                att_ref.at[layer, r], lse_ref.at[layer, r], score_ref, weight_ref,
                functools.partial(plan.advance, TIMES["attend"]),
            )
        for k in (1, 2, 3, 4):
            save(k, layer)
        need(layer, 1)
        for r in range(sz.rows):
            rows = rows_of(r)
            middle = state_ref[rows, :] + dot_nn(att_ref[layer, r], whole_rows(wo.at[layer], slice(None))) + vec[5:6, :]
            middle_ref[layer, rows, :] = middle
            hat, _ = normalise(middle)
            second_ref[rows, :] = (hat * vec[1:2, :] + vec[6:7, :]).astype(BF16)
            state_ref[rows, :] = middle + vec[7:8, :]
            plan.advance(TIMES["project"])
        save(5, layer)
        need(layer, 3)
        parts = sz.hidden // model
        for c in range(parts):
            if c == parts // 2:
                need(layer, 2)
            units = slice(c * model, (c + 1) * model)
            for r in range(sz.rows):
                rows = rows_of(r)
                hidden = dot_nn(second_ref[rows, :], whole_rows(wu.at[layer], units)) + up[:, units]
                state_ref[rows, :] += dot_nn(gelu(hidden).astype(BF16), some_rows(wd.at[layer], c * model, model))
            plan.advance(TIMES["forward"])
        keep(layer)
        if layer == 0:
            x_ref[...] = state_ref[...]
            copies.start("x", x_ref, x_out)
        else:
            for r in range(sz.rows):
                out_act_ref[r] = state_ref[rows_of(r), :].astype(BF16)
    plan.flush()
    for rims in all_rims:
        rims.drain()
    if depth:
        gather.drain()
    copies.drain()


WHOLE = pl.BlockSpec(memory_space=pltpu.VMEM)
ANYWHERE = pl.BlockSpec(memory_space=pl.ANY)


def attend_scratch(sz):
    units = sz.chunks * sz.pairs
    coarse = sz.width - sz.start[1]
    wide = ((units, sz.width, 128), F32)
    return [
        ((coarse, 128), jnp.int32), wide, (wide[0], BF16), ((coarse, 128), F32), wide, (wide[0], BF16),
        ((units, coarse, 128), BF16),
    ]


def forward(sz, depth, tokens, weights):
    n, rows, run = sz.model, sz.rows, sz.run
    saved = [
        ((LAYERS, rows, run, n), BF16), ((LAYERS, rows, sz.bank, n), BF16), ((LAYERS, rows, sz.bank, n), BF16),
        ((LAYERS, rows, run, n), BF16), ((LAYERS, rows, sz.chunks, sz.pairs, 128), F32), ((LAYERS, sz.tokens, n), F32),
    ]
    outs = [((rows, run, n), BF16), ((sz.tokens, n), F32)] + saved
    out_specs = [WHOLE] + [ANYWHERE] * (1 + SAVED)
    scratch = []
    if depth:
        full = [((LAYERS, depth, 2, 2, 2) + share.shape[1:], BF16) for share in weights[:4]]
        full.append(((LAYERS, depth, 2, 2, 2, BLOCK, 128), BF16))
        outs += full
        out_specs += [ANYWHERE] * 5
        scratch += full
    rim = sz.rim // rows
    scratch += saved + [
        ((sz.tokens, n), F32), ((8, n), F32), ((1, sz.hidden), F32), ((sz.chunks, sz.width, 128), F32),
        ((sz.tokens, n), BF16), ((sz.tokens, n), F32)] + attend_scratch(sz)[:3] + [((LAYERS, rows, 2, rim, n), BF16),
        ((LAYERS, rows, 1, BLOCK, n), BF16), ((LAYERS, rows, rim, n), BF16), ((LAYERS, rows, rim, n), BF16),
        ((LAYERS, rows, sz.seq, BLOCK, n), BF16),
    ]
    scratch = [pltpu.VMEM(shape, dtype) for shape, dtype in scratch]
    scratch += [pltpu.SemaphoreType.DMA((LAYERS, rows, sz.seq + 1))] * 2
    scratch += [pltpu.SemaphoreType.DMA((LAYERS * (SAVED + 5) + 1,))]
    if depth:
        arrays = 6 * LAYERS
        scratch += [pltpu.VMEM((BLOCK, 128), F32), pltpu.VMEM((LAYERS, BLOCK, 128), BF16)]
        scratch += [pltpu.SemaphoreType.DMA((arrays,))] + [pltpu.SemaphoreType.DMA((arrays, depth + 6))] * 2
    results = pl.pallas_call(
        functools.partial(forward_kernel, sz, depth),
        out_shape=[jax.ShapeDtypeStruct(shape, dtype) for shape, dtype in outs],
        in_specs=[WHOLE] * (1 + len(weights)),
        out_specs=out_specs,
        scratch_shapes=scratch,
        compiler_params=pltpu.CompilerParams(
            collective_id=0, has_side_effects=True, vmem_limit_bytes=VMEM_LIMIT
        ),
        name="forward",
    )(tokens, *weights)
    return results[0], results[1], results[2 : 2 + SAVED], (results[2 + SAVED :] if depth else weights)


def store_blocks(ref, at, columns, value):
    per = ref.shape[4]
    for k in range(value.shape[0] // per):
        i = at + k
        ref[i // 8, (i // 4) % 2, (i // 2) % 2, i % 2, :, columns] = value[k * per : (k + 1) * per]


def unpack_share(sz, small, layer, gains_ref, biases_ref, up_ref):
    place = lax.axis_index("dp") * lax.axis_size("seq") + lax.axis_index("seq")
    wide = up_ref.shape[-1]
    vec, up = small[0:8, 0:BLOCK], small[8:9, 0:wide]
    for j in range(1, 128 // BLOCK):
        vec = jnp.where(place % (128 // BLOCK) == j, small[0:8, j * BLOCK : (j + 1) * BLOCK], vec)
    for j in range(1, 128 // wide):
        up = jnp.where(place % (128 // wide) == j, small[8:9, j * wide : (j + 1) * wide], up)
    gains_ref[layer] = vec[0:2]
    for k in range(6):
        biases_ref[k, layer : layer + 1, :] = vec[2 + k : 3 + k]
    up_ref[layer : layer + 1, :] = up


GRADS = 8
EARLY = 4


def backward_kernel(sz, depth, *refs):
    refs = list(refs)
    take_refs = lambda n: [refs.pop(0) for _ in range(n)]
    prefix_ref, cot_ref, tokens_ref, x_in = take_refs(4)
    saved_in, wholes_in = take_refs(SAVED), take_refs(5)
    gin_ref = take_refs(1)[0]
    out_refs = take_refs(7) if depth else [take_refs(GRADS) for _ in range(LAYERS)]
    (q_ref, key_ref, value_ref, att_ref, lse_ref, middle_ref), (wq, wo, wu, wd, ws) = take_refs(SAVED), take_refs(5)
    (
        x_ref, g_ref, vec, up, mask_ref, second_ref, gd_ref, gs_ref, go_ref, gm_ref, dq_ref, dkey_ref, dvalue_ref,
        gvec_ref, gupb_ref, dk_ref, dv_ref, levels_ref, normed_ref, rims_out, tops_out, low_ref, high_ref, tops_ref,
    ) = take_refs(24)
    index_ref, score_ref, weight_ref, own_ref, back_ref, dscore_ref, coarse_ref = take_refs(7)
    rim_send, rim_recv, copy_sem = take_refs(3)
    model, run = sz.model, sz.run
    half = sz.hidden // 2
    plan, copies = Plan(600e3, 150e3), Copies(copy_sem)
    inside = {"q": q_ref, "key": key_ref, "value": value_ref, "att": att_ref, "lse": lse_ref, "middle": middle_ref,
              "wq": wq, "wo": wo, "wu": wu, "wd": wd, "ws": ws}
    outside = dict(zip(inside, list(saved_in) + list(wholes_in)))

    def load(layer, *names):
        if layer >= 0:
            for name in names:
                copies.start(name, outside[name].at[layer], inside[name])

    load(LAYERS - 1, "middle", "ws", "wu", "wd", "wo", "att", "q", "key", "value", "lse", "wq")
    copies.start("x", x_in, x_ref)
    me, dp = lax.axis_index("seq"), lax.axis_index("dp")
    peers = [((dp, lax.rem(me + k, sz.seq)), None) for k in range(1, sz.seq)]
    scatters = {}
    if depth:
        grads = take_refs(GRADS)
        early = take_refs(EARLY)
        own_grads = lambda layer: (early if layer == 0 else grads[:EARLY]) + grads[EARLY:]
        buffers = [take_refs(SCATTER_BUFFERS) for _ in grads]
        send_sem, recv_sem, free_sem, small_sums = take_refs(4)
        gqkv, gwout, gwup, gwdown = out_refs[:4]
        grid = Grid(depth)
        for layer in reversed(range(LAYERS)):
            sums = [gwup.at[layer, :, 0:half], gwup.at[layer, :, half:], gwdown.at[layer], gwout.at[layer]]
            sums += [gqkv.at[layer, :, k * model : (k + 1) * model] for k in range(3)] + [small_sums.at[layer]]
            scatters[layer] = Scatter(
                grid, plan, own_grads(layer), buffers, sums, send_sem.at[layer], recv_sem.at[layer], free_sem,
                layer < LAYERS - 1, layer > 0,
            )
        peers += [(grid.partner("x"), None)]
        peers += [(grid.at(other, grid.x, grid.y, grid.c), None) for other in scatters[0].others]
    greet(peers)
    fill_mask(sz, mask_ref)
    fill_index(sz, index_ref)
    fill_own(sz, own_ref)
    coarse = coarse_matrix(run)
    rows_of = lambda r: pl.ds(r * run, run)
    per_micro = prefix_ref.shape[0]
    place = me * run + lax.broadcasted_iota(jnp.int32, (run, model), 0)
    for r in range(sz.rows):
        kept = place >= prefix_ref[r % per_micro, r // per_micro]
        g_ref[rows_of(r), :] = jnp.where(kept, cot_ref[r].astype(F32), 0.0)
    all_rims = []
    for layer in reversed(range(LAYERS)):
        gup_a, gup_b, gdown, gout, gq, gk, gv, small_ref = own_grads(layer) if depth else out_refs[layer]

        def launch(*pieces, layer=layer):
            for p in pieces if depth else ():
                begin = functools.partial(scatters[layer].begin, p)
                above = scatters.get(layer + 1)
                if above is None or above.done[p]:
                    begin()
                else:
                    above.next[p] = begin

        def room(*pieces, layer=layer):
            if depth and layer < LAYERS - 1:
                for p in pieces:
                    scatters[layer + 1].need(p)

        gvec_ref[...] = jnp.zeros_like(gvec_ref)
        copies.wait("middle", "ws")
        unpack_small(sz, whole_rows(ws, slice(None)), vec, up)
        load(layer - 1, "ws")
        for r in range(sz.rows):
            rows = rows_of(r)
            hat, _ = normalise(middle_ref[rows, :])
            second_ref[rows, :] = (hat * vec[1:2, :] + vec[6:7, :]).astype(BF16)
            grad = g_ref[rows, :].astype(BF16)
            gd_ref[rows, :] = grad
            gvec_ref[7:8, :] += jnp.sum(grad.astype(F32), axis=0, keepdims=True)
        copies.wait("wu", "wd")
        plan.advance(TIMES["start"])
        parts = sz.hidden // model
        for c in range(parts):
            units = slice(c * model, (c + 1) * model)
            w_up = whole_rows(wu, units)
            hidden = dot_nn(second_ref[...], w_up) + up[:, units]
            active, slope = gelu_both(hidden)
            per = gdown.shape[4]
            store_blocks(gdown, c * model // per, slice(None), dot_tn(active.astype(BF16), gd_ref[...]).astype(BF16))
            grad_hidden = (slope * dot_nt(gd_ref[...], some_rows(wd, c * model, model))).astype(BF16)
            gupb_ref[:, units] = jnp.sum(grad_hidden.astype(F32), axis=0, keepdims=True)
            target, at = (gup_a, gup_b)[c * 2 // parts], c % (parts // 2)
            store_blocks(
                target, 0, slice(at * model, (at + 1) * model), dot_tn(second_ref[...], grad_hidden).astype(BF16)
            )
            back = dot_nt(grad_hidden, w_up)
            if c == 0:
                gs_ref[...] = back
            else:
                gs_ref[...] += back
            if c == parts // 2 - 1:
                launch(0)
            plan.advance(TIMES["back"])
        launch(2, 1)
        load(layer - 1, "wu", "wd")
        copies.wait("wo")
        for r in range(sz.rows):
            rows = rows_of(r)
            hat, inverse = normalise(middle_ref[rows, :])
            grad = gs_ref[rows, :]
            gvec_ref[1:2, :] += jnp.sum(grad * hat, axis=0, keepdims=True)
            gvec_ref[6:7, :] += jnp.sum(grad, axis=0, keepdims=True)
            gm = g_ref[rows, :] + norm_back(grad, hat, inverse, vec[1:2, :])
            gm_ref[rows, :] = gm
            branch = gm.astype(BF16)
            gd_ref[rows, :] = branch
            gvec_ref[5:6, :] += jnp.sum(branch.astype(F32), axis=0, keepdims=True)
            go_ref[r] = dot_nt(branch, whole_rows(wo, slice(None))).astype(BF16)
        plan.advance(TIMES["branch"])
        load(layer - 1, "middle", "wo")
        copies.wait("att", "q", "key", "value", "lse")
        store_blocks(
            gout, 0, slice(None), sum(dot_tn(att_ref[r], gd_ref[rows_of(r), :]) for r in range(sz.rows)).astype(BF16)
        )
        launch(3)
        rims = []
        n = sz.count[TOP]
        for r in range(sz.rows):
            dkey, dvalue = dkey_ref.at[r], dvalue_ref.at[r]
            dkey[...] = jnp.zeros(dkey.shape, F32)
            dvalue[...] = jnp.zeros(dvalue.shape, F32)
            attend_back(
                sz, q_ref.at[r], key_ref.at[r], value_ref.at[r], mask_ref, index_ref, own_ref, lse_ref.at[r],
                go_ref.at[r], dq_ref.at[r], dkey, dvalue, score_ref, back_ref, weight_ref, dscore_ref, coarse_ref,
                functools.partial(plan.advance, TIMES["attend_back"]),
            )
            for kind, bank in ((0, dkey), (1, dvalue)):
                for level in range(TOP):
                    rims_out[layer, r, 0, rim_rows(level, kind), :] = bank[pl.ds(sz.offset[level], BLOCK), :].astype(BF16)
                    rims_out[layer, r, 1, rim_rows(level, kind), :] = bank[
                        pl.ds(sz.offset[level] + BLOCK + sz.count[level], BLOCK), :
                    ].astype(BF16)
            for s in range(sz.seq):
                at = pl.ds(sz.offset[TOP] + s * n, n)
                tops_out[layer, r, s] = jnp.concatenate([dkey[at, :], dvalue[at, :]], axis=0).astype(BF16)
            rims.append(
                Rims(
                    sz, rims_out.at[layer, r, 1], rims_out.at[layer, r, 0], tops_out.at[layer, r], low_ref.at[layer, r],
                    high_ref.at[layer, r], tops_ref.at[layer, r], rim_send.at[layer, r], rim_recv.at[layer, r],
                )
            )
            rims[-1].start()
        all_rims += rims
        load(layer - 1, "att", "q", "key", "value", "lse")
        if layer == LAYERS - 1:
            copies.wait("x")
        layer_input = (lambda r: tokens_ref[r].astype(F32)) if layer == 0 else (lambda r: x_ref[rows_of(r), :])
        for r in range(sz.rows):
            hat, _ = normalise(layer_input(r))
            normed_ref[r] = (hat * vec[0:1, :] + vec[2:3, :]).astype(BF16)
            gvec_ref[3:4, :] += jnp.sum(dq_ref[r].astype(F32), axis=0, keepdims=True)
        room(4)
        store_blocks(gq, 0, slice(None), sum(dot_tn(normed_ref[r], dq_ref[r]) for r in range(sz.rows)).astype(BF16))
        launch(4)
        plan.advance(TIMES["levels"])
        for r in range(sz.rows):
            rims[r].arrive()
            for kind, bank, out in ((0, dkey_ref.at[r], dk_ref), (1, dvalue_ref.at[r], dv_ref)):
                base = 0
                for level in range(LEVELS):
                    n = sz.count[level]
                    if level == TOP:
                        top = sum(tops_ref[layer, r, s, kind * n : kind * n + n, :].astype(F32) for s in range(sz.seq))
                        levels_ref[pl.ds(base, 2 * n), :] = jnp.concatenate(
                            [top, jnp.zeros((n, model), F32)], axis=0
                        ).astype(BF16)
                        continue
                    own = bank[pl.ds(sz.offset[level] + BLOCK, n), :]
                    first = low_ref[layer, r, rim_rows(level, kind), :].astype(F32)
                    final = high_ref[layer, r, rim_rows(level, kind), :].astype(F32)
                    if n == BLOCK:
                        own = own + first + final
                    else:
                        between = [own[BLOCK : n - BLOCK]] if n > 2 * BLOCK else []
                        own = jnp.concatenate([own[:BLOCK] + first, *between, own[n - BLOCK :] + final], axis=0)
                    if level == 0:
                        fine = own
                    else:
                        levels_ref[pl.ds(base, n), :] = own.astype(BF16)
                        base += n
                out[rows_of(r), :] = (fine + dot_tn(coarse, levels_ref[...])).astype(BF16)
            gvec_ref[4:5, :] += jnp.sum(dv_ref[rows_of(r), :].astype(F32), axis=0, keepdims=True)
            plan.advance(TIMES["levels"])
        for k, (out, source) in enumerate(((gk, dk_ref), (gv, dv_ref))):
            room(5 + k)
            store_blocks(
                out, 0, slice(None),
                sum(dot_tn(normed_ref[r], source[rows_of(r), :]) for r in range(sz.rows)).astype(BF16),
            )
            launch(5 + k)
        copies.wait("wq")
        for r in range(sz.rows):
            rows = rows_of(r)
            grad = dot_nt(dq_ref[r], whole_rows(wq, slice(0, model)))
            grad = grad + dot_nt(dk_ref[rows, :], whole_rows(wq, slice(model, 2 * model)))
            grad = grad + dot_nt(dv_ref[rows, :], whole_rows(wq, slice(2 * model, 3 * model)))
            hat, inverse = normalise(layer_input(r))
            gvec_ref[0:1, :] += jnp.sum(grad * hat, axis=0, keepdims=True)
            gvec_ref[2:3, :] += jnp.sum(grad, axis=0, keepdims=True)
            g_ref[rows, :] = gm_ref[rows, :] + norm_back(grad, hat, inverse, vec[0:1, :])
            plan.advance(TIMES["finish"])
        load(layer - 1, "wq")
        if layer == 0:
            copies.start("gin", g_ref, gin_ref)
        room(7)
        for i in range(model // BLOCK):
            top = gvec_ref[:, 128 * (i // 8) : 128 * (i // 8) + 128]
            side = jnp.broadcast_to(gupb_ref[:, 128 * (i // 2) : 128 * (i // 2) + 128], (8, 128))
            store_blocks(small_ref, i, slice(None), jnp.concatenate([top, side], axis=0).astype(BF16))
        launch(7)
    plan.flush()
    if depth:
        for layer in range(LAYERS):
            unpack_share(sz, small_sums[layer], layer, *out_refs[4:7])
    for rim in all_rims:
        rim.drain()
    for scatter in scatters.values():
        scatter.drain()
    copies.drain()


def backward(sz, depth, prefix_len, cotangent, tokens, x, saved, wholes):
    n, rows, run = sz.model, sz.rows, sz.run
    per = sz.hidden * BLOCK // n
    lead = (n // BLOCK // 8, 2, 2, 2)
    half = sz.hidden // 2
    blocks = [(BLOCK, half), (BLOCK, half), (per, n), (BLOCK, n), (BLOCK, n), (BLOCK, n), (BLOCK, n), (BLOCK, 128)]
    pieces = [(lead + block, BF16) for block in blocks]
    outs = [((sz.tokens, n), F32)]
    if depth:
        outs += [((LAYERS,) + shape, F32) for shape in (
            (BLOCK, 3 * n), (BLOCK, n), (BLOCK, sz.hidden), (per, n), (2, BLOCK)
        )]
        outs += [((6, LAYERS, BLOCK), F32), ((LAYERS, per), F32)]
    else:
        outs += pieces * LAYERS
    rim = sz.rim // rows
    scratch = [(array.shape[1:], array.dtype) for array in list(saved) + list(wholes)]
    scratch += [
        ((sz.tokens, n), F32), ((sz.tokens, n), F32), ((8, n), F32), ((1, sz.hidden), F32),
        ((sz.chunks, sz.width, 128), F32), ((sz.tokens, n), BF16),
        ((sz.tokens, n), BF16), ((sz.tokens, n), F32), ((rows, run, n), BF16), ((sz.tokens, n), F32),
        ((rows, run, n), BF16), ((rows, sz.bank, n), F32), ((rows, sz.bank, n), F32), ((8, n), F32),
        ((1, sz.hidden), F32), ((sz.tokens, n), BF16), ((sz.tokens, n), BF16), ((run, n), BF16), ((rows, run, n), BF16),
        ((LAYERS, rows, 2, rim, n), BF16), ((LAYERS, rows, sz.seq, BLOCK, n), BF16), ((LAYERS, rows, rim, n), BF16),
        ((LAYERS, rows, rim, n), BF16), ((LAYERS, rows, sz.seq, BLOCK, n), BF16),
    ]
    scratch += attend_scratch(sz)
    scratch = [pltpu.VMEM(shape, dtype) for shape, dtype in scratch]
    scratch += [pltpu.SemaphoreType.DMA((LAYERS, rows, sz.seq + 1))] * 2
    scratch += [pltpu.SemaphoreType.DMA((LAYERS * (SAVED + 5) + 2,))]
    if depth:
        scratch += [pltpu.VMEM(shape, dtype) for shape, dtype in pieces + pieces[:EARLY]]
        for p, block in enumerate(blocks):
            scratch += scatter_buffers(depth, block, p in FLAT_SUMS)
        scratch += [pltpu.SemaphoreType.DMA((LAYERS, GRADS, 2 + depth))] * 2
        scratch += [pltpu.SemaphoreType.REGULAR((GRADS,)), pltpu.VMEM((LAYERS, BLOCK, 128), F32)]
    result = pl.pallas_call(
        functools.partial(backward_kernel, sz, depth),
        out_shape=[jax.ShapeDtypeStruct(shape, dtype) for shape, dtype in outs],
        in_specs=[pl.BlockSpec(memory_space=pltpu.SMEM), WHOLE, WHOLE] + [ANYWHERE] * (1 + SAVED + 5),
        out_specs=[ANYWHERE] + [WHOLE] * (len(outs) - 1),
        scratch_shapes=scratch,
        compiler_params=pltpu.CompilerParams(
            collective_id=1, has_side_effects=True, vmem_limit_bytes=VMEM_LIMIT
        ),
        name="backward",
    )(prefix_len, cotangent, tokens, x, *saved, *wholes)
    return result[0], list(result[1:])


def direct(rows):
    return lax.axis_size("seq") == 4 and lax.axis_size("dp") % 2 == 0 and rows % BLOCK == 0


def pack_small(gains, biases, up_bias):
    layers, _, features = gains.shape
    tiles = features // BLOCK
    vec = jnp.concatenate([gains, biases], axis=1).reshape(layers, 8, tiles, BLOCK).transpose(0, 2, 1, 3)
    vec = jnp.tile(vec, (1, 1, 1, 128 // BLOCK))
    up = up_bias.reshape(layers, tiles, 1, up_bias.shape[1] // tiles)
    up = jnp.broadcast_to(jnp.tile(up, (1, 1, 1, 128 // up.shape[3])), (layers, tiles, 8, 128))
    return jnp.concatenate([vec, up], axis=2).reshape(layers, features, 128)


def whole_weights(w_qkv, w_out, w_up, w_down, gains, biases, up_bias):
    whole = lambda array, axis: lax.all_gather(array, AXES, axis=axis, tiled=True)
    small = pack_small(whole(gains, 2), whole(biases, 2), whole(up_bias, 1))
    tiles = small.shape[1] // BLOCK
    arrays = (whole(w_qkv, 1), whole(w_out, 1), whole(w_up, 1), whole(w_down, 1), small)
    return [
        array.reshape(LAYERS, tiles // 8, 2, 2, 2, array.shape[1] // tiles, array.shape[2]) for array in arrays
    ]


def collect_kernel(count, *refs):
    for source, target in zip(refs[:count], refs[count:]):
        target[...] = source[...]


def collect(*arrays):
    count = len(arrays)
    return pl.pallas_call(
        functools.partial(collect_kernel, count),
        out_shape=[jax.ShapeDtypeStruct(array.shape, array.dtype) for array in arrays],
        in_specs=[WHOLE] * count,
        out_specs=[WHOLE] * count,
        compiler_params=pltpu.CompilerParams(vmem_limit_bytes=VMEM_LIMIT),
        name="collect",
    )(*arrays)


def scatter_by_sums(sz, parts):
    gqkv, gout, gup, small, gdown = parts
    spread = lambda array, axis: lax.psum_scatter(
        array.astype(F32), AXES, scatter_dimension=axis, tiled=True
    )
    tiles = small.reshape(sz.model // BLOCK, BLOCK, 128)
    vec = jnp.concatenate(
        [tiles[i, :8, BLOCK * (i % 8) : BLOCK * (i % 8) + BLOCK] for i in range(sz.model // BLOCK)], axis=1
    )
    wide = sz.hidden * BLOCK // sz.model
    per = 128 // wide
    up = jnp.concatenate(
        [tiles[i, 8, wide * (i % per) : wide * (i % per) + wide] for i in range(sz.model // BLOCK)], axis=0
    )
    vec = spread(vec, 1)
    return spread(gqkv, 0), spread(gout, 0), spread(gup, 0), spread(gdown, 0), vec[:2], vec[2:], spread(up, 0)


def on_device(
    tokens_in, grad_output, prefix_len, w_qkv, w_out, w_up, w_down, norm_gains, bias_rows, up_bias
):
    micro, rows, run, model = tokens_in.shape
    sz = Sizes(micro * rows, run, model, w_up.shape[2], lax.axis_size("seq"))
    depth = lax.axis_size("dp") // 2 if direct(w_qkv.shape[1]) else 0
    if depth:
        weights = (w_qkv, w_out, w_up, w_down, norm_gains, bias_rows.transpose(1, 0, 2), up_bias)
    else:
        weights = whole_weights(w_qkv, w_out, w_up, w_down, norm_gains, bias_rows, up_bias)
    by_row = (sz.rows, run, model)
    out_act, x_one, saved, wholes = forward(sz, depth, tokens_in.reshape(by_row), weights)
    grad, parts = backward(
        sz, depth, prefix_len.T, grad_output.reshape(by_row), tokens_in.reshape(by_row), x_one, saved, wholes
    )
    if depth:
        out_act, grad, *parts = collect(out_act, grad, *parts)
        results = parts[:5] + [parts[5].transpose(1, 0, 2), parts[6]]
    else:
        layers = []
        for layer in range(LAYERS):
            pieces = [piece.reshape(-1, piece.shape[-1]) for piece in parts[GRADS * layer : GRADS * (layer + 1)]]
            up_a, up_b, down, out, dq, dk, dv, small = pieces
            qkv, up = jnp.concatenate([dq, dk, dv], axis=1), jnp.concatenate([up_a, up_b], axis=1)
            layers.append(scatter_by_sums(sz, (qkv, out, up, small, down)))
        results = [jnp.stack([layer[k] for layer in layers], axis=0) for k in range(7)]
    return (out_act.reshape(tokens_in.shape), grad.reshape(tokens_in.shape), *results)


def solution(mesh):
    tokens, shard = P(None, "dp", "seq", None), P(None, AXES, None)
    small, bias = P(None, None, AXES), P(None, AXES)
    return jax.shard_map(
        on_device,
        mesh=mesh,
        in_specs=(tokens, tokens, P(None, "dp"), shard, shard, shard, shard, small, small, bias),
        out_specs=(tokens, tokens, shard, shard, shard, shard, small, small, bias),
        check_vma=False,
    )
```

```python
import functools
import math

import jax
import jax.numpy as jnp
from jax import lax
from jax.experimental import pallas as pl
from jax.experimental.pallas import tpu as pltpu
from jax.sharding import PartitionSpec as P

HDIM = 64
BLOCK = 16
LEVELS = 6
LAYERS = 2
TOP = LEVELS - 1
CHUNK = 64
LN2 = math.log(2.0)
F32 = jnp.float32
BF16 = jnp.bfloat16
NEG = -1e30
VMEM_LIMIT = 62 * 2**20
AXES = ("dp", "seq")


def dot_nn(a, b):
    return lax.dot_general(a, b, (((1,), (0,)), ((), ())), preferred_element_type=F32)


def dot_nt(a, b):
    return lax.dot_general(a, b, (((1,), (1,)), ((), ())), preferred_element_type=F32)


def dot_tn(a, b):
    return lax.dot_general(a, b, (((0,), (0,)), ((), ())), preferred_element_type=F32)


class Sizes:
    def __init__(self, rows, run, model, hidden, seq):
        self.rows, self.run, self.model, self.hidden, self.seq = rows, run, model, hidden, seq
        self.tokens = rows * run
        self.pairs = model // 128
        self.chunks = run // CHUNK
        self.count = [run >> level for level in range(LEVELS)]
        self.top_keys = self.count[TOP] * seq
        self.offset, at = [], 0
        for level in range(TOP):
            self.offset.append(at)
            at += self.count[level] + 2 * BLOCK
        self.offset.append(at)
        self.bank = at + self.top_keys
        self.keys = [CHUNK + 2 * BLOCK, CHUNK // 2 + 2 * BLOCK] + [2 * BLOCK] * (TOP - 2) + [self.top_keys]
        self.start = [sum(self.keys[:level]) for level in range(LEVELS)]
        self.width = sum(self.keys)
        self.rim = rows * TOP * 2 * BLOCK


def normalise(values):
    centred = values - jnp.mean(values, axis=-1, keepdims=True)
    spread = jnp.mean(centred * centred, axis=-1, keepdims=True)
    inverse = lax.rsqrt(spread + 1e-05)
    return centred * inverse, inverse


def norm_back(grad, hat, inverse, gain):
    scaled = grad * gain
    first = jnp.mean(scaled, axis=-1, keepdims=True)
    second = jnp.mean(scaled * hat, axis=-1, keepdims=True)
    return inverse * (scaled - first - hat * second)


GELU_C = math.sqrt(2.0 / math.pi)


def gelu(v):
    return 0.5 * v * (1.0 + jnp.tanh(GELU_C * (v + 0.044715 * (v * v * v))))


def gelu_both(v):
    square = v * v
    t = jnp.tanh(GELU_C * (v + 0.044715 * (square * v)))
    half = 0.5 * (1.0 + t)
    slope = half + 0.5 * v * (1.0 - t * t) * (GELU_C * (1.0 + 3.0 * 0.044715 * square))
    return v * half, slope


def row_loop(total, step, body):
    def go(j, carry):
        body(pl.ds(pl.multiple_of(j * step, step), step))
        return carry

    lax.fori_loop(0, total // step, go, 0)


def coarse_matrix(run):
    row = lax.broadcasted_iota(jnp.int32, (run, run), 0)
    col = lax.broadcasted_iota(jnp.int32, (run, run), 1)
    out = jnp.zeros((run, run), F32)
    base = 0
    for level in range(1, LEVELS):
        n = run >> level
        hit = (row >= base) & (row < base + n) & ((col >> level) == row - base)
        out = jnp.where(hit, 2.0**-level, out)
        base += n
    return out.astype(BF16)


COARSE = [0] + [CHUNK - (CHUNK >> (level - 1)) for level in range(1, LEVELS + 1)]


def chunk_matrix():
    row = lax.broadcasted_iota(jnp.int32, (CHUNK, CHUNK), 0)
    col = lax.broadcasted_iota(jnp.int32, (CHUNK, CHUNK), 1)
    out = jnp.zeros((CHUNK, CHUNK), F32)
    for level in range(1, LEVELS):
        at, end = COARSE[level], COARSE[level + 1]
        out = jnp.where((row >= at) & (row < end) & ((col >> level) == row - at), 2.0**-level, out)
    return out.astype(BF16)


def sum_matrix():
    token = lax.broadcasted_iota(jnp.int32, (128, 128), 0)
    col = lax.broadcasted_iota(jnp.int32, (128, 128), 1)
    place, within = col % CHUNK, token % CHUNK
    out = jnp.zeros((128, 128), F32)
    for level in range(1, LEVELS):
        at, end = COARSE[level], COARSE[level + 1]
        out = jnp.where((place >= at) & (place < end) & ((within >> level) == place - at), 1.0, out)
    return jnp.where(token // CHUNK == col // CHUNK, out, 0.0).astype(BF16)


def fill_index(sz, index_ref):
    lane = lax.broadcasted_iota(jnp.int32, (8, 128), 1)
    for level in range(1, LEVELS):
        value = (lane // CHUNK) * CHUNK + COARSE[level] + ((lane % CHUNK) >> level)
        for k in range(sz.keys[level] // 8):
            index_ref[pl.ds(sz.start[level] - sz.start[1] + 8 * k, 8), :] = value


def fill_own(sz, own_ref):
    place = lax.broadcasted_iota(jnp.int32, (8, 128), 1) % CHUNK
    for level in range(1, LEVELS):
        value = jnp.where((place >= COARSE[level]) & (place < COARSE[level + 1]), 1.0, 0.0)
        for k in range(sz.keys[level] // 8):
            own_ref[pl.ds(sz.start[level] - sz.start[1] + 8 * k, 8), :] = value


def fill_mask(sz, mask_ref):
    place = lax.axis_index("seq")
    for i in range(sz.chunks):
        for level in range(LEVELS):
            shape = (sz.keys[level], 128)
            key = lax.broadcasted_iota(jnp.int32, shape, 0)
            token = lax.broadcasted_iota(jnp.int32, shape, 1) % CHUNK
            per_run = sz.count[level] // BLOCK
            if level == TOP:
                query_block = ((place * sz.run + i * CHUNK + token) >> TOP) // BLOCK
                allowed = jnp.abs(query_block - key // BLOCK) == 1
            else:
                own = (i * CHUNK >> level) // BLOCK
                if level >= 2:
                    key_block = own - 1 + 2 * (key // BLOCK)
                    allowed = key >= 0
                else:
                    key_block = own - 1 + key // BLOCK
                    distance = jnp.abs(key_block - own - (token >> level) // BLOCK)
                    allowed = distance <= 1 if level == 0 else distance == 1
                whole = place * per_run + key_block
                allowed = allowed & (whole >= 0) & (whole < per_run * sz.seq)
            mask_ref[i, pl.ds(sz.start[level], sz.keys[level])] = jnp.where(allowed, level * LN2, NEG)


def key_slices(sz, i, level):
    if level == TOP:
        return [(sz.offset[TOP], sz.top_keys)]
    if level < 2:
        return [(sz.offset[level] + (CHUNK >> level) * i, sz.keys[level])]
    own = (i * CHUNK) // (BLOCK << level)
    return [(sz.offset[level] + BLOCK * own, BLOCK), (sz.offset[level] + BLOCK * (own + 2), BLOCK)]


def take(ref, pieces, lanes):
    parts = [ref[rows_at(at, size), lanes] for at, size in pieces]
    return parts[0] if len(parts) == 1 else jnp.concatenate(parts, axis=0)


def rows_at(at, size):
    return pl.ds(at if isinstance(at, int) else pl.multiple_of(at, BLOCK), size)


def give(ref, pieces, lanes, value):
    done = 0
    for at, size in pieces:
        ref[rows_at(at, size), lanes] += value[done : done + size]
        done += size


def two_heads(block):
    first = lax.broadcasted_iota(jnp.int32, block.shape, 1) < HDIM
    zero = jnp.zeros_like(block)
    return jnp.concatenate([jnp.where(first, block, zero), jnp.where(first, zero, block)], axis=0)


def one_row(block):
    first = lax.broadcasted_iota(jnp.int32, (CHUNK, 128), 1) < HDIM
    return jnp.where(first, block[:CHUNK], block[CHUNK:])


class Units:
    def __init__(self, sz, q_ref, key_ref, value_ref):
        self.sz, self.q_ref, self.key_ref, self.value_ref = sz, q_ref, key_ref, value_ref
        self.all = [(i, pair) for i in range(sz.chunks) for pair in range(sz.pairs)]
        self.pieces = []
        for i in range(sz.chunks):
            levels = [key_slices(sz, i, level) for level in range(LEVELS)]
            self.pieces.append((levels[0], sum(levels[1:], [])))
        matrix = chunk_matrix()
        self.fine = [q_ref[self.tokens(i), :] for i in range(sz.chunks)]
        self.coarse = [dot_nn(matrix, fine).astype(BF16) for fine in self.fine]

    def tokens(self, i):
        return pl.ds(i * CHUNK, CHUNK)

    def lanes(self, pair):
        return slice(128 * pair, 128 * pair + 128)

    def queries(self, i, pair):
        lanes = self.lanes(pair)
        return two_heads(self.fine[i][:, lanes]), two_heads(self.coarse[i][:, lanes])

    def keys(self, i, pair):
        return [take(self.key_ref, pieces, self.lanes(pair)) for pieces in self.pieces[i]]

    def values(self, i, pair):
        return take(self.value_ref, self.pieces[i][0] + self.pieces[i][1], self.lanes(pair))

    def scores(self, u, i, pair, mask_ref, index_ref, out_ref):
        base = self.sz.start[1]
        (fine_keys, coarse_keys), (fine, coarse) = self.keys(i, pair), self.queries(i, pair)
        out_ref[u, :base] = dot_nt(fine_keys, fine) + mask_ref[i, :base]
        upper = jnp.take_along_axis(dot_nt(coarse_keys, coarse), index_ref[...], axis=1)
        out_ref[u, base:] = upper + mask_ref[i, base:]


def attend(sz, q_ref, key_ref, value_ref, mask_ref, index_ref, att_ref, lse_ref, score_ref, weight_ref, pause):
    units = Units(sz, q_ref, key_ref, value_ref)
    for u, (i, pair) in enumerate(units.all):
        units.scores(u, i, pair, mask_ref, index_ref, score_ref)
    pause()
    for u, (i, pair) in enumerate(units.all):
        scores = score_ref[u]
        peak = jnp.max(scores, axis=0, keepdims=True)
        weights = jnp.exp(scores - peak)
        total = jnp.sum(weights, axis=0, keepdims=True)
        lse_ref[i, pair : pair + 1, :] = peak + jnp.log(total)
        weight_ref[u] = (weights * (1.0 / total)).astype(BF16)
    pause()
    for u, (i, pair) in enumerate(units.all):
        mixed = dot_tn(weight_ref[u], units.values(i, pair))
        att_ref[units.tokens(i), units.lanes(pair)] = one_row(mixed).astype(BF16)
    pause()


def attend_back(
    sz, q_ref, key_ref, value_ref, mask_ref, index_ref, own_ref, lse_ref, go_ref, dq_ref, dkey_ref, dvalue_ref,
    score_ref, back_ref, weight_ref, dscore_ref, coarse_ref, pause
):
    units = Units(sz, q_ref, key_ref, value_ref)
    sums, matrix, base = sum_matrix(), chunk_matrix(), sz.start[1]
    for u, (i, pair) in enumerate(units.all):
        units.scores(u, i, pair, mask_ref, index_ref, score_ref)
    pause()
    for u, (i, pair) in enumerate(units.all):
        go = two_heads(go_ref[units.tokens(i), units.lanes(pair)])
        back_ref[u] = dot_nt(units.values(i, pair), go)
    for u, (i, pair) in enumerate(units.all):
        weights = jnp.exp(score_ref[u] - lse_ref[i, pair : pair + 1, :])
        weight_ref[u] = weights.astype(BF16)
        back = back_ref[u]
        inner = jnp.sum(weights * back, axis=0, keepdims=True)
        dscore_ref[u] = (weights * (back - inner)).astype(BF16)
    pause()
    for u, (i, pair) in enumerate(units.all):
        go = two_heads(go_ref[units.tokens(i), units.lanes(pair)])
        give(dvalue_ref, units.pieces[i][0] + units.pieces[i][1], units.lanes(pair), dot_nn(weight_ref[u], go))
    for u, (i, pair) in enumerate(units.all):
        coarse_ref[u] = (dot_nn(dscore_ref[u, base:], sums) * own_ref[...]).astype(BF16)
    pause()
    for u, (i, pair) in enumerate(units.all):
        (first, upper), (fine, coarse) = units.pieces[i], units.queries(i, pair)
        give(dkey_ref, first, units.lanes(pair), dot_nn(dscore_ref[u, :base], fine))
        give(dkey_ref, upper, units.lanes(pair), dot_nn(coarse_ref[u], coarse))
    pause()
    for u, (i, pair) in enumerate(units.all):
        fine_keys, coarse_keys = units.keys(i, pair)
        fine = one_row(dot_tn(dscore_ref[u, :base], fine_keys))
        coarse = one_row(dot_tn(coarse_ref[u], coarse_keys)).astype(BF16)
        dq_ref[units.tokens(i), units.lanes(pair)] = ((fine + dot_tn(matrix, coarse)) * HDIM**-0.5).astype(BF16)
    pause()


def rim_rows(level, kind):
    return pl.ds((level * 2 + kind) * BLOCK, BLOCK)


def unpack_small(sz, small, vec_ref, up_ref):
    lane = lax.broadcasted_iota(jnp.int32, (BLOCK, 128), 1)
    tiles = [small[BLOCK * i : BLOCK * i + BLOCK, :].astype(F32) for i in range(sz.model // BLOCK)]
    for c in range(sz.model // 128):
        total = tiles[8 * c]
        for j in range(1, 8):
            total = jnp.where(lane // 16 == j, tiles[8 * c + j], total)
        vec_ref[:, 128 * c : 128 * c + 128] = total[:8]
    wide = sz.hidden * BLOCK // sz.model
    for c in range(sz.hidden // 128):
        total = tiles[2 * c]
        total = jnp.where(lane >= wide, tiles[2 * c + 1], total)
        up_ref[:, 128 * c : 128 * c + 128] = total[8:9]


def place_rims(sz, low_ref, high_ref, tops_ref, key_ref, value_ref):
    for kind, bank in ((0, key_ref), (1, value_ref)):
        for level in range(TOP):
            bank[pl.ds(sz.offset[level], BLOCK), :] = low_ref[rim_rows(level, kind), :]
            bank[pl.ds(sz.offset[level] + BLOCK + sz.count[level], BLOCK), :] = high_ref[rim_rows(level, kind), :]
        n = sz.count[TOP]
        for s in range(0, sz.seq, 2):
            pair = [tops_ref[s + k, kind * n : kind * n + n, :] for k in range(2)]
            bank[pl.ds(sz.offset[TOP] + s * n, 2 * n), :] = jnp.concatenate(pair, axis=0)


MESH = pl.DeviceIdType.MESH


class Grid:
    def __init__(self, depth):
        dp, seq = lax.axis_index("dp"), lax.axis_index("seq")
        self.depth = depth
        self.z, self.x, self.y, self.c = dp // 2, dp % 2, seq // 2, seq % 2

    def at(self, z, x, y, c):
        return (z * 2 + x, y * 2 + c)

    def index(self, z, x, y, c):
        return z * 8 + x * 4 + y * 2 + c

    def partner(self, axis):
        z, x, y, c = self.z, self.x, self.y, self.c
        return self.at(z, 1 - x if axis == "x" else x, 1 - y if axis == "y" else y, 1 - c if axis == "c" else c)

    def up(self, by):
        return self.at(self.z + by, self.x, self.y, self.c)


def greet(devices):
    barrier = pltpu.get_barrier_semaphore()
    peers = jnp.int32(0)
    for where, condition in devices:
        signal = functools.partial(pl.semaphore_signal, barrier, inc=1, device_id=where, device_id_type=MESH)
        if condition is None:
            signal()
            peers += 1
        else:
            pl.when(condition)(signal)
            peers += condition.astype(jnp.int32)
    pl.semaphore_wait(barrier, peers)


def both(first, second):
    if first is None:
        return second
    return first if second is None else first & second


def when(condition, act):
    if condition is None:
        act()
    else:
        pl.when(condition)(act)


class Plan:
    HOP = 1.5

    def __init__(self, core, links):
        self.rate = {"core": core, "plane": links, "z": links}
        self.now, self.count, self.waiting = 0.0, 0, []
        self.free = dict.fromkeys(self.rate, 0.0)

    def send(self, link, size):
        self.free[link] = max(self.now, self.free[link]) + size / self.rate[link]
        return self.free[link] + self.HOP

    def later(self, ready, act):
        self.count += 1
        self.waiting.append((ready, self.count, act))

    def pop(self):
        first = min(self.waiting, key=lambda entry: entry[:2])
        self.waiting.remove(first)
        self.now = max(self.now, first[0])
        first[2]()

    def advance(self, time):
        self.now += time
        while self.waiting and min(entry[0] for entry in self.waiting) <= self.now:
            self.pop()

    def until(self, done):
        while not done():
            self.pop()

    def flush(self):
        while self.waiting:
            self.pop()


class Gather:
    def __init__(self, grid, plan, pieces, local_sem, send_sem, recv_sem):
        self.grid, self.plan, self.pieces = grid, plan, pieces
        self.local_sem, self.send_sem, self.recv_sem = local_sem, send_sem, recv_sem
        z, x, y, c = grid.z, grid.x, grid.y, grid.c
        self.others = [lax.rem(z + k, grid.depth) for k in range(1, grid.depth)]
        self.one, self.two, self.lines = [], [], []
        for p in range(len(pieces)):
            y_first = (c ^ (FLIP * (p % 2))) == 0
            pick = lambda first, second: jnp.where(y_first, first, second)
            one, two = (pick(x, 1 - x), pick(1 - y, y)), (pick(1 - x, x), pick(y, 1 - y))
            self.one.append(grid.at(z, *one, c))
            self.two.append(grid.at(z, *two, c))
            self.lines.append([(x, y), one, two, (1 - x, 1 - y)])
        self.ids, self.count = [], 0
        for piece in pieces:
            self.ids.append(list(range(self.count, self.count + len(piece))))
            self.count += len(piece)
        self.sends = []
        self.done = [False] * len(pieces)
        self.passed, self.parked = [False] * len(pieces), []

    def size(self, p):
        return sum(2 * share.shape[0] * share.shape[1] for share, _ in self.pieces[p])

    def copy(self, array, source, target, slot, landing, to):
        return pltpu.make_async_remote_copy(
            src_ref=source, dst_ref=target, send_sem=self.send_sem.at[array, slot],
            recv_sem=self.recv_sem.at[array, landing], device_id=to, device_id_type=MESH,
        )

    def begin(self, p):
        grid = self.grid
        for array, (share, whole) in zip(self.ids[p], self.pieces[p]):
            mine = whole.at[grid.z, grid.x, grid.y, grid.c]
            pltpu.make_async_copy(share, mine, self.local_sem.at[array]).start()
            for k, other in enumerate(self.others):
                copy = self.copy(array, share, mine, k, k, grid.at(other, grid.x, grid.y, grid.c))
                copy.start()
                self.sends.append(copy)
        ready = self.plan.send("z", 2 * grid.depth * self.size(p))
        self.plan.later(ready, functools.partial(self.enter, p))

    def enter(self, p):
        if p >= GATE and not self.passed[p - GATE]:
            self.parked.append(p)
        else:
            self.along(p)

    def line(self, p, whole, k):
        xx, yy = self.lines[p][k]
        return whole.at[:, xx, yy, self.grid.c]

    def pass_line(self, p, k, slots, landing):
        xx, yy = self.lines[p][k]
        for array, (_, whole) in zip(self.ids[p], self.pieces[p]):
            line = self.line(p, whole, k)
            for name, slot in slots.items():
                if name == "core":
                    copy = self.copy(array, line, line, slot, 2 + self.grid.depth + xx * 2 + yy, self.grid.partner("c"))
                else:
                    copy = self.copy(array, line, line, slot, landing[name], {"one": self.one[p], "two": self.two[p]}[name])
                copy.start()
                self.sends.append(copy)

    def receive(self, p, landing, k):
        for array, (_, whole) in zip(self.ids[p], self.pieces[p]):
            line = self.line(p, whole, k)
            self.copy(array, line, line, 0, landing, self.one[p]).wait_recv()

    def along(self, p):
        grid, size, plan = self.grid, self.size(p), self.plan
        base = grid.depth - 1
        for array, (share, whole) in zip(self.ids[p], self.pieces[p]):
            mine = whole.at[grid.z, grid.x, grid.y, grid.c]
            pltpu.make_async_copy(share, mine, self.local_sem.at[array]).wait()
            for k in range(grid.depth - 1):
                self.copy(array, share, mine, k, k, self.one[p]).wait_recv()
        self.pass_line(p, 0, {"one": base, "two": base + 1, "core": base + 2}, {"one": base, "two": base + 1})
        line = grid.depth * size
        plan.later(plan.send("plane", line), functools.partial(self.after_one, p))
        plan.later(plan.send("plane", line), functools.partial(self.after_two, p))
        plan.send("core", line)

    def after_one(self, p):
        grid, plan = self.grid, self.plan
        base = grid.depth - 1
        self.receive(p, base, 1)
        self.pass_line(p, 1, {"two": base + 3, "core": base + 4}, {"two": base + 2})
        line = grid.depth * self.size(p)
        plan.later(plan.send("plane", line), functools.partial(self.after_both, p))
        plan.send("core", line)
        self.passed[p] = True
        if p + GATE in self.parked:
            self.parked.remove(p + GATE)
            self.along(p + GATE)

    def after_two(self, p):
        base = self.grid.depth - 1
        self.receive(p, base + 1, 2)
        self.pass_line(p, 2, {"core": base + 5}, {})
        self.plan.send("core", self.grid.depth * self.size(p))

    def after_both(self, p):
        base = self.grid.depth - 1
        self.receive(p, base + 2, 3)
        self.pass_line(p, 3, {"core": base + 6}, {})
        ready = self.plan.send("core", self.grid.depth * self.size(p))
        self.plan.later(ready, functools.partial(self.finish, p))

    def finish(self, p):
        grid = self.grid
        for array, (_, whole) in zip(self.ids[p], self.pieces[p]):
            for xx, yy in self.lines[p]:
                line = whole.at[:, xx, yy, 1 - grid.c]
                self.copy(array, line, line, 0, 2 + grid.depth + xx * 2 + yy, self.one[p]).wait_recv()
        self.done[p] = True

    def begin_flat(self, p, z_time):
        grid = self.grid
        self.passed[p] = True
        for array, (share, whole) in zip(self.ids[p], self.pieces[p]):
            mine = whole.at[grid.z, grid.x, grid.y, grid.c]
            pltpu.make_async_copy(share, mine, self.local_sem.at[array]).start()
            for slot, to in enumerate((self.one[p], self.two[p])):
                self.push(array, share, mine, slot, slot, to)
        ready = self.plan.send("plane", 2 * self.size(p))
        self.plan.later(ready, functools.partial(self.flat_plane, p, z_time))

    def push(self, array, source, target, slot, landing, to):
        copy = self.copy(array, source, target, slot, landing, to)
        copy.start()
        self.sends.append(copy)

    def flat_block(self, p, whole, k):
        xx, yy = self.lines[p][k]
        return whole.at[self.grid.z, xx, yy, self.grid.c]

    def flat_receive(self, p, landing, pick):
        for array, (_, whole) in zip(self.ids[p], self.pieces[p]):
            ref = pick(whole)
            self.copy(array, ref, ref, 0, landing, self.one[p]).wait_recv()

    def flat_plane(self, p, z_time):
        self.flat_receive(p, 0, lambda whole: self.flat_block(p, whole, 1))
        for array, (_, whole) in zip(self.ids[p], self.pieces[p]):
            block = self.flat_block(p, whole, 1)
            self.push(array, block, block, 2, 2, self.two[p])
        ready = self.plan.send("plane", self.size(p))
        self.plan.later(max(ready, z_time), functools.partial(self.flat_along, p))

    def flat_along(self, p):
        grid = self.grid
        self.flat_receive(p, 1, lambda whole: self.flat_block(p, whole, 2))
        self.flat_receive(p, 2, lambda whole: self.flat_block(p, whole, 3))
        for array, (share, whole) in zip(self.ids[p], self.pieces[p]):
            mine = whole.at[grid.z, grid.x, grid.y, grid.c]
            pltpu.make_async_copy(share, mine, self.local_sem.at[array]).wait()
            plane = whole.at[grid.z, :, :, grid.c]
            for k, other in enumerate(self.others):
                self.push(array, plane, plane, 3 + k, 3 + k, grid.at(other, grid.x, grid.y, grid.c))
        ready = self.plan.send("z", 8 * grid.depth * self.size(p))
        self.plan.later(ready, functools.partial(self.flat_core, p))

    def flat_core(self, p):
        grid = self.grid
        for k in range(grid.depth - 1):
            self.flat_receive(p, 3 + k, lambda whole: whole.at[grid.z, :, :, grid.c])
        for array, (_, whole) in zip(self.ids[p], self.pieces[p]):
            mine = whole.at[:, :, :, grid.c]
            self.push(array, mine, mine, 2 + grid.depth, 2 + grid.depth, grid.partner("c"))
        ready = self.plan.send("core", 4 * grid.depth * self.size(p))
        self.plan.later(ready, functools.partial(self.flat_finish, p))

    def flat_finish(self, p):
        self.flat_receive(p, 2 + self.grid.depth, lambda whole: whole.at[:, :, :, 1 - self.grid.c])
        self.done[p] = True

    def need(self, p):
        self.plan.until(lambda: self.done[p])

    def drain(self):
        for copy in self.sends:
            copy.wait_send()


class Scatter:
    def __init__(self, grid, plan, pieces, buffers, sums, send_sem, recv_sem, free_sem, again, more):
        self.grid, self.plan, self.pieces, self.buffers, self.sums = grid, plan, pieces, buffers, sums
        self.free_sem, self.again, self.more = free_sem, again, more
        self.next = {}
        self.done = [False] * len(pieces)
        self.send_sem, self.recv_sem = send_sem, recv_sem
        self.copies = [[] for _ in pieces]
        z, x, y, c = grid.z, grid.x, grid.y, grid.c
        self.others = [lax.rem(z + k, grid.depth) for k in range(1, grid.depth)]
        self.x_first = [(c ^ (FLIP * (p % 2))) == 0 for p in range(len(pieces))]
        pick = lambda p, first, second: jnp.where(self.x_first[p], first, second)
        self.one = [grid.at(z, pick(p, 1 - x, x), pick(p, y, 1 - y), c) for p in range(len(pieces))]
        self.two = [grid.at(z, pick(p, x, 1 - x), pick(p, 1 - y, y), c) for p in range(len(pieces))]
        self.mine = [(pick(p, x, y), pick(p, y, x)) for p in range(len(pieces))]

    def move(self, p, source, target, to):
        stage = len(self.copies[p])
        copy = pltpu.make_async_remote_copy(
            src_ref=source, dst_ref=target, send_sem=self.send_sem.at[p, stage], recv_sem=self.recv_sem.at[p, stage],
            device_id=to, device_id_type=MESH,
        )
        copy.start()
        self.copies[p].append(copy)

    def step(self, link, blocks, p, act):
        piece = self.pieces[p]
        ready = self.plan.send(link, 2 * blocks * piece.shape[4] * piece.shape[5])
        self.plan.later(ready, functools.partial(act, p))

    def senders(self):
        grid = self.grid
        along = [grid.at(other, grid.x, grid.y, grid.c) for other in self.others]
        return [grid.partner("c"), grid.partner("x"), grid.partner("y")] + along

    def begin(self, p):
        if self.again:
            pl.semaphore_wait(self.free_sem.at[p], len(self.senders()))
        self.move(p, self.pieces[p].at[:, :, :, 1 - self.grid.c], self.buffers[p][0], self.grid.partner("c"))
        self.step("core", 4 * self.grid.depth, p, self.flat_along if p in FLAT_SUMS else self.first)

    def place(self, p, one, two):
        return jnp.where(self.x_first[p], one, two), jnp.where(self.x_first[p], two, one)

    def first(self, p):
        grid = self.grid
        piece, (from_core, to_one, from_one) = self.pieces[p], self.buffers[p][:3]
        self.copies[p][0].wait_recv()
        for zz in range(grid.depth):
            for two in range(2):
                xx, yy = self.place(p, 1 - self.mine[p][0], two)
                total = piece[zz, xx, yy, grid.c].astype(F32) + from_core[zz, xx, yy].astype(F32)
                to_one[zz, two] = total.astype(BF16)
        self.move(p, to_one, from_one, self.one[p])
        self.step("plane", 2 * grid.depth, p, self.second)

    def second(self, p):
        grid = self.grid
        piece, (from_core, _, from_one, to_two, from_two) = self.pieces[p], self.buffers[p][:5]
        self.copies[p][1].wait_recv()
        other = 1 - self.mine[p][1]
        xx, yy = self.place(p, self.mine[p][0], other)
        for zz in range(grid.depth):
            total = piece[zz, xx, yy, grid.c].astype(F32) + from_core[zz, xx, yy].astype(F32)
            to_two[zz] = (total + from_one[zz, other].astype(F32)).astype(BF16)
        self.move(p, to_two, from_two, self.two[p])
        self.step("plane", grid.depth, p, self.along)

    def along(self, p):
        grid = self.grid
        piece, (from_core, _, from_one, _, from_two, ready, from_z) = self.pieces[p], self.buffers[p]
        self.copies[p][2].wait_recv()
        for zz in range(grid.depth):
            total = piece[zz, grid.x, grid.y, grid.c].astype(F32) + from_core[zz, grid.x, grid.y].astype(F32)
            total = total + from_one[zz, self.mine[p][1]].astype(F32) + from_two[zz].astype(F32)
            ready[zz] = total.astype(BF16)
        for k, other in enumerate(self.others):
            self.move(p, ready.at[other], from_z.at[k], grid.at(other, grid.x, grid.y, grid.c))
        self.step("z", 2 * grid.depth, p, self.finish)

    def flat_total(self, p, xx, yy):
        grid = self.grid
        from_core, _, from_z = self.buffers[p][:3]
        total = self.pieces[p][grid.z, xx, yy, grid.c].astype(F32) + from_core[grid.z, xx, yy].astype(F32)
        for k in range(grid.depth - 1):
            total = total + from_z[k, xx, yy].astype(F32)
        return total

    def flat_along(self, p):
        grid = self.grid
        piece, (from_core, to_z, from_z) = self.pieces[p], self.buffers[p][:3]
        self.copies[p][0].wait_recv()
        for k, other in enumerate(self.others):
            for xx in range(2):
                for yy in range(2):
                    total = piece[other, xx, yy, grid.c].astype(F32) + from_core[other, xx, yy].astype(F32)
                    to_z[k, xx, yy] = total.astype(BF16)
            self.move(p, to_z.at[k], from_z.at[k], grid.at(other, grid.x, grid.y, grid.c))
        self.step("z", 8 * grid.depth, p, self.flat_first)

    def flat_first(self, p):
        to_one, from_one = self.buffers[p][3:5]
        for k in range(self.grid.depth - 1):
            self.copies[p][1 + k].wait_recv()
        for two in range(2):
            to_one[two] = self.flat_total(p, *self.place(p, 1 - self.mine[p][0], two)).astype(BF16)
        self.move(p, to_one, from_one, self.one[p])
        self.step("plane", 2, p, self.flat_second)

    def flat_second(self, p):
        from_one, to_two, from_two = self.buffers[p][4:7]
        self.copies[p][self.grid.depth].wait_recv()
        other = 1 - self.mine[p][1]
        total = self.flat_total(p, *self.place(p, self.mine[p][0], other)) + from_one[other].astype(F32)
        to_two[...] = total.astype(BF16)
        self.move(p, to_two, from_two, self.two[p])
        self.step("plane", 1, p, self.finish)

    def finish(self, p):
        if p in FLAT_SUMS:
            from_one, _, from_two = self.buffers[p][4:7]
            self.copies[p][self.grid.depth + 1].wait_recv()
            total = self.flat_total(p, self.grid.x, self.grid.y) + from_one[self.mine[p][1]].astype(F32)
            self.close(p, total + from_two[...].astype(F32))
            return
        ready, from_z = self.buffers[p][5:7]
        total = ready[self.grid.z].astype(F32)
        for k in range(self.grid.depth - 1):
            self.copies[p][3 + k].wait_recv()
            total = total + from_z[k].astype(F32)
        self.close(p, total)

    def close(self, p, total):
        self.sums[p][...] = total
        if self.more:
            for copy in self.copies[p]:
                copy.wait_send()
            for device in self.senders():
                pl.semaphore_signal(self.free_sem.at[p], inc=1, device_id=device, device_id_type=MESH)
        self.done[p] = True
        if p in self.next:
            self.next.pop(p)()

    def need(self, p):
        self.plan.until(lambda: self.done[p])

    def drain(self):
        for copies in self.copies:
            for copy in copies if not self.more else []:
                copy.wait_send()


FLIP = 1
GATE = 2
FLAT = 5
FLAT_SUMS = (3, 4)
SCATTER_BUFFERS = 7


def scatter_buffers(depth, block, flat):
    leads = ((depth, 2, 2), (depth, 2), (depth, 2), (depth,), (depth,), (depth,), (depth - 1,))
    if flat:
        leads = ((depth, 2, 2), (depth - 1, 2, 2), (depth - 1, 2, 2), (2,), (2,), (), ())
    return [pltpu.VMEM(lead + tuple(block), BF16) for lead in leads]


class Rims:
    def __init__(self, sz, ahead, behind, tops, low, high, all_tops, send_sem, recv_sem):
        self.sz, self.low, self.high, self.all_tops, self.tops = sz, low, high, all_tops, tops
        self.me, self.dp = lax.axis_index("seq"), lax.axis_index("dp")
        me, dp, seq = self.me, self.dp, sz.seq
        make = lambda source, target, k, to: pltpu.make_async_remote_copy(
            src_ref=source, dst_ref=target, send_sem=send_sem.at[k], recv_sem=recv_sem.at[k],
            device_id=(dp, to), device_id_type=MESH,
        )
        self.ahead = lambda: make(ahead, low, 0, me + 1)
        self.behind = lambda: make(behind, high, 1, me - 1)
        self.rest = []
        for k in range(1, seq):
            other = lax.rem(me + k, seq)
            source = tops.at[0] if tops.shape[0] == 1 else tops.at[other]
            self.rest.append(make(source, all_tops.at[me], 1 + k, other))

    def start(self):
        when(self.me + 1 < self.sz.seq, lambda: self.ahead().start())
        when(self.me > 0, lambda: self.behind().start())
        for copy in self.rest:
            copy.start()
        self.all_tops[self.me] = self.tops[0] if self.tops.shape[0] == 1 else self.tops[self.me]

        def no_low():
            self.low[...] = jnp.zeros_like(self.low)

        def no_high():
            self.high[...] = jnp.zeros_like(self.high)

        when(self.me == 0, no_low)
        when(self.me == self.sz.seq - 1, no_high)

    def arrive(self):
        when(self.me > 0, lambda: self.ahead().wait_recv())
        when(self.me + 1 < self.sz.seq, lambda: self.behind().wait_recv())
        for copy in self.rest:
            copy.wait_recv()

    def drain(self):
        when(self.me + 1 < self.sz.seq, lambda: self.ahead().wait_send())
        when(self.me > 0, lambda: self.behind().wait_send())
        for copy in self.rest:
            copy.wait_send()


class Copies:
    def __init__(self, sem):
        self.sem, self.open, self.count = sem, {}, 0

    def start(self, name, source, target):
        copy = pltpu.make_async_copy(source, target, self.sem.at[self.count])
        self.count += 1
        copy.start()
        self.open[name] = copy

    def wait(self, *names):
        for name in names:
            if name in self.open:
                self.open.pop(name).wait()

    def drain(self):
        self.wait(*list(self.open))


def whole_rows(ref, columns):
    value = ref[:, :, :, :, :, columns]
    return value.reshape(-1, value.shape[-1])


def some_rows(ref, at, rows):
    per = ref.shape[4]
    blocks = [ref[i // 8, (i // 4) % 2, (i // 2) % 2, i % 2] for i in range(at // per, (at + rows) // per)]
    return jnp.concatenate(blocks, axis=0)


def make_share(sz, gains, biases_ref, layer, up, wide_ref, share_ref):
    wide = up.shape[-1]
    wide_ref[...] = jnp.zeros_like(wide_ref)
    wide_ref[0:2, 0:BLOCK] = gains.astype(F32)
    for k in range(6):
        wide_ref[2 + k : 3 + k, 0:BLOCK] = biases_ref[k, layer : layer + 1, :].astype(F32)
    wide_ref[8:16, 0:wide] = jnp.broadcast_to(up.astype(F32), (8, wide))
    row = lax.broadcasted_iota(jnp.int32, (128, 128), 0)
    lane = lax.broadcasted_iota(jnp.int32, (128, 128), 1)
    top = jnp.where((row < BLOCK) & (lane % BLOCK == row), 1.0, 0.0).astype(BF16)
    low = jnp.where((row < wide) & (lane % wide == row), 1.0, 0.0).astype(BF16)
    values = wide_ref[...].astype(BF16)
    share_ref[...] = jnp.concatenate([dot_nn(values, top)[:8], dot_nn(values, low)[8:]], axis=0).astype(BF16)


SAVED = 6
TIMES = {"before": 2.2, "attend": 0.8, "project": 1.0, "forward": 1.4, "start": 1.5, "back": 1.9, "branch": 2.0, "attend_back": 0.6,
         "levels": 1.0, "finish": 1.2}


def forward_kernel(sz, depth, *refs):
    refs = list(refs)
    take_refs = lambda n: [refs.pop(0) for _ in range(n)]
    tokens_ref = take_refs(1)[0]
    if depth:
        shares, (gains_ref, biases_ref, upb_ref) = take_refs(4), take_refs(3)
    else:
        wholes = take_refs(5)
    out_act_ref, x_out = take_refs(2)
    saved_out = take_refs(SAVED)
    if depth:
        wholes_out, wholes = take_refs(5), take_refs(5)
    q_ref, key_ref, value_ref, att_ref, lse_ref, middle_ref = take_refs(SAVED)
    x_ref, vec, up, mask_ref, second_ref, state_ref = take_refs(6)
    index_ref, score_ref, weight_ref = take_refs(3)
    rims_out, tops_out, low_ref, high_ref, tops_ref, rim_send, rim_recv, copy_sem = take_refs(8)
    model, run = sz.model, sz.run
    wq, wo, wu, wd, ws = wholes
    plan, copies = Plan(450e3, 110e3), Copies(copy_sem)
    me, dp = lax.axis_index("seq"), lax.axis_index("dp")
    peers = [((dp, lax.rem(me + k, sz.seq)), None) for k in range(1, sz.seq)]
    if depth:
        wide_ref, share_ref, local_sem, send_sem, recv_sem = take_refs(5)
        grid = Grid(depth)
        half = sz.hidden // 2
        pieces = []
        for layer in range(LAYERS):
            part = lambda k, columns: (shares[k].at[layer, :, columns], wholes[k].at[layer, :, :, :, :, :, columns])
            pieces.append([part(0, slice(None)), (share_ref.at[layer], ws.at[layer])])
            pieces.append([part(1, slice(None)), part(2, slice(0, half))])
            pieces.append([part(2, slice(half, None))])
            pieces.append([part(3, slice(None))])
        gather = Gather(grid, plan, pieces, local_sem, send_sem, recv_sem)
        peers += [(grid.partner("x"), None)] + [(grid.at(other, grid.x, grid.y, grid.c), None) for other in gather.others]
        greet(peers)
        for layer in range(LAYERS):
            make_share(
                sz, gains_ref[layer], biases_ref, layer, upb_ref[layer : layer + 1, :], wide_ref, share_ref.at[layer]
            )
        gather.begin(0)
        for p in range(1, 4):
            plan.later(3.0 + 3.0 * p, functools.partial(gather.begin, p))
        for p in range(4, 8):
            if p == FLAT:
                plan.later(1.0, functools.partial(gather.begin_flat, p, 24.0))
            else:
                plan.later(14.0 + 3.0 * (p - 4), functools.partial(gather.begin, p))

        def need(layer, k):
            gather.need(4 * layer + k)

        def keep(layer):
            for k in range(5):
                copies.start(("weights", layer, k), wholes[k].at[layer], wholes_out[k].at[layer])
    else:
        greet(peers)
        need = lambda layer, k: None
        keep = lambda layer: None

    def save(k, layer):
        source = (q_ref, key_ref, value_ref, att_ref, lse_ref, middle_ref)[k]
        copies.start(("saved", k, layer), source.at[layer], saved_out[k].at[layer])

    fill_mask(sz, mask_ref)
    fill_index(sz, index_ref)
    coarse = coarse_matrix(run)
    rows_of = lambda r: pl.ds(r * run, run)
    for r in range(sz.rows):
        state_ref[rows_of(r), :] = tokens_ref[r].astype(F32)
    all_rims = []
    for layer in range(LAYERS):
        need(layer, 0)
        unpack_small(sz, whole_rows(ws.at[layer], slice(None)), vec, up)
        rims = []
        for r in range(sz.rows):
            hat, _ = normalise(state_ref[rows_of(r), :])
            normed = (hat * vec[0:1, :] + vec[2:3, :]).astype(BF16)
            tops = []
            for kind, bank in ((0, key_ref.at[layer, r]), (1, value_ref.at[layer, r])):
                mixed = dot_nn(normed, whole_rows(wq.at[layer], slice((1 + kind) * model, (2 + kind) * model)))
                if kind == 1:
                    mixed = mixed + vec[4:5, :]
                mixed = mixed.astype(BF16)
                levels = dot_nn(coarse, mixed).astype(BF16)
                base = 0
                for level in range(LEVELS):
                    n = sz.count[level]
                    if level == 0:
                        now = mixed
                    else:
                        now = levels[base : base + n]
                        base += n
                    if level < TOP:
                        bank[pl.ds(sz.offset[level] + BLOCK, n), :] = now
                        rims_out[layer, r, 0, rim_rows(level, kind), :] = now[n - BLOCK :]
                        rims_out[layer, r, 1, rim_rows(level, kind), :] = now[:BLOCK]
                    else:
                        tops.append(now)
            tops_out[layer, r, 0] = jnp.concatenate(tops, axis=0)
            rims.append(
                Rims(
                    sz, rims_out.at[layer, r, 0], rims_out.at[layer, r, 1], tops_out.at[layer, r], low_ref.at[layer, r],
                    high_ref.at[layer, r], tops_ref.at[layer, r], rim_send.at[layer, r], rim_recv.at[layer, r],
                )
            )
            rims[-1].start()
            queries = (dot_nn(normed, whole_rows(wq.at[layer], slice(0, model))) + vec[3:4, :]).astype(BF16)
            q_ref[layer, r] = queries * jnp.asarray(HDIM**-0.5, BF16)
            plan.advance(TIMES["before"])
        save(0, layer)
        all_rims += rims
        for r in range(sz.rows):
            rims[r].arrive()
            place_rims(
                sz, low_ref.at[layer, r], high_ref.at[layer, r], tops_ref.at[layer, r], key_ref.at[layer, r],
                value_ref.at[layer, r],
            )
            attend(
                sz, q_ref.at[layer, r], key_ref.at[layer, r], value_ref.at[layer, r], mask_ref, index_ref,
                att_ref.at[layer, r], lse_ref.at[layer, r], score_ref, weight_ref,
                functools.partial(plan.advance, TIMES["attend"]),
            )
        for k in (1, 2, 3, 4):
            save(k, layer)
        need(layer, 1)
        for r in range(sz.rows):
            rows = rows_of(r)
            middle = state_ref[rows, :] + dot_nn(att_ref[layer, r], whole_rows(wo.at[layer], slice(None))) + vec[5:6, :]
            middle_ref[layer, rows, :] = middle
            hat, _ = normalise(middle)
            second_ref[rows, :] = (hat * vec[1:2, :] + vec[6:7, :]).astype(BF16)
            state_ref[rows, :] = middle + vec[7:8, :]
            plan.advance(TIMES["project"])
        save(5, layer)
        need(layer, 3)
        parts = sz.hidden // model
        for c in range(parts):
            if c == parts // 2:
                need(layer, 2)
            units = slice(c * model, (c + 1) * model)
            for r in range(sz.rows):
                rows = rows_of(r)
                hidden = dot_nn(second_ref[rows, :], whole_rows(wu.at[layer], units)) + up[:, units]
                state_ref[rows, :] += dot_nn(gelu(hidden).astype(BF16), some_rows(wd.at[layer], c * model, model))
            plan.advance(TIMES["forward"])
        keep(layer)
        if layer == 0:
            x_ref[...] = state_ref[...]
            copies.start("x", x_ref, x_out)
        else:
            for r in range(sz.rows):
                out_act_ref[r] = state_ref[rows_of(r), :].astype(BF16)
    plan.flush()
    for rims in all_rims:
        rims.drain()
    if depth:
        gather.drain()
    copies.drain()


WHOLE = pl.BlockSpec(memory_space=pltpu.VMEM)
ANYWHERE = pl.BlockSpec(memory_space=pl.ANY)


def attend_scratch(sz):
    units = sz.chunks * sz.pairs
    coarse = sz.width - sz.start[1]
    wide = ((units, sz.width, 128), F32)
    return [
        ((coarse, 128), jnp.int32), wide, (wide[0], BF16), ((coarse, 128), F32), wide, (wide[0], BF16),
        ((units, coarse, 128), BF16),
    ]


def forward(sz, depth, tokens, weights):
    n, rows, run = sz.model, sz.rows, sz.run
    saved = [
        ((LAYERS, rows, run, n), BF16), ((LAYERS, rows, sz.bank, n), BF16), ((LAYERS, rows, sz.bank, n), BF16),
        ((LAYERS, rows, run, n), BF16), ((LAYERS, rows, sz.chunks, sz.pairs, 128), F32), ((LAYERS, sz.tokens, n), F32),
    ]
    outs = [((rows, run, n), BF16), ((sz.tokens, n), F32)] + saved
    out_specs = [WHOLE] + [ANYWHERE] * (1 + SAVED)
    scratch = []
    if depth:
        full = [((LAYERS, depth, 2, 2, 2) + share.shape[1:], BF16) for share in weights[:4]]
        full.append(((LAYERS, depth, 2, 2, 2, BLOCK, 128), BF16))
        outs += full
        out_specs += [ANYWHERE] * 5
        scratch += full
    rim = sz.rim // rows
    scratch += saved + [
        ((sz.tokens, n), F32), ((8, n), F32), ((1, sz.hidden), F32), ((sz.chunks, sz.width, 128), F32),
        ((sz.tokens, n), BF16), ((sz.tokens, n), F32)] + attend_scratch(sz)[:3] + [((LAYERS, rows, 2, rim, n), BF16),
        ((LAYERS, rows, 1, BLOCK, n), BF16), ((LAYERS, rows, rim, n), BF16), ((LAYERS, rows, rim, n), BF16),
        ((LAYERS, rows, sz.seq, BLOCK, n), BF16),
    ]
    scratch = [pltpu.VMEM(shape, dtype) for shape, dtype in scratch]
    scratch += [pltpu.SemaphoreType.DMA((LAYERS, rows, sz.seq + 1))] * 2
    scratch += [pltpu.SemaphoreType.DMA((LAYERS * (SAVED + 5) + 1,))]
    if depth:
        arrays = 6 * LAYERS
        scratch += [pltpu.VMEM((BLOCK, 128), F32), pltpu.VMEM((LAYERS, BLOCK, 128), BF16)]
        scratch += [pltpu.SemaphoreType.DMA((arrays,))] + [pltpu.SemaphoreType.DMA((arrays, depth + 6))] * 2
    results = pl.pallas_call(
        functools.partial(forward_kernel, sz, depth),
        out_shape=[jax.ShapeDtypeStruct(shape, dtype) for shape, dtype in outs],
        in_specs=[WHOLE] * (1 + len(weights)),
        out_specs=out_specs,
        scratch_shapes=scratch,
        compiler_params=pltpu.CompilerParams(
            collective_id=0, has_side_effects=True, vmem_limit_bytes=VMEM_LIMIT
        ),
        name="forward",
    )(tokens, *weights)
    return results[0], results[1], results[2 : 2 + SAVED], (results[2 + SAVED :] if depth else weights)


def store_blocks(ref, at, columns, value):
    per = ref.shape[4]
    for k in range(value.shape[0] // per):
        i = at + k
        ref[i // 8, (i // 4) % 2, (i // 2) % 2, i % 2, :, columns] = value[k * per : (k + 1) * per]


def unpack_share(sz, small, layer, gains_ref, biases_ref, up_ref):
    place = lax.axis_index("dp") * lax.axis_size("seq") + lax.axis_index("seq")
    wide = up_ref.shape[-1]
    vec, up = small[0:8, 0:BLOCK], small[8:9, 0:wide]
    for j in range(1, 128 // BLOCK):
        vec = jnp.where(place % (128 // BLOCK) == j, small[0:8, j * BLOCK : (j + 1) * BLOCK], vec)
    for j in range(1, 128 // wide):
        up = jnp.where(place % (128 // wide) == j, small[8:9, j * wide : (j + 1) * wide], up)
    gains_ref[layer] = vec[0:2]
    for k in range(6):
        biases_ref[k, layer : layer + 1, :] = vec[2 + k : 3 + k]
    up_ref[layer : layer + 1, :] = up


GRADS = 8
EARLY = 4


def backward_kernel(sz, depth, *refs):
    refs = list(refs)
    take_refs = lambda n: [refs.pop(0) for _ in range(n)]
    prefix_ref, cot_ref, tokens_ref, x_in = take_refs(4)
    saved_in, wholes_in = take_refs(SAVED), take_refs(5)
    gin_ref = take_refs(1)[0]
    out_refs = take_refs(7) if depth else [take_refs(GRADS) for _ in range(LAYERS)]
    (q_ref, key_ref, value_ref, att_ref, lse_ref, middle_ref), (wq, wo, wu, wd, ws) = take_refs(SAVED), take_refs(5)
    (
        x_ref, g_ref, vec, up, mask_ref, second_ref, gd_ref, gs_ref, go_ref, gm_ref, dq_ref, dkey_ref, dvalue_ref,
        gvec_ref, gupb_ref, dk_ref, dv_ref, levels_ref, normed_ref, rims_out, tops_out, low_ref, high_ref, tops_ref,
    ) = take_refs(24)
    index_ref, score_ref, weight_ref, own_ref, back_ref, dscore_ref, coarse_ref = take_refs(7)
    rim_send, rim_recv, copy_sem = take_refs(3)
    model, run = sz.model, sz.run
    half = sz.hidden // 2
    plan, copies = Plan(600e3, 175e3), Copies(copy_sem)
    inside = {"q": q_ref, "key": key_ref, "value": value_ref, "att": att_ref, "lse": lse_ref, "middle": middle_ref,
              "wq": wq, "wo": wo, "wu": wu, "wd": wd, "ws": ws}
    outside = dict(zip(inside, list(saved_in) + list(wholes_in)))

    def load(layer, *names):
        if layer >= 0:
            for name in names:
                copies.start(name, outside[name].at[layer], inside[name])

    load(LAYERS - 1, "middle", "ws", "wu", "wd", "wo", "att", "q", "key", "value", "lse", "wq")
    copies.start("x", x_in, x_ref)
    me, dp = lax.axis_index("seq"), lax.axis_index("dp")
    peers = [((dp, lax.rem(me + k, sz.seq)), None) for k in range(1, sz.seq)]
    scatters = {}
    if depth:
        grads = take_refs(GRADS)
        early = take_refs(EARLY)
        own_grads = lambda layer: (early if layer == 0 else grads[:EARLY]) + grads[EARLY:]
        buffers = [take_refs(SCATTER_BUFFERS) for _ in grads]
        send_sem, recv_sem, free_sem, small_sums = take_refs(4)
        gqkv, gwout, gwup, gwdown = out_refs[:4]
        grid = Grid(depth)
        for layer in reversed(range(LAYERS)):
            sums = [gwup.at[layer, :, 0:half], gwup.at[layer, :, half:], gwdown.at[layer], gwout.at[layer]]
            sums += [gqkv.at[layer, :, k * model : (k + 1) * model] for k in range(3)] + [small_sums.at[layer]]
            scatters[layer] = Scatter(
                grid, plan, own_grads(layer), buffers, sums, send_sem.at[layer], recv_sem.at[layer], free_sem,
                layer < LAYERS - 1, layer > 0,
            )
        peers += [(grid.partner("x"), None)]
        peers += [(grid.at(other, grid.x, grid.y, grid.c), None) for other in scatters[0].others]
    greet(peers)
    fill_mask(sz, mask_ref)
    fill_index(sz, index_ref)
    fill_own(sz, own_ref)
    coarse = coarse_matrix(run)
    rows_of = lambda r: pl.ds(r * run, run)
    per_micro = prefix_ref.shape[0]
    place = me * run + lax.broadcasted_iota(jnp.int32, (run, model), 0)
    for r in range(sz.rows):
        kept = place >= prefix_ref[r % per_micro, r // per_micro]
        g_ref[rows_of(r), :] = jnp.where(kept, cot_ref[r].astype(F32), 0.0)
    all_rims = []
    for layer in reversed(range(LAYERS)):
        gup_a, gup_b, gdown, gout, gq, gk, gv, small_ref = own_grads(layer) if depth else out_refs[layer]

        def launch(*pieces, layer=layer):
            for p in pieces if depth else ():
                begin = functools.partial(scatters[layer].begin, p)
                above = scatters.get(layer + 1)
                if above is None or above.done[p]:
                    begin()
                else:
                    above.next[p] = begin

        def room(*pieces, layer=layer):
            if depth and layer < LAYERS - 1:
                for p in pieces:
                    scatters[layer + 1].need(p)

        gvec_ref[...] = jnp.zeros_like(gvec_ref)
        copies.wait("middle", "ws")
        unpack_small(sz, whole_rows(ws, slice(None)), vec, up)
        load(layer - 1, "ws")
        for r in range(sz.rows):
            rows = rows_of(r)
            hat, _ = normalise(middle_ref[rows, :])
            second_ref[rows, :] = (hat * vec[1:2, :] + vec[6:7, :]).astype(BF16)
            grad = g_ref[rows, :].astype(BF16)
            gd_ref[rows, :] = grad
            gvec_ref[7:8, :] += jnp.sum(grad.astype(F32), axis=0, keepdims=True)
        copies.wait("wu", "wd")
        plan.advance(TIMES["start"])
        parts = sz.hidden // model
        for c in range(parts):
            units = slice(c * model, (c + 1) * model)
            w_up = whole_rows(wu, units)
            hidden = dot_nn(second_ref[...], w_up) + up[:, units]
            active, slope = gelu_both(hidden)
            per = gdown.shape[4]
            store_blocks(gdown, c * model // per, slice(None), dot_tn(active.astype(BF16), gd_ref[...]).astype(BF16))
            grad_hidden = (slope * dot_nt(gd_ref[...], some_rows(wd, c * model, model))).astype(BF16)
            gupb_ref[:, units] = jnp.sum(grad_hidden.astype(F32), axis=0, keepdims=True)
            target, at = (gup_a, gup_b)[c * 2 // parts], c % (parts // 2)
            store_blocks(
                target, 0, slice(at * model, (at + 1) * model), dot_tn(second_ref[...], grad_hidden).astype(BF16)
            )
            back = dot_nt(grad_hidden, w_up)
            if c == 0:
                gs_ref[...] = back
            else:
                gs_ref[...] += back
            if c == parts // 2 - 1:
                launch(0)
            plan.advance(TIMES["back"])
        launch(2, 1)
        load(layer - 1, "wu", "wd")
        copies.wait("wo")
        for r in range(sz.rows):
            rows = rows_of(r)
            hat, inverse = normalise(middle_ref[rows, :])
            grad = gs_ref[rows, :]
            gvec_ref[1:2, :] += jnp.sum(grad * hat, axis=0, keepdims=True)
            gvec_ref[6:7, :] += jnp.sum(grad, axis=0, keepdims=True)
            gm = g_ref[rows, :] + norm_back(grad, hat, inverse, vec[1:2, :])
            gm_ref[rows, :] = gm
            branch = gm.astype(BF16)
            gd_ref[rows, :] = branch
            gvec_ref[5:6, :] += jnp.sum(branch.astype(F32), axis=0, keepdims=True)
            go_ref[r] = dot_nt(branch, whole_rows(wo, slice(None))).astype(BF16)
        plan.advance(TIMES["branch"])
        load(layer - 1, "middle", "wo")
        copies.wait("att", "q", "key", "value", "lse")
        store_blocks(
            gout, 0, slice(None), sum(dot_tn(att_ref[r], gd_ref[rows_of(r), :]) for r in range(sz.rows)).astype(BF16)
        )
        launch(3)
        rims = []
        n = sz.count[TOP]
        for r in range(sz.rows):
            dkey, dvalue = dkey_ref.at[r], dvalue_ref.at[r]
            dkey[...] = jnp.zeros(dkey.shape, F32)
            dvalue[...] = jnp.zeros(dvalue.shape, F32)
            attend_back(
                sz, q_ref.at[r], key_ref.at[r], value_ref.at[r], mask_ref, index_ref, own_ref, lse_ref.at[r],
                go_ref.at[r], dq_ref.at[r], dkey, dvalue, score_ref, back_ref, weight_ref, dscore_ref, coarse_ref,
                functools.partial(plan.advance, TIMES["attend_back"]),
            )
            for kind, bank in ((0, dkey), (1, dvalue)):
                for level in range(TOP):
                    rims_out[layer, r, 0, rim_rows(level, kind), :] = bank[pl.ds(sz.offset[level], BLOCK), :].astype(BF16)
                    rims_out[layer, r, 1, rim_rows(level, kind), :] = bank[
                        pl.ds(sz.offset[level] + BLOCK + sz.count[level], BLOCK), :
                    ].astype(BF16)
            for s in range(sz.seq):
                at = pl.ds(sz.offset[TOP] + s * n, n)
                tops_out[layer, r, s] = jnp.concatenate([dkey[at, :], dvalue[at, :]], axis=0).astype(BF16)
            rims.append(
                Rims(
                    sz, rims_out.at[layer, r, 1], rims_out.at[layer, r, 0], tops_out.at[layer, r], low_ref.at[layer, r],
                    high_ref.at[layer, r], tops_ref.at[layer, r], rim_send.at[layer, r], rim_recv.at[layer, r],
                )
            )
            rims[-1].start()
        all_rims += rims
        load(layer - 1, "att", "q", "key", "value", "lse")
        if layer == LAYERS - 1:
            copies.wait("x")
        layer_input = (lambda r: tokens_ref[r].astype(F32)) if layer == 0 else (lambda r: x_ref[rows_of(r), :])
        for r in range(sz.rows):
            hat, _ = normalise(layer_input(r))
            normed_ref[r] = (hat * vec[0:1, :] + vec[2:3, :]).astype(BF16)
            gvec_ref[3:4, :] += jnp.sum(dq_ref[r].astype(F32), axis=0, keepdims=True)
        room(4)
        store_blocks(gq, 0, slice(None), sum(dot_tn(normed_ref[r], dq_ref[r]) for r in range(sz.rows)).astype(BF16))
        launch(4)
        plan.advance(TIMES["levels"])
        for r in range(sz.rows):
            rims[r].arrive()
            for kind, bank, out in ((0, dkey_ref.at[r], dk_ref), (1, dvalue_ref.at[r], dv_ref)):
                base = 0
                for level in range(LEVELS):
                    n = sz.count[level]
                    if level == TOP:
                        top = sum(tops_ref[layer, r, s, kind * n : kind * n + n, :].astype(F32) for s in range(sz.seq))
                        levels_ref[pl.ds(base, 2 * n), :] = jnp.concatenate(
                            [top, jnp.zeros((n, model), F32)], axis=0
                        ).astype(BF16)
                        continue
                    own = bank[pl.ds(sz.offset[level] + BLOCK, n), :]
                    first = low_ref[layer, r, rim_rows(level, kind), :].astype(F32)
                    final = high_ref[layer, r, rim_rows(level, kind), :].astype(F32)
                    if n == BLOCK:
                        own = own + first + final
                    else:
                        between = [own[BLOCK : n - BLOCK]] if n > 2 * BLOCK else []
                        own = jnp.concatenate([own[:BLOCK] + first, *between, own[n - BLOCK :] + final], axis=0)
                    if level == 0:
                        fine = own
                    else:
                        levels_ref[pl.ds(base, n), :] = own.astype(BF16)
                        base += n
                out[rows_of(r), :] = (fine + dot_tn(coarse, levels_ref[...])).astype(BF16)
            gvec_ref[4:5, :] += jnp.sum(dv_ref[rows_of(r), :].astype(F32), axis=0, keepdims=True)
            plan.advance(TIMES["levels"])
        for k, (out, source) in enumerate(((gk, dk_ref), (gv, dv_ref))):
            room(5 + k)
            store_blocks(
                out, 0, slice(None),
                sum(dot_tn(normed_ref[r], source[rows_of(r), :]) for r in range(sz.rows)).astype(BF16),
            )
            launch(5 + k)
        copies.wait("wq")
        for r in range(sz.rows):
            rows = rows_of(r)
            grad = dot_nt(dq_ref[r], whole_rows(wq, slice(0, model)))
            grad = grad + dot_nt(dk_ref[rows, :], whole_rows(wq, slice(model, 2 * model)))
            grad = grad + dot_nt(dv_ref[rows, :], whole_rows(wq, slice(2 * model, 3 * model)))
            hat, inverse = normalise(layer_input(r))
            gvec_ref[0:1, :] += jnp.sum(grad * hat, axis=0, keepdims=True)
            gvec_ref[2:3, :] += jnp.sum(grad, axis=0, keepdims=True)
            g_ref[rows, :] = gm_ref[rows, :] + norm_back(grad, hat, inverse, vec[0:1, :])
            plan.advance(TIMES["finish"])
        load(layer - 1, "wq")
        if layer == 0:
            copies.start("gin", g_ref, gin_ref)
        room(7)
        for i in range(model // BLOCK):
            top = gvec_ref[:, 128 * (i // 8) : 128 * (i // 8) + 128]
            side = jnp.broadcast_to(gupb_ref[:, 128 * (i // 2) : 128 * (i // 2) + 128], (8, 128))
            store_blocks(small_ref, i, slice(None), jnp.concatenate([top, side], axis=0).astype(BF16))
        launch(7)
    plan.flush()
    if depth:
        for layer in range(LAYERS):
            unpack_share(sz, small_sums[layer], layer, *out_refs[4:7])
    for rim in all_rims:
        rim.drain()
    for scatter in scatters.values():
        scatter.drain()
    copies.drain()


def backward(sz, depth, prefix_len, cotangent, tokens, x, saved, wholes):
    n, rows, run = sz.model, sz.rows, sz.run
    per = sz.hidden * BLOCK // n
    lead = (n // BLOCK // 8, 2, 2, 2)
    half = sz.hidden // 2
    blocks = [(BLOCK, half), (BLOCK, half), (per, n), (BLOCK, n), (BLOCK, n), (BLOCK, n), (BLOCK, n), (BLOCK, 128)]
    pieces = [(lead + block, BF16) for block in blocks]
    outs = [((sz.tokens, n), F32)]
    if depth:
        outs += [((LAYERS,) + shape, F32) for shape in (
            (BLOCK, 3 * n), (BLOCK, n), (BLOCK, sz.hidden), (per, n), (2, BLOCK)
        )]
        outs += [((6, LAYERS, BLOCK), F32), ((LAYERS, per), F32)]
    else:
        outs += pieces * LAYERS
    rim = sz.rim // rows
    scratch = [(array.shape[1:], array.dtype) for array in list(saved) + list(wholes)]
    scratch += [
        ((sz.tokens, n), F32), ((sz.tokens, n), F32), ((8, n), F32), ((1, sz.hidden), F32),
        ((sz.chunks, sz.width, 128), F32), ((sz.tokens, n), BF16),
        ((sz.tokens, n), BF16), ((sz.tokens, n), F32), ((rows, run, n), BF16), ((sz.tokens, n), F32),
        ((rows, run, n), BF16), ((rows, sz.bank, n), F32), ((rows, sz.bank, n), F32), ((8, n), F32),
        ((1, sz.hidden), F32), ((sz.tokens, n), BF16), ((sz.tokens, n), BF16), ((run, n), BF16), ((rows, run, n), BF16),
        ((LAYERS, rows, 2, rim, n), BF16), ((LAYERS, rows, sz.seq, BLOCK, n), BF16), ((LAYERS, rows, rim, n), BF16),
        ((LAYERS, rows, rim, n), BF16), ((LAYERS, rows, sz.seq, BLOCK, n), BF16),
    ]
    scratch += attend_scratch(sz)
    scratch = [pltpu.VMEM(shape, dtype) for shape, dtype in scratch]
    scratch += [pltpu.SemaphoreType.DMA((LAYERS, rows, sz.seq + 1))] * 2
    scratch += [pltpu.SemaphoreType.DMA((LAYERS * (SAVED + 5) + 2,))]
    if depth:
        scratch += [pltpu.VMEM(shape, dtype) for shape, dtype in pieces + pieces[:EARLY]]
        for p, block in enumerate(blocks):
            scratch += scatter_buffers(depth, block, p in FLAT_SUMS)
        scratch += [pltpu.SemaphoreType.DMA((LAYERS, GRADS, 2 + depth))] * 2
        scratch += [pltpu.SemaphoreType.REGULAR((GRADS,)), pltpu.VMEM((LAYERS, BLOCK, 128), F32)]
    result = pl.pallas_call(
        functools.partial(backward_kernel, sz, depth),
        out_shape=[jax.ShapeDtypeStruct(shape, dtype) for shape, dtype in outs],
        in_specs=[pl.BlockSpec(memory_space=pltpu.SMEM), WHOLE, WHOLE] + [ANYWHERE] * (1 + SAVED + 5),
        out_specs=[ANYWHERE] + [WHOLE] * (len(outs) - 1),
        scratch_shapes=scratch,
        compiler_params=pltpu.CompilerParams(
            collective_id=1, has_side_effects=True, vmem_limit_bytes=VMEM_LIMIT
        ),
        name="backward",
    )(prefix_len, cotangent, tokens, x, *saved, *wholes)
    return result[0], list(result[1:])


def direct(rows):
    return lax.axis_size("seq") == 4 and lax.axis_size("dp") % 2 == 0 and rows % BLOCK == 0


def pack_small(gains, biases, up_bias):
    layers, _, features = gains.shape
    tiles = features // BLOCK
    vec = jnp.concatenate([gains, biases], axis=1).reshape(layers, 8, tiles, BLOCK).transpose(0, 2, 1, 3)
    vec = jnp.tile(vec, (1, 1, 1, 128 // BLOCK))
    up = up_bias.reshape(layers, tiles, 1, up_bias.shape[1] // tiles)
    up = jnp.broadcast_to(jnp.tile(up, (1, 1, 1, 128 // up.shape[3])), (layers, tiles, 8, 128))
    return jnp.concatenate([vec, up], axis=2).reshape(layers, features, 128)


def whole_weights(w_qkv, w_out, w_up, w_down, gains, biases, up_bias):
    whole = lambda array, axis: lax.all_gather(array, AXES, axis=axis, tiled=True)
    small = pack_small(whole(gains, 2), whole(biases, 2), whole(up_bias, 1))
    tiles = small.shape[1] // BLOCK
    arrays = (whole(w_qkv, 1), whole(w_out, 1), whole(w_up, 1), whole(w_down, 1), small)
    return [
        array.reshape(LAYERS, tiles // 8, 2, 2, 2, array.shape[1] // tiles, array.shape[2]) for array in arrays
    ]


def collect_kernel(count, *refs):
    for source, target in zip(refs[:count], refs[count:]):
        target[...] = source[...]


def collect(*arrays):
    count = len(arrays)
    return pl.pallas_call(
        functools.partial(collect_kernel, count),
        out_shape=[jax.ShapeDtypeStruct(array.shape, array.dtype) for array in arrays],
        in_specs=[WHOLE] * count,
        out_specs=[WHOLE] * count,
        compiler_params=pltpu.CompilerParams(vmem_limit_bytes=VMEM_LIMIT),
        name="collect",
    )(*arrays)


def scatter_by_sums(sz, parts):
    gqkv, gout, gup, small, gdown = parts
    spread = lambda array, axis: lax.psum_scatter(
        array.astype(F32), AXES, scatter_dimension=axis, tiled=True
    )
    tiles = small.reshape(sz.model // BLOCK, BLOCK, 128)
    vec = jnp.concatenate(
        [tiles[i, :8, BLOCK * (i % 8) : BLOCK * (i % 8) + BLOCK] for i in range(sz.model // BLOCK)], axis=1
    )
    wide = sz.hidden * BLOCK // sz.model
    per = 128 // wide
    up = jnp.concatenate(
        [tiles[i, 8, wide * (i % per) : wide * (i % per) + wide] for i in range(sz.model // BLOCK)], axis=0
    )
    vec = spread(vec, 1)
    return spread(gqkv, 0), spread(gout, 0), spread(gup, 0), spread(gdown, 0), vec[:2], vec[2:], spread(up, 0)


def on_device(
    tokens_in, grad_output, prefix_len, w_qkv, w_out, w_up, w_down, norm_gains, bias_rows, up_bias
):
    micro, rows, run, model = tokens_in.shape
    sz = Sizes(micro * rows, run, model, w_up.shape[2], lax.axis_size("seq"))
    depth = lax.axis_size("dp") // 2 if direct(w_qkv.shape[1]) else 0
    if depth:
        weights = (w_qkv, w_out, w_up, w_down, norm_gains, bias_rows.transpose(1, 0, 2), up_bias)
    else:
        weights = whole_weights(w_qkv, w_out, w_up, w_down, norm_gains, bias_rows, up_bias)
    by_row = (sz.rows, run, model)
    out_act, x_one, saved, wholes = forward(sz, depth, tokens_in.reshape(by_row), weights)
    grad, parts = backward(
        sz, depth, prefix_len.T, grad_output.reshape(by_row), tokens_in.reshape(by_row), x_one, saved, wholes
    )
    if depth:
        out_act, grad, *parts = collect(out_act, grad, *parts)
        results = parts[:5] + [parts[5].transpose(1, 0, 2), parts[6]]
    else:
        layers = []
        for layer in range(LAYERS):
            pieces = [piece.reshape(-1, piece.shape[-1]) for piece in parts[GRADS * layer : GRADS * (layer + 1)]]
            up_a, up_b, down, out, dq, dk, dv, small = pieces
            qkv, up = jnp.concatenate([dq, dk, dv], axis=1), jnp.concatenate([up_a, up_b], axis=1)
            layers.append(scatter_by_sums(sz, (qkv, out, up, small, down)))
        results = [jnp.stack([layer[k] for layer in layers], axis=0) for k in range(7)]
    return (out_act.reshape(tokens_in.shape), grad.reshape(tokens_in.shape), *results)


def solution(mesh):
    tokens, shard = P(None, "dp", "seq", None), P(None, AXES, None)
    small, bias = P(None, None, AXES), P(None, AXES)
    return jax.shard_map(
        on_device,
        mesh=mesh,
        in_specs=(tokens, tokens, P(None, "dp"), shard, shard, shard, shard, small, small, bias),
        out_specs=(tokens, tokens, shard, shard, shard, shard, small, small, bias),
        check_vma=False,
    )
```
